32 devices in a mesh: seq: 16 (over z, x, core), head: 2 (over y).
Axes of the slice: x: 2, y: 2, z: 4, core: 2. Of those that a mesh axis runs over, the one named last changes fastest.
Arguments:
- queries: bfloat16 [6144, 5120], P(('seq', 'head')), may hold values from -6 to 6
- keys: bfloat16 [6144, 1024], P(('seq', 'head')), may hold values from -6 to 6
- values: bfloat16 [6144, 1024], P(('seq', 'head')), may hold values from -6 to 6
- outputs: bfloat16 [6144, 5120], P(('seq', 'head')), may hold values from -2 to 2
- output_gradient: bfloat16 [6144, 5120], P(('seq', 'head')), may hold values from -6 to 6
- lse: bfloat16 [6144, 40], P(('seq', 'head'))
- ranks: int32 [6144], P(('seq', 'head')), may hold values from 0 to 2048, as said below
Outputs:
- query_grads: bfloat16 [6144, 5120], P(('seq', 'head'))
- key_gradient_output: bfloat16 [6144, 1024], P(('seq', 'head'))
- value_gradient: bfloat16 [6144, 1024], P(('seq', 'head'))
The draws below stay inside these ranges and needn't reach their ends.
Inputs may be any that keep to these rules, and one draw needn't show every extreme that they name: Home shard s holds slots s * 384 to (s + 1) * 384 - 1. Its live slots are its first c_s slots, with 1 <= c_s <= 384, holding the consecutive ranks P_s, P_s + 1, ..., where P_s is the number of survivors of the shards before s; its other slots hold 2048. One shard holds exactly 384 survivors; all shards together 2048.
All inputs are finite; a program needn't handle non-finite values.
Results may differ from the reference program's by a relative error of at most 0.0056.
Values may be sent and summed in bfloat16 or wider, within the bound.
No kernel may reach another device: no remote copies, remote signals or barrier semaphores. Data moves between devices by JAX's collectives and lax.ppermute only.
A program may use at most 64 MiB of HBM per device.

```python
import jax
import jax.numpy as jnp
from jax import lax

QUERY_HEADS = 40
KEY_VALUE_HEADS = 8
HEAD_SIZE = 128
BALANCED_TOKENS = 128
SHARD_CAPACITY = 384
N_SEQ = 16


def surviving_counts(key):
    base = jax.random.fold_in(key, 101)
    biggest = jax.random.randint(jax.random.fold_in(base, 1), (), 0, N_SEQ)
    weights = jax.random.randint(jax.random.fold_in(base, 2), (N_SEQ,), 50, 101)
    shard = jnp.arange(N_SEQ, dtype=jnp.int32)
    others = shard != biggest
    weights = jnp.where(others, weights, 0)
    removal = 2 * BALANCED_TOKENS * weights // jnp.sum(weights)
    remaining = 2 * BALANCED_TOKENS - jnp.sum(removal)
    order = jnp.cumsum(others.astype(jnp.int32)) - 1
    extra = (others & (order < remaining)).astype(jnp.int32)
    count_table = jnp.where(others, BALANCED_TOKENS - removal - extra, 3 * BALANCED_TOKENS)
    return count_table.astype(jnp.int32)


def draw_ranks(key, part):
    count_table = surviving_counts(key)
    starts = jnp.cumsum(count_table) - count_table
    within = jnp.arange(3 * BALANCED_TOKENS, dtype=jnp.int32)
    alive = within[None, :] < count_table[:, None]
    result = jnp.where(alive, starts[:, None] + within[None, :], BALANCED_TOKENS * N_SEQ)
    return result.reshape(-1).astype(jnp.int32)


def draw_lse(key, part):
    ranks = draw_ranks(key, part)
    surviving_tokens = BALANCED_TOKENS * N_SEQ
    tree_level = 0.5 * jnp.log(jnp.minimum(ranks, surviving_tokens - 1).astype(jnp.float32) + 1.0)
    noise_key = jax.random.fold_in(key, 202)
    noise = jax.random.uniform(noise_key, (ranks.shape[0], QUERY_HEADS), jnp.float32, 0.0, 1.0)
    return (tree_level[:, None] + noise).astype(jnp.bfloat16)


def block_scale(key, extent, split, smallest, largest):
    def one(axis_at, parts):
        heights = jax.random.uniform(jax.random.fold_in(jax.random.fold_in(key, 6), axis_at), (parts,), jnp.float32, smallest / len(split), largest / len(split))
        return jnp.repeat(jnp.exp(heights), extent[axis_at] // parts).reshape((-1,) + (1,) * (len(extent) - axis_at - 1))

    gain = one(*split[0])
    for cut in split[1:]:
        gain = gain * one(*cut)
    return gain


def centred(stream_key, shape, spread, limit, pieces=(), held_as=jnp.bfloat16):
    factor_of = block_scale(stream_key, shape, pieces, -0.22, 0.18) if pieces else 1.0
    values = jax.random.normal(stream_key, shape, jnp.float32) * spread * factor_of
    return jnp.minimum(jnp.maximum(values, -limit), limit).astype(held_as)


def setup_inputs(seed: int = 0) -> dict:
    splits = jax.random.split(jax.random.key(seed), 8)
    queries = centred(splits[0], (N_SEQ * SHARD_CAPACITY, QUERY_HEADS * HEAD_SIZE), 1.0, 6.0, ((0, 32),))
    keys = centred(splits[1], (N_SEQ * SHARD_CAPACITY, KEY_VALUE_HEADS * HEAD_SIZE), 1.0, 6.0, ((0, 32),))
    values = centred(splits[2], (N_SEQ * SHARD_CAPACITY, KEY_VALUE_HEADS * HEAD_SIZE), 1.0, 6.0, ((0, 32),))
    outputs = centred(splits[3], (N_SEQ * SHARD_CAPACITY, QUERY_HEADS * HEAD_SIZE), 0.3, 2.0, ((0, 32),))
    output_gradient = centred(splits[4], (N_SEQ * SHARD_CAPACITY, QUERY_HEADS * HEAD_SIZE), 1.0, 6.0, ((0, 32),))
    lse = draw_lse(jax.random.fold_in(splits[7], 71), 0)
    ranks = draw_ranks(jax.random.fold_in(splits[7], 71), 0)
    return dict(queries=queries, keys=keys, values=values, outputs=outputs, output_gradient=output_gradient, lse=lse, ranks=ranks)


def head_backward(args):
    query_g, key_gradient, value_g, grad_g, lse_g, delta_g = args
    surviving_tokens = key_gradient.shape[0]
    scale = HEAD_SIZE ** -0.5
    key_f = key_gradient.astype(jnp.float32)
    value_f = value_g.astype(jnp.float32)
    key_owner_rank = jnp.arange(surviving_tokens, dtype=jnp.int32)
    block_list = surviving_tokens // 512
    group_size = query_g.shape[1]
    query_b = query_g.reshape(block_list, 512, group_size, HEAD_SIZE)
    grad_b = grad_g.reshape(block_list, 512, group_size, HEAD_SIZE)
    lse_b = lse_g.reshape(block_list, 512, group_size)
    delta_b = delta_g.reshape(block_list, 512, group_size)

    def step(carry, inputs):
        key_accumulator, value_accumulator = carry
        query_blk, grad_blk, lse_blk, delta_blk, block_index = inputs
        query_rank = block_index * 512 + jnp.arange(512, dtype=jnp.int32)
        query_f = query_blk.astype(jnp.float32)
        grad_f = grad_blk.astype(jnp.float32)
        scores = jnp.einsum("qmc,kc->mqk", query_f, key_f) * scale
        mask = key_owner_rank[None, None, :] <= query_rank[None, :, None]
        probs = jnp.where(mask, jnp.exp(scores - lse_blk.astype(jnp.float32).T[:, :, None]), 0.0)
        dprob = jnp.einsum("qmc,kc->mqk", grad_f, value_f)
        dscore = probs * (dprob - delta_blk.astype(jnp.float32).T[:, :, None])
        probs_low = lax.optimization_barrier(probs.astype(jnp.bfloat16)).astype(jnp.float32)
        dscore_low = lax.optimization_barrier(dscore.astype(jnp.bfloat16)).astype(jnp.float32)
        query_result = scale * jnp.einsum("mqk,kc->qmc", dscore_low, key_f)
        key_accumulator = key_accumulator + scale * jnp.einsum("mqk,qmc->kc", dscore_low, query_f)
        value_accumulator = value_accumulator + jnp.einsum("mqk,qmc->kc", probs_low, grad_f)
        return (key_accumulator, value_accumulator), query_result

    zero_fill = jnp.zeros((surviving_tokens, HEAD_SIZE), jnp.float32)
    (key_accumulator, value_accumulator), query_result = lax.scan(
        step, (zero_fill, zero_fill), (query_b, grad_b, lse_b, delta_b, jnp.arange(block_list, dtype=jnp.int32)))
    return query_result.reshape(surviving_tokens, group_size, HEAD_SIZE), key_accumulator, value_accumulator


def reference(queries, keys, values, outputs, output_gradient, lse, ranks):
    surviving_tokens = BALANCED_TOKENS * N_SEQ
    row_total = ranks.shape[0]
    group_size = QUERY_HEADS // KEY_VALUE_HEADS
    target_rank = jnp.where(ranks < surviving_tokens, ranks, surviving_tokens).astype(jnp.int32)
    slot_index = jnp.zeros((surviving_tokens,), jnp.int32).at[target_rank].set(
        jnp.arange(row_total, dtype=jnp.int32), mode="drop")
    query_shard = queries[slot_index].reshape(surviving_tokens, KEY_VALUE_HEADS, group_size, HEAD_SIZE)
    key_shard = keys[slot_index].reshape(surviving_tokens, KEY_VALUE_HEADS, HEAD_SIZE)
    value_shard = values[slot_index].reshape(surviving_tokens, KEY_VALUE_HEADS, HEAD_SIZE)
    gradient_shard = output_gradient[slot_index].reshape(surviving_tokens, KEY_VALUE_HEADS, group_size, HEAD_SIZE)
    output_shard = outputs[slot_index].reshape(surviving_tokens, KEY_VALUE_HEADS, group_size, HEAD_SIZE)
    logsumexp_shard = lse[slot_index].reshape(surviving_tokens, KEY_VALUE_HEADS, group_size)
    delta_s = jnp.sum(gradient_shard.astype(jnp.float32) * output_shard.astype(jnp.float32), axis=-1).astype(jnp.bfloat16)
    query_result, key_result, value_result = lax.map(head_backward, (
        query_shard.transpose(1, 0, 2, 3), key_shard.transpose(1, 0, 2), value_shard.transpose(1, 0, 2),
        gradient_shard.transpose(1, 0, 2, 3), logsumexp_shard.transpose(1, 0, 2), delta_s.transpose(1, 0, 2)))
    query_row_block = query_result.transpose(1, 0, 2, 3).reshape(surviving_tokens, QUERY_HEADS * HEAD_SIZE).astype(jnp.bfloat16)
    key_row_block = key_result.transpose(1, 0, 2).reshape(surviving_tokens, KEY_VALUE_HEADS * HEAD_SIZE).astype(jnp.bfloat16)
    value_row_block = value_result.transpose(1, 0, 2).reshape(surviving_tokens, KEY_VALUE_HEADS * HEAD_SIZE).astype(jnp.bfloat16)
    query_grads = jnp.zeros((row_total, QUERY_HEADS * HEAD_SIZE), jnp.bfloat16).at[slot_index].set(query_row_block)
    key_gradient_output = jnp.zeros((row_total, KEY_VALUE_HEADS * HEAD_SIZE), jnp.bfloat16).at[slot_index].set(key_row_block)
    value_gradient = jnp.zeros((row_total, KEY_VALUE_HEADS * HEAD_SIZE), jnp.bfloat16).at[slot_index].set(value_row_block)
    return (query_grads, key_gradient_output, value_gradient)
```

```python
import jax
import jax.numpy as jnp
from jax import lax
from jax.experimental import pallas as pl
from jax.experimental.pallas import tpu as pltpu
from jax.sharding import Mesh
from jax.sharding import PartitionSpec as P

QUERY_HEADS = 40
KEY_VALUE_HEADS = 8
HEAD_SIZE = 128
BALANCED_TOKENS = 128


block_keys = 512


def per_device(queries, keys, values, outputs, output_gradient, lse, ranks, seq="seq"):
    sequence_count = lax.axis_size(seq)
    head_total = lax.axis_size("head")
    home_rows = queries.shape[0]
    capacity = home_rows * head_total
    slots = capacity // sequence_count
    surviving_tokens = BALANCED_TOKENS * sequence_count
    group_size = QUERY_HEADS // KEY_VALUE_HEADS
    local_key_value = KEY_VALUE_HEADS // head_total
    scale = HEAD_SIZE ** (-0.5)

    def split_heads(array):
        return array.reshape(home_rows, head_total, array.shape[1] // head_total)

    moved = (
        lax.all_to_all(split_heads(queries), "head", split_axis=1, concat_axis=0, tiled=True),
        lax.all_to_all(split_heads(keys), "head", split_axis=1, concat_axis=0, tiled=True),
        lax.all_to_all(split_heads(values), "head", split_axis=1, concat_axis=0, tiled=True),
        lax.all_to_all(
            split_heads(output_gradient), "head", split_axis=1, concat_axis=0, tiled=True
        ),
        lax.all_to_all(split_heads(lse), "head", split_axis=1, concat_axis=0, tiled=True),
        lax.all_to_all(split_heads(outputs), "head", split_axis=1, concat_axis=0, tiled=True),
    )
    shard_rank_list = lax.all_gather(ranks, "head", axis=0, tiled=True)
    first_rank = shard_rank_list[0]
    living_count = jnp.sum((shard_rank_list < surviving_tokens).astype(jnp.int32))
    table = lax.all_gather(
        jnp.stack([first_rank, living_count])[None, :], seq, axis=0, tiled=True
    )

    def to_pairs(array):
        flat = array.reshape(slots, sequence_count, array.shape[-1])
        return jnp.roll(flat, first_rank, axis=1)

    arrived = (
        lax.all_to_all(to_pairs(moved[0]), seq, split_axis=1, concat_axis=1, tiled=True),
        lax.all_to_all(to_pairs(moved[1]), seq, split_axis=1, concat_axis=1, tiled=True),
        lax.all_to_all(to_pairs(moved[2]), seq, split_axis=1, concat_axis=1, tiled=True),
        lax.all_to_all(to_pairs(moved[3]), seq, split_axis=1, concat_axis=1, tiled=True),
        lax.all_to_all(to_pairs(moved[4]), seq, split_axis=1, concat_axis=1, tiled=True),
        lax.all_to_all(to_pairs(moved[5]), seq, split_axis=1, concat_axis=1, tiled=True),
    )
    my_index = lax.axis_index(seq)
    starts = table[:, 0]
    count_table = table[:, 1]
    offset = (my_index - starts) % sequence_count
    within = jnp.arange(slots, dtype=jnp.int32)[:, None] * sequence_count + offset[None, :]
    alive = within < count_table[None, :]
    target_rank = jnp.where(
        alive, (starts[None, :] + within) // sequence_count, BALANCED_TOKENS
    ).reshape(-1)

    def place(array):
        width = array.shape[-1]
        return (
            jnp.zeros((BALANCED_TOKENS, width), array.dtype)
            .at[target_rank]
            .set(array.reshape(slots * sequence_count, width), mode="drop")
        )

    query_row_block = place(arrived[0]).reshape(
        BALANCED_TOKENS, local_key_value, group_size, HEAD_SIZE
    )
    key_row_block = place(arrived[1]).reshape(BALANCED_TOKENS, local_key_value, HEAD_SIZE)
    value_row_block = place(arrived[2]).reshape(BALANCED_TOKENS, local_key_value, HEAD_SIZE)
    grad_rows = place(arrived[3]).reshape(BALANCED_TOKENS, local_key_value, group_size, HEAD_SIZE)
    lse_rows = (
        place(arrived[4]).astype(jnp.float32).reshape(BALANCED_TOKENS, local_key_value, group_size)
    )
    out_rows = (
        place(arrived[5])
        .astype(jnp.float32)
        .reshape(BALANCED_TOKENS, local_key_value, group_size, HEAD_SIZE)
    )
    delta_rows = (
        jnp.sum(grad_rows.astype(jnp.float32) * out_rows, axis=-1)
        .astype(jnp.bfloat16)
        .astype(jnp.float32)
    )
    gathered = (
        lax.all_gather(key_row_block, seq, axis=0, tiled=True),
        lax.all_gather(value_row_block, seq, axis=0, tiled=True),
    )
    all_keys = gathered[0].reshape(sequence_count, BALANCED_TOKENS, local_key_value, HEAD_SIZE)
    all_values = gathered[1].reshape(sequence_count, BALANCED_TOKENS, local_key_value, HEAD_SIZE)
    rows_per = block_keys // sequence_count
    inner = 1
    outer = BALANCED_TOKENS // rows_per // inner
    query_rank = jnp.arange(BALANCED_TOKENS, dtype=jnp.int32) * sequence_count + my_index
    lse_t = lse_rows.transpose(1, 2, 0)
    delta_t = delta_rows.transpose(1, 2, 0)
    position = jnp.arange(sequence_count * rows_per, dtype=jnp.int32)

    def key_step(query_acc, row_start):
        key_blk = lax.dynamic_slice_in_dim(all_keys, row_start, rows_per, 1).reshape(
            sequence_count * rows_per, local_key_value, HEAD_SIZE
        )
        value_blk = lax.dynamic_slice_in_dim(all_values, row_start, rows_per, 1).reshape(
            sequence_count * rows_per, local_key_value, HEAD_SIZE
        )
        key_owner_rank = (row_start + position % rows_per) * sequence_count + position // rows_per
        mask = key_owner_rank[None, None, None, :] <= query_rank[None, None, :, None]
        scores = (
            jnp.einsum(
                "rgmc,kgc->gmrk", query_row_block, key_blk, preferred_element_type=jnp.float32
            )
            * scale
        )
        probs = jnp.where(mask, jnp.exp(scores - lse_t[..., None]), 0.0)
        dprob = jnp.einsum(
            "rgmc,kgc->gmrk", grad_rows, value_blk, preferred_element_type=jnp.float32
        )
        dscore = probs * (dprob - delta_t[..., None])
        probs_low = probs.astype(jnp.bfloat16)
        dscore_low = dscore.astype(jnp.bfloat16)
        query_acc = query_acc + scale * jnp.einsum(
            "gmrk,kgc->rgmc", dscore_low, key_blk, preferred_element_type=jnp.float32
        )
        key_part = scale * jnp.einsum(
            "gmrk,rgmc->kgc", dscore_low, query_row_block, preferred_element_type=jnp.float32
        )
        value_part = jnp.einsum(
            "gmrk,rgmc->kgc", probs_low, grad_rows, preferred_element_type=jnp.float32
        )
        return (
            query_acc,
            key_part.reshape(sequence_count, rows_per, local_key_value * HEAD_SIZE),
            value_part.reshape(sequence_count, rows_per, local_key_value * HEAD_SIZE),
        )

    def outer_step(query_acc, outer_index):

        def inner_step(query_inner, inner_index):
            row_start = (outer_index * inner + inner_index) * rows_per
            query_new, key_part, value_part = key_step(query_inner, row_start)
            return (query_new, (key_part, value_part))

        query_acc, (key_parts, value_parts) = lax.scan(
            inner_step, query_acc, jnp.arange(inner, dtype=jnp.int32)
        )
        key_parts = key_parts.transpose(1, 0, 2, 3).reshape(
            sequence_count, inner * rows_per, local_key_value * HEAD_SIZE
        )
        value_parts = value_parts.transpose(1, 0, 2, 3).reshape(
            sequence_count, inner * rows_per, local_key_value * HEAD_SIZE
        )
        received = (
            lax.all_to_all(key_parts, seq, split_axis=0, concat_axis=0, tiled=True),
            lax.all_to_all(value_parts, seq, split_axis=0, concat_axis=0, tiled=True),
        )
        return (query_acc, (jnp.sum(received[0], axis=0), jnp.sum(received[1], axis=0)))

    start_acc = jnp.zeros((BALANCED_TOKENS, local_key_value, group_size, HEAD_SIZE), jnp.float32)
    query_acc, (key_sums, value_sums) = lax.scan(
        outer_step, start_acc, jnp.arange(outer, dtype=jnp.int32)
    )
    query_done = query_acc.reshape(
        BALANCED_TOKENS, local_key_value * group_size * HEAD_SIZE
    ).astype(jnp.bfloat16)
    key_done = key_sums.reshape(BALANCED_TOKENS, local_key_value * HEAD_SIZE).astype(jnp.bfloat16)
    value_done = value_sums.reshape(BALANCED_TOKENS, local_key_value * HEAD_SIZE).astype(
        jnp.bfloat16
    )
    safe_rows = jnp.minimum(target_rank, BALANCED_TOKENS - 1)
    alive_flat = alive.reshape(-1)

    def collect(array):
        picked = jnp.where(alive_flat[:, None], array[safe_rows], jnp.zeros((), array.dtype))
        return picked.reshape(slots, sequence_count, array.shape[-1])

    returned = (
        lax.all_to_all(collect(query_done), seq, split_axis=1, concat_axis=1, tiled=True),
        lax.all_to_all(collect(key_done), seq, split_axis=1, concat_axis=1, tiled=True),
        lax.all_to_all(collect(value_done), seq, split_axis=1, concat_axis=1, tiled=True),
    )

    def to_home(array):
        unrolled = jnp.roll(array, -first_rank, axis=1)
        return unrolled.reshape(capacity, 1, array.shape[-1])

    homed = (
        lax.all_to_all(to_home(returned[0]), "head", split_axis=0, concat_axis=1, tiled=True),
        lax.all_to_all(to_home(returned[1]), "head", split_axis=0, concat_axis=1, tiled=True),
        lax.all_to_all(to_home(returned[2]), "head", split_axis=0, concat_axis=1, tiled=True),
    )
    query_grads = homed[0].reshape(home_rows, head_total * homed[0].shape[-1])
    key_gradient_output = homed[1].reshape(home_rows, head_total * homed[1].shape[-1])
    value_gradient = homed[2].reshape(home_rows, head_total * homed[2].shape[-1])
    return (query_grads, key_gradient_output, value_gradient)


LOG2E = 1.4426950408889634
KEY_TILE = 256
ROW_TILE = 128
INFO_ROWS = 16


def attention_kernel(
    counts_ref, limits_ref, q_ref, do_ref, lse_ref, delta_ref, bound_ref, kv0, kv1, kv2, kv3,
    dq_ref, d0, d1, d2, d3, dqt, acc_k, acc_v, tiles,
):
    home_rows = q_ref.shape[0] // counts_ref.shape[0]
    blocks = counts_ref.shape[0]
    group = q_ref.shape[1] // HEAD_SIZE
    scale = HEAD_SIZE ** (-0.5)
    shift = home_rows - ROW_TILE

    def add_tile(n, tile, live):
        @pl.when(live)
        def _():
            tiles[n] = tile

        return n + live.astype(jnp.int32)

    live_tiles = jnp.int32(0)
    for block in range(blocks):
        for t in range(2):
            live_tiles = add_tile(live_tiles, 2 * block + t, counts_ref[block] > t * ROW_TILE)

    dq_ref[...] = jnp.zeros_like(dq_ref)

    def zero_tile(n, carry):
        dqt[tiles[n]] = jnp.zeros(dqt.shape[1:], jnp.float32)
        return carry

    lax.fori_loop(0, live_tiles, zero_tile, 0)

    def row_start(tile):
        return pl.multiple_of((tile // 2) * home_rows + (tile % 2) * shift, 64)

    def stack(ref, tile):
        rows = ref[pl.ds(row_start(tile), ROW_TILE), :]
        return jnp.concatenate(
            [rows[:, h * HEAD_SIZE : (h + 1) * HEAD_SIZE] for h in range(group)], axis=0
        )

    def run_block(index, kv, out):
        limit = limits_ref[index]
        key_tiles = (limit + KEY_TILE - 1) // KEY_TILE
        out[...] = jnp.zeros_like(out)

        def key_step(kt, carry):
            start = pl.multiple_of(kt * KEY_TILE, KEY_TILE)
            key = kv[pl.ds(start, KEY_TILE), :HEAD_SIZE]
            value = kv[pl.ds(start, KEY_TILE), HEAD_SIZE:]
            key_t = key.T
            acc_k[...] = jnp.zeros_like(acc_k)
            acc_v[...] = jnp.zeros_like(acc_v)

            def row_step(n, inner):
                tile = tiles[n]
                q = stack(q_ref, tile)
                do = stack(do_ref, tile)
                lse = lse_ref[pl.ds(tile, 1), :]
                delta = delta_ref[pl.ds(tile, 1), :]
                bound = bound_ref[pl.ds(tile, 1), :]
                if index > 0:
                    bound = jnp.where(bound >= 0, limit - 1, -1)
                position = start + lax.broadcasted_iota(jnp.int32, (KEY_TILE, 1), 0)
                dims = (((1,), (1,)), ((), ()))
                scores = lax.dot_general(key, q, dims, preferred_element_type=jnp.float32)
                prob = jnp.where(
                    position <= bound, jnp.exp2(scores * (scale * LOG2E) - lse), 0.0
                )
                dprob = lax.dot_general(value, do, dims, preferred_element_type=jnp.float32)
                dscore = (prob * (dprob - delta)).astype(jnp.bfloat16)
                acc_v[...] += jnp.dot(
                    prob.astype(jnp.bfloat16), do, preferred_element_type=jnp.float32
                )
                acc_k[...] += jnp.dot(dscore, q, preferred_element_type=jnp.float32)
                dqt[tile] += jnp.dot(key_t, dscore, preferred_element_type=jnp.float32)
                return inner

            lax.fori_loop(0, live_tiles, row_step, 0)
            out[pl.ds(start, KEY_TILE), :HEAD_SIZE] = (acc_k[...] * scale).astype(out.dtype)
            out[pl.ds(start, KEY_TILE), HEAD_SIZE:] = acc_v[...].astype(out.dtype)
            return carry

        lax.fori_loop(0, key_tiles, key_step, 0)

    run_block(3, kv3, d3)
    run_block(2, kv2, d2)
    run_block(1, kv1, d1)
    run_block(0, kv0, d0)

    def finish(n, carry):
        tile = tiles[n]
        block = tile // 2

        def put(offset, first):
            for h in range(group):
                part = (dqt[tile, :, h * HEAD_SIZE : (h + 1) * HEAD_SIZE] * scale).T
                start = pl.multiple_of(block * home_rows + offset, 64)
                dq_ref[pl.ds(start, ROW_TILE - first), h * HEAD_SIZE : (h + 1) * HEAD_SIZE] = part[
                    first:
                ].astype(dq_ref.dtype)

        @pl.when(tile % 2 == 0)
        def _():
            put(0, 0)

        @pl.when(tile % 2 == 1)
        def _():
            put(ROW_TILE, 2 * ROW_TILE - home_rows)

        return carry

    lax.fori_loop(0, live_tiles, finish, 0)


def attention(counts, limits, q, do, lse, delta, bound, kvs):
    capacity = d_rows = kvs[0].shape[0]
    plane_rows, width = q.shape
    bf16, f32 = jnp.bfloat16, jnp.float32
    smem = pl.BlockSpec(memory_space=pltpu.SMEM)
    vmem = pl.BlockSpec(memory_space=pltpu.VMEM)
    columns = 2 * HEAD_SIZE
    tile_count = 2 * counts.shape[0]
    return pl.pallas_call(
        attention_kernel,
        out_shape=(
            jax.ShapeDtypeStruct((plane_rows, width), bf16),
            jax.ShapeDtypeStruct((capacity, columns), f32),
            jax.ShapeDtypeStruct((capacity, columns), bf16),
            jax.ShapeDtypeStruct((capacity, columns), bf16),
            jax.ShapeDtypeStruct((capacity, columns), bf16),
        ),
        in_specs=[smem, smem] + [vmem] * 9,
        out_specs=[vmem] * 5,
        scratch_shapes=[
            pltpu.VMEM((tile_count, HEAD_SIZE, width), f32),
            pltpu.VMEM((KEY_TILE, HEAD_SIZE), f32),
            pltpu.VMEM((KEY_TILE, HEAD_SIZE), f32),
            pltpu.SMEM((tile_count + 1,), jnp.int32),
        ],
        compiler_params=pltpu.CompilerParams(vmem_limit_bytes=48 * 1024 * 1024),
        cost_estimate=pl.CostEstimate(
            flops=10_000_000_000, bytes_accessed=12_000_000, transcendentals=8_000_000
        ),
        name="attention",
    )(counts, limits, q, do, lse, delta, bound, *kvs)


def plane_device(queries, keys, values, outputs, output_gradient, lse, ranks):
    planes = lax.axis_size("outer")
    plane = ("inner", "head")
    blocks = lax.axis_size(plane)
    home_rows = queries.shape[0]
    plane_rows = blocks * home_rows
    capacity = plane_rows // 2
    surviving_tokens = BALANCED_TOKENS * planes * blocks // 2
    surviving_tokens = BALANCED_TOKENS * planes * lax.axis_size("inner")
    group_size = QUERY_HEADS // KEY_VALUE_HEADS
    bf16, f32 = jnp.bfloat16, jnp.float32

    count = jnp.sum((ranks < surviving_tokens).astype(jnp.int32))
    delta = jnp.sum(
        (output_gradient.astype(f32) * outputs.astype(f32)).reshape(
            home_rows, QUERY_HEADS, HEAD_SIZE
        ),
        axis=-1,
    ).astype(bf16)

    pairs = jnp.stack(
        [keys.reshape(home_rows, blocks, HEAD_SIZE), values.reshape(home_rows, blocks, HEAD_SIZE)],
        axis=2,
    ).reshape(home_rows, blocks, 2 * HEAD_SIZE)
    pairs = pairs.transpose(1, 0, 2)
    small = jnp.concatenate(
        [
            lse.T.reshape(blocks, group_size, home_rows),
            delta.T.reshape(blocks, group_size, home_rows),
            jnp.full((blocks, 1, home_rows), count.astype(bf16)),
        ],
        axis=1,
    )
    small = jnp.pad(
        small, ((0, 0), (0, INFO_ROWS - small.shape[1]), (0, 2 * HEAD_SIZE - home_rows))
    )
    sent = jnp.concatenate([pairs, small], axis=1)
    arrived = lax.all_to_all(sent, plane, split_axis=0, concat_axis=0, tiled=True)
    q = lax.all_to_all(queries, plane, split_axis=1, concat_axis=0, tiled=True)
    do = lax.all_to_all(output_gradient, plane, split_axis=1, concat_axis=0, tiled=True)

    info = arrived[:, home_rows:, :home_rows].astype(f32)
    counts = info[:, 2 * group_size, 0].astype(jnp.int32)
    starts = jnp.cumsum(counts) - counts
    total = jnp.sum(counts)

    within = jnp.arange(home_rows, dtype=jnp.int32)
    local = jnp.where(within[None, :] < counts[:, None], starts[:, None] + within[None, :], -1)
    pick = (
        jnp.arange(capacity, dtype=jnp.int32)[:, None] == local.reshape(1, plane_rows)
    ).astype(bf16)
    plane_kv = arrived[:, :home_rows].reshape(plane_rows, 2 * HEAD_SIZE)
    mine = jnp.dot(pick, plane_kv, preferred_element_type=f32).astype(bf16)
    tail = jnp.zeros((INFO_ROWS, 2 * HEAD_SIZE), bf16).at[0, :blocks].set(counts.astype(bf16))
    shipped = jnp.concatenate([mine, tail], axis=0)

    up = [
        lax.ppermute(shipped, "outer", [(i, i + k) for i in range(planes - k)])
        for k in range(1, planes)
    ]
    limits = jnp.stack(
        [total] + [jnp.sum(u[capacity, :blocks].astype(f32)).astype(jnp.int32) for u in up]
    )
    worst = total
    for k in range(1, planes):
        other = lax.ppermute(
            jnp.full((8, 128), total), "outer", [(i, i ^ k) for i in range(planes)]
        )
        worst = jnp.maximum(worst, other[0, 0])

    def tiled_rows(array):
        first = array[:, :, :ROW_TILE]
        second = array[:, :, home_rows - ROW_TILE :]
        return jnp.stack([first, second], axis=1).reshape(2 * blocks, group_size * ROW_TILE)

    lse_rows = tiled_rows(info[:, :group_size] * LOG2E)
    delta_rows = tiled_rows(info[:, group_size : 2 * group_size])
    again = jnp.arange(ROW_TILE) < 2 * ROW_TILE - home_rows
    bound = jnp.stack(
        [local[:, :ROW_TILE], jnp.where(again[None, :], -1, local[:, home_rows - ROW_TILE :])],
        axis=1,
    ).reshape(2 * blocks, ROW_TILE)
    bound = jnp.tile(bound, (1, group_size))

    dq, own, *down = attention(
        counts, jnp.minimum(limits, capacity), q, do, lse_rows, delta_rows, bound,
        [mine] + [u[:capacity] for u in up],
    )
    for k in range(1, planes):
        back = lax.ppermute(down[k - 1], "outer", [(i + k, i) for i in range(planes - k)])
        own = own + back.astype(f32)
    spread = lax.dot_general(
        pick, own.astype(bf16), (((0,), (0,)), ((), ())), preferred_element_type=f32
    ).astype(bf16)
    dq_home = lax.all_to_all(dq, plane, split_axis=0, concat_axis=1, tiled=True)
    kv_home = lax.all_to_all(
        spread.reshape(blocks, home_rows, 2 * HEAD_SIZE),
        plane, split_axis=0, concat_axis=0, tiled=True,
    )
    dk = kv_home[:, :, :HEAD_SIZE].transpose(1, 0, 2).reshape(home_rows, blocks * HEAD_SIZE)
    dv = kv_home[:, :, HEAD_SIZE:].transpose(1, 0, 2).reshape(home_rows, blocks * HEAD_SIZE)
    return (dq_home, dk, dv), worst <= capacity


def solution(mesh):
    spec = P(("seq", "head"), None)
    general = jax.shard_map(
        per_device,
        mesh=mesh,
        in_specs=(spec,) * 6 + (P(("seq", "head")),),
        out_specs=(spec,) * 3,
        check_vma=False,
    )
    heads = mesh.shape["head"]
    inner = max(KEY_VALUE_HEADS // heads, 1)
    planes = mesh.shape["seq"] // inner
    if planes != 4:
        return general

    def both(*args):
        def device(*blocks):
            fast, fits = plane_device(*blocks)
            slow = lambda: per_device(*blocks, seq=("outer", "inner"))
            return lax.cond(fits, lambda: fast, slow)

        folded = Mesh(mesh.devices.reshape(planes, inner, heads), ("outer", "inner", "head"))
        axes = ("outer", "inner", "head")
        return jax.shard_map(
            device,
            mesh=folded,
            in_specs=(P(axes, None),) * 6 + (P(axes),),
            out_specs=(P(axes, None),) * 3,
            check_vma=False,
        )(*args)

    return both
```

```python
import jax
import jax.numpy as jnp
from jax import lax
from jax.experimental import pallas as pl
from jax.experimental.pallas import tpu as pltpu
from jax.sharding import Mesh
from jax.sharding import PartitionSpec as P

QUERY_HEADS = 40
KEY_VALUE_HEADS = 8
HEAD_SIZE = 128
BALANCED_TOKENS = 128


block_keys = 512


def per_device(queries, keys, values, outputs, output_gradient, lse, ranks, seq="seq"):
    sequence_count = lax.axis_size(seq)
    head_total = lax.axis_size("head")
    home_rows = queries.shape[0]
    capacity = home_rows * head_total
    slots = capacity // sequence_count
    surviving_tokens = BALANCED_TOKENS * sequence_count
    group_size = QUERY_HEADS // KEY_VALUE_HEADS
    local_key_value = KEY_VALUE_HEADS // head_total
    scale = HEAD_SIZE ** (-0.5)

    def split_heads(array):
        return array.reshape(home_rows, head_total, array.shape[1] // head_total)

    moved = (
        lax.all_to_all(split_heads(queries), "head", split_axis=1, concat_axis=0, tiled=True),
        lax.all_to_all(split_heads(keys), "head", split_axis=1, concat_axis=0, tiled=True),
        lax.all_to_all(split_heads(values), "head", split_axis=1, concat_axis=0, tiled=True),
        lax.all_to_all(
            split_heads(output_gradient), "head", split_axis=1, concat_axis=0, tiled=True
        ),
        lax.all_to_all(split_heads(lse), "head", split_axis=1, concat_axis=0, tiled=True),
        lax.all_to_all(split_heads(outputs), "head", split_axis=1, concat_axis=0, tiled=True),
    )
    shard_rank_list = lax.all_gather(ranks, "head", axis=0, tiled=True)
    first_rank = shard_rank_list[0]
    living_count = jnp.sum((shard_rank_list < surviving_tokens).astype(jnp.int32))
    table = lax.all_gather(
        jnp.stack([first_rank, living_count])[None, :], seq, axis=0, tiled=True
    )

    def to_pairs(array):
        flat = array.reshape(slots, sequence_count, array.shape[-1])
        return jnp.roll(flat, first_rank, axis=1)

    arrived = (
        lax.all_to_all(to_pairs(moved[0]), seq, split_axis=1, concat_axis=1, tiled=True),
        lax.all_to_all(to_pairs(moved[1]), seq, split_axis=1, concat_axis=1, tiled=True),
        lax.all_to_all(to_pairs(moved[2]), seq, split_axis=1, concat_axis=1, tiled=True),
        lax.all_to_all(to_pairs(moved[3]), seq, split_axis=1, concat_axis=1, tiled=True),
        lax.all_to_all(to_pairs(moved[4]), seq, split_axis=1, concat_axis=1, tiled=True),
        lax.all_to_all(to_pairs(moved[5]), seq, split_axis=1, concat_axis=1, tiled=True),
    )
    my_index = lax.axis_index(seq)
    starts = table[:, 0]
    count_table = table[:, 1]
    offset = (my_index - starts) % sequence_count
    within = jnp.arange(slots, dtype=jnp.int32)[:, None] * sequence_count + offset[None, :]
    alive = within < count_table[None, :]
    target_rank = jnp.where(
        alive, (starts[None, :] + within) // sequence_count, BALANCED_TOKENS
    ).reshape(-1)

    def place(array):
        width = array.shape[-1]
        return (
            jnp.zeros((BALANCED_TOKENS, width), array.dtype)
            .at[target_rank]
            .set(array.reshape(slots * sequence_count, width), mode="drop")
        )

    query_row_block = place(arrived[0]).reshape(
        BALANCED_TOKENS, local_key_value, group_size, HEAD_SIZE
    )
    key_row_block = place(arrived[1]).reshape(BALANCED_TOKENS, local_key_value, HEAD_SIZE)
    value_row_block = place(arrived[2]).reshape(BALANCED_TOKENS, local_key_value, HEAD_SIZE)
    grad_rows = place(arrived[3]).reshape(BALANCED_TOKENS, local_key_value, group_size, HEAD_SIZE)
    lse_rows = (
        place(arrived[4]).astype(jnp.float32).reshape(BALANCED_TOKENS, local_key_value, group_size)
    )
    out_rows = (
        place(arrived[5])
        .astype(jnp.float32)
        .reshape(BALANCED_TOKENS, local_key_value, group_size, HEAD_SIZE)
    )
    delta_rows = (
        jnp.sum(grad_rows.astype(jnp.float32) * out_rows, axis=-1)
        .astype(jnp.bfloat16)
        .astype(jnp.float32)
    )
    gathered = (
        lax.all_gather(key_row_block, seq, axis=0, tiled=True),
        lax.all_gather(value_row_block, seq, axis=0, tiled=True),
    )
    all_keys = gathered[0].reshape(sequence_count, BALANCED_TOKENS, local_key_value, HEAD_SIZE)
    all_values = gathered[1].reshape(sequence_count, BALANCED_TOKENS, local_key_value, HEAD_SIZE)
    rows_per = block_keys // sequence_count
    inner = 1
    outer = BALANCED_TOKENS // rows_per // inner
    query_rank = jnp.arange(BALANCED_TOKENS, dtype=jnp.int32) * sequence_count + my_index
    lse_t = lse_rows.transpose(1, 2, 0)
    delta_t = delta_rows.transpose(1, 2, 0)
    position = jnp.arange(sequence_count * rows_per, dtype=jnp.int32)

    def key_step(query_acc, row_start):
        key_blk = lax.dynamic_slice_in_dim(all_keys, row_start, rows_per, 1).reshape(
            sequence_count * rows_per, local_key_value, HEAD_SIZE
        )
        value_blk = lax.dynamic_slice_in_dim(all_values, row_start, rows_per, 1).reshape(
            sequence_count * rows_per, local_key_value, HEAD_SIZE
        )
        key_owner_rank = (row_start + position % rows_per) * sequence_count + position // rows_per
        mask = key_owner_rank[None, None, None, :] <= query_rank[None, None, :, None]
        scores = (
            jnp.einsum(
                "rgmc,kgc->gmrk", query_row_block, key_blk, preferred_element_type=jnp.float32
            )
            * scale
        )
        probs = jnp.where(mask, jnp.exp(scores - lse_t[..., None]), 0.0)
        dprob = jnp.einsum(
            "rgmc,kgc->gmrk", grad_rows, value_blk, preferred_element_type=jnp.float32
        )
        dscore = probs * (dprob - delta_t[..., None])
        probs_low = probs.astype(jnp.bfloat16)
        dscore_low = dscore.astype(jnp.bfloat16)
        query_acc = query_acc + scale * jnp.einsum(
            "gmrk,kgc->rgmc", dscore_low, key_blk, preferred_element_type=jnp.float32
        )
        key_part = scale * jnp.einsum(
            "gmrk,rgmc->kgc", dscore_low, query_row_block, preferred_element_type=jnp.float32
        )
        value_part = jnp.einsum(
            "gmrk,rgmc->kgc", probs_low, grad_rows, preferred_element_type=jnp.float32
        )
        return (
            query_acc,
            key_part.reshape(sequence_count, rows_per, local_key_value * HEAD_SIZE),
            value_part.reshape(sequence_count, rows_per, local_key_value * HEAD_SIZE),
        )

    def outer_step(query_acc, outer_index):

        def inner_step(query_inner, inner_index):
            row_start = (outer_index * inner + inner_index) * rows_per
            query_new, key_part, value_part = key_step(query_inner, row_start)
            return (query_new, (key_part, value_part))

        query_acc, (key_parts, value_parts) = lax.scan(
            inner_step, query_acc, jnp.arange(inner, dtype=jnp.int32)
        )
        key_parts = key_parts.transpose(1, 0, 2, 3).reshape(
            sequence_count, inner * rows_per, local_key_value * HEAD_SIZE
        )
        value_parts = value_parts.transpose(1, 0, 2, 3).reshape(
            sequence_count, inner * rows_per, local_key_value * HEAD_SIZE
        )
        received = (
            lax.all_to_all(key_parts, seq, split_axis=0, concat_axis=0, tiled=True),
            lax.all_to_all(value_parts, seq, split_axis=0, concat_axis=0, tiled=True),
        )
        return (query_acc, (jnp.sum(received[0], axis=0), jnp.sum(received[1], axis=0)))

    start_acc = jnp.zeros((BALANCED_TOKENS, local_key_value, group_size, HEAD_SIZE), jnp.float32)
    query_acc, (key_sums, value_sums) = lax.scan(
        outer_step, start_acc, jnp.arange(outer, dtype=jnp.int32)
    )
    query_done = query_acc.reshape(
        BALANCED_TOKENS, local_key_value * group_size * HEAD_SIZE
    ).astype(jnp.bfloat16)
    key_done = key_sums.reshape(BALANCED_TOKENS, local_key_value * HEAD_SIZE).astype(jnp.bfloat16)
    value_done = value_sums.reshape(BALANCED_TOKENS, local_key_value * HEAD_SIZE).astype(
        jnp.bfloat16
    )
    safe_rows = jnp.minimum(target_rank, BALANCED_TOKENS - 1)
    alive_flat = alive.reshape(-1)

    def collect(array):
        picked = jnp.where(alive_flat[:, None], array[safe_rows], jnp.zeros((), array.dtype))
        return picked.reshape(slots, sequence_count, array.shape[-1])

    returned = (
        lax.all_to_all(collect(query_done), seq, split_axis=1, concat_axis=1, tiled=True),
        lax.all_to_all(collect(key_done), seq, split_axis=1, concat_axis=1, tiled=True),
        lax.all_to_all(collect(value_done), seq, split_axis=1, concat_axis=1, tiled=True),
    )

    def to_home(array):
        unrolled = jnp.roll(array, -first_rank, axis=1)
        return unrolled.reshape(capacity, 1, array.shape[-1])

    homed = (
        lax.all_to_all(to_home(returned[0]), "head", split_axis=0, concat_axis=1, tiled=True),
        lax.all_to_all(to_home(returned[1]), "head", split_axis=0, concat_axis=1, tiled=True),
        lax.all_to_all(to_home(returned[2]), "head", split_axis=0, concat_axis=1, tiled=True),
    )
    query_grads = homed[0].reshape(home_rows, head_total * homed[0].shape[-1])
    key_gradient_output = homed[1].reshape(home_rows, head_total * homed[1].shape[-1])
    value_gradient = homed[2].reshape(home_rows, head_total * homed[2].shape[-1])
    return (query_grads, key_gradient_output, value_gradient)

LOG2E = 1.4426950408889634
KEY_TILE = 256
ROW_TILE = 128
INFO_ROWS = 16
AUX_LANES = 256
SMEM = pl.BlockSpec(memory_space=pltpu.SMEM)
VMEM = pl.BlockSpec(memory_space=pltpu.VMEM)
ANY = pl.BlockSpec(memory_space=pl.ANY)
GROUP = QUERY_HEADS // KEY_VALUE_HEADS
WIDTH = GROUP * HEAD_SIZE


def pack_pairs_kernel(count_ref, k_ref, v_ref, out_ref):
    home_rows = k_ref.shape[0]
    info = jnp.full((INFO_ROWS, 2 * HEAD_SIZE), count_ref[0].astype(jnp.float32))
    for g in range(KEY_VALUE_HEADS):
        columns = slice(g * HEAD_SIZE, (g + 1) * HEAD_SIZE)
        out_ref[g, :home_rows, :HEAD_SIZE] = k_ref[:, columns]
        out_ref[g, :home_rows, HEAD_SIZE:] = v_ref[:, columns]
        out_ref[g, home_rows:, :] = info.astype(out_ref.dtype)


def pack_pairs(count, keys, values):
    home_rows = keys.shape[0]
    return pl.pallas_call(
        pack_pairs_kernel,
        out_shape=jax.ShapeDtypeStruct(
            (KEY_VALUE_HEADS, home_rows + INFO_ROWS, 2 * HEAD_SIZE), keys.dtype
        ),
        in_specs=[SMEM, VMEM, VMEM],
        out_specs=VMEM,
        name="pack_pairs",
    )(count, keys, values)


def pack_rows_kernel(me_ref, lse_ref, q_hbm, do_hbm, o_hbm, *rest):
    blocks = KEY_VALUE_HEADS
    outs = rest[:blocks]
    do_v, o_v, columns, lse_t, delta_t, aux, in_sem, copy_sem = rest[blocks:]
    home_rows = q_hbm.shape[0]
    me = me_ref[0]
    loads = [
        pltpu.make_async_copy(do_hbm, do_v, in_sem.at[0]),
        pltpu.make_async_copy(o_hbm, o_v, in_sem.at[1]),
    ]
    for load in loads:
        load.start()
    copies = []
    for k in range(blocks):
        start = pl.multiple_of((me ^ k) * WIDTH, HEAD_SIZE)
        for n, source in enumerate((q_hbm, do_hbm)):
            copy = pltpu.make_async_copy(
                source.at[:, pl.ds(start, WIDTH)],
                outs[k].at[pl.ds(0, home_rows), pl.ds(n * WIDTH, WIDTH)],
                copy_sem.at[3 * k + n],
            )
            copy.start()
            copies.append(copy)
    for load in loads:
        load.wait()
    columns[...] = jnp.zeros_like(columns)
    for g in range(blocks):
        columns[:, 8 * g : 8 * g + GROUP] = lse_ref[:, g * GROUP : (g + 1) * GROUP].astype(
            jnp.float32
        )
    lse_t[:, :home_rows] = columns[...].T
    for h in range(QUERY_HEADS):
        lanes = slice(h * HEAD_SIZE, (h + 1) * HEAD_SIZE)
        product = do_v[:, lanes].astype(jnp.float32) * o_v[:, lanes].astype(jnp.float32)
        column = 8 * (h // GROUP) + h % GROUP
        columns[:, column : column + 1] = jnp.sum(product, axis=1, keepdims=True)
    delta_t[:, :home_rows] = columns[...].T
    for k in range(blocks):
        head = pl.ds(pl.multiple_of((me ^ k) * 8, 8), 8)
        rows = jnp.concatenate([lse_t[head, :], delta_t[head, :]], axis=0)
        aux[k] = rows.astype(aux.dtype)
        copy = pltpu.make_async_copy(
            aux.at[k],
            outs[k].at[pl.ds(home_rows, INFO_ROWS), pl.ds(0, AUX_LANES)],
            copy_sem.at[3 * k + 2],
        )
        copy.start()
        copies.append(copy)
    for copy in copies:
        copy.wait()


def pack_rows(me, lse, queries, output_gradient, outputs):
    home_rows = queries.shape[0]
    blocks = KEY_VALUE_HEADS
    bf16, f32 = jnp.bfloat16, jnp.float32
    payload = jax.ShapeDtypeStruct((home_rows + INFO_ROWS, 2 * WIDTH), bf16)
    return pl.pallas_call(
        pack_rows_kernel,
        out_shape=(payload,) * blocks,
        in_specs=[SMEM, VMEM, ANY, ANY, ANY],
        out_specs=[ANY] * blocks,
        scratch_shapes=[
            pltpu.VMEM(outputs.shape, bf16),
            pltpu.VMEM(outputs.shape, bf16),
            pltpu.VMEM((home_rows, HEAD_SIZE), f32),
            pltpu.VMEM((HEAD_SIZE, AUX_LANES), f32),
            pltpu.VMEM((HEAD_SIZE, AUX_LANES), f32),
            pltpu.VMEM((blocks, INFO_ROWS, AUX_LANES), bf16),
            pltpu.SemaphoreType.DMA((2,)),
            pltpu.SemaphoreType.DMA((3 * blocks,)),
        ],
        compiler_params=pltpu.CompilerParams(vmem_limit_bytes=32 * 1024 * 1024),
        name="pack_rows",
    )(me, lse, queries, output_gradient, outputs)


def attention_kernel(
    me_ref, counts_ref, limits_ref, *rest,
):
    blocks = KEY_VALUE_HEADS
    payloads = rest[:blocks]
    kvs = rest[blocks : blocks + 4]
    dqs = rest[blocks + 4 : 2 * blocks + 4]
    downs = rest[2 * blocks + 4 : 2 * blocks + 8]
    (
        q_s, do_s, aux_s, lse_s, delta_s, dqt, acc_k, acc_v, tiles, starts, sems,
    ) = rest[2 * blocks + 8 :]
    capacity = kvs[0].shape[0]
    home_rows = dqs[0].shape[0]
    scale = HEAD_SIZE ** (-0.5)
    shift = home_rows - ROW_TILE
    me = me_ref[0]

    def copies(k):
        source = me ^ k
        start = pl.multiple_of(source * home_rows, 64)
        return [
            pltpu.make_async_copy(
                payloads[k].at[pl.ds(0, home_rows), pl.ds(0, WIDTH)],
                q_s.at[pl.ds(start, home_rows), :],
                sems.at[3 * k],
            ),
            pltpu.make_async_copy(
                payloads[k].at[pl.ds(0, home_rows), pl.ds(WIDTH, WIDTH)],
                do_s.at[pl.ds(start, home_rows), :],
                sems.at[3 * k + 1],
            ),
            pltpu.make_async_copy(
                payloads[k].at[pl.ds(home_rows, INFO_ROWS), pl.ds(0, AUX_LANES)],
                aux_s.at[source],
                sems.at[3 * k + 2],
            ),
        ]

    for k in range(blocks):
        for copy in copies(k):
            copy.start()

    live_tiles = jnp.int32(0)
    total = jnp.int32(0)
    for block in range(blocks):
        count = counts_ref[block]
        starts[block] = total
        total = total + count
        for t in range(2):
            live = count > t * ROW_TILE

            @pl.when(live)
            def _():
                tiles[live_tiles] = 2 * block + t

            live_tiles = live_tiles + live.astype(jnp.int32)

    def zero_tile(n, carry):
        dqt[tiles[n]] = jnp.zeros(dqt.shape[1:], jnp.float32)
        return carry

    lax.fori_loop(0, live_tiles, zero_tile, 0)

    for k in range(blocks):
        for copy in copies(k):
            copy.wait()

    for block in range(blocks):
        lanes = aux_s[block].astype(jnp.float32)
        shifted = pltpu.roll(lanes, AUX_LANES - shift, axis=1)
        for t, rows in enumerate((lanes, shifted)):
            for h in range(GROUP):
                columns = slice(h * ROW_TILE, (h + 1) * ROW_TILE)
                lse_s[2 * block + t : 2 * block + t + 1, columns] = (
                    rows[h : h + 1, :ROW_TILE] * LOG2E
                )
                delta_s[2 * block + t : 2 * block + t + 1, columns] = rows[
                    8 + h : 9 + h, :ROW_TILE
                ]

    lane = lax.broadcasted_iota(jnp.int32, (1, WIDTH), 1) % ROW_TILE

    def stack(ref, tile):
        start = pl.multiple_of((tile // 2) * home_rows + (tile % 2) * shift, 64)
        rows = ref[pl.ds(start, ROW_TILE), :]
        return jnp.concatenate(
            [rows[:, h * HEAD_SIZE : (h + 1) * HEAD_SIZE] for h in range(GROUP)], axis=0
        )

    def run_block(index, kv, out):
        limit = jnp.minimum(limits_ref[index], capacity)
        key_tiles = (limit + KEY_TILE - 1) // KEY_TILE
        out[...] = jnp.zeros_like(out)

        def key_step(kt, carry):
            start = pl.multiple_of(kt * KEY_TILE, KEY_TILE)
            key = kv[pl.ds(start, KEY_TILE), :HEAD_SIZE]
            value = kv[pl.ds(start, KEY_TILE), HEAD_SIZE:]
            key_t = key.T
            acc_k[...] = jnp.zeros_like(acc_k)
            acc_v[...] = jnp.zeros_like(acc_v)
            position = start + lax.broadcasted_iota(jnp.int32, (KEY_TILE, 1), 0)

            def row_step(n, inner):
                tile = tiles[n]
                block = tile // 2
                second = tile % 2
                q = stack(q_s, tile)
                do = stack(do_s, tile)
                lse = lse_s[pl.ds(tile, 1), :]
                delta = delta_s[pl.ds(tile, 1), :]
                first = second * (ROW_TILE - shift)
                last = counts_ref[block] - second * shift
                alive = (lane >= first) & (lane < last)
                if index > 0:
                    top = jnp.full(lane.shape, limit - 1)
                else:
                    top = starts[block] + second * shift + lane
                bound = jnp.where(alive, top, -1)
                dims = (((1,), (1,)), ((), ()))
                scores = lax.dot_general(key, q, dims, preferred_element_type=jnp.float32)
                prob = jnp.where(
                    position <= bound, jnp.exp2(scores * (scale * LOG2E) - lse), 0.0
                )
                dprob = lax.dot_general(value, do, dims, preferred_element_type=jnp.float32)
                dscore = (prob * (dprob - delta)).astype(jnp.bfloat16)
                acc_v[...] += jnp.dot(
                    prob.astype(jnp.bfloat16), do, preferred_element_type=jnp.float32
                )
                acc_k[...] += jnp.dot(dscore, q, preferred_element_type=jnp.float32)
                dqt[tile] += jnp.dot(key_t, dscore, preferred_element_type=jnp.float32)
                return inner

            lax.fori_loop(0, live_tiles, row_step, 0)
            out[pl.ds(start, KEY_TILE), :HEAD_SIZE] = (acc_k[...] * scale).astype(out.dtype)
            out[pl.ds(start, KEY_TILE), HEAD_SIZE:] = acc_v[...].astype(out.dtype)
            return carry

        lax.fori_loop(0, key_tiles, key_step, 0)

    for index in (3, 2, 1, 0):
        run_block(index, kvs[index], downs[index])
    full = jnp.where(total > capacity, 1.0, 0.0)
    for index in (1, 2, 3):
        downs[index][pl.ds(capacity, INFO_ROWS), :] = jnp.full(
            (INFO_ROWS, 2 * HEAD_SIZE), full
        ).astype(jnp.bfloat16)

    for k in range(blocks):
        block = me ^ k
        for t, (offset, skip) in enumerate(((0, 0), (ROW_TILE, ROW_TILE - shift))):
            live = counts_ref[block] > t * ROW_TILE
            rows = pl.ds(offset, ROW_TILE - skip)

            @pl.when(live)
            def _():
                for h in range(GROUP):
                    columns = slice(h * HEAD_SIZE, (h + 1) * HEAD_SIZE)
                    part = (dqt[2 * block + t, :, columns] * scale).T
                    dqs[k][rows, columns] = part[skip:].astype(jnp.bfloat16)

            @pl.when(jnp.logical_not(live))
            def _():
                dqs[k][rows, :] = jnp.zeros((ROW_TILE - skip, WIDTH), jnp.bfloat16)


def attention(me, counts, limits, payloads, kvs):
    bf16, f32 = jnp.bfloat16, jnp.float32
    blocks = KEY_VALUE_HEADS
    home_rows = payloads[0].shape[0] - INFO_ROWS
    capacity = kvs[0].shape[0]
    columns = 2 * HEAD_SIZE
    plane_rows = blocks * home_rows
    lowered = jax.ShapeDtypeStruct((capacity + INFO_ROWS, columns), bf16)
    return pl.pallas_call(
        attention_kernel,
        out_shape=(jax.ShapeDtypeStruct((home_rows, WIDTH), bf16),) * blocks
        + (jax.ShapeDtypeStruct((capacity, columns), f32),)
        + (lowered,) * 3,
        in_specs=[SMEM] * 3 + [ANY] * blocks + [VMEM] * 4,
        out_specs=[VMEM] * (blocks + 4),
        scratch_shapes=[
            pltpu.VMEM((plane_rows, WIDTH), bf16),
            pltpu.VMEM((plane_rows, WIDTH), bf16),
            pltpu.VMEM((blocks, INFO_ROWS, AUX_LANES), bf16),
            pltpu.VMEM((2 * blocks, WIDTH), f32),
            pltpu.VMEM((2 * blocks, WIDTH), f32),
            pltpu.VMEM((2 * blocks, HEAD_SIZE, WIDTH), f32),
            pltpu.VMEM((KEY_TILE, HEAD_SIZE), f32),
            pltpu.VMEM((KEY_TILE, HEAD_SIZE), f32),
            pltpu.SMEM((2 * blocks + 1,), jnp.int32),
            pltpu.SMEM((blocks,), jnp.int32),
            pltpu.SemaphoreType.DMA((3 * blocks,)),
        ],
        compiler_params=pltpu.CompilerParams(vmem_limit_bytes=48 * 1024 * 1024),
        cost_estimate=pl.CostEstimate(
            flops=10_000_000_000, bytes_accessed=12_000_000, transcendentals=8_000_000
        ),
        name="attention",
    )(me, counts, limits, *payloads, *kvs)


def unpack_rows_kernel(me_ref, *rest):
    blocks = KEY_VALUE_HEADS
    parts, out, sems = rest[:blocks], rest[blocks], rest[blocks + 1]
    copies = []
    for k in range(blocks):
        start = pl.multiple_of((me_ref[0] ^ k) * WIDTH, HEAD_SIZE)
        copy = pltpu.make_async_copy(parts[k], out.at[:, pl.ds(start, WIDTH)], sems.at[k])
        copy.start()
        copies.append(copy)
    for copy in copies:
        copy.wait()


def unpack_rows(me, parts):
    blocks = KEY_VALUE_HEADS
    home_rows = parts[0].shape[0]
    return pl.pallas_call(
        unpack_rows_kernel,
        out_shape=jax.ShapeDtypeStruct((home_rows, blocks * WIDTH), jnp.bfloat16),
        in_specs=[SMEM] + [ANY] * blocks,
        out_specs=ANY,
        scratch_shapes=[pltpu.SemaphoreType.DMA((blocks,))],
        name="unpack_rows",
    )(me, *parts)


def plane_device(queries, keys, values, outputs, output_gradient, lse, ranks):
    planes = lax.axis_size("outer")
    plane = ("inner", "head")
    blocks = KEY_VALUE_HEADS
    home_rows = queries.shape[0]
    plane_rows = blocks * home_rows
    capacity = plane_rows // 2
    surviving_tokens = BALANCED_TOKENS * planes * lax.axis_size("inner")
    bf16, f32 = jnp.bfloat16, jnp.float32
    me = lax.axis_index(plane).reshape(1).astype(jnp.int32)

    def swap(array, k):
        return lax.ppermute(array, plane, [(i, i ^ k) for i in range(blocks)])

    count = jnp.sum((ranks < surviving_tokens).astype(jnp.int32)).reshape(1)
    sent = pack_pairs(count, keys, values)
    arrived = lax.all_to_all(sent, plane, split_axis=0, concat_axis=0, tiled=True)
    packed = pack_rows(me, lse, queries, output_gradient, outputs)
    payloads = [packed[0]] + [swap(packed[k], k) for k in range(1, blocks)]

    counts = arrived[:, home_rows, 0].astype(jnp.int32)
    starts = jnp.cumsum(counts) - counts
    total = jnp.sum(counts)
    within = jnp.arange(home_rows, dtype=jnp.int32)
    local = jnp.where(within[None, :] < counts[:, None], starts[:, None] + within[None, :], -1)
    pick = (
        jnp.arange(capacity, dtype=jnp.int32)[:, None] == local.reshape(1, plane_rows)
    ).astype(bf16)
    plane_kv = arrived[:, :home_rows].reshape(plane_rows, 2 * HEAD_SIZE)
    mine = jnp.dot(pick, plane_kv, preferred_element_type=f32).astype(bf16)
    tail = jnp.zeros((INFO_ROWS, 2 * HEAD_SIZE), bf16).at[0, :blocks].set(counts.astype(bf16))
    shipped = jnp.concatenate([mine, tail], axis=0)
    up = [
        lax.ppermute(shipped, "outer", [(i, i + k) for i in range(planes - k)])
        for k in range(1, planes)
    ]
    limits = jnp.stack(
        [total] + [jnp.sum(u[capacity, :blocks].astype(f32)).astype(jnp.int32) for u in up]
    )

    results = attention(me, counts, limits, payloads, [mine] + up)
    dqs, own, down = results[:blocks], results[blocks], results[blocks + 1 :]
    own = own.astype(f32)
    full = jnp.max(limits) > capacity
    for k in (3, 2, 1):
        back = lax.ppermute(down[k - 1], "outer", [(i + k, i) for i in range(planes - k)])
        own = own + back[:capacity].astype(f32)
        full = full | (back[capacity, 0] > 0)
    dq_home = unpack_rows(me, [dqs[0]] + [swap(dqs[k], k) for k in range(1, blocks)])
    spread = lax.dot_general(
        pick, own.astype(bf16), (((0,), (0,)), ((), ())), preferred_element_type=f32
    ).astype(bf16)
    kv_home = lax.all_to_all(
        spread.reshape(blocks, home_rows, 2 * HEAD_SIZE),
        plane, split_axis=0, concat_axis=0, tiled=True,
    )
    dk = kv_home[:, :, :HEAD_SIZE].transpose(1, 0, 2).reshape(home_rows, blocks * HEAD_SIZE)
    dv = kv_home[:, :, HEAD_SIZE:].transpose(1, 0, 2).reshape(home_rows, blocks * HEAD_SIZE)
    return (dq_home, dk, dv), full


def solution(mesh):
    spec = P(("seq", "head"), None)
    heads = mesh.shape["head"]
    inner = max(KEY_VALUE_HEADS // heads, 1)
    planes = mesh.shape["seq"] // inner
    if planes != 4 or inner * heads != KEY_VALUE_HEADS:
        return jax.shard_map(
            per_device,
            mesh=mesh,
            in_specs=(spec,) * 6 + (P(("seq", "head")),),
            out_specs=(spec,) * 3,
            check_vma=False,
        )
    axes = ("outer", "inner", "head")

    def device(*blocks):
        fast, full = plane_device(*blocks)
        return lax.cond(full, lambda: per_device(*blocks, seq=("outer", "inner")), lambda: fast)

    return jax.shard_map(
        device,
        mesh=Mesh(mesh.devices.reshape(planes, inner, heads), axes),
        in_specs=(P(axes, None),) * 6 + (P(axes),),
        out_specs=(P(axes, None),) * 3,
        check_vma=False,
    )
```

```python
import jax
import jax.numpy as jnp
from jax import lax
from jax.experimental import pallas as pl
from jax.experimental.pallas import tpu as pltpu
from jax.sharding import Mesh
from jax.sharding import PartitionSpec as P

QUERY_HEADS = 40
KEY_VALUE_HEADS = 8
HEAD_SIZE = 128
BALANCED_TOKENS = 128


block_keys = 512


def per_device(queries, keys, values, outputs, output_gradient, lse, ranks, seq="seq"):
    sequence_count = lax.axis_size(seq)
    head_total = lax.axis_size("head")
    home_rows = queries.shape[0]
    capacity = home_rows * head_total
    slots = capacity // sequence_count
    surviving_tokens = BALANCED_TOKENS * sequence_count
    group_size = QUERY_HEADS // KEY_VALUE_HEADS
    local_key_value = KEY_VALUE_HEADS // head_total
    scale = HEAD_SIZE ** (-0.5)

    def split_heads(array):
        return array.reshape(home_rows, head_total, array.shape[1] // head_total)

    moved = (
        lax.all_to_all(split_heads(queries), "head", split_axis=1, concat_axis=0, tiled=True),
        lax.all_to_all(split_heads(keys), "head", split_axis=1, concat_axis=0, tiled=True),
        lax.all_to_all(split_heads(values), "head", split_axis=1, concat_axis=0, tiled=True),
        lax.all_to_all(
            split_heads(output_gradient), "head", split_axis=1, concat_axis=0, tiled=True
        ),
        lax.all_to_all(split_heads(lse), "head", split_axis=1, concat_axis=0, tiled=True),
        lax.all_to_all(split_heads(outputs), "head", split_axis=1, concat_axis=0, tiled=True),
    )
    shard_rank_list = lax.all_gather(ranks, "head", axis=0, tiled=True)
    first_rank = shard_rank_list[0]
    living_count = jnp.sum((shard_rank_list < surviving_tokens).astype(jnp.int32))
    table = lax.all_gather(
        jnp.stack([first_rank, living_count])[None, :], seq, axis=0, tiled=True
    )

    def to_pairs(array):
        flat = array.reshape(slots, sequence_count, array.shape[-1])
        return jnp.roll(flat, first_rank, axis=1)

    arrived = (
        lax.all_to_all(to_pairs(moved[0]), seq, split_axis=1, concat_axis=1, tiled=True),
        lax.all_to_all(to_pairs(moved[1]), seq, split_axis=1, concat_axis=1, tiled=True),
        lax.all_to_all(to_pairs(moved[2]), seq, split_axis=1, concat_axis=1, tiled=True),
        lax.all_to_all(to_pairs(moved[3]), seq, split_axis=1, concat_axis=1, tiled=True),
        lax.all_to_all(to_pairs(moved[4]), seq, split_axis=1, concat_axis=1, tiled=True),
        lax.all_to_all(to_pairs(moved[5]), seq, split_axis=1, concat_axis=1, tiled=True),
    )
    my_index = lax.axis_index(seq)
    starts = table[:, 0]
    count_table = table[:, 1]
    offset = (my_index - starts) % sequence_count
    within = jnp.arange(slots, dtype=jnp.int32)[:, None] * sequence_count + offset[None, :]
    alive = within < count_table[None, :]
    target_rank = jnp.where(
        alive, (starts[None, :] + within) // sequence_count, BALANCED_TOKENS
    ).reshape(-1)

    def place(array):
        width = array.shape[-1]
        return (
            jnp.zeros((BALANCED_TOKENS, width), array.dtype)
            .at[target_rank]
            .set(array.reshape(slots * sequence_count, width), mode="drop")
        )

    query_row_block = place(arrived[0]).reshape(
        BALANCED_TOKENS, local_key_value, group_size, HEAD_SIZE
    )
    key_row_block = place(arrived[1]).reshape(BALANCED_TOKENS, local_key_value, HEAD_SIZE)
    value_row_block = place(arrived[2]).reshape(BALANCED_TOKENS, local_key_value, HEAD_SIZE)
    grad_rows = place(arrived[3]).reshape(BALANCED_TOKENS, local_key_value, group_size, HEAD_SIZE)
    lse_rows = (
        place(arrived[4]).astype(jnp.float32).reshape(BALANCED_TOKENS, local_key_value, group_size)
    )
    out_rows = (
        place(arrived[5])
        .astype(jnp.float32)
        .reshape(BALANCED_TOKENS, local_key_value, group_size, HEAD_SIZE)
    )
    delta_rows = (
        jnp.sum(grad_rows.astype(jnp.float32) * out_rows, axis=-1)
        .astype(jnp.bfloat16)
        .astype(jnp.float32)
    )
    gathered = (
        lax.all_gather(key_row_block, seq, axis=0, tiled=True),
        lax.all_gather(value_row_block, seq, axis=0, tiled=True),
    )
    all_keys = gathered[0].reshape(sequence_count, BALANCED_TOKENS, local_key_value, HEAD_SIZE)
    all_values = gathered[1].reshape(sequence_count, BALANCED_TOKENS, local_key_value, HEAD_SIZE)
    rows_per = block_keys // sequence_count
    inner = 1
    outer = BALANCED_TOKENS // rows_per // inner
    query_rank = jnp.arange(BALANCED_TOKENS, dtype=jnp.int32) * sequence_count + my_index
    lse_t = lse_rows.transpose(1, 2, 0)
    delta_t = delta_rows.transpose(1, 2, 0)
    position = jnp.arange(sequence_count * rows_per, dtype=jnp.int32)

    def key_step(query_acc, row_start):
        key_blk = lax.dynamic_slice_in_dim(all_keys, row_start, rows_per, 1).reshape(
            sequence_count * rows_per, local_key_value, HEAD_SIZE
        )
        value_blk = lax.dynamic_slice_in_dim(all_values, row_start, rows_per, 1).reshape(
            sequence_count * rows_per, local_key_value, HEAD_SIZE
        )
        key_owner_rank = (row_start + position % rows_per) * sequence_count + position // rows_per
        mask = key_owner_rank[None, None, None, :] <= query_rank[None, None, :, None]
        scores = (
            jnp.einsum(
                "rgmc,kgc->gmrk", query_row_block, key_blk, preferred_element_type=jnp.float32
            )
            * scale
        )
        probs = jnp.where(mask, jnp.exp(scores - lse_t[..., None]), 0.0)
        dprob = jnp.einsum(
            "rgmc,kgc->gmrk", grad_rows, value_blk, preferred_element_type=jnp.float32
        )
        dscore = probs * (dprob - delta_t[..., None])
        probs_low = probs.astype(jnp.bfloat16)
        dscore_low = dscore.astype(jnp.bfloat16)
        query_acc = query_acc + scale * jnp.einsum(
            "gmrk,kgc->rgmc", dscore_low, key_blk, preferred_element_type=jnp.float32
        )
        key_part = scale * jnp.einsum(
            "gmrk,rgmc->kgc", dscore_low, query_row_block, preferred_element_type=jnp.float32
        )
        value_part = jnp.einsum(
            "gmrk,rgmc->kgc", probs_low, grad_rows, preferred_element_type=jnp.float32
        )
        return (
            query_acc,
            key_part.reshape(sequence_count, rows_per, local_key_value * HEAD_SIZE),
            value_part.reshape(sequence_count, rows_per, local_key_value * HEAD_SIZE),
        )

    def outer_step(query_acc, outer_index):

        def inner_step(query_inner, inner_index):
            row_start = (outer_index * inner + inner_index) * rows_per
            query_new, key_part, value_part = key_step(query_inner, row_start)
            return (query_new, (key_part, value_part))

        query_acc, (key_parts, value_parts) = lax.scan(
            inner_step, query_acc, jnp.arange(inner, dtype=jnp.int32)
        )
        key_parts = key_parts.transpose(1, 0, 2, 3).reshape(
            sequence_count, inner * rows_per, local_key_value * HEAD_SIZE
        )
        value_parts = value_parts.transpose(1, 0, 2, 3).reshape(
            sequence_count, inner * rows_per, local_key_value * HEAD_SIZE
        )
        received = (
            lax.all_to_all(key_parts, seq, split_axis=0, concat_axis=0, tiled=True),
            lax.all_to_all(value_parts, seq, split_axis=0, concat_axis=0, tiled=True),
        )
        return (query_acc, (jnp.sum(received[0], axis=0), jnp.sum(received[1], axis=0)))

    start_acc = jnp.zeros((BALANCED_TOKENS, local_key_value, group_size, HEAD_SIZE), jnp.float32)
    query_acc, (key_sums, value_sums) = lax.scan(
        outer_step, start_acc, jnp.arange(outer, dtype=jnp.int32)
    )
    query_done = query_acc.reshape(
        BALANCED_TOKENS, local_key_value * group_size * HEAD_SIZE
    ).astype(jnp.bfloat16)
    key_done = key_sums.reshape(BALANCED_TOKENS, local_key_value * HEAD_SIZE).astype(jnp.bfloat16)
    value_done = value_sums.reshape(BALANCED_TOKENS, local_key_value * HEAD_SIZE).astype(
        jnp.bfloat16
    )
    safe_rows = jnp.minimum(target_rank, BALANCED_TOKENS - 1)
    alive_flat = alive.reshape(-1)

    def collect(array):
        picked = jnp.where(alive_flat[:, None], array[safe_rows], jnp.zeros((), array.dtype))
        return picked.reshape(slots, sequence_count, array.shape[-1])

    returned = (
        lax.all_to_all(collect(query_done), seq, split_axis=1, concat_axis=1, tiled=True),
        lax.all_to_all(collect(key_done), seq, split_axis=1, concat_axis=1, tiled=True),
        lax.all_to_all(collect(value_done), seq, split_axis=1, concat_axis=1, tiled=True),
    )

    def to_home(array):
        unrolled = jnp.roll(array, -first_rank, axis=1)
        return unrolled.reshape(capacity, 1, array.shape[-1])

    homed = (
        lax.all_to_all(to_home(returned[0]), "head", split_axis=0, concat_axis=1, tiled=True),
        lax.all_to_all(to_home(returned[1]), "head", split_axis=0, concat_axis=1, tiled=True),
        lax.all_to_all(to_home(returned[2]), "head", split_axis=0, concat_axis=1, tiled=True),
    )
    query_grads = homed[0].reshape(home_rows, head_total * homed[0].shape[-1])
    key_gradient_output = homed[1].reshape(home_rows, head_total * homed[1].shape[-1])
    value_gradient = homed[2].reshape(home_rows, head_total * homed[2].shape[-1])
    return (query_grads, key_gradient_output, value_gradient)

LOG2E = 1.4426950408889634
KEY_TILE = 256
ROW_TILE = 128
INFO_ROWS = 16
AUX_LANES = 256
SMEM = pl.BlockSpec(memory_space=pltpu.SMEM)
VMEM = pl.BlockSpec(memory_space=pltpu.VMEM)
ANY = pl.BlockSpec(memory_space=pl.ANY)
GROUP = QUERY_HEADS // KEY_VALUE_HEADS
WIDTH = GROUP * HEAD_SIZE


def pack_pairs_kernel(count_ref, k_ref, v_ref, out_ref):
    home_rows = k_ref.shape[0]
    info = jnp.full((INFO_ROWS, 2 * HEAD_SIZE), count_ref[0].astype(jnp.float32))
    for g in range(KEY_VALUE_HEADS):
        columns = slice(g * HEAD_SIZE, (g + 1) * HEAD_SIZE)
        out_ref[g, :home_rows, :HEAD_SIZE] = k_ref[:, columns]
        out_ref[g, :home_rows, HEAD_SIZE:] = v_ref[:, columns]
        out_ref[g, home_rows:, :] = info.astype(out_ref.dtype)


def pack_pairs(count, keys, values):
    home_rows = keys.shape[0]
    return pl.pallas_call(
        pack_pairs_kernel,
        out_shape=jax.ShapeDtypeStruct(
            (KEY_VALUE_HEADS, home_rows + INFO_ROWS, 2 * HEAD_SIZE), keys.dtype
        ),
        in_specs=[SMEM, VMEM, VMEM],
        out_specs=VMEM,
        name="pack_pairs",
    )(count, keys, values)


def pack_rows_kernel(me_ref, lse_ref, q_ref, do_ref, o_ref, *rest):
    blocks = KEY_VALUE_HEADS
    outs = rest[:blocks]
    columns, lse_t, delta_t = rest[blocks:]
    home_rows = q_ref.shape[0]
    me = me_ref[0]
    columns[...] = jnp.zeros_like(columns)
    for g in range(blocks):
        columns[:, 8 * g : 8 * g + GROUP] = lse_ref[:, g * GROUP : (g + 1) * GROUP].astype(
            jnp.float32
        )
    lse_t[:, :home_rows] = columns[...].T
    for h in range(QUERY_HEADS):
        lanes = slice(h * HEAD_SIZE, (h + 1) * HEAD_SIZE)
        product = do_ref[:, lanes].astype(jnp.float32) * o_ref[:, lanes].astype(jnp.float32)
        column = 8 * (h // GROUP) + h % GROUP
        columns[:, column : column + 1] = jnp.sum(product, axis=1, keepdims=True)
    delta_t[:, :home_rows] = columns[...].T
    for k in range(blocks):
        start = pl.multiple_of((me ^ k) * WIDTH, HEAD_SIZE)
        outs[k][:home_rows, :WIDTH] = q_ref[:, pl.ds(start, WIDTH)]
        outs[k][:home_rows, WIDTH:] = do_ref[:, pl.ds(start, WIDTH)]
        head = pl.ds(pl.multiple_of((me ^ k) * 8, 8), 8)
        rows = jnp.concatenate([lse_t[head, :], delta_t[head, :]], axis=0)
        outs[k][home_rows:, :AUX_LANES] = rows.astype(jnp.bfloat16)


def pack_rows(me, lse, queries, output_gradient, outputs):
    home_rows = queries.shape[0]
    blocks = KEY_VALUE_HEADS
    bf16, f32 = jnp.bfloat16, jnp.float32
    payload = jax.ShapeDtypeStruct((home_rows + INFO_ROWS, 2 * WIDTH), bf16)
    return pl.pallas_call(
        pack_rows_kernel,
        out_shape=(payload,) * blocks,
        in_specs=[SMEM] + [VMEM] * 4,
        out_specs=[VMEM] * blocks,
        scratch_shapes=[
            pltpu.VMEM((home_rows, HEAD_SIZE), f32),
            pltpu.VMEM((HEAD_SIZE, AUX_LANES), f32),
            pltpu.VMEM((HEAD_SIZE, AUX_LANES), f32),
        ],
        compiler_params=pltpu.CompilerParams(vmem_limit_bytes=32 * 1024 * 1024),
        name="pack_rows",
    )(me, lse, queries, output_gradient, outputs)


def attention_kernel(
    me_ref, counts_ref, limits_ref, *rest,
):
    blocks = KEY_VALUE_HEADS
    payloads = rest[:blocks]
    kvs = rest[blocks : blocks + 4]
    dqs = rest[blocks + 4 : 2 * blocks + 4]
    downs = rest[2 * blocks + 4 : 2 * blocks + 8]
    (
        q_s, do_s, aux_s, lse_s, delta_s, dqt, acc_k, acc_v, tiles, starts, sems,
    ) = rest[2 * blocks + 8 :]
    capacity = kvs[0].shape[0]
    home_rows = dqs[0].shape[0]
    scale = HEAD_SIZE ** (-0.5)
    shift = home_rows - ROW_TILE
    me = me_ref[0]

    def copies(k):
        source = me ^ k
        start = pl.multiple_of(source * home_rows, 64)
        return [
            pltpu.make_async_copy(
                payloads[k].at[pl.ds(0, home_rows), pl.ds(0, WIDTH)],
                q_s.at[pl.ds(start, home_rows), :],
                sems.at[3 * k],
            ),
            pltpu.make_async_copy(
                payloads[k].at[pl.ds(0, home_rows), pl.ds(WIDTH, WIDTH)],
                do_s.at[pl.ds(start, home_rows), :],
                sems.at[3 * k + 1],
            ),
            pltpu.make_async_copy(
                payloads[k].at[pl.ds(home_rows, INFO_ROWS), pl.ds(0, AUX_LANES)],
                aux_s.at[source],
                sems.at[3 * k + 2],
            ),
        ]

    for k in range(blocks):
        for copy in copies(k):
            copy.start()

    live_tiles = jnp.int32(0)
    total = jnp.int32(0)
    for block in range(blocks):
        count = counts_ref[block]
        starts[block] = total
        total = total + count
        for t in range(2):
            live = count > t * ROW_TILE

            @pl.when(live)
            def _():
                tiles[live_tiles] = 2 * block + t

            live_tiles = live_tiles + live.astype(jnp.int32)

    def zero_tile(n, carry):
        dqt[tiles[n]] = jnp.zeros(dqt.shape[1:], jnp.float32)
        return carry

    lax.fori_loop(0, live_tiles, zero_tile, 0)

    for k in range(blocks):
        for copy in copies(k):
            copy.wait()

    for block in range(blocks):
        lanes = aux_s[block].astype(jnp.float32)
        shifted = pltpu.roll(lanes, AUX_LANES - shift, axis=1)
        for t, rows in enumerate((lanes, shifted)):
            for h in range(GROUP):
                columns = slice(h * ROW_TILE, (h + 1) * ROW_TILE)
                lse_s[2 * block + t : 2 * block + t + 1, columns] = (
                    rows[h : h + 1, :ROW_TILE] * LOG2E
                )
                delta_s[2 * block + t : 2 * block + t + 1, columns] = rows[
                    8 + h : 9 + h, :ROW_TILE
                ]

    lane = lax.broadcasted_iota(jnp.int32, (1, WIDTH), 1) % ROW_TILE

    def stack(ref, tile):
        start = pl.multiple_of((tile // 2) * home_rows + (tile % 2) * shift, 64)
        rows = ref[pl.ds(start, ROW_TILE), :]
        return jnp.concatenate(
            [rows[:, h * HEAD_SIZE : (h + 1) * HEAD_SIZE] for h in range(GROUP)], axis=0
        )

    def run_block(index, kv, out):
        limit = jnp.minimum(limits_ref[index], capacity)
        key_tiles = (limit + KEY_TILE - 1) // KEY_TILE
        out[...] = jnp.zeros_like(out)

        def key_step(kt, carry):
            start = pl.multiple_of(kt * KEY_TILE, KEY_TILE)
            key = kv[pl.ds(start, KEY_TILE), :HEAD_SIZE]
            value = kv[pl.ds(start, KEY_TILE), HEAD_SIZE:]
            key_t = key.T
            acc_k[...] = jnp.zeros_like(acc_k)
            acc_v[...] = jnp.zeros_like(acc_v)
            position = start + lax.broadcasted_iota(jnp.int32, (KEY_TILE, 1), 0)

            def row_step(n, inner):
                tile = tiles[n]
                block = tile // 2
                second = tile % 2
                q = stack(q_s, tile)
                do = stack(do_s, tile)
                lse = lse_s[pl.ds(tile, 1), :]
                delta = delta_s[pl.ds(tile, 1), :]
                first = second * (ROW_TILE - shift)
                last = counts_ref[block] - second * shift
                alive = (lane >= first) & (lane < last)
                if index > 0:
                    top = jnp.full(lane.shape, limit - 1)
                else:
                    top = starts[block] + second * shift + lane
                bound = jnp.where(alive, top, -1)
                dims = (((1,), (1,)), ((), ()))
                scores = lax.dot_general(key, q, dims, preferred_element_type=jnp.float32)
                prob = jnp.where(
                    position <= bound, jnp.exp2(scores * (scale * LOG2E) - lse), 0.0
                )
                dprob = lax.dot_general(value, do, dims, preferred_element_type=jnp.float32)
                dscore = (prob * (dprob - delta)).astype(jnp.bfloat16)
                acc_v[...] += jnp.dot(
                    prob.astype(jnp.bfloat16), do, preferred_element_type=jnp.float32
                )
                acc_k[...] += jnp.dot(dscore, q, preferred_element_type=jnp.float32)
                dqt[tile] += jnp.dot(key_t, dscore, preferred_element_type=jnp.float32)
                return inner

            lax.fori_loop(0, live_tiles, row_step, 0)
            out[pl.ds(start, KEY_TILE), :HEAD_SIZE] = (acc_k[...] * scale).astype(out.dtype)
            out[pl.ds(start, KEY_TILE), HEAD_SIZE:] = acc_v[...].astype(out.dtype)
            return carry

        lax.fori_loop(0, key_tiles, key_step, 0)

    for index in (3, 2, 1, 0):
        run_block(index, kvs[index], downs[index])
    full = jnp.where(total > capacity, 1.0, 0.0)
    for index in (1, 2, 3):
        downs[index][pl.ds(capacity, INFO_ROWS), :] = jnp.full(
            (INFO_ROWS, 2 * HEAD_SIZE), full
        ).astype(jnp.bfloat16)

    for k in range(blocks):
        block = me ^ k
        for t, (offset, skip) in enumerate(((0, 0), (ROW_TILE, ROW_TILE - shift))):
            live = counts_ref[block] > t * ROW_TILE
            rows = pl.ds(offset, ROW_TILE - skip)

            @pl.when(live)
            def _():
                for h in range(GROUP):
                    columns = slice(h * HEAD_SIZE, (h + 1) * HEAD_SIZE)
                    part = (dqt[2 * block + t, :, columns] * scale).T
                    dqs[k][rows, columns] = part[skip:].astype(jnp.bfloat16)

            @pl.when(jnp.logical_not(live))
            def _():
                dqs[k][rows, :] = jnp.zeros((ROW_TILE - skip, WIDTH), jnp.bfloat16)


def attention(me, counts, limits, payloads, kvs):
    bf16, f32 = jnp.bfloat16, jnp.float32
    blocks = KEY_VALUE_HEADS
    home_rows = payloads[0].shape[0] - INFO_ROWS
    capacity = kvs[0].shape[0]
    columns = 2 * HEAD_SIZE
    plane_rows = blocks * home_rows
    lowered = jax.ShapeDtypeStruct((capacity + INFO_ROWS, columns), bf16)
    return pl.pallas_call(
        attention_kernel,
        out_shape=(jax.ShapeDtypeStruct((home_rows, WIDTH), bf16),) * blocks
        + (jax.ShapeDtypeStruct((capacity, columns), f32),)
        + (lowered,) * 3,
        in_specs=[SMEM] * 3 + [ANY] * blocks + [VMEM] * 4,
        out_specs=[VMEM] * (blocks + 4),
        scratch_shapes=[
            pltpu.VMEM((plane_rows, WIDTH), bf16),
            pltpu.VMEM((plane_rows, WIDTH), bf16),
            pltpu.VMEM((blocks, INFO_ROWS, AUX_LANES), bf16),
            pltpu.VMEM((2 * blocks, WIDTH), f32),
            pltpu.VMEM((2 * blocks, WIDTH), f32),
            pltpu.VMEM((2 * blocks, HEAD_SIZE, WIDTH), f32),
            pltpu.VMEM((KEY_TILE, HEAD_SIZE), f32),
            pltpu.VMEM((KEY_TILE, HEAD_SIZE), f32),
            pltpu.SMEM((2 * blocks + 1,), jnp.int32),
            pltpu.SMEM((blocks,), jnp.int32),
            pltpu.SemaphoreType.DMA((3 * blocks,)),
        ],
        compiler_params=pltpu.CompilerParams(vmem_limit_bytes=48 * 1024 * 1024),
        cost_estimate=pl.CostEstimate(
            flops=10_000_000_000, bytes_accessed=12_000_000, transcendentals=8_000_000
        ),
        name="attention",
    )(me, counts, limits, *payloads, *kvs)


def unpack_rows_kernel(me_ref, *rest):
    blocks = KEY_VALUE_HEADS
    parts, out = rest[:blocks], rest[blocks]
    for k in range(blocks):
        start = pl.multiple_of((me_ref[0] ^ k) * WIDTH, HEAD_SIZE)
        out[:, pl.ds(start, WIDTH)] = parts[k][...]


def unpack_rows(me, parts):
    blocks = KEY_VALUE_HEADS
    home_rows = parts[0].shape[0]
    return pl.pallas_call(
        unpack_rows_kernel,
        out_shape=jax.ShapeDtypeStruct((home_rows, blocks * WIDTH), jnp.bfloat16),
        in_specs=[SMEM] + [VMEM] * blocks,
        out_specs=VMEM,
        name="unpack_rows",
    )(me, *parts)


def plane_device(queries, keys, values, outputs, output_gradient, lse, ranks):
    planes = lax.axis_size("outer")
    plane = ("inner", "head")
    blocks = KEY_VALUE_HEADS
    home_rows = queries.shape[0]
    plane_rows = blocks * home_rows
    capacity = plane_rows // 2
    surviving_tokens = BALANCED_TOKENS * planes * lax.axis_size("inner")
    bf16, f32 = jnp.bfloat16, jnp.float32
    me = lax.axis_index(plane).reshape(1).astype(jnp.int32)

    def swap(array, k):
        return lax.ppermute(array, plane, [(i, i ^ k) for i in range(blocks)])

    count = jnp.sum((ranks < surviving_tokens).astype(jnp.int32)).reshape(1)
    sent = pack_pairs(count, keys, values)
    lse, sent = lax.optimization_barrier((lse, sent))
    arrived = lax.all_to_all(sent, plane, split_axis=0, concat_axis=0, tiled=True)
    packed = pack_rows(me, lse, queries, output_gradient, outputs)
    payloads = [packed[0]] + [swap(packed[k], k) for k in range(1, blocks)]

    counts = arrived[:, home_rows, 0].astype(jnp.int32)
    starts = jnp.cumsum(counts) - counts
    total = jnp.sum(counts)
    within = jnp.arange(home_rows, dtype=jnp.int32)
    local = jnp.where(within[None, :] < counts[:, None], starts[:, None] + within[None, :], -1)
    pick = (
        jnp.arange(capacity, dtype=jnp.int32)[:, None] == local.reshape(1, plane_rows)
    ).astype(bf16)
    plane_kv = arrived[:, :home_rows].reshape(plane_rows, 2 * HEAD_SIZE)
    mine = jnp.dot(pick, plane_kv, preferred_element_type=f32).astype(bf16)
    tail = jnp.zeros((INFO_ROWS, 2 * HEAD_SIZE), bf16).at[0, :blocks].set(counts.astype(bf16))
    shipped = jnp.concatenate([mine, tail], axis=0)
    up = [
        lax.ppermute(shipped, "outer", [(i, i + k) for i in range(planes - k)])
        for k in range(1, planes)
    ]
    limits = jnp.stack(
        [total] + [jnp.sum(u[capacity, :blocks].astype(f32)).astype(jnp.int32) for u in up]
    )

    results = attention(me, counts, limits, payloads, [mine] + up)
    dqs, own, down = results[:blocks], results[blocks], results[blocks + 1 :]
    own = own.astype(f32)
    full = jnp.max(limits) > capacity
    for k in (3, 2, 1):
        back = lax.ppermute(down[k - 1], "outer", [(i + k, i) for i in range(planes - k)])
        own = own + back[:capacity].astype(f32)
        full = full | (back[capacity, 0] > 0)
    dq_home = unpack_rows(me, [dqs[0]] + [swap(dqs[k], k) for k in range(1, blocks)])
    own, dq_home = lax.optimization_barrier((own, dq_home))
    spread = lax.dot_general(
        pick, own.astype(bf16), (((0,), (0,)), ((), ())), preferred_element_type=f32
    ).astype(bf16)
    kv_home = lax.all_to_all(
        spread.reshape(blocks, home_rows, 2 * HEAD_SIZE),
        plane, split_axis=0, concat_axis=0, tiled=True,
    )
    dk = kv_home[:, :, :HEAD_SIZE].transpose(1, 0, 2).reshape(home_rows, blocks * HEAD_SIZE)
    dv = kv_home[:, :, HEAD_SIZE:].transpose(1, 0, 2).reshape(home_rows, blocks * HEAD_SIZE)
    return (dq_home, dk, dv), full


def solution(mesh):
    spec = P(("seq", "head"), None)
    heads = mesh.shape["head"]
    inner = max(KEY_VALUE_HEADS // heads, 1)
    planes = mesh.shape["seq"] // inner
    if planes != 4 or inner * heads != KEY_VALUE_HEADS:
        return jax.shard_map(
            per_device,
            mesh=mesh,
            in_specs=(spec,) * 6 + (P(("seq", "head")),),
            out_specs=(spec,) * 3,
            check_vma=False,
        )
    axes = ("outer", "inner", "head")

    def device(*blocks):
        fast, full = plane_device(*blocks)
        return lax.cond(full, lambda: per_device(*blocks, seq=("outer", "inner")), lambda: fast)

    return jax.shard_map(
        device,
        mesh=Mesh(mesh.devices.reshape(planes, inner, heads), axes),
        in_specs=(P(axes, None),) * 6 + (P(axes),),
        out_specs=(P(axes, None),) * 3,
        check_vma=False,
    )
```

```python
import functools

import jax
import jax.numpy as jnp
from jax import lax
from jax.experimental import pallas as pl
from jax.experimental.pallas import tpu as pltpu
from jax.sharding import Mesh
from jax.sharding import PartitionSpec as P

QUERY_HEADS = 40
KEY_VALUE_HEADS = 8
HEAD_SIZE = 128
BALANCED_TOKENS = 128


block_keys = 512


def per_device(queries, keys, values, outputs, output_gradient, lse, ranks, seq="seq"):
    sequence_count = lax.axis_size(seq)
    head_total = lax.axis_size("head")
    home_rows = queries.shape[0]
    capacity = home_rows * head_total
    slots = capacity // sequence_count
    surviving_tokens = BALANCED_TOKENS * sequence_count
    group_size = QUERY_HEADS // KEY_VALUE_HEADS
    local_key_value = KEY_VALUE_HEADS // head_total
    scale = HEAD_SIZE ** (-0.5)

    def split_heads(array):
        return array.reshape(home_rows, head_total, array.shape[1] // head_total)

    moved = (
        lax.all_to_all(split_heads(queries), "head", split_axis=1, concat_axis=0, tiled=True),
        lax.all_to_all(split_heads(keys), "head", split_axis=1, concat_axis=0, tiled=True),
        lax.all_to_all(split_heads(values), "head", split_axis=1, concat_axis=0, tiled=True),
        lax.all_to_all(
            split_heads(output_gradient), "head", split_axis=1, concat_axis=0, tiled=True
        ),
        lax.all_to_all(split_heads(lse), "head", split_axis=1, concat_axis=0, tiled=True),
        lax.all_to_all(split_heads(outputs), "head", split_axis=1, concat_axis=0, tiled=True),
    )
    shard_rank_list = lax.all_gather(ranks, "head", axis=0, tiled=True)
    first_rank = shard_rank_list[0]
    living_count = jnp.sum((shard_rank_list < surviving_tokens).astype(jnp.int32))
    table = lax.all_gather(
        jnp.stack([first_rank, living_count])[None, :], seq, axis=0, tiled=True
    )

    def to_pairs(array):
        flat = array.reshape(slots, sequence_count, array.shape[-1])
        return jnp.roll(flat, first_rank, axis=1)

    arrived = (
        lax.all_to_all(to_pairs(moved[0]), seq, split_axis=1, concat_axis=1, tiled=True),
        lax.all_to_all(to_pairs(moved[1]), seq, split_axis=1, concat_axis=1, tiled=True),
        lax.all_to_all(to_pairs(moved[2]), seq, split_axis=1, concat_axis=1, tiled=True),
        lax.all_to_all(to_pairs(moved[3]), seq, split_axis=1, concat_axis=1, tiled=True),
        lax.all_to_all(to_pairs(moved[4]), seq, split_axis=1, concat_axis=1, tiled=True),
        lax.all_to_all(to_pairs(moved[5]), seq, split_axis=1, concat_axis=1, tiled=True),
    )
    my_index = lax.axis_index(seq)
    starts = table[:, 0]
    count_table = table[:, 1]
    offset = (my_index - starts) % sequence_count
    within = jnp.arange(slots, dtype=jnp.int32)[:, None] * sequence_count + offset[None, :]
    alive = within < count_table[None, :]
    target_rank = jnp.where(
        alive, (starts[None, :] + within) // sequence_count, BALANCED_TOKENS
    ).reshape(-1)

    def place(array):
        width = array.shape[-1]
        return (
            jnp.zeros((BALANCED_TOKENS, width), array.dtype)
            .at[target_rank]
            .set(array.reshape(slots * sequence_count, width), mode="drop")
        )

    query_row_block = place(arrived[0]).reshape(
        BALANCED_TOKENS, local_key_value, group_size, HEAD_SIZE
    )
    key_row_block = place(arrived[1]).reshape(BALANCED_TOKENS, local_key_value, HEAD_SIZE)
    value_row_block = place(arrived[2]).reshape(BALANCED_TOKENS, local_key_value, HEAD_SIZE)
    grad_rows = place(arrived[3]).reshape(BALANCED_TOKENS, local_key_value, group_size, HEAD_SIZE)
    lse_rows = (
        place(arrived[4]).astype(jnp.float32).reshape(BALANCED_TOKENS, local_key_value, group_size)
    )
    out_rows = (
        place(arrived[5])
        .astype(jnp.float32)
        .reshape(BALANCED_TOKENS, local_key_value, group_size, HEAD_SIZE)
    )
    delta_rows = (
        jnp.sum(grad_rows.astype(jnp.float32) * out_rows, axis=-1)
        .astype(jnp.bfloat16)
        .astype(jnp.float32)
    )
    gathered = (
        lax.all_gather(key_row_block, seq, axis=0, tiled=True),
        lax.all_gather(value_row_block, seq, axis=0, tiled=True),
    )
    all_keys = gathered[0].reshape(sequence_count, BALANCED_TOKENS, local_key_value, HEAD_SIZE)
    all_values = gathered[1].reshape(sequence_count, BALANCED_TOKENS, local_key_value, HEAD_SIZE)
    rows_per = block_keys // sequence_count
    inner = 1
    outer = BALANCED_TOKENS // rows_per // inner
    query_rank = jnp.arange(BALANCED_TOKENS, dtype=jnp.int32) * sequence_count + my_index
    lse_t = lse_rows.transpose(1, 2, 0)
    delta_t = delta_rows.transpose(1, 2, 0)
    position = jnp.arange(sequence_count * rows_per, dtype=jnp.int32)

    def key_step(query_acc, row_start):
        key_blk = lax.dynamic_slice_in_dim(all_keys, row_start, rows_per, 1).reshape(
            sequence_count * rows_per, local_key_value, HEAD_SIZE
        )
        value_blk = lax.dynamic_slice_in_dim(all_values, row_start, rows_per, 1).reshape(
            sequence_count * rows_per, local_key_value, HEAD_SIZE
        )
        key_owner_rank = (row_start + position % rows_per) * sequence_count + position // rows_per
        mask = key_owner_rank[None, None, None, :] <= query_rank[None, None, :, None]
        scores = (
            jnp.einsum(
                "rgmc,kgc->gmrk", query_row_block, key_blk, preferred_element_type=jnp.float32
            )
            * scale
        )
        probs = jnp.where(mask, jnp.exp(scores - lse_t[..., None]), 0.0)
        dprob = jnp.einsum(
            "rgmc,kgc->gmrk", grad_rows, value_blk, preferred_element_type=jnp.float32
        )
        dscore = probs * (dprob - delta_t[..., None])
        probs_low = probs.astype(jnp.bfloat16)
        dscore_low = dscore.astype(jnp.bfloat16)
        query_acc = query_acc + scale * jnp.einsum(
            "gmrk,kgc->rgmc", dscore_low, key_blk, preferred_element_type=jnp.float32
        )
        key_part = scale * jnp.einsum(
            "gmrk,rgmc->kgc", dscore_low, query_row_block, preferred_element_type=jnp.float32
        )
        value_part = jnp.einsum(
            "gmrk,rgmc->kgc", probs_low, grad_rows, preferred_element_type=jnp.float32
        )
        return (
            query_acc,
            key_part.reshape(sequence_count, rows_per, local_key_value * HEAD_SIZE),
            value_part.reshape(sequence_count, rows_per, local_key_value * HEAD_SIZE),
        )

    def outer_step(query_acc, outer_index):

        def inner_step(query_inner, inner_index):
            row_start = (outer_index * inner + inner_index) * rows_per
            query_new, key_part, value_part = key_step(query_inner, row_start)
            return (query_new, (key_part, value_part))

        query_acc, (key_parts, value_parts) = lax.scan(
            inner_step, query_acc, jnp.arange(inner, dtype=jnp.int32)
        )
        key_parts = key_parts.transpose(1, 0, 2, 3).reshape(
            sequence_count, inner * rows_per, local_key_value * HEAD_SIZE
        )
        value_parts = value_parts.transpose(1, 0, 2, 3).reshape(
            sequence_count, inner * rows_per, local_key_value * HEAD_SIZE
        )
        received = (
            lax.all_to_all(key_parts, seq, split_axis=0, concat_axis=0, tiled=True),
            lax.all_to_all(value_parts, seq, split_axis=0, concat_axis=0, tiled=True),
        )
        return (query_acc, (jnp.sum(received[0], axis=0), jnp.sum(received[1], axis=0)))

    start_acc = jnp.zeros((BALANCED_TOKENS, local_key_value, group_size, HEAD_SIZE), jnp.float32)
    query_acc, (key_sums, value_sums) = lax.scan(
        outer_step, start_acc, jnp.arange(outer, dtype=jnp.int32)
    )
    query_done = query_acc.reshape(
        BALANCED_TOKENS, local_key_value * group_size * HEAD_SIZE
    ).astype(jnp.bfloat16)
    key_done = key_sums.reshape(BALANCED_TOKENS, local_key_value * HEAD_SIZE).astype(jnp.bfloat16)
    value_done = value_sums.reshape(BALANCED_TOKENS, local_key_value * HEAD_SIZE).astype(
        jnp.bfloat16
    )
    safe_rows = jnp.minimum(target_rank, BALANCED_TOKENS - 1)
    alive_flat = alive.reshape(-1)

    def collect(array):
        picked = jnp.where(alive_flat[:, None], array[safe_rows], jnp.zeros((), array.dtype))
        return picked.reshape(slots, sequence_count, array.shape[-1])

    returned = (
        lax.all_to_all(collect(query_done), seq, split_axis=1, concat_axis=1, tiled=True),
        lax.all_to_all(collect(key_done), seq, split_axis=1, concat_axis=1, tiled=True),
        lax.all_to_all(collect(value_done), seq, split_axis=1, concat_axis=1, tiled=True),
    )

    def to_home(array):
        unrolled = jnp.roll(array, -first_rank, axis=1)
        return unrolled.reshape(capacity, 1, array.shape[-1])

    homed = (
        lax.all_to_all(to_home(returned[0]), "head", split_axis=0, concat_axis=1, tiled=True),
        lax.all_to_all(to_home(returned[1]), "head", split_axis=0, concat_axis=1, tiled=True),
        lax.all_to_all(to_home(returned[2]), "head", split_axis=0, concat_axis=1, tiled=True),
    )
    query_grads = homed[0].reshape(home_rows, head_total * homed[0].shape[-1])
    key_gradient_output = homed[1].reshape(home_rows, head_total * homed[1].shape[-1])
    value_gradient = homed[2].reshape(home_rows, head_total * homed[2].shape[-1])
    return (query_grads, key_gradient_output, value_gradient)

LOG2E = 1.4426950408889634
KEY_TILE = 256
ROW_TILE = 128
INFO_ROWS = 16
AUX_LANES = 256
SMEM = pl.BlockSpec(memory_space=pltpu.SMEM)
VMEM = pl.BlockSpec(memory_space=pltpu.VMEM)
ANY = pl.BlockSpec(memory_space=pl.ANY)
GROUP = QUERY_HEADS // KEY_VALUE_HEADS
WIDTH = GROUP * HEAD_SIZE
CHIPS = (0, 5, 4, 1)
CORE = 2
SHARD_TILES = 3
PASS_ROWS = (256, 512, 768)


def pack_pairs_kernel(limit, ranks_ref, k_ref, v_ref, out_ref):
    home_rows = k_ref.shape[0]
    live = jnp.where(ranks_ref[...] < limit, 1.0, 0.0)
    info = jnp.broadcast_to(
        jnp.sum(live, axis=1, keepdims=True), (INFO_ROWS, 2 * HEAD_SIZE)
    ).astype(out_ref.dtype)
    for g in range(KEY_VALUE_HEADS):
        columns = slice(g * HEAD_SIZE, (g + 1) * HEAD_SIZE)
        out_ref[g, :home_rows, :HEAD_SIZE] = k_ref[:, columns]
        out_ref[g, :home_rows, HEAD_SIZE:] = v_ref[:, columns]
        out_ref[g, home_rows:, :] = info


def pack_pairs(limit, ranks, keys, values):
    home_rows = keys.shape[0]
    return pl.pallas_call(
        functools.partial(pack_pairs_kernel, limit),
        out_shape=jax.ShapeDtypeStruct(
            (KEY_VALUE_HEADS, home_rows + INFO_ROWS, 2 * HEAD_SIZE), keys.dtype
        ),
        in_specs=[VMEM] * 3,
        out_specs=VMEM,
        name="pack_pairs",
    )(ranks.reshape(1, home_rows), keys, values)


def pack_rows_kernel(me_ref, lse_ref, q_ref, do_ref, o_ref, *rest):
    blocks = KEY_VALUE_HEADS
    outs = rest[: len(CHIPS)]
    columns, lse_t, delta_t = rest[len(CHIPS) :]
    home_rows = q_ref.shape[0]
    me = me_ref[0]
    columns[...] = jnp.zeros_like(columns)
    for g in range(blocks):
        columns[:, 8 * g : 8 * g + GROUP] = lse_ref[:, g * GROUP : (g + 1) * GROUP].astype(
            jnp.float32
        )
    lse_t[:, :home_rows] = columns[...].T
    for h in range(QUERY_HEADS):
        lanes = slice(h * HEAD_SIZE, (h + 1) * HEAD_SIZE)
        product = do_ref[:, lanes].astype(jnp.float32) * o_ref[:, lanes].astype(jnp.float32)
        column = 8 * (h // GROUP) + h % GROUP
        columns[:, column : column + 1] = jnp.sum(product, axis=1, keepdims=True)
    delta_t[:, :home_rows] = columns[...].T
    for n, chip in enumerate(CHIPS):
        for m, core in enumerate((0, CORE)):
            to = me ^ chip ^ core
            start = pl.multiple_of(to * WIDTH, HEAD_SIZE)
            first = m * (home_rows + INFO_ROWS)
            rows = slice(first, first + home_rows)
            outs[n][rows, :WIDTH] = q_ref[:, pl.ds(start, WIDTH)]
            outs[n][rows, WIDTH:] = do_ref[:, pl.ds(start, WIDTH)]
            head = pl.ds(pl.multiple_of(to * 8, 8), 8)
            small = jnp.concatenate([lse_t[head, :], delta_t[head, :]], axis=0)
            outs[n][first + home_rows : first + home_rows + INFO_ROWS, :AUX_LANES] = small.astype(
                jnp.bfloat16
            )


def pack_rows(me, lse, queries, output_gradient, outputs):
    home_rows = queries.shape[0]
    bf16, f32 = jnp.bfloat16, jnp.float32
    payload = jax.ShapeDtypeStruct((2 * (home_rows + INFO_ROWS), 2 * WIDTH), bf16)
    return pl.pallas_call(
        pack_rows_kernel,
        out_shape=(payload,) * len(CHIPS),
        in_specs=[SMEM] + [VMEM] * 4,
        out_specs=[VMEM] * len(CHIPS),
        scratch_shapes=[
            pltpu.VMEM((home_rows, HEAD_SIZE), f32),
            pltpu.VMEM((HEAD_SIZE, AUX_LANES), f32),
            pltpu.VMEM((HEAD_SIZE, AUX_LANES), f32),
        ],
        compiler_params=pltpu.CompilerParams(vmem_limit_bytes=32 * 1024 * 1024),
        name="pack_rows",
    )(me, lse, queries, output_gradient, outputs)


def load_rows(me, counts_ref, payloads, q_s, do_s, aux_s, sems):
    home_rows = q_s.shape[0] // KEY_VALUE_HEADS
    entries = []
    for n, chip in enumerate(CHIPS):
        for m, core in enumerate((0, CORE)):
            entries.append((payloads[2 * n + m], chip ^ core))
    plans = []
    for n, (payload, partner) in enumerate(entries):
        source = me ^ partner
        start = pl.multiple_of(source * home_rows, 64)
        shard = counts_ref[source & ~1] + counts_ref[source | 1]
        needed = ((source & 1) == 0) | (shard > ROW_TILE)
        plans.append(
            (
                needed,
                [
                    pltpu.make_async_copy(
                        payload.at[pl.ds(0, home_rows), pl.ds(0, WIDTH)],
                        q_s.at[pl.ds(start, home_rows), :],
                        sems.at[3 * n],
                    ),
                    pltpu.make_async_copy(
                        payload.at[pl.ds(0, home_rows), pl.ds(WIDTH, WIDTH)],
                        do_s.at[pl.ds(start, home_rows), :],
                        sems.at[3 * n + 1],
                    ),
                    pltpu.make_async_copy(
                        payload.at[pl.ds(home_rows, INFO_ROWS), pl.ds(0, AUX_LANES)],
                        aux_s.at[source],
                        sems.at[3 * n + 2],
                    ),
                ],
            )
        )

    def each(act):
        for needed, copies in plans:

            @pl.when(needed)
            def _():
                for copy in copies:
                    act(copy)

    return each


def list_tiles(counts_ref, tiles, starts):
    length = jnp.int32(0)
    total = jnp.int32(0)
    for shard in range(KEY_VALUE_HEADS // 2):
        count = counts_ref[2 * shard] + counts_ref[2 * shard + 1]
        starts[shard] = total
        total = total + count
        for t in range(SHARD_TILES):
            live = count > t * ROW_TILE

            @pl.when(live)
            def _():
                tiles[length] = SHARD_TILES * shard + t

            length = length + live.astype(jnp.int32)
    return length, total


def spread_lanes(aux_s, lse_s, delta_s):
    lane = lax.broadcasted_iota(jnp.int32, (INFO_ROWS, ROW_TILE), 1)
    for shard in range(KEY_VALUE_HEADS // 2):
        low = aux_s[2 * shard].astype(jnp.float32)
        high = aux_s[2 * shard + 1].astype(jnp.float32)
        half = ROW_TILE // 2
        middle = jnp.where(
            lane < half, low[:, ROW_TILE:], pltpu.roll(high[:, :ROW_TILE], half, axis=1)
        )
        last = pltpu.roll(high, AUX_LANES - half, axis=1)[:, :ROW_TILE]
        for t, rows in enumerate((low[:, :ROW_TILE], middle, last)):
            row = SHARD_TILES * shard + t
            for h in range(GROUP):
                columns = slice(h * ROW_TILE, (h + 1) * ROW_TILE)
                lse_s[row : row + 1, columns] = rows[h : h + 1] * LOG2E
                delta_s[row : row + 1, columns] = rows[8 + h : 9 + h]


def row_tile(tile, q_s, do_s, lse_s, delta_s):
    def stack(ref):
        rows = ref[pl.ds(pl.multiple_of(tile * ROW_TILE, ROW_TILE), ROW_TILE), :]
        return jnp.concatenate(
            [rows[:, h * HEAD_SIZE : (h + 1) * HEAD_SIZE] for h in range(GROUP)], axis=0
        )

    return stack(q_s), stack(do_s), lse_s[pl.ds(tile, 1), :], delta_s[pl.ds(tile, 1), :]


def tile_step(key, value, key_t, rows, position, bound, acc_k, acc_v, add_dq):
    q, do, lse, delta = rows
    scale = HEAD_SIZE ** (-0.5)
    dims = (((1,), (1,)), ((), ()))
    scores = lax.dot_general(key, q, dims, preferred_element_type=jnp.float32)
    prob = jnp.where(position <= bound, jnp.exp2(scores * (scale * LOG2E) - lse), 0.0)
    dprob = lax.dot_general(value, do, dims, preferred_element_type=jnp.float32)
    dscore = (prob * (dprob - delta)).astype(jnp.bfloat16)
    acc_v[...] += jnp.dot(prob.astype(jnp.bfloat16), do, preferred_element_type=jnp.float32)
    acc_k[...] += jnp.dot(dscore, q, preferred_element_type=jnp.float32)
    add_dq(jnp.dot(key_t, dscore, preferred_element_type=jnp.float32))


def far_kernel(me_ref, counts_ref, limits_ref, *rest):
    payloads, kvs, rest = rest[:8], rest[8:11], rest[11:]
    downs, dqt_out, rest = rest[:3], rest[3], rest[4:]
    (
        q_s, do_s, aux_s, lse_s, delta_s, dqt, kv_s, acc_k, acc_v, tiles, starts, sems, kv_sem,
        down_sem, dq_sem, down_s,
    ) = rest
    capacity = downs[0].shape[0] - INFO_ROWS
    scale = HEAD_SIZE ** (-0.5)
    each = load_rows(me_ref[0], counts_ref, payloads, q_s, do_s, aux_s, sems)
    each(lambda copy: copy.start())
    kv_copies = [
        pltpu.make_async_copy(kvs[n].at[pl.ds(0, capacity), :], kv_s.at[n], kv_sem.at[n])
        for n in range(3)
    ]
    for copy in kv_copies:
        copy.start()
    length, total = list_tiles(counts_ref, tiles, starts)

    def zero_tile(n, carry):
        dqt[tiles[n]] = jnp.zeros(dqt.shape[1:], jnp.float32)
        return carry

    lax.fori_loop(0, length, zero_tile, 0)
    full = jnp.where(total > capacity, 1.0, 0.0)
    for n in range(3):
        down_s[n, capacity:, :] = jnp.full((INFO_ROWS, 2 * HEAD_SIZE), full).astype(jnp.bfloat16)
    each(lambda copy: copy.wait())
    for copy in kv_copies:
        copy.wait()
    spread_lanes(aux_s, lse_s, delta_s)
    lane = lax.broadcasted_iota(jnp.int32, (1, WIDTH), 1) % ROW_TILE

    def block_step(step, carry):
        index = 2 - step
        limit = jnp.minimum(limits_ref[index + 1], capacity)

        def run(rows):
            key = kv_s[index, :rows, :HEAD_SIZE]
            value = kv_s[index, :rows, HEAD_SIZE:]
            key_t = key.T
            acc_k[:rows] = jnp.zeros((rows, HEAD_SIZE), jnp.float32)
            acc_v[:rows] = jnp.zeros((rows, HEAD_SIZE), jnp.float32)
            position = lax.broadcasted_iota(jnp.int32, (rows, 1), 0)

            def row_step(n, inner):
                tile = tiles[n]
                shard = tile // SHARD_TILES
                count = counts_ref[2 * shard] + counts_ref[2 * shard + 1]
                alive = lane < count - (tile % SHARD_TILES) * ROW_TILE
                bound = jnp.where(alive, limit - 1, -1)

                def add_dq(part):
                    dqt[tile] += part

                tile_step(
                    key, value, key_t, row_tile(tile, q_s, do_s, lse_s, delta_s), position, bound,
                    acc_k.at[pl.ds(0, rows), :], acc_v.at[pl.ds(0, rows), :], add_dq,
                )
                return inner

            lax.fori_loop(0, length, row_step, 0)
            down_s[index, :rows, :HEAD_SIZE] = (acc_k[:rows] * scale).astype(jnp.bfloat16)
            down_s[index, :rows, HEAD_SIZE:] = acc_v[:rows].astype(jnp.bfloat16)
            if rows < capacity:
                down_s[index, rows:capacity, :] = jnp.zeros(
                    (capacity - rows, 2 * HEAD_SIZE), jnp.bfloat16
                )

        below = 0
        for rows in PASS_ROWS:

            @pl.when((limit > below) & (limit <= rows))
            def _():
                run(rows)

            below = rows

        @pl.when(limit == 0)
        def _():
            down_s[index, :capacity, :] = jnp.zeros((capacity, 2 * HEAD_SIZE), jnp.bfloat16)

        return carry

    lax.fori_loop(0, 3, block_step, 0)
    down_copies = [
        pltpu.make_async_copy(down_s.at[n], downs[n], down_sem.at[n]) for n in range(3)
    ]
    for copy in down_copies:
        copy.start()

    def dq_copy(n):
        tile = tiles[n]
        return pltpu.make_async_copy(dqt.at[tile], dqt_out.at[tile], dq_sem.at[n])

    def start_dq(n, carry):
        dq_copy(n).start()
        return carry

    def wait_dq(n, carry):
        dq_copy(n).wait()
        return carry

    lax.fori_loop(0, length, start_dq, 0)
    for copy in down_copies:
        copy.wait()
    lax.fori_loop(0, length, wait_dq, 0)


def own_kernel(me_ref, counts_ref, *rest):
    payloads, kv, dqt_in, rest = rest[:8], rest[8], rest[9], rest[11:]
    kept, passed, own, rest = rest[:4], rest[4], rest[5], rest[6:]
    q_s, do_s, aux_s, lse_s, delta_s, dqt, acc_k, acc_v, tiles, starts, sems, dq_sem = rest
    capacity = kv.shape[0]
    home_rows = kept[0].shape[0]
    scale = HEAD_SIZE ** (-0.5)
    me = me_ref[0]
    each = load_rows(me, counts_ref, payloads, q_s, do_s, aux_s, sems)
    each(lambda copy: copy.start())
    length, total = list_tiles(counts_ref, tiles, starts)
    limit = jnp.minimum(total, capacity)

    def dq_copy(n):
        tile = tiles[n]
        return pltpu.make_async_copy(dqt_in.at[tile], dqt.at[tile], dq_sem.at[n])

    def start_dq(n, carry):
        dq_copy(n).start()
        return carry

    def wait_dq(n, carry):
        dq_copy(n).wait()
        return carry

    lax.fori_loop(0, length, start_dq, 0)
    own[...] = jnp.zeros_like(own)
    each(lambda copy: copy.wait())
    spread_lanes(aux_s, lse_s, delta_s)
    lax.fori_loop(0, length, wait_dq, 0)
    lane = lax.broadcasted_iota(jnp.int32, (1, WIDTH), 1) % ROW_TILE

    def key_step(kt, carry):
        start = pl.multiple_of(kt * KEY_TILE, KEY_TILE)
        key = kv[pl.ds(start, KEY_TILE), :HEAD_SIZE]
        value = kv[pl.ds(start, KEY_TILE), HEAD_SIZE:]
        key_t = key.T
        acc_k[...] = jnp.zeros_like(acc_k)
        acc_v[...] = jnp.zeros_like(acc_v)
        position = start + lax.broadcasted_iota(jnp.int32, (KEY_TILE, 1), 0)

        def row_step(n, inner):
            tile = tiles[n]
            shard = tile // SHARD_TILES
            offset = (tile % SHARD_TILES) * ROW_TILE
            count = counts_ref[2 * shard] + counts_ref[2 * shard + 1]
            first = starts[shard] + offset

            @pl.when(first + ROW_TILE > start)
            def _():
                bound = jnp.where(lane < count - offset, first + lane, -1)

                def add_dq(part):
                    dqt[tile] += part

                tile_step(
                    key, value, key_t, row_tile(tile, q_s, do_s, lse_s, delta_s), position, bound,
                    acc_k, acc_v, add_dq,
                )

            return inner

        lax.fori_loop(0, length, row_step, 0)
        own[pl.ds(start, KEY_TILE), :HEAD_SIZE] = acc_k[...] * scale
        own[pl.ds(start, KEY_TILE), HEAD_SIZE:] = acc_v[...]
        return carry

    lax.fori_loop(0, (limit + KEY_TILE - 1) // KEY_TILE, key_step, 0)

    half = ROW_TILE // 2
    outs = [(chip, kept[n]) for n, chip in enumerate(CHIPS)]
    outs += [(chip ^ CORE, passed.at[n]) for n, chip in enumerate(CHIPS)]
    for partner, out in outs:
        block = me ^ partner
        shard = block // 2
        count = counts_ref[block & ~1] + counts_ref[block | 1]

        def put(rows, t, first):
            live = count > t * ROW_TILE
            size = rows.stop - rows.start

            @pl.when(live)
            def _():
                for h in range(GROUP):
                    columns = slice(h * HEAD_SIZE, (h + 1) * HEAD_SIZE)
                    part = (dqt[SHARD_TILES * shard + t, :, columns] * scale).T
                    out[rows, columns] = part[first : first + size].astype(jnp.bfloat16)

            @pl.when(jnp.logical_not(live))
            def _():
                out[rows, :] = jnp.zeros((size, WIDTH), jnp.bfloat16)

        @pl.when((block & 1) == 0)
        def _():
            put(slice(0, ROW_TILE), 0, 0)
            put(slice(ROW_TILE, home_rows), 1, 0)

        @pl.when((block & 1) == 1)
        def _():
            put(slice(0, half), 1, half)
            put(slice(half, home_rows), 2, 0)


def row_scratch(plane_rows):
    bf16, f32 = jnp.bfloat16, jnp.float32
    blocks = KEY_VALUE_HEADS
    tile_count = plane_rows // ROW_TILE
    return [
        pltpu.VMEM((plane_rows, WIDTH), bf16),
        pltpu.VMEM((plane_rows, WIDTH), bf16),
        pltpu.VMEM((blocks, INFO_ROWS, AUX_LANES), bf16),
        pltpu.VMEM((tile_count, WIDTH), f32),
        pltpu.VMEM((tile_count, WIDTH), f32),
        pltpu.VMEM((tile_count, HEAD_SIZE, WIDTH), f32),
    ]


def far_attention(me, counts, limits, payloads, kvs):
    bf16, f32 = jnp.bfloat16, jnp.float32
    blocks = KEY_VALUE_HEADS
    rows = kvs[0].shape[0]
    columns = 2 * HEAD_SIZE
    plane_rows = 2 * (rows - INFO_ROWS)
    tile_count = plane_rows // ROW_TILE
    return pl.pallas_call(
        far_kernel,
        out_shape=(jax.ShapeDtypeStruct((rows, columns), bf16),) * 3
        + (jax.ShapeDtypeStruct((tile_count, HEAD_SIZE, WIDTH), f32),),
        in_specs=[SMEM] * 3 + [ANY] * (blocks + 3),
        out_specs=[ANY] * 4,
        scratch_shapes=row_scratch(plane_rows)
        + [
            pltpu.VMEM((3, rows - INFO_ROWS, columns), bf16),
            pltpu.VMEM((rows - INFO_ROWS, HEAD_SIZE), f32),
            pltpu.VMEM((rows - INFO_ROWS, HEAD_SIZE), f32),
            pltpu.SMEM((tile_count + 1,), jnp.int32),
            pltpu.SMEM((blocks,), jnp.int32),
            pltpu.SemaphoreType.DMA((3 * blocks,)),
            pltpu.SemaphoreType.DMA((3,)),
            pltpu.SemaphoreType.DMA((3,)),
            pltpu.SemaphoreType.DMA((tile_count,)),
            pltpu.VMEM((3, rows, columns), bf16),
        ],
        compiler_params=pltpu.CompilerParams(vmem_limit_bytes=48 * 1024 * 1024),
        cost_estimate=pl.CostEstimate(
            flops=10_000_000_000, bytes_accessed=12_000_000, transcendentals=8_000_000
        ),
        name="far_attention",
    )(me, counts, limits, *payloads, *kvs)


def own_attention(me, counts, payloads, kv, dqt, note):
    bf16, f32 = jnp.bfloat16, jnp.float32
    blocks = KEY_VALUE_HEADS
    plane_rows = 2 * kv.shape[0]
    tile_count = plane_rows // ROW_TILE
    return pl.pallas_call(
        own_kernel,
        out_shape=(jax.ShapeDtypeStruct((plane_rows // blocks, WIDTH), bf16),) * 4
        + (jax.ShapeDtypeStruct((4, plane_rows // blocks, WIDTH), bf16),)
        + (jax.ShapeDtypeStruct(kv.shape, f32),),
        in_specs=[SMEM] * 2 + [ANY] * blocks + [VMEM, ANY, ANY],
        out_specs=[VMEM] * 6,
        scratch_shapes=row_scratch(plane_rows)
        + [
            pltpu.VMEM((KEY_TILE, HEAD_SIZE), f32),
            pltpu.VMEM((KEY_TILE, HEAD_SIZE), f32),
            pltpu.SMEM((tile_count + 1,), jnp.int32),
            pltpu.SMEM((blocks,), jnp.int32),
            pltpu.SemaphoreType.DMA((3 * blocks,)),
            pltpu.SemaphoreType.DMA((tile_count,)),
        ],
        compiler_params=pltpu.CompilerParams(vmem_limit_bytes=48 * 1024 * 1024),
        cost_estimate=pl.CostEstimate(
            flops=1_000_000, bytes_accessed=100_000, transcendentals=1_000
        ),
        name="own_attention",
    )(me, counts, *payloads, kv, dqt, note)


def unpack_rows_kernel(me_ref, kept, passed, *rest):
    pairs, out = rest[:3], rest[3]
    home_rows = kept.shape[0]
    me = me_ref[0]

    def put(partner, rows):
        start = pl.multiple_of((me ^ partner) * WIDTH, HEAD_SIZE)
        out[:, pl.ds(start, WIDTH)] = rows

    put(0, kept[...])
    put(CORE, passed[...])
    for chip, pair in zip(CHIPS[1:], pairs):
        put(chip, pair[:home_rows])
        put(chip ^ CORE, pair[home_rows:])


def unpack_rows(me, kept, passed, pairs):
    home_rows = kept.shape[0]
    return pl.pallas_call(
        unpack_rows_kernel,
        out_shape=jax.ShapeDtypeStruct((home_rows, KEY_VALUE_HEADS * WIDTH), jnp.bfloat16),
        in_specs=[SMEM] + [VMEM] * 5,
        out_specs=VMEM,
        name="unpack_rows",
    )(me, kept, passed, *pairs)


def plane_device(queries, keys, values, outputs, output_gradient, lse, ranks):
    planes = lax.axis_size("outer")
    plane = ("inner", "head")
    blocks = KEY_VALUE_HEADS
    home_rows = queries.shape[0]
    plane_rows = blocks * home_rows
    capacity = plane_rows // 2
    surviving_tokens = BALANCED_TOKENS * planes * lax.axis_size("inner")
    bf16, f32 = jnp.bfloat16, jnp.float32
    me = lax.axis_index(plane).reshape(1).astype(jnp.int32)

    def swap(array, k):
        return lax.ppermute(array, plane, [(i, i ^ k) for i in range(blocks)])

    sent = pack_pairs(surviving_tokens, ranks, keys, values)
    lse, sent = lax.optimization_barrier((lse, sent))
    arrived = lax.all_to_all(sent, plane, split_axis=0, concat_axis=0, tiled=True)
    packed = pack_rows(me, lse, queries, output_gradient, outputs)
    block_rows = home_rows + INFO_ROWS
    payloads = []
    for n, chip in enumerate(CHIPS):
        pair = swap(packed[n], chip) if chip else packed[n]
        payloads += [pair, swap(pair[block_rows:], CORE)]

    counts = arrived[:, home_rows, 0].astype(jnp.int32)
    starts = jnp.cumsum(counts) - counts
    total = jnp.sum(counts)
    within = jnp.arange(home_rows, dtype=jnp.int32)
    local = jnp.where(within[None, :] < counts[:, None], starts[:, None] + within[None, :], -1)
    pick = (
        jnp.arange(capacity, dtype=jnp.int32)[:, None] == local.reshape(1, plane_rows)
    ).astype(bf16)
    plane_kv = arrived[:, :home_rows].reshape(plane_rows, 2 * HEAD_SIZE)
    mine = jnp.dot(pick, plane_kv, preferred_element_type=f32).astype(bf16)
    tail = jnp.zeros((INFO_ROWS, 2 * HEAD_SIZE), bf16).at[0, :blocks].set(counts.astype(bf16))
    shipped = jnp.concatenate([mine, tail], axis=0)
    up = [
        lax.ppermute(shipped, "outer", [(i, i + k) for i in range(planes - k)])
        for k in range(1, planes)
    ]
    limits = jnp.stack(
        [total] + [jnp.sum(u[capacity, :blocks].astype(f32)).astype(jnp.int32) for u in up]
    )

    *down, dqt = far_attention(me, counts, limits, payloads, up)
    note = swap(down[0][capacity:, :HEAD_SIZE], CORE)
    *kept, passed, own = own_attention(me, counts, payloads, mine, dqt, note)
    full = jnp.max(limits) > capacity
    for k in (3, 2, 1):
        back = lax.ppermute(down[k - 1], "outer", [(i + k, i) for i in range(planes - k)])
        own = own + back[:capacity].astype(f32)
        full = full | (back[capacity, 0] > 0)
    passed = swap(passed, CORE)
    pairs = [
        swap(jnp.concatenate([kept[n], passed[n]], axis=0), CHIPS[n]) for n in range(1, len(CHIPS))
    ]
    own, pairs = lax.optimization_barrier((own, pairs))
    dq_home = unpack_rows(me, kept[0], passed[0], pairs)
    spread = lax.dot_general(
        pick, own.astype(bf16), (((0,), (0,)), ((), ())), preferred_element_type=f32
    ).astype(bf16)
    kv_home = lax.all_to_all(
        spread.reshape(blocks, home_rows, 2 * HEAD_SIZE),
        plane, split_axis=0, concat_axis=0, tiled=True,
    )
    dk = kv_home[:, :, :HEAD_SIZE].transpose(1, 0, 2).reshape(home_rows, blocks * HEAD_SIZE)
    dv = kv_home[:, :, HEAD_SIZE:].transpose(1, 0, 2).reshape(home_rows, blocks * HEAD_SIZE)
    return (dq_home, dk, dv), full


def solution(mesh):
    spec = P(("seq", "head"), None)
    heads = mesh.shape["head"]
    inner = max(KEY_VALUE_HEADS // heads, 1)
    planes = mesh.shape["seq"] // inner
    if planes != 4 or inner * heads != KEY_VALUE_HEADS:
        return jax.shard_map(
            per_device,
            mesh=mesh,
            in_specs=(spec,) * 6 + (P(("seq", "head")),),
            out_specs=(spec,) * 3,
            check_vma=False,
        )
    axes = ("outer", "inner", "head")

    def device(*blocks):
        fast, full = plane_device(*blocks)
        return lax.cond(full, lambda: per_device(*blocks, seq=("outer", "inner")), lambda: fast)

    return jax.shard_map(
        device,
        mesh=Mesh(mesh.devices.reshape(planes, inner, heads), axes),
        in_specs=(P(axes, None),) * 6 + (P(axes),),
        out_specs=(P(axes, None),) * 3,
        check_vma=False,
    )
```

```python
import functools

import jax
import jax.numpy as jnp
from jax import lax
from jax.experimental import pallas as pl
from jax.experimental.pallas import tpu as pltpu
from jax.sharding import Mesh
from jax.sharding import PartitionSpec as P

QUERY_HEADS = 40
KEY_VALUE_HEADS = 8
HEAD_SIZE = 128
BALANCED_TOKENS = 128


block_keys = 512


def per_device(queries, keys, values, outputs, output_gradient, lse, ranks, seq="seq"):
    sequence_count = lax.axis_size(seq)
    head_total = lax.axis_size("head")
    home_rows = queries.shape[0]
    capacity = home_rows * head_total
    slots = capacity // sequence_count
    surviving_tokens = BALANCED_TOKENS * sequence_count
    group_size = QUERY_HEADS // KEY_VALUE_HEADS
    local_key_value = KEY_VALUE_HEADS // head_total
    scale = HEAD_SIZE ** (-0.5)

    def split_heads(array):
        return array.reshape(home_rows, head_total, array.shape[1] // head_total)

    moved = (
        lax.all_to_all(split_heads(queries), "head", split_axis=1, concat_axis=0, tiled=True),
        lax.all_to_all(split_heads(keys), "head", split_axis=1, concat_axis=0, tiled=True),
        lax.all_to_all(split_heads(values), "head", split_axis=1, concat_axis=0, tiled=True),
        lax.all_to_all(
            split_heads(output_gradient), "head", split_axis=1, concat_axis=0, tiled=True
        ),
        lax.all_to_all(split_heads(lse), "head", split_axis=1, concat_axis=0, tiled=True),
        lax.all_to_all(split_heads(outputs), "head", split_axis=1, concat_axis=0, tiled=True),
    )
    shard_rank_list = lax.all_gather(ranks, "head", axis=0, tiled=True)
    first_rank = shard_rank_list[0]
    living_count = jnp.sum((shard_rank_list < surviving_tokens).astype(jnp.int32))
    table = lax.all_gather(
        jnp.stack([first_rank, living_count])[None, :], seq, axis=0, tiled=True
    )

    def to_pairs(array):
        flat = array.reshape(slots, sequence_count, array.shape[-1])
        return jnp.roll(flat, first_rank, axis=1)

    arrived = (
        lax.all_to_all(to_pairs(moved[0]), seq, split_axis=1, concat_axis=1, tiled=True),
        lax.all_to_all(to_pairs(moved[1]), seq, split_axis=1, concat_axis=1, tiled=True),
        lax.all_to_all(to_pairs(moved[2]), seq, split_axis=1, concat_axis=1, tiled=True),
        lax.all_to_all(to_pairs(moved[3]), seq, split_axis=1, concat_axis=1, tiled=True),
        lax.all_to_all(to_pairs(moved[4]), seq, split_axis=1, concat_axis=1, tiled=True),
        lax.all_to_all(to_pairs(moved[5]), seq, split_axis=1, concat_axis=1, tiled=True),
    )
    my_index = lax.axis_index(seq)
    starts = table[:, 0]
    count_table = table[:, 1]
    offset = (my_index - starts) % sequence_count
    within = jnp.arange(slots, dtype=jnp.int32)[:, None] * sequence_count + offset[None, :]
    alive = within < count_table[None, :]
    target_rank = jnp.where(
        alive, (starts[None, :] + within) // sequence_count, BALANCED_TOKENS
    ).reshape(-1)

    def place(array):
        width = array.shape[-1]
        return (
            jnp.zeros((BALANCED_TOKENS, width), array.dtype)
            .at[target_rank]
            .set(array.reshape(slots * sequence_count, width), mode="drop")
        )

    query_row_block = place(arrived[0]).reshape(
        BALANCED_TOKENS, local_key_value, group_size, HEAD_SIZE
    )
    key_row_block = place(arrived[1]).reshape(BALANCED_TOKENS, local_key_value, HEAD_SIZE)
    value_row_block = place(arrived[2]).reshape(BALANCED_TOKENS, local_key_value, HEAD_SIZE)
    grad_rows = place(arrived[3]).reshape(BALANCED_TOKENS, local_key_value, group_size, HEAD_SIZE)
    lse_rows = (
        place(arrived[4]).astype(jnp.float32).reshape(BALANCED_TOKENS, local_key_value, group_size)
    )
    out_rows = (
        place(arrived[5])
        .astype(jnp.float32)
        .reshape(BALANCED_TOKENS, local_key_value, group_size, HEAD_SIZE)
    )
    delta_rows = (
        jnp.sum(grad_rows.astype(jnp.float32) * out_rows, axis=-1)
        .astype(jnp.bfloat16)
        .astype(jnp.float32)
    )
    gathered = (
        lax.all_gather(key_row_block, seq, axis=0, tiled=True),
        lax.all_gather(value_row_block, seq, axis=0, tiled=True),
    )
    all_keys = gathered[0].reshape(sequence_count, BALANCED_TOKENS, local_key_value, HEAD_SIZE)
    all_values = gathered[1].reshape(sequence_count, BALANCED_TOKENS, local_key_value, HEAD_SIZE)
    rows_per = block_keys // sequence_count
    inner = 1
    outer = BALANCED_TOKENS // rows_per // inner
    query_rank = jnp.arange(BALANCED_TOKENS, dtype=jnp.int32) * sequence_count + my_index
    lse_t = lse_rows.transpose(1, 2, 0)
    delta_t = delta_rows.transpose(1, 2, 0)
    position = jnp.arange(sequence_count * rows_per, dtype=jnp.int32)

    def key_step(query_acc, row_start):
        key_blk = lax.dynamic_slice_in_dim(all_keys, row_start, rows_per, 1).reshape(
            sequence_count * rows_per, local_key_value, HEAD_SIZE
        )
        value_blk = lax.dynamic_slice_in_dim(all_values, row_start, rows_per, 1).reshape(
            sequence_count * rows_per, local_key_value, HEAD_SIZE
        )
        key_owner_rank = (row_start + position % rows_per) * sequence_count + position // rows_per
        mask = key_owner_rank[None, None, None, :] <= query_rank[None, None, :, None]
        scores = (
            jnp.einsum(
                "rgmc,kgc->gmrk", query_row_block, key_blk, preferred_element_type=jnp.float32
            )
            * scale
        )
        probs = jnp.where(mask, jnp.exp(scores - lse_t[..., None]), 0.0)
        dprob = jnp.einsum(
            "rgmc,kgc->gmrk", grad_rows, value_blk, preferred_element_type=jnp.float32
        )
        dscore = probs * (dprob - delta_t[..., None])
        probs_low = probs.astype(jnp.bfloat16)
        dscore_low = dscore.astype(jnp.bfloat16)
        query_acc = query_acc + scale * jnp.einsum(
            "gmrk,kgc->rgmc", dscore_low, key_blk, preferred_element_type=jnp.float32
        )
        key_part = scale * jnp.einsum(
            "gmrk,rgmc->kgc", dscore_low, query_row_block, preferred_element_type=jnp.float32
        )
        value_part = jnp.einsum(
            "gmrk,rgmc->kgc", probs_low, grad_rows, preferred_element_type=jnp.float32
        )
        return (
            query_acc,
            key_part.reshape(sequence_count, rows_per, local_key_value * HEAD_SIZE),
            value_part.reshape(sequence_count, rows_per, local_key_value * HEAD_SIZE),
        )

    def outer_step(query_acc, outer_index):

        def inner_step(query_inner, inner_index):
            row_start = (outer_index * inner + inner_index) * rows_per
            query_new, key_part, value_part = key_step(query_inner, row_start)
            return (query_new, (key_part, value_part))

        query_acc, (key_parts, value_parts) = lax.scan(
            inner_step, query_acc, jnp.arange(inner, dtype=jnp.int32)
        )
        key_parts = key_parts.transpose(1, 0, 2, 3).reshape(
            sequence_count, inner * rows_per, local_key_value * HEAD_SIZE
        )
        value_parts = value_parts.transpose(1, 0, 2, 3).reshape(
            sequence_count, inner * rows_per, local_key_value * HEAD_SIZE
        )
        received = (
            lax.all_to_all(key_parts, seq, split_axis=0, concat_axis=0, tiled=True),
            lax.all_to_all(value_parts, seq, split_axis=0, concat_axis=0, tiled=True),
        )
        return (query_acc, (jnp.sum(received[0], axis=0), jnp.sum(received[1], axis=0)))

    start_acc = jnp.zeros((BALANCED_TOKENS, local_key_value, group_size, HEAD_SIZE), jnp.float32)
    query_acc, (key_sums, value_sums) = lax.scan(
        outer_step, start_acc, jnp.arange(outer, dtype=jnp.int32)
    )
    query_done = query_acc.reshape(
        BALANCED_TOKENS, local_key_value * group_size * HEAD_SIZE
    ).astype(jnp.bfloat16)
    key_done = key_sums.reshape(BALANCED_TOKENS, local_key_value * HEAD_SIZE).astype(jnp.bfloat16)
    value_done = value_sums.reshape(BALANCED_TOKENS, local_key_value * HEAD_SIZE).astype(
        jnp.bfloat16
    )
    safe_rows = jnp.minimum(target_rank, BALANCED_TOKENS - 1)
    alive_flat = alive.reshape(-1)

    def collect(array):
        picked = jnp.where(alive_flat[:, None], array[safe_rows], jnp.zeros((), array.dtype))
        return picked.reshape(slots, sequence_count, array.shape[-1])

    returned = (
        lax.all_to_all(collect(query_done), seq, split_axis=1, concat_axis=1, tiled=True),
        lax.all_to_all(collect(key_done), seq, split_axis=1, concat_axis=1, tiled=True),
        lax.all_to_all(collect(value_done), seq, split_axis=1, concat_axis=1, tiled=True),
    )

    def to_home(array):
        unrolled = jnp.roll(array, -first_rank, axis=1)
        return unrolled.reshape(capacity, 1, array.shape[-1])

    homed = (
        lax.all_to_all(to_home(returned[0]), "head", split_axis=0, concat_axis=1, tiled=True),
        lax.all_to_all(to_home(returned[1]), "head", split_axis=0, concat_axis=1, tiled=True),
        lax.all_to_all(to_home(returned[2]), "head", split_axis=0, concat_axis=1, tiled=True),
    )
    query_grads = homed[0].reshape(home_rows, head_total * homed[0].shape[-1])
    key_gradient_output = homed[1].reshape(home_rows, head_total * homed[1].shape[-1])
    value_gradient = homed[2].reshape(home_rows, head_total * homed[2].shape[-1])
    return (query_grads, key_gradient_output, value_gradient)

LOG2E = 1.4426950408889634
KEY_TILE = 256
ROW_TILE = 128
INFO_ROWS = 16
AUX_LANES = 256
SMEM = pl.BlockSpec(memory_space=pltpu.SMEM)
VMEM = pl.BlockSpec(memory_space=pltpu.VMEM)
ANY = pl.BlockSpec(memory_space=pl.ANY)
GROUP = QUERY_HEADS // KEY_VALUE_HEADS
WIDTH = GROUP * HEAD_SIZE
CHIPS = (5, 4, 1)
CORE = 2
SHARD_TILES = 3
PASS_ROWS = (256, 512, 768)


def pack_pairs_kernel(limit, ranks_ref, k_ref, v_ref, out_ref):
    home_rows = k_ref.shape[0]
    live = jnp.where(ranks_ref[...] < limit, 1.0, 0.0)
    info = jnp.broadcast_to(
        jnp.sum(live, axis=1, keepdims=True), (INFO_ROWS, 2 * HEAD_SIZE)
    ).astype(out_ref.dtype)
    for g in range(KEY_VALUE_HEADS):
        columns = slice(g * HEAD_SIZE, (g + 1) * HEAD_SIZE)
        out_ref[g, :home_rows, :HEAD_SIZE] = k_ref[:, columns]
        out_ref[g, :home_rows, HEAD_SIZE:] = v_ref[:, columns]
        out_ref[g, home_rows:, :] = info


def pack_pairs(limit, ranks, keys, values):
    home_rows = keys.shape[0]
    return pl.pallas_call(
        functools.partial(pack_pairs_kernel, limit),
        out_shape=jax.ShapeDtypeStruct(
            (KEY_VALUE_HEADS, home_rows + INFO_ROWS, 2 * HEAD_SIZE), keys.dtype
        ),
        in_specs=[VMEM] * 3,
        out_specs=VMEM,
        name="pack_pairs",
    )(ranks.reshape(1, home_rows), keys, values)


def pack_rows_kernel(partners, me_ref, q_hbm, do_hbm, out, sems):
    copies = []
    for n, partner in enumerate(partners):
        start = pl.multiple_of((me_ref[0] ^ partner) * WIDTH, HEAD_SIZE)
        for m, source in enumerate((q_hbm, do_hbm)):
            copies.append(
                pltpu.make_async_copy(
                    source.at[:, pl.ds(start, WIDTH)],
                    out.at[n, :, pl.ds(m * WIDTH, WIDTH)],
                    sems.at[2 * n + m],
                )
            )
    for copy in copies:
        copy.start()
    for copy in copies:
        copy.wait()


def pack_rows(partners, me, queries, output_gradient):
    home_rows = queries.shape[0]
    return pl.pallas_call(
        functools.partial(pack_rows_kernel, partners),
        out_shape=jax.ShapeDtypeStruct((len(partners), home_rows, 2 * WIDTH), queries.dtype),
        in_specs=[SMEM, ANY, ANY],
        out_specs=VMEM,
        scratch_shapes=[pltpu.SemaphoreType.DMA((2 * len(partners),))],
        name="pack_rows",
    )(me, queries, output_gradient)


def pack_small_kernel(lse_ref, do_ref, o_ref, out, columns, lanes):
    home_rows = do_ref.shape[0]
    columns[...] = jnp.zeros_like(columns)
    for g in range(KEY_VALUE_HEADS):
        columns[:, 16 * g : 16 * g + GROUP] = lse_ref[:, g * GROUP : (g + 1) * GROUP].astype(
            jnp.float32
        )
    for h in range(QUERY_HEADS):
        head = slice(h * HEAD_SIZE, (h + 1) * HEAD_SIZE)
        product = do_ref[:, head].astype(jnp.float32) * o_ref[:, head].astype(jnp.float32)
        column = 16 * (h // GROUP) + 8 + h % GROUP
        columns[:, column : column + 1] = jnp.sum(product, axis=1, keepdims=True)
    lanes[...] = jnp.zeros_like(lanes)
    lanes[:, :home_rows] = columns[...].T
    for g in range(KEY_VALUE_HEADS):
        out[g] = lanes[16 * g : 16 * g + INFO_ROWS, :].astype(out.dtype)


def pack_small(lse, output_gradient, outputs):
    f32 = jnp.float32
    return pl.pallas_call(
        pack_small_kernel,
        out_shape=jax.ShapeDtypeStruct((KEY_VALUE_HEADS, INFO_ROWS, AUX_LANES), jnp.bfloat16),
        in_specs=[VMEM] * 3,
        out_specs=VMEM,
        scratch_shapes=[
            pltpu.VMEM((lse.shape[0], HEAD_SIZE), f32),
            pltpu.VMEM((HEAD_SIZE, AUX_LANES), f32),
        ],
        compiler_params=pltpu.CompilerParams(vmem_limit_bytes=32 * 1024 * 1024),
        name="pack_small",
    )(lse, output_gradient, outputs)


def compact_kernel(arrived, out, counts_ref):
    home_rows = arrived.shape[1] - INFO_ROWS
    capacity = out.shape[0] - INFO_ROWS
    row = lax.broadcasted_iota(jnp.int32, (capacity, home_rows), 0)
    within = lax.broadcasted_iota(jnp.int32, (capacity, home_rows), 1)
    total = jnp.int32(0)
    picked = []
    for block in range(KEY_VALUE_HEADS):
        count = jnp.max(arrived[block, home_rows:, :].astype(jnp.float32)).astype(jnp.int32)
        counts_ref[block] = count
        hit = (row == within + total) & (within < count)
        picked.append(jnp.where(hit, 1.0, 0.0).astype(jnp.bfloat16))
        total = total + count
    acc = jnp.zeros((capacity, out.shape[1]), jnp.float32)
    for block in range(KEY_VALUE_HEADS):
        acc += jnp.dot(
            picked[block], arrived[block, :home_rows, :], preferred_element_type=jnp.float32
        )
    out[:capacity, :] = acc.astype(out.dtype)
    line = lax.broadcasted_iota(jnp.int32, (INFO_ROWS, out.shape[1]), 0)
    out[capacity:, :] = (
        jnp.where(line == 0, total // 64, jnp.where(line == 1, total % 64, 0))
        .astype(jnp.float32)
        .astype(out.dtype)
    )


def compact(arrived):
    blocks, rows, columns = arrived.shape
    capacity = blocks * (rows - INFO_ROWS) // 2
    return pl.pallas_call(
        compact_kernel,
        out_shape=(
            jax.ShapeDtypeStruct((capacity + INFO_ROWS, columns), arrived.dtype),
            jax.ShapeDtypeStruct((blocks,), jnp.int32),
        ),
        in_specs=[VMEM],
        out_specs=(VMEM, SMEM),
        compiler_params=pltpu.CompilerParams(vmem_limit_bytes=32 * 1024 * 1024),
        name="compact",
    )(arrived)


def load_rows(me, counts_ref, arrays, q_s, do_s, sems):
    home_rows = q_s.shape[0] // KEY_VALUE_HEADS
    q_hbm, do_hbm, beside, pairs, crossed = arrays
    column = pl.multiple_of(me * WIDTH, HEAD_SIZE)
    left, right = pl.ds(0, WIDTH), pl.ds(WIDTH, WIDTH)
    sources = [
        (0, q_hbm.at[:, pl.ds(column, WIDTH)], do_hbm.at[:, pl.ds(column, WIDTH)]),
        (CORE, beside.at[0, :, left], beside.at[0, :, right]),
    ]
    for chip, pair, cross in zip(CHIPS, pairs, crossed):
        sources.append((chip, pair.at[0, :, left], pair.at[0, :, right]))
        sources.append((chip ^ CORE, cross.at[0, :, left], cross.at[0, :, right]))
    plans = []
    for n, (partner, q, do) in enumerate(sources):
        source = me ^ partner
        rows = pl.ds(pl.multiple_of(source * home_rows, 64), home_rows)
        shard = counts_ref[source & ~1] + counts_ref[source | 1]
        needed = ((source & 1) == 0) | (shard > ROW_TILE)
        plans.append(
            (
                needed,
                [
                    pltpu.make_async_copy(q, q_s.at[rows, :], sems.at[2 * n]),
                    pltpu.make_async_copy(do, do_s.at[rows, :], sems.at[2 * n + 1]),
                ],
            )
        )

    def each(act):
        for needed, copies in plans:

            @pl.when(needed)
            def _():
                for copy in copies:
                    act(copy)

    return each


def list_tiles(counts_ref, tiles, starts):
    length = jnp.int32(0)
    total = jnp.int32(0)
    for shard in range(KEY_VALUE_HEADS // 2):
        count = counts_ref[2 * shard] + counts_ref[2 * shard + 1]
        starts[shard] = total
        total = total + count
        for t in range(SHARD_TILES):
            live = count > t * ROW_TILE

            @pl.when(live)
            def _():
                tiles[length] = SHARD_TILES * shard + t

            length = length + live.astype(jnp.int32)
    return length, total


def spread_lanes(aux_s, lse_s, delta_s):
    lane = lax.broadcasted_iota(jnp.int32, (INFO_ROWS, ROW_TILE), 1)
    for shard in range(KEY_VALUE_HEADS // 2):
        low = aux_s[2 * shard].astype(jnp.float32)
        high = aux_s[2 * shard + 1].astype(jnp.float32)
        half = ROW_TILE // 2
        middle = jnp.where(
            lane < half, low[:, ROW_TILE:], pltpu.roll(high[:, :ROW_TILE], half, axis=1)
        )
        last = pltpu.roll(high, AUX_LANES - half, axis=1)[:, :ROW_TILE]
        for t, rows in enumerate((low[:, :ROW_TILE], middle, last)):
            row = SHARD_TILES * shard + t
            for h in range(GROUP):
                columns = slice(h * ROW_TILE, (h + 1) * ROW_TILE)
                lse_s[row : row + 1, columns] = rows[h : h + 1] * LOG2E
                delta_s[row : row + 1, columns] = rows[8 + h : 9 + h]


def row_tile(tile, q_s, do_s, lse_s, delta_s):
    def stack(ref):
        rows = ref[pl.ds(pl.multiple_of(tile * ROW_TILE, ROW_TILE), ROW_TILE), :]
        return jnp.concatenate(
            [rows[:, h * HEAD_SIZE : (h + 1) * HEAD_SIZE] for h in range(GROUP)], axis=0
        )

    return stack(q_s), stack(do_s), lse_s[pl.ds(tile, 1), :], delta_s[pl.ds(tile, 1), :]


def tile_step(key, value, key_t, rows, position, bound, acc_k, acc_v, add_dq):
    q, do, lse, delta = rows
    scale = HEAD_SIZE ** (-0.5)
    dims = (((1,), (1,)), ((), ()))
    scores = lax.dot_general(key, q, dims, preferred_element_type=jnp.float32)
    prob = jnp.where(position <= bound, jnp.exp2(scores * (scale * LOG2E) - lse), 0.0)
    dprob = lax.dot_general(value, do, dims, preferred_element_type=jnp.float32)
    dscore = (prob * (dprob - delta)).astype(jnp.bfloat16)
    acc_v[...] += jnp.dot(prob.astype(jnp.bfloat16), do, preferred_element_type=jnp.float32)
    acc_k[...] += jnp.dot(dscore, q, preferred_element_type=jnp.float32)
    add_dq(jnp.dot(key_t, dscore, preferred_element_type=jnp.float32))


def far_kernel(me_ref, counts_ref, *rest):
    aux_s, arrays, kvs, rest = rest[0], rest[1:10], rest[10:13], rest[13:]
    arrays = (*arrays[:3], arrays[3:6], arrays[6:9])
    downs, dqt_out, full_ref, rest = rest[:3], rest[3], rest[4], rest[5:]
    (
        q_s, do_s, lse_s, delta_s, dqt, kv_s, acc_k, acc_v, tiles, starts, limits, sems, kv_sem,
        down_sem, dq_sem, down_s,
    ) = rest
    capacity = downs[0].shape[0] - INFO_ROWS
    scale = HEAD_SIZE ** (-0.5)
    each = load_rows(me_ref[0], counts_ref, arrays, q_s, do_s, sems)
    each(lambda copy: copy.start())
    kv_copies = [
        pltpu.make_async_copy(kvs[n], kv_s.at[n], kv_sem.at[n])
        for n in range(3)
    ]
    for copy in kv_copies:
        copy.start()
    length, total = list_tiles(counts_ref, tiles, starts)

    def zero_tile(n, carry):
        dqt[tiles[n]] = jnp.zeros(dqt.shape[1:], jnp.float32)
        return carry

    lax.fori_loop(0, length, zero_tile, 0)
    spread_lanes(aux_s, lse_s, delta_s)
    for copy in kv_copies:
        copy.wait()
    most = total
    for n in range(3):
        info = kv_s[n, capacity:, :].astype(jnp.float32)
        limit = (jnp.max(info[0:1]) * 64.0 + jnp.max(info[1:2])).astype(jnp.int32)
        limits[n] = jnp.minimum(limit, capacity)
        most = jnp.maximum(most, limit)
    full = most > capacity
    full_ref[0] = full.astype(jnp.int32)
    for n in range(3):
        down_s[n, capacity:, :] = jnp.full(
            (INFO_ROWS, 2 * HEAD_SIZE), jnp.where(full, 1.0, 0.0)
        ).astype(jnp.bfloat16)
    each(lambda copy: copy.wait())
    lane = lax.broadcasted_iota(jnp.int32, (1, WIDTH), 1) % ROW_TILE

    def block_step(step, carry):
        index = 2 - step
        limit = limits[index]

        def run(rows):
            key = kv_s[index, :rows, :HEAD_SIZE]
            value = kv_s[index, :rows, HEAD_SIZE:]
            key_t = key.T
            acc_k[:rows] = jnp.zeros((rows, HEAD_SIZE), jnp.float32)
            acc_v[:rows] = jnp.zeros((rows, HEAD_SIZE), jnp.float32)
            position = lax.broadcasted_iota(jnp.int32, (rows, 1), 0)

            def row_step(n, inner):
                tile = tiles[n]
                shard = tile // SHARD_TILES
                count = counts_ref[2 * shard] + counts_ref[2 * shard + 1]
                alive = lane < count - (tile % SHARD_TILES) * ROW_TILE
                bound = jnp.where(alive, limit - 1, -1)

                def add_dq(part):
                    dqt[tile] += part

                tile_step(
                    key, value, key_t, row_tile(tile, q_s, do_s, lse_s, delta_s), position, bound,
                    acc_k.at[pl.ds(0, rows), :], acc_v.at[pl.ds(0, rows), :], add_dq,
                )
                return inner

            lax.fori_loop(0, length, row_step, 0)
            down_s[index, :rows, :HEAD_SIZE] = (acc_k[:rows] * scale).astype(jnp.bfloat16)
            down_s[index, :rows, HEAD_SIZE:] = acc_v[:rows].astype(jnp.bfloat16)
            if rows < capacity:
                down_s[index, rows:capacity, :] = jnp.zeros(
                    (capacity - rows, 2 * HEAD_SIZE), jnp.bfloat16
                )

        below = 0
        for rows in PASS_ROWS:

            @pl.when((limit > below) & (limit <= rows))
            def _():
                run(rows)

            below = rows

        @pl.when(limit == 0)
        def _():
            down_s[index, :capacity, :] = jnp.zeros((capacity, 2 * HEAD_SIZE), jnp.bfloat16)

        return carry

    lax.fori_loop(0, 3, block_step, 0)
    down_copies = [
        pltpu.make_async_copy(down_s.at[n], downs[n], down_sem.at[n]) for n in range(3)
    ]
    for copy in down_copies:
        copy.start()

    def dq_copy(n):
        tile = tiles[n]
        return pltpu.make_async_copy(dqt.at[tile], dqt_out.at[tile], dq_sem.at[n])

    def start_dq(n, carry):
        dq_copy(n).start()
        return carry

    def wait_dq(n, carry):
        dq_copy(n).wait()
        return carry

    lax.fori_loop(0, length, start_dq, 0)
    for copy in down_copies:
        copy.wait()
    lax.fori_loop(0, length, wait_dq, 0)


def own_kernel(me_ref, counts_ref, *rest):
    aux_s, arrays, kv, dqt_in, rest = rest[0], rest[1:10], rest[10], rest[11], rest[13:]
    arrays = (*arrays[:3], arrays[3:6], arrays[6:9])
    kept, passed, own, rest = rest[:4], rest[4:8], rest[8], rest[9:]
    q_s, do_s, lse_s, delta_s, dqt, acc_k, acc_v, tiles, starts, sems, dq_sem = rest
    capacity = kv.shape[0] - INFO_ROWS
    home_rows = kept[0].shape[0]
    scale = HEAD_SIZE ** (-0.5)
    me = me_ref[0]
    each = load_rows(me, counts_ref, arrays, q_s, do_s, sems)
    each(lambda copy: copy.start())
    length, total = list_tiles(counts_ref, tiles, starts)
    limit = jnp.minimum(total, capacity)

    def dq_copy(n):
        tile = tiles[n]
        return pltpu.make_async_copy(dqt_in.at[tile], dqt.at[tile], dq_sem.at[n])

    def start_dq(n, carry):
        dq_copy(n).start()
        return carry

    def wait_dq(n, carry):
        dq_copy(n).wait()
        return carry

    lax.fori_loop(0, length, start_dq, 0)
    own[...] = jnp.zeros_like(own)
    spread_lanes(aux_s, lse_s, delta_s)
    each(lambda copy: copy.wait())
    lax.fori_loop(0, length, wait_dq, 0)
    lane = lax.broadcasted_iota(jnp.int32, (1, WIDTH), 1) % ROW_TILE

    def key_step(kt, carry):
        start = pl.multiple_of(kt * KEY_TILE, KEY_TILE)
        key = kv[pl.ds(start, KEY_TILE), :HEAD_SIZE]
        value = kv[pl.ds(start, KEY_TILE), HEAD_SIZE:]
        key_t = key.T
        acc_k[...] = jnp.zeros_like(acc_k)
        acc_v[...] = jnp.zeros_like(acc_v)
        position = start + lax.broadcasted_iota(jnp.int32, (KEY_TILE, 1), 0)

        def row_step(n, inner):
            tile = tiles[n]
            shard = tile // SHARD_TILES
            offset = (tile % SHARD_TILES) * ROW_TILE
            count = counts_ref[2 * shard] + counts_ref[2 * shard + 1]
            first = starts[shard] + offset

            @pl.when(first + ROW_TILE > start)
            def _():
                bound = jnp.where(lane < count - offset, first + lane, -1)

                def add_dq(part):
                    dqt[tile] += part

                tile_step(
                    key, value, key_t, row_tile(tile, q_s, do_s, lse_s, delta_s), position, bound,
                    acc_k, acc_v, add_dq,
                )

            return inner

        lax.fori_loop(0, length, row_step, 0)
        own[pl.ds(start, KEY_TILE), :HEAD_SIZE] = acc_k[...] * scale
        own[pl.ds(start, KEY_TILE), HEAD_SIZE:] = acc_v[...]
        return carry

    lax.fori_loop(0, (limit + KEY_TILE - 1) // KEY_TILE, key_step, 0)

    half = ROW_TILE // 2
    outs = [(chip, kept[n]) for n, chip in enumerate((0, *CHIPS))]
    outs += [(chip ^ CORE, passed[n]) for n, chip in enumerate((0, *CHIPS))]
    for partner, out in outs:
        block = me ^ partner
        shard = block // 2
        count = counts_ref[block & ~1] + counts_ref[block | 1]

        def put(rows, t, first):
            live = count > t * ROW_TILE
            size = rows.stop - rows.start

            @pl.when(live)
            def _():
                for h in range(GROUP):
                    columns = slice(h * HEAD_SIZE, (h + 1) * HEAD_SIZE)
                    part = (dqt[SHARD_TILES * shard + t, :, columns] * scale).T
                    out[rows, columns] = part[first : first + size].astype(jnp.bfloat16)

            @pl.when(jnp.logical_not(live))
            def _():
                out[rows, :] = jnp.zeros((size, WIDTH), jnp.bfloat16)

        @pl.when((block & 1) == 0)
        def _():
            put(slice(0, ROW_TILE), 0, 0)
            put(slice(ROW_TILE, home_rows), 1, 0)

        @pl.when((block & 1) == 1)
        def _():
            put(slice(0, half), 1, half)
            put(slice(half, home_rows), 2, 0)


def row_scratch(plane_rows):
    bf16, f32 = jnp.bfloat16, jnp.float32
    tile_count = plane_rows // ROW_TILE
    return [
        pltpu.VMEM((plane_rows, WIDTH), bf16),
        pltpu.VMEM((plane_rows, WIDTH), bf16),
        pltpu.VMEM((tile_count, WIDTH), f32),
        pltpu.VMEM((tile_count, WIDTH), f32),
        pltpu.VMEM((tile_count, HEAD_SIZE, WIDTH), f32),
    ]


def far_attention(me, counts, small, arrays, kvs):
    bf16, f32 = jnp.bfloat16, jnp.float32
    blocks = KEY_VALUE_HEADS
    rows = kvs[0].shape[0]
    columns = 2 * HEAD_SIZE
    plane_rows = 2 * (rows - INFO_ROWS)
    tile_count = plane_rows // ROW_TILE
    return pl.pallas_call(
        far_kernel,
        out_shape=(jax.ShapeDtypeStruct((rows, columns), bf16),) * 3
        + (
            jax.ShapeDtypeStruct((tile_count, HEAD_SIZE, WIDTH), f32),
            jax.ShapeDtypeStruct((1,), jnp.int32),
        ),
        in_specs=[SMEM] * 2 + [VMEM] + [ANY] * 12,
        out_specs=[ANY] * 4 + [SMEM],
        scratch_shapes=row_scratch(plane_rows)
        + [
            pltpu.VMEM((3, rows, columns), bf16),
            pltpu.VMEM((rows - INFO_ROWS, HEAD_SIZE), f32),
            pltpu.VMEM((rows - INFO_ROWS, HEAD_SIZE), f32),
            pltpu.SMEM((tile_count + 1,), jnp.int32),
            pltpu.SMEM((blocks,), jnp.int32),
            pltpu.SMEM((3,), jnp.int32),
            pltpu.SemaphoreType.DMA((2 * blocks,)),
            pltpu.SemaphoreType.DMA((3,)),
            pltpu.SemaphoreType.DMA((3,)),
            pltpu.SemaphoreType.DMA((tile_count,)),
            pltpu.VMEM((3, rows, columns), bf16),
        ],
        compiler_params=pltpu.CompilerParams(vmem_limit_bytes=48 * 1024 * 1024),
        cost_estimate=pl.CostEstimate(
            flops=10_000_000_000, bytes_accessed=12_000_000, transcendentals=8_000_000
        ),
        name="far_attention",
    )(me, counts, small, *arrays, *kvs)


def own_attention(me, counts, small, arrays, kv, dqt, note):
    bf16, f32 = jnp.bfloat16, jnp.float32
    blocks = KEY_VALUE_HEADS
    capacity = kv.shape[0] - INFO_ROWS
    plane_rows = 2 * capacity
    tile_count = plane_rows // ROW_TILE
    return pl.pallas_call(
        own_kernel,
        out_shape=(jax.ShapeDtypeStruct((plane_rows // blocks, WIDTH), bf16),) * 8
        + (jax.ShapeDtypeStruct((capacity, 2 * HEAD_SIZE), f32),),
        in_specs=[SMEM] * 2 + [VMEM] + [ANY] * 9 + [VMEM, ANY, ANY],
        out_specs=[VMEM] * 9,
        scratch_shapes=row_scratch(plane_rows)
        + [
            pltpu.VMEM((KEY_TILE, HEAD_SIZE), f32),
            pltpu.VMEM((KEY_TILE, HEAD_SIZE), f32),
            pltpu.SMEM((tile_count + 1,), jnp.int32),
            pltpu.SMEM((blocks,), jnp.int32),
            pltpu.SemaphoreType.DMA((2 * blocks,)),
            pltpu.SemaphoreType.DMA((tile_count,)),
        ],
        compiler_params=pltpu.CompilerParams(vmem_limit_bytes=48 * 1024 * 1024),
        cost_estimate=pl.CostEstimate(
            flops=1_000_000, bytes_accessed=100_000, transcendentals=1_000
        ),
        name="own_attention",
    )(me, counts, small, *arrays, kv, dqt, note)


def unpack_rows_kernel(me_ref, kept, passed, *rest):
    pairs, out = rest[:3], rest[3]
    home_rows = kept.shape[0]
    me = me_ref[0]

    def put(partner, rows):
        start = pl.multiple_of((me ^ partner) * WIDTH, HEAD_SIZE)
        out[:, pl.ds(start, WIDTH)] = rows

    put(0, kept[...])
    put(CORE, passed[...])
    for chip, pair in zip(CHIPS, pairs):
        put(chip, pair[:home_rows])
        put(chip ^ CORE, pair[home_rows:])


def unpack_rows(me, kept, passed, pairs):
    home_rows = kept.shape[0]
    return pl.pallas_call(
        unpack_rows_kernel,
        out_shape=jax.ShapeDtypeStruct((home_rows, KEY_VALUE_HEADS * WIDTH), jnp.bfloat16),
        in_specs=[SMEM] + [VMEM] * 5,
        out_specs=VMEM,
        name="unpack_rows",
    )(me, kept, passed, *pairs)


def plane_device(queries, keys, values, outputs, output_gradient, lse, ranks):
    planes = lax.axis_size("outer")
    plane = ("inner", "head")
    blocks = KEY_VALUE_HEADS
    home_rows = queries.shape[0]
    plane_rows = blocks * home_rows
    capacity = plane_rows // 2
    surviving_tokens = BALANCED_TOKENS * planes * lax.axis_size("inner")
    bf16, f32 = jnp.bfloat16, jnp.float32
    me = lax.axis_index(plane).reshape(1).astype(jnp.int32)

    def swap(array, k):
        return lax.ppermute(array, plane, [(i, i ^ k) for i in range(blocks)])

    sent = pack_pairs(surviving_tokens, ranks, keys, values)
    arrived = lax.all_to_all(sent, plane, split_axis=0, concat_axis=0, tiled=True)
    packed = [
        pack_rows((chip, chip ^ CORE), me, queries, output_gradient) for chip in CHIPS
    ]
    pairs = [swap(rows, chip) for rows, chip in zip(packed, CHIPS)]
    beside = swap(pack_rows((CORE,), me, queries, output_gradient), CORE)
    small = lax.all_to_all(
        pack_small(lse, output_gradient, outputs), plane, split_axis=0, concat_axis=0, tiled=True
    )
    crossed = [swap(pair[1:], CORE) for pair in pairs]
    arrays = [queries, output_gradient, beside, *pairs, *crossed]

    mine, counts = compact(arrived)
    up = [
        lax.ppermute(mine, "outer", [(i, i + k) for i in range(planes - k)])
        for k in range(1, planes)
    ]

    *down, dqt, full = far_attention(me, counts, small, arrays, up)
    note = swap(down[0][capacity:, :HEAD_SIZE], CORE)
    *dqs, own = own_attention(me, counts, small, arrays, mine, dqt, note)
    kept, passed = dqs[:4], dqs[4:]
    full = full[0] > 0
    for k in (3, 2, 1):
        back = lax.ppermute(down[k - 1], "outer", [(i + k, i) for i in range(planes - k)])
        own = own + back[:capacity].astype(f32)
        full = full | (back[capacity, 0] > 0)
    passed = [swap(rows, CORE) for rows in passed]
    joined = [jnp.concatenate([kept[n], passed[n]], axis=0) for n in range(1, 4)]
    own, joined[2] = lax.optimization_barrier((own, joined[2]))
    pairs = [swap(rows, chip) for rows, chip in zip(joined, CHIPS)]
    dq_home = unpack_rows(me, kept[0], passed[0], pairs)

    starts = jnp.cumsum(counts) - counts
    within = jnp.arange(home_rows, dtype=jnp.int32)
    local = jnp.where(within[None, :] < counts[:, None], starts[:, None] + within[None, :], -1)
    pick = (
        jnp.arange(capacity, dtype=jnp.int32)[:, None] == local.reshape(1, plane_rows)
    ).astype(bf16)
    spread = lax.dot_general(
        pick, own.astype(bf16), (((0,), (0,)), ((), ())), preferred_element_type=f32
    ).astype(bf16)
    kv_home = lax.all_to_all(
        spread.reshape(blocks, home_rows, 2 * HEAD_SIZE),
        plane, split_axis=0, concat_axis=0, tiled=True,
    )
    dk = kv_home[:, :, :HEAD_SIZE].transpose(1, 0, 2).reshape(home_rows, blocks * HEAD_SIZE)
    dv = kv_home[:, :, HEAD_SIZE:].transpose(1, 0, 2).reshape(home_rows, blocks * HEAD_SIZE)
    return (dq_home, dk, dv), full


def solution(mesh):
    spec = P(("seq", "head"), None)
    heads = mesh.shape["head"]
    inner = max(KEY_VALUE_HEADS // heads, 1)
    planes = mesh.shape["seq"] // inner
    if planes != 4 or inner * heads != KEY_VALUE_HEADS:
        return jax.shard_map(
            per_device,
            mesh=mesh,
            in_specs=(spec,) * 6 + (P(("seq", "head")),),
            out_specs=(spec,) * 3,
            check_vma=False,
        )
    axes = ("outer", "inner", "head")

    def device(*blocks):
        fast, full = plane_device(*blocks)
        return lax.cond(full, lambda: per_device(*blocks, seq=("outer", "inner")), lambda: fast)

    return jax.shard_map(
        device,
        mesh=Mesh(mesh.devices.reshape(planes, inner, heads), axes),
        in_specs=(P(axes, None),) * 6 + (P(axes),),
        out_specs=(P(axes, None),) * 3,
        check_vma=False,
    )
```

```python
import functools

import jax
import jax.numpy as jnp
from jax import lax
from jax.experimental import pallas as pl
from jax.experimental.pallas import tpu as pltpu
from jax.sharding import Mesh
from jax.sharding import PartitionSpec as P

QUERY_HEADS = 40
KEY_VALUE_HEADS = 8
HEAD_SIZE = 128
BALANCED_TOKENS = 128


block_keys = 512


def per_device(queries, keys, values, outputs, output_gradient, lse, ranks, seq="seq"):
    sequence_count = lax.axis_size(seq)
    head_total = lax.axis_size("head")
    home_rows = queries.shape[0]
    capacity = home_rows * head_total
    slots = capacity // sequence_count
    surviving_tokens = BALANCED_TOKENS * sequence_count
    group_size = QUERY_HEADS // KEY_VALUE_HEADS
    local_key_value = KEY_VALUE_HEADS // head_total
    scale = HEAD_SIZE ** (-0.5)

    def split_heads(array):
        return array.reshape(home_rows, head_total, array.shape[1] // head_total)

    moved = (
        lax.all_to_all(split_heads(queries), "head", split_axis=1, concat_axis=0, tiled=True),
        lax.all_to_all(split_heads(keys), "head", split_axis=1, concat_axis=0, tiled=True),
        lax.all_to_all(split_heads(values), "head", split_axis=1, concat_axis=0, tiled=True),
        lax.all_to_all(
            split_heads(output_gradient), "head", split_axis=1, concat_axis=0, tiled=True
        ),
        lax.all_to_all(split_heads(lse), "head", split_axis=1, concat_axis=0, tiled=True),
        lax.all_to_all(split_heads(outputs), "head", split_axis=1, concat_axis=0, tiled=True),
    )
    shard_rank_list = lax.all_gather(ranks, "head", axis=0, tiled=True)
    first_rank = shard_rank_list[0]
    living_count = jnp.sum((shard_rank_list < surviving_tokens).astype(jnp.int32))
    table = lax.all_gather(
        jnp.stack([first_rank, living_count])[None, :], seq, axis=0, tiled=True
    )

    def to_pairs(array):
        flat = array.reshape(slots, sequence_count, array.shape[-1])
        return jnp.roll(flat, first_rank, axis=1)

    arrived = (
        lax.all_to_all(to_pairs(moved[0]), seq, split_axis=1, concat_axis=1, tiled=True),
        lax.all_to_all(to_pairs(moved[1]), seq, split_axis=1, concat_axis=1, tiled=True),
        lax.all_to_all(to_pairs(moved[2]), seq, split_axis=1, concat_axis=1, tiled=True),
        lax.all_to_all(to_pairs(moved[3]), seq, split_axis=1, concat_axis=1, tiled=True),
        lax.all_to_all(to_pairs(moved[4]), seq, split_axis=1, concat_axis=1, tiled=True),
        lax.all_to_all(to_pairs(moved[5]), seq, split_axis=1, concat_axis=1, tiled=True),
    )
    my_index = lax.axis_index(seq)
    starts = table[:, 0]
    count_table = table[:, 1]
    offset = (my_index - starts) % sequence_count
    within = jnp.arange(slots, dtype=jnp.int32)[:, None] * sequence_count + offset[None, :]
    alive = within < count_table[None, :]
    target_rank = jnp.where(
        alive, (starts[None, :] + within) // sequence_count, BALANCED_TOKENS
    ).reshape(-1)

    def place(array):
        width = array.shape[-1]
        return (
            jnp.zeros((BALANCED_TOKENS, width), array.dtype)
            .at[target_rank]
            .set(array.reshape(slots * sequence_count, width), mode="drop")
        )

    query_row_block = place(arrived[0]).reshape(
        BALANCED_TOKENS, local_key_value, group_size, HEAD_SIZE
    )
    key_row_block = place(arrived[1]).reshape(BALANCED_TOKENS, local_key_value, HEAD_SIZE)
    value_row_block = place(arrived[2]).reshape(BALANCED_TOKENS, local_key_value, HEAD_SIZE)
    grad_rows = place(arrived[3]).reshape(BALANCED_TOKENS, local_key_value, group_size, HEAD_SIZE)
    lse_rows = (
        place(arrived[4]).astype(jnp.float32).reshape(BALANCED_TOKENS, local_key_value, group_size)
    )
    out_rows = (
        place(arrived[5])
        .astype(jnp.float32)
        .reshape(BALANCED_TOKENS, local_key_value, group_size, HEAD_SIZE)
    )
    delta_rows = (
        jnp.sum(grad_rows.astype(jnp.float32) * out_rows, axis=-1)
        .astype(jnp.bfloat16)
        .astype(jnp.float32)
    )
    gathered = (
        lax.all_gather(key_row_block, seq, axis=0, tiled=True),
        lax.all_gather(value_row_block, seq, axis=0, tiled=True),
    )
    all_keys = gathered[0].reshape(sequence_count, BALANCED_TOKENS, local_key_value, HEAD_SIZE)
    all_values = gathered[1].reshape(sequence_count, BALANCED_TOKENS, local_key_value, HEAD_SIZE)
    rows_per = block_keys // sequence_count
    inner = 1
    outer = BALANCED_TOKENS // rows_per // inner
    query_rank = jnp.arange(BALANCED_TOKENS, dtype=jnp.int32) * sequence_count + my_index
    lse_t = lse_rows.transpose(1, 2, 0)
    delta_t = delta_rows.transpose(1, 2, 0)
    position = jnp.arange(sequence_count * rows_per, dtype=jnp.int32)

    def key_step(query_acc, row_start):
        key_blk = lax.dynamic_slice_in_dim(all_keys, row_start, rows_per, 1).reshape(
            sequence_count * rows_per, local_key_value, HEAD_SIZE
        )
        value_blk = lax.dynamic_slice_in_dim(all_values, row_start, rows_per, 1).reshape(
            sequence_count * rows_per, local_key_value, HEAD_SIZE
        )
        key_owner_rank = (row_start + position % rows_per) * sequence_count + position // rows_per
        mask = key_owner_rank[None, None, None, :] <= query_rank[None, None, :, None]
        scores = (
            jnp.einsum(
                "rgmc,kgc->gmrk", query_row_block, key_blk, preferred_element_type=jnp.float32
            )
            * scale
        )
        probs = jnp.where(mask, jnp.exp(scores - lse_t[..., None]), 0.0)
        dprob = jnp.einsum(
            "rgmc,kgc->gmrk", grad_rows, value_blk, preferred_element_type=jnp.float32
        )
        dscore = probs * (dprob - delta_t[..., None])
        probs_low = probs.astype(jnp.bfloat16)
        dscore_low = dscore.astype(jnp.bfloat16)
        query_acc = query_acc + scale * jnp.einsum(
            "gmrk,kgc->rgmc", dscore_low, key_blk, preferred_element_type=jnp.float32
        )
        key_part = scale * jnp.einsum(
            "gmrk,rgmc->kgc", dscore_low, query_row_block, preferred_element_type=jnp.float32
        )
        value_part = jnp.einsum(
            "gmrk,rgmc->kgc", probs_low, grad_rows, preferred_element_type=jnp.float32
        )
        return (
            query_acc,
            key_part.reshape(sequence_count, rows_per, local_key_value * HEAD_SIZE),
            value_part.reshape(sequence_count, rows_per, local_key_value * HEAD_SIZE),
        )

    def outer_step(query_acc, outer_index):

        def inner_step(query_inner, inner_index):
            row_start = (outer_index * inner + inner_index) * rows_per
            query_new, key_part, value_part = key_step(query_inner, row_start)
            return (query_new, (key_part, value_part))

        query_acc, (key_parts, value_parts) = lax.scan(
            inner_step, query_acc, jnp.arange(inner, dtype=jnp.int32)
        )
        key_parts = key_parts.transpose(1, 0, 2, 3).reshape(
            sequence_count, inner * rows_per, local_key_value * HEAD_SIZE
        )
        value_parts = value_parts.transpose(1, 0, 2, 3).reshape(
            sequence_count, inner * rows_per, local_key_value * HEAD_SIZE
        )
        received = (
            lax.all_to_all(key_parts, seq, split_axis=0, concat_axis=0, tiled=True),
            lax.all_to_all(value_parts, seq, split_axis=0, concat_axis=0, tiled=True),
        )
        return (query_acc, (jnp.sum(received[0], axis=0), jnp.sum(received[1], axis=0)))

    start_acc = jnp.zeros((BALANCED_TOKENS, local_key_value, group_size, HEAD_SIZE), jnp.float32)
    query_acc, (key_sums, value_sums) = lax.scan(
        outer_step, start_acc, jnp.arange(outer, dtype=jnp.int32)
    )
    query_done = query_acc.reshape(
        BALANCED_TOKENS, local_key_value * group_size * HEAD_SIZE
    ).astype(jnp.bfloat16)
    key_done = key_sums.reshape(BALANCED_TOKENS, local_key_value * HEAD_SIZE).astype(jnp.bfloat16)
    value_done = value_sums.reshape(BALANCED_TOKENS, local_key_value * HEAD_SIZE).astype(
        jnp.bfloat16
    )
    safe_rows = jnp.minimum(target_rank, BALANCED_TOKENS - 1)
    alive_flat = alive.reshape(-1)

    def collect(array):
        picked = jnp.where(alive_flat[:, None], array[safe_rows], jnp.zeros((), array.dtype))
        return picked.reshape(slots, sequence_count, array.shape[-1])

    returned = (
        lax.all_to_all(collect(query_done), seq, split_axis=1, concat_axis=1, tiled=True),
        lax.all_to_all(collect(key_done), seq, split_axis=1, concat_axis=1, tiled=True),
        lax.all_to_all(collect(value_done), seq, split_axis=1, concat_axis=1, tiled=True),
    )

    def to_home(array):
        unrolled = jnp.roll(array, -first_rank, axis=1)
        return unrolled.reshape(capacity, 1, array.shape[-1])

    homed = (
        lax.all_to_all(to_home(returned[0]), "head", split_axis=0, concat_axis=1, tiled=True),
        lax.all_to_all(to_home(returned[1]), "head", split_axis=0, concat_axis=1, tiled=True),
        lax.all_to_all(to_home(returned[2]), "head", split_axis=0, concat_axis=1, tiled=True),
    )
    query_grads = homed[0].reshape(home_rows, head_total * homed[0].shape[-1])
    key_gradient_output = homed[1].reshape(home_rows, head_total * homed[1].shape[-1])
    value_gradient = homed[2].reshape(home_rows, head_total * homed[2].shape[-1])
    return (query_grads, key_gradient_output, value_gradient)

LOG2E = 1.4426950408889634
KEY_TILE = 256
ROW_TILE = 128
INFO_ROWS = 16
AUX_LANES = 256
SMEM = pl.BlockSpec(memory_space=pltpu.SMEM)
VMEM = pl.BlockSpec(memory_space=pltpu.VMEM)
HBM = pl.BlockSpec(memory_space=pltpu.HBM)
GROUP = QUERY_HEADS // KEY_VALUE_HEADS
WIDTH = GROUP * HEAD_SIZE
CHIPS = (5, 4, 1)
CORE = 2
SHARD_TILES = 3
PASS_ROWS = (256, 512, 768)


def pack_pairs_kernel(limit, ranks_ref, k_ref, v_ref, out_ref):
    home_rows = k_ref.shape[0]
    live = jnp.where(ranks_ref[...] < limit, 1.0, 0.0)
    info = jnp.broadcast_to(
        jnp.sum(live, axis=1, keepdims=True), (INFO_ROWS, 2 * HEAD_SIZE)
    ).astype(out_ref.dtype)
    for g in range(KEY_VALUE_HEADS):
        columns = slice(g * HEAD_SIZE, (g + 1) * HEAD_SIZE)
        out_ref[g, :home_rows, :HEAD_SIZE] = k_ref[:, columns]
        out_ref[g, :home_rows, HEAD_SIZE:] = v_ref[:, columns]
        out_ref[g, home_rows:, :] = info


def pack_pairs(limit, ranks, keys, values):
    home_rows = keys.shape[0]
    return pl.pallas_call(
        functools.partial(pack_pairs_kernel, limit),
        out_shape=jax.ShapeDtypeStruct(
            (KEY_VALUE_HEADS, home_rows + INFO_ROWS, 2 * HEAD_SIZE), keys.dtype
        ),
        in_specs=[VMEM] * 3,
        out_specs=VMEM,
        name="pack_pairs",
    )(ranks.reshape(1, home_rows), keys, values)


def pack_rows_kernel(partners, me_ref, q_hbm, do_hbm, out, sems):
    copies = []
    for n, partner in enumerate(partners):
        start = pl.multiple_of((me_ref[0] ^ partner) * WIDTH, HEAD_SIZE)
        for m, source in enumerate((q_hbm, do_hbm)):
            copies.append(
                pltpu.make_async_copy(
                    source.at[:, pl.ds(start, WIDTH)],
                    out.at[n, :, pl.ds(m * WIDTH, WIDTH)],
                    sems.at[2 * n + m],
                )
            )
    for copy in copies:
        copy.start()
    for copy in copies:
        copy.wait()


def pack_rows(partners, me, queries, output_gradient):
    home_rows = queries.shape[0]
    return pl.pallas_call(
        functools.partial(pack_rows_kernel, partners),
        out_shape=jax.ShapeDtypeStruct((len(partners), home_rows, 2 * WIDTH), queries.dtype),
        in_specs=[SMEM, HBM, HBM],
        out_specs=VMEM,
        scratch_shapes=[pltpu.SemaphoreType.DMA((2 * len(partners),))],
        name="pack_rows",
    )(me, queries, output_gradient)


def pack_small_kernel(lse_ref, do_ref, o_ref, out, columns, lanes):
    home_rows = do_ref.shape[0]
    columns[...] = jnp.zeros_like(columns)
    for g in range(KEY_VALUE_HEADS):
        columns[:, 16 * g : 16 * g + GROUP] = lse_ref[:, g * GROUP : (g + 1) * GROUP].astype(
            jnp.float32
        )
    for h in range(QUERY_HEADS):
        head = slice(h * HEAD_SIZE, (h + 1) * HEAD_SIZE)
        product = do_ref[:, head].astype(jnp.float32) * o_ref[:, head].astype(jnp.float32)
        column = 16 * (h // GROUP) + 8 + h % GROUP
        columns[:, column : column + 1] = jnp.sum(product, axis=1, keepdims=True)
    lanes[...] = jnp.zeros_like(lanes)
    lanes[:, :home_rows] = columns[...].T
    for g in range(KEY_VALUE_HEADS):
        out[g] = lanes[16 * g : 16 * g + INFO_ROWS, :].astype(out.dtype)


def pack_small(lse, output_gradient, outputs):
    f32 = jnp.float32
    return pl.pallas_call(
        pack_small_kernel,
        out_shape=jax.ShapeDtypeStruct((KEY_VALUE_HEADS, INFO_ROWS, AUX_LANES), jnp.bfloat16),
        in_specs=[VMEM] * 3,
        out_specs=VMEM,
        scratch_shapes=[
            pltpu.VMEM((lse.shape[0], HEAD_SIZE), f32),
            pltpu.VMEM((HEAD_SIZE, AUX_LANES), f32),
        ],
        compiler_params=pltpu.CompilerParams(vmem_limit_bytes=32 * 1024 * 1024),
        name="pack_small",
    )(lse, output_gradient, outputs)


def compact_kernel(arrived, out, counts_ref):
    home_rows = arrived.shape[1] - INFO_ROWS
    capacity = out.shape[0] - INFO_ROWS
    row = lax.broadcasted_iota(jnp.int32, (capacity, home_rows), 0)
    within = lax.broadcasted_iota(jnp.int32, (capacity, home_rows), 1)
    total = jnp.int32(0)
    picked = []
    for block in range(KEY_VALUE_HEADS):
        count = jnp.max(arrived[block, home_rows:, :].astype(jnp.float32)).astype(jnp.int32)
        counts_ref[block] = count
        hit = (row == within + total) & (within < count)
        picked.append(jnp.where(hit, 1.0, 0.0).astype(jnp.bfloat16))
        total = total + count
    acc = jnp.zeros((capacity, out.shape[1]), jnp.float32)
    for block in range(KEY_VALUE_HEADS):
        acc += jnp.dot(
            picked[block], arrived[block, :home_rows, :], preferred_element_type=jnp.float32
        )
    out[:capacity, :] = acc.astype(out.dtype)
    line = lax.broadcasted_iota(jnp.int32, (INFO_ROWS, out.shape[1]), 0)
    out[capacity:, :] = (
        jnp.where(line == 0, total // 64, jnp.where(line == 1, total % 64, 0))
        .astype(jnp.float32)
        .astype(out.dtype)
    )


def compact(arrived):
    blocks, rows, columns = arrived.shape
    capacity = blocks * (rows - INFO_ROWS) // 2
    return pl.pallas_call(
        compact_kernel,
        out_shape=(
            jax.ShapeDtypeStruct((capacity + INFO_ROWS, columns), arrived.dtype),
            jax.ShapeDtypeStruct((blocks,), jnp.int32),
        ),
        in_specs=[VMEM],
        out_specs=(VMEM, SMEM),
        compiler_params=pltpu.CompilerParams(vmem_limit_bytes=32 * 1024 * 1024),
        name="compact",
    )(arrived)


def load_rows(me, counts_ref, arrays, q_s, do_s, sems):
    home_rows = q_s.shape[0] // KEY_VALUE_HEADS
    q_hbm, do_hbm, beside, pairs, crossed = arrays
    column = pl.multiple_of(me * WIDTH, HEAD_SIZE)
    left, right = pl.ds(0, WIDTH), pl.ds(WIDTH, WIDTH)
    sources = [
        (0, q_hbm.at[:, pl.ds(column, WIDTH)], do_hbm.at[:, pl.ds(column, WIDTH)]),
        (CORE, beside.at[0, :, left], beside.at[0, :, right]),
    ]
    for chip, pair, cross in zip(CHIPS, pairs, crossed):
        sources.append((chip, pair.at[0, :, left], pair.at[0, :, right]))
        sources.append((chip ^ CORE, cross.at[0, :, left], cross.at[0, :, right]))
    plans = []
    for n, (partner, q, do) in enumerate(sources):
        source = me ^ partner
        rows = pl.ds(pl.multiple_of(source * home_rows, 64), home_rows)
        shard = counts_ref[source & ~1] + counts_ref[source | 1]
        needed = ((source & 1) == 0) | (shard > ROW_TILE)
        plans.append(
            (
                needed,
                [
                    pltpu.make_async_copy(q, q_s.at[rows, :], sems.at[2 * n]),
                    pltpu.make_async_copy(do, do_s.at[rows, :], sems.at[2 * n + 1]),
                ],
            )
        )

    def each(act):
        for needed, copies in plans:

            @pl.when(needed)
            def _():
                for copy in copies:
                    act(copy)

    return each


def list_tiles(counts_ref, tiles, starts):
    length = jnp.int32(0)
    total = jnp.int32(0)
    for shard in range(KEY_VALUE_HEADS // 2):
        count = counts_ref[2 * shard] + counts_ref[2 * shard + 1]
        starts[shard] = total
        total = total + count
        for t in range(SHARD_TILES):
            live = count > t * ROW_TILE

            @pl.when(live)
            def _():
                tiles[length] = SHARD_TILES * shard + t

            length = length + live.astype(jnp.int32)
    return length, total


def spread_lanes(aux_s, lse_s, delta_s):
    lane = lax.broadcasted_iota(jnp.int32, (INFO_ROWS, ROW_TILE), 1)
    for shard in range(KEY_VALUE_HEADS // 2):
        low = aux_s[2 * shard].astype(jnp.float32)
        high = aux_s[2 * shard + 1].astype(jnp.float32)
        half = ROW_TILE // 2
        middle = jnp.where(
            lane < half, low[:, ROW_TILE:], pltpu.roll(high[:, :ROW_TILE], half, axis=1)
        )
        last = pltpu.roll(high, AUX_LANES - half, axis=1)[:, :ROW_TILE]
        for t, rows in enumerate((low[:, :ROW_TILE], middle, last)):
            row = SHARD_TILES * shard + t
            for h in range(GROUP):
                columns = slice(h * ROW_TILE, (h + 1) * ROW_TILE)
                lse_s[row : row + 1, columns] = rows[h : h + 1] * LOG2E
                delta_s[row : row + 1, columns] = rows[8 + h : 9 + h]


def row_tile(tile, q_s, do_s, lse_s, delta_s):
    def stack(ref):
        rows = ref[pl.ds(pl.multiple_of(tile * ROW_TILE, ROW_TILE), ROW_TILE), :]
        return jnp.concatenate(
            [rows[:, h * HEAD_SIZE : (h + 1) * HEAD_SIZE] for h in range(GROUP)], axis=0
        )

    return stack(q_s), stack(do_s), lse_s[pl.ds(tile, 1), :], delta_s[pl.ds(tile, 1), :]


def tile_step(key, value, key_t, rows, position, bound, acc_k, acc_v, add_dq):
    q, do, lse, delta = rows
    scale = HEAD_SIZE ** (-0.5)
    dims = (((1,), (1,)), ((), ()))
    scores = lax.dot_general(key, q, dims, preferred_element_type=jnp.float32)
    prob = jnp.where(position <= bound, jnp.exp2(scores * (scale * LOG2E) - lse), 0.0)
    dprob = lax.dot_general(value, do, dims, preferred_element_type=jnp.float32)
    dscore = (prob * (dprob - delta)).astype(jnp.bfloat16)
    acc_v[...] += jnp.dot(prob.astype(jnp.bfloat16), do, preferred_element_type=jnp.float32)
    acc_k[...] += jnp.dot(dscore, q, preferred_element_type=jnp.float32)
    add_dq(jnp.dot(key_t, dscore, preferred_element_type=jnp.float32))


def far_kernel(me_ref, counts_ref, *rest):
    aux_s, arrays, kvs, rest = rest[0], rest[1:10], rest[10:13], rest[13:]
    arrays = (*arrays[:3], arrays[3:6], arrays[6:9])
    downs, dqt_out, full_ref, rest = rest[:3], rest[3], rest[4], rest[5:]
    (
        q_s, do_s, lse_s, delta_s, dqt, kv_s, acc_k, acc_v, tiles, starts, limits, sems, kv_sem,
        down_sem, dq_sem, down_s,
    ) = rest
    capacity = downs[0].shape[0] - INFO_ROWS
    scale = HEAD_SIZE ** (-0.5)
    each = load_rows(me_ref[0], counts_ref, arrays, q_s, do_s, sems)
    each(lambda copy: copy.start())
    kv_copies = [
        pltpu.make_async_copy(kvs[n], kv_s.at[n], kv_sem.at[n])
        for n in range(3)
    ]
    for copy in kv_copies:
        copy.start()
    length, total = list_tiles(counts_ref, tiles, starts)

    def zero_tile(n, carry):
        dqt[tiles[n]] = jnp.zeros(dqt.shape[1:], jnp.float32)
        return carry

    lax.fori_loop(0, length, zero_tile, 0)
    spread_lanes(aux_s, lse_s, delta_s)
    for copy in kv_copies:
        copy.wait()
    most = total
    for n in range(3):
        info = kv_s[n, capacity:, :].astype(jnp.float32)
        limit = (jnp.max(info[0:1]) * 64.0 + jnp.max(info[1:2])).astype(jnp.int32)
        limits[n] = jnp.minimum(limit, capacity)
        most = jnp.maximum(most, limit)
    full = most > capacity
    full_ref[0] = full.astype(jnp.int32)
    for n in range(3):
        down_s[n, capacity:, :] = jnp.full(
            (INFO_ROWS, 2 * HEAD_SIZE), jnp.where(full, 1.0, 0.0)
        ).astype(jnp.bfloat16)
    each(lambda copy: copy.wait())
    lane = lax.broadcasted_iota(jnp.int32, (1, WIDTH), 1) % ROW_TILE

    def block_step(step, carry):
        index = 2 - step
        limit = limits[index]

        def run(rows):
            key = kv_s[index, :rows, :HEAD_SIZE]
            value = kv_s[index, :rows, HEAD_SIZE:]
            key_t = key.T
            acc_k[:rows] = jnp.zeros((rows, HEAD_SIZE), jnp.float32)
            acc_v[:rows] = jnp.zeros((rows, HEAD_SIZE), jnp.float32)
            position = lax.broadcasted_iota(jnp.int32, (rows, 1), 0)

            def row_step(n, inner):
                tile = tiles[n]
                shard = tile // SHARD_TILES
                count = counts_ref[2 * shard] + counts_ref[2 * shard + 1]
                alive = lane < count - (tile % SHARD_TILES) * ROW_TILE
                bound = jnp.where(alive, limit - 1, -1)

                def add_dq(part):
                    dqt[tile] += part

                tile_step(
                    key, value, key_t, row_tile(tile, q_s, do_s, lse_s, delta_s), position, bound,
                    acc_k.at[pl.ds(0, rows), :], acc_v.at[pl.ds(0, rows), :], add_dq,
                )
                return inner

            lax.fori_loop(0, length, row_step, 0)
            down_s[index, :rows, :HEAD_SIZE] = (acc_k[:rows] * scale).astype(jnp.bfloat16)
            down_s[index, :rows, HEAD_SIZE:] = acc_v[:rows].astype(jnp.bfloat16)
            if rows < capacity:
                down_s[index, rows:capacity, :] = jnp.zeros(
                    (capacity - rows, 2 * HEAD_SIZE), jnp.bfloat16
                )

        below = 0
        for rows in PASS_ROWS:

            @pl.when((limit > below) & (limit <= rows))
            def _():
                run(rows)

            below = rows

        @pl.when(limit == 0)
        def _():
            down_s[index, :capacity, :] = jnp.zeros((capacity, 2 * HEAD_SIZE), jnp.bfloat16)

        return carry

    lax.fori_loop(0, 3, block_step, 0)
    down_copies = [
        pltpu.make_async_copy(down_s.at[n], downs[n], down_sem.at[n]) for n in range(3)
    ]
    for copy in down_copies:
        copy.start()

    def dq_copy(n):
        tile = tiles[n]
        return pltpu.make_async_copy(dqt.at[tile], dqt_out.at[tile], dq_sem.at[n])

    def start_dq(n, carry):
        dq_copy(n).start()
        return carry

    def wait_dq(n, carry):
        dq_copy(n).wait()
        return carry

    lax.fori_loop(0, length, start_dq, 0)
    for copy in down_copies:
        copy.wait()
    lax.fori_loop(0, length, wait_dq, 0)


def own_kernel(me_ref, counts_ref, *rest):
    aux_s, arrays, kv, dqt_in, rest = rest[0], rest[1:10], rest[10], rest[11], rest[13:]
    arrays = (*arrays[:3], arrays[3:6], arrays[6:9])
    dq_out, own, rest = rest[0], rest[1], rest[2:]
    q_s, do_s, lse_s, delta_s, dqt, acc_k, acc_v, tiles, starts, sems, dq_sem, dq_s, out_sem = rest
    capacity = kv.shape[0] - INFO_ROWS
    home_rows = dq_out.shape[1]
    scale = HEAD_SIZE ** (-0.5)
    me = me_ref[0]
    each = load_rows(me, counts_ref, arrays, q_s, do_s, sems)
    each(lambda copy: copy.start())
    length, total = list_tiles(counts_ref, tiles, starts)
    limit = jnp.minimum(total, capacity)

    def dq_copy(n):
        tile = tiles[n]
        return pltpu.make_async_copy(dqt_in.at[tile], dqt.at[tile], dq_sem.at[n])

    def start_dq(n, carry):
        dq_copy(n).start()
        return carry

    def wait_dq(n, carry):
        dq_copy(n).wait()
        return carry

    lax.fori_loop(0, length, start_dq, 0)
    own[...] = jnp.zeros_like(own)
    spread_lanes(aux_s, lse_s, delta_s)
    each(lambda copy: copy.wait())
    lax.fori_loop(0, length, wait_dq, 0)
    lane = lax.broadcasted_iota(jnp.int32, (1, WIDTH), 1) % ROW_TILE

    def key_step(kt, carry):
        start = pl.multiple_of(kt * KEY_TILE, KEY_TILE)
        key = kv[pl.ds(start, KEY_TILE), :HEAD_SIZE]
        value = kv[pl.ds(start, KEY_TILE), HEAD_SIZE:]
        key_t = key.T
        acc_k[...] = jnp.zeros_like(acc_k)
        acc_v[...] = jnp.zeros_like(acc_v)
        position = start + lax.broadcasted_iota(jnp.int32, (KEY_TILE, 1), 0)

        def row_step(n, inner):
            tile = tiles[n]
            shard = tile // SHARD_TILES
            offset = (tile % SHARD_TILES) * ROW_TILE
            count = counts_ref[2 * shard] + counts_ref[2 * shard + 1]
            first = starts[shard] + offset

            @pl.when(first + ROW_TILE > start)
            def _():
                bound = jnp.where(lane < count - offset, first + lane, -1)

                def add_dq(part):
                    dqt[tile] += part

                tile_step(
                    key, value, key_t, row_tile(tile, q_s, do_s, lse_s, delta_s), position, bound,
                    acc_k, acc_v, add_dq,
                )

            return inner

        lax.fori_loop(0, length, row_step, 0)
        own[pl.ds(start, KEY_TILE), :HEAD_SIZE] = acc_k[...] * scale
        own[pl.ds(start, KEY_TILE), HEAD_SIZE:] = acc_v[...]
        return carry

    lax.fori_loop(0, (limit + KEY_TILE - 1) // KEY_TILE, key_step, 0)

    half = ROW_TILE // 2
    copies = []
    for block in range(KEY_VALUE_HEADS):
        shard = block // 2
        count = counts_ref[2 * shard] + counts_ref[2 * shard + 1]
        if block % 2 == 0:
            pieces = ((0, ROW_TILE, 0, 0), (ROW_TILE, half, 1, 0))
        else:
            pieces = ((0, half, 1, half), (half, ROW_TILE, 2, 0))
        for offset, size, t, first in pieces:
            live = count > t * ROW_TILE
            rows = slice(offset, offset + size)

            @pl.when(live)
            def _():
                for h in range(GROUP):
                    columns = slice(h * HEAD_SIZE, (h + 1) * HEAD_SIZE)
                    part = (dqt[SHARD_TILES * shard + t, :, columns] * scale).T
                    dq_s[block, rows, columns] = part[first : first + size].astype(jnp.bfloat16)

            @pl.when(jnp.logical_not(live))
            def _():
                dq_s[block, rows, :] = jnp.zeros((size, WIDTH), jnp.bfloat16)

        copy = pltpu.make_async_copy(dq_s.at[block], dq_out.at[block], out_sem.at[block])
        copy.start()
        copies.append(copy)
    for copy in copies:
        copy.wait()


def row_scratch(plane_rows):
    bf16, f32 = jnp.bfloat16, jnp.float32
    tile_count = plane_rows // ROW_TILE
    return [
        pltpu.VMEM((plane_rows, WIDTH), bf16),
        pltpu.VMEM((plane_rows, WIDTH), bf16),
        pltpu.VMEM((tile_count, WIDTH), f32),
        pltpu.VMEM((tile_count, WIDTH), f32),
        pltpu.VMEM((tile_count, HEAD_SIZE, WIDTH), f32),
    ]


def far_attention(me, counts, small, arrays, kvs):
    bf16, f32 = jnp.bfloat16, jnp.float32
    blocks = KEY_VALUE_HEADS
    rows = kvs[0].shape[0]
    columns = 2 * HEAD_SIZE
    plane_rows = 2 * (rows - INFO_ROWS)
    tile_count = plane_rows // ROW_TILE
    return pl.pallas_call(
        far_kernel,
        out_shape=(jax.ShapeDtypeStruct((rows, columns), bf16),) * 3
        + (
            jax.ShapeDtypeStruct((tile_count, HEAD_SIZE, WIDTH), f32),
            jax.ShapeDtypeStruct((1,), jnp.int32),
        ),
        in_specs=[SMEM] * 2 + [VMEM] + [HBM] * 12,
        out_specs=[HBM] * 4 + [SMEM],
        scratch_shapes=row_scratch(plane_rows)
        + [
            pltpu.VMEM((3, rows, columns), bf16),
            pltpu.VMEM((rows - INFO_ROWS, HEAD_SIZE), f32),
            pltpu.VMEM((rows - INFO_ROWS, HEAD_SIZE), f32),
            pltpu.SMEM((tile_count + 1,), jnp.int32),
            pltpu.SMEM((blocks,), jnp.int32),
            pltpu.SMEM((3,), jnp.int32),
            pltpu.SemaphoreType.DMA((2 * blocks,)),
            pltpu.SemaphoreType.DMA((3,)),
            pltpu.SemaphoreType.DMA((3,)),
            pltpu.SemaphoreType.DMA((tile_count,)),
            pltpu.VMEM((3, rows, columns), bf16),
        ],
        compiler_params=pltpu.CompilerParams(vmem_limit_bytes=48 * 1024 * 1024),
        cost_estimate=pl.CostEstimate(
            flops=10_000_000_000, bytes_accessed=12_000_000, transcendentals=8_000_000
        ),
        name="far_attention",
    )(me, counts, small, *arrays, *kvs)


def own_attention(me, counts, small, arrays, kv, dqt, note):
    bf16, f32 = jnp.bfloat16, jnp.float32
    blocks = KEY_VALUE_HEADS
    capacity = kv.shape[0] - INFO_ROWS
    plane_rows = 2 * capacity
    tile_count = plane_rows // ROW_TILE
    return pl.pallas_call(
        own_kernel,
        out_shape=(
            jax.ShapeDtypeStruct((blocks, plane_rows // blocks, WIDTH), bf16),
            jax.ShapeDtypeStruct((capacity, 2 * HEAD_SIZE), f32),
        ),
        in_specs=[SMEM] * 2 + [VMEM] + [HBM] * 9 + [VMEM, HBM, HBM],
        out_specs=[HBM, VMEM],
        scratch_shapes=row_scratch(plane_rows)
        + [
            pltpu.VMEM((KEY_TILE, HEAD_SIZE), f32),
            pltpu.VMEM((KEY_TILE, HEAD_SIZE), f32),
            pltpu.SMEM((tile_count + 1,), jnp.int32),
            pltpu.SMEM((blocks,), jnp.int32),
            pltpu.SemaphoreType.DMA((2 * blocks,)),
            pltpu.SemaphoreType.DMA((tile_count,)),
            pltpu.VMEM((blocks, plane_rows // blocks, WIDTH), bf16),
            pltpu.SemaphoreType.DMA((blocks,)),
        ],
        compiler_params=pltpu.CompilerParams(vmem_limit_bytes=48 * 1024 * 1024),
        cost_estimate=pl.CostEstimate(
            flops=1_000_000, bytes_accessed=100_000, transcendentals=1_000
        ),
        name="own_attention",
    )(me, counts, small, *arrays, kv, dqt, note)


def unpack_rows_kernel(parts, out):
    for g in range(KEY_VALUE_HEADS):
        out[:, g * WIDTH : (g + 1) * WIDTH] = parts[g]


def unpack_rows(parts):
    return pl.pallas_call(
        unpack_rows_kernel,
        out_shape=jax.ShapeDtypeStruct((parts.shape[1], KEY_VALUE_HEADS * WIDTH), parts.dtype),
        in_specs=[VMEM],
        out_specs=VMEM,
        name="unpack_rows",
    )(parts)


def combine_kernel(counts_ref, own, *rest):
    backs, out = rest[:3], rest[3]
    home_rows = out.shape[1]
    capacity = own.shape[0]
    total = own[...]
    for back in backs:
        total += back[:capacity, :].astype(jnp.float32)
    total = total.astype(jnp.bfloat16)
    within = lax.broadcasted_iota(jnp.int32, (home_rows, capacity), 0)
    place = lax.broadcasted_iota(jnp.int32, (home_rows, capacity), 1)
    start = jnp.int32(0)
    for block in range(KEY_VALUE_HEADS):
        count = counts_ref[block]
        hit = (place == within + start) & (within < count)
        out[block] = jnp.dot(
            jnp.where(hit, 1.0, 0.0).astype(jnp.bfloat16),
            total,
            preferred_element_type=jnp.float32,
        ).astype(jnp.bfloat16)
        start = start + count


def combine(counts, own, backs, home_rows):
    blocks = KEY_VALUE_HEADS
    return pl.pallas_call(
        combine_kernel,
        out_shape=jax.ShapeDtypeStruct((blocks, home_rows, own.shape[1]), jnp.bfloat16),
        in_specs=[SMEM] + [VMEM] * 4,
        out_specs=VMEM,
        compiler_params=pltpu.CompilerParams(vmem_limit_bytes=32 * 1024 * 1024),
        name="combine",
    )(counts, own, *backs)


def plane_device(queries, keys, values, outputs, output_gradient, lse, ranks):
    planes = lax.axis_size("outer")
    plane = ("inner", "head")
    blocks = KEY_VALUE_HEADS
    home_rows = queries.shape[0]
    plane_rows = blocks * home_rows
    capacity = plane_rows // 2
    surviving_tokens = BALANCED_TOKENS * planes * lax.axis_size("inner")
    bf16, f32 = jnp.bfloat16, jnp.float32
    me = lax.axis_index(plane).reshape(1).astype(jnp.int32)

    def swap(array, k):
        return lax.ppermute(array, plane, [(i, i ^ k) for i in range(blocks)])

    sent = pack_pairs(surviving_tokens, ranks, keys, values)
    arrived = lax.all_to_all(sent, plane, split_axis=0, concat_axis=0, tiled=True)
    packed = [
        pack_rows((chip, chip ^ CORE), me, queries, output_gradient) for chip in CHIPS
    ]
    pairs = [swap(rows, chip) for rows, chip in zip(packed, CHIPS)]
    beside = swap(pack_rows((CORE,), me, queries, output_gradient), CORE)
    small = lax.all_to_all(
        pack_small(lse, output_gradient, outputs), plane, split_axis=0, concat_axis=0, tiled=True
    )
    mine, counts = compact(arrived)
    up = [lax.ppermute(mine, "outer", [(i, i + 1) for i in range(planes - 1)])]
    up[0], small = lax.optimization_barrier((up[0], small))
    up.append(lax.ppermute(up[0], "outer", [(i, i + 1) for i in range(1, planes - 1)]))
    up.append(lax.ppermute(up[1], "outer", [(i, i + 1) for i in range(2, planes - 1)]))
    up[2], *pairs = lax.optimization_barrier((up[2], *pairs))
    crossed = [swap(pair[1:], CORE) for pair in pairs]
    arrays = [queries, output_gradient, beside, *pairs, *crossed]

    *down, dqt, full = far_attention(me, counts, small, arrays, up)
    note = swap(down[0][capacity:, :HEAD_SIZE], CORE)
    backs = [
        lax.ppermute(down[k - 1], "outer", [(i + k, i) for i in range(planes - k)])
        for k in (3, 2, 1)
    ]
    dq, own = own_attention(me, counts, small, arrays, mine, dqt, note)
    dq_home = unpack_rows(
        lax.all_to_all(dq, plane, split_axis=0, concat_axis=0, tiled=True)
    )
    kv_home = lax.all_to_all(
        combine(counts, own, backs, home_rows), plane, split_axis=0, concat_axis=0, tiled=True
    )
    full = full[0] > 0
    for back in backs:
        full = full | (back[capacity, 0] > 0)
    dk = kv_home[:, :, :HEAD_SIZE].transpose(1, 0, 2).reshape(home_rows, blocks * HEAD_SIZE)
    dv = kv_home[:, :, HEAD_SIZE:].transpose(1, 0, 2).reshape(home_rows, blocks * HEAD_SIZE)
    return (dq_home, dk, dv), full


def solution(mesh):
    spec = P(("seq", "head"), None)
    heads = mesh.shape["head"]
    inner = max(KEY_VALUE_HEADS // heads, 1)
    planes = mesh.shape["seq"] // inner
    if planes != 4 or inner * heads != KEY_VALUE_HEADS:
        return jax.shard_map(
            per_device,
            mesh=mesh,
            in_specs=(spec,) * 6 + (P(("seq", "head")),),
            out_specs=(spec,) * 3,
            check_vma=False,
        )
    axes = ("outer", "inner", "head")

    def device(*blocks):
        fast, full = plane_device(*blocks)
        return lax.cond(full, lambda: per_device(*blocks, seq=("outer", "inner")), lambda: fast)

    return jax.shard_map(
        device,
        mesh=Mesh(mesh.devices.reshape(planes, inner, heads), axes),
        in_specs=(P(axes, None),) * 6 + (P(axes),),
        out_specs=(P(axes, None),) * 3,
        check_vma=False,
    )
```

```python
import functools

import jax
import jax.numpy as jnp
from jax import lax
from jax.experimental import pallas as pl
from jax.experimental.pallas import tpu as pltpu
from jax.sharding import Mesh
from jax.sharding import PartitionSpec as P

QUERY_HEADS = 40
KEY_VALUE_HEADS = 8
HEAD_SIZE = 128
BALANCED_TOKENS = 128


block_keys = 512


def per_device(queries, keys, values, outputs, output_gradient, lse, ranks, seq="seq"):
    sequence_count = lax.axis_size(seq)
    head_total = lax.axis_size("head")
    home_rows = queries.shape[0]
    capacity = home_rows * head_total
    slots = capacity // sequence_count
    surviving_tokens = BALANCED_TOKENS * sequence_count
    group_size = QUERY_HEADS // KEY_VALUE_HEADS
    local_key_value = KEY_VALUE_HEADS // head_total
    scale = HEAD_SIZE ** (-0.5)

    def split_heads(array):
        return array.reshape(home_rows, head_total, array.shape[1] // head_total)

    moved = (
        lax.all_to_all(split_heads(queries), "head", split_axis=1, concat_axis=0, tiled=True),
        lax.all_to_all(split_heads(keys), "head", split_axis=1, concat_axis=0, tiled=True),
        lax.all_to_all(split_heads(values), "head", split_axis=1, concat_axis=0, tiled=True),
        lax.all_to_all(
            split_heads(output_gradient), "head", split_axis=1, concat_axis=0, tiled=True
        ),
        lax.all_to_all(split_heads(lse), "head", split_axis=1, concat_axis=0, tiled=True),
        lax.all_to_all(split_heads(outputs), "head", split_axis=1, concat_axis=0, tiled=True),
    )
    shard_rank_list = lax.all_gather(ranks, "head", axis=0, tiled=True)
    first_rank = shard_rank_list[0]
    living_count = jnp.sum((shard_rank_list < surviving_tokens).astype(jnp.int32))
    table = lax.all_gather(
        jnp.stack([first_rank, living_count])[None, :], seq, axis=0, tiled=True
    )

    def to_pairs(array):
        flat = array.reshape(slots, sequence_count, array.shape[-1])
        return jnp.roll(flat, first_rank, axis=1)

    arrived = (
        lax.all_to_all(to_pairs(moved[0]), seq, split_axis=1, concat_axis=1, tiled=True),
        lax.all_to_all(to_pairs(moved[1]), seq, split_axis=1, concat_axis=1, tiled=True),
        lax.all_to_all(to_pairs(moved[2]), seq, split_axis=1, concat_axis=1, tiled=True),
        lax.all_to_all(to_pairs(moved[3]), seq, split_axis=1, concat_axis=1, tiled=True),
        lax.all_to_all(to_pairs(moved[4]), seq, split_axis=1, concat_axis=1, tiled=True),
        lax.all_to_all(to_pairs(moved[5]), seq, split_axis=1, concat_axis=1, tiled=True),
    )
    my_index = lax.axis_index(seq)
    starts = table[:, 0]
    count_table = table[:, 1]
    offset = (my_index - starts) % sequence_count
    within = jnp.arange(slots, dtype=jnp.int32)[:, None] * sequence_count + offset[None, :]
    alive = within < count_table[None, :]
    target_rank = jnp.where(
        alive, (starts[None, :] + within) // sequence_count, BALANCED_TOKENS
    ).reshape(-1)

    def place(array):
        width = array.shape[-1]
        return (
            jnp.zeros((BALANCED_TOKENS, width), array.dtype)
            .at[target_rank]
            .set(array.reshape(slots * sequence_count, width), mode="drop")
        )

    query_row_block = place(arrived[0]).reshape(
        BALANCED_TOKENS, local_key_value, group_size, HEAD_SIZE
    )
    key_row_block = place(arrived[1]).reshape(BALANCED_TOKENS, local_key_value, HEAD_SIZE)
    value_row_block = place(arrived[2]).reshape(BALANCED_TOKENS, local_key_value, HEAD_SIZE)
    grad_rows = place(arrived[3]).reshape(BALANCED_TOKENS, local_key_value, group_size, HEAD_SIZE)
    lse_rows = (
        place(arrived[4]).astype(jnp.float32).reshape(BALANCED_TOKENS, local_key_value, group_size)
    )
    out_rows = (
        place(arrived[5])
        .astype(jnp.float32)
        .reshape(BALANCED_TOKENS, local_key_value, group_size, HEAD_SIZE)
    )
    delta_rows = (
        jnp.sum(grad_rows.astype(jnp.float32) * out_rows, axis=-1)
        .astype(jnp.bfloat16)
        .astype(jnp.float32)
    )
    gathered = (
        lax.all_gather(key_row_block, seq, axis=0, tiled=True),
        lax.all_gather(value_row_block, seq, axis=0, tiled=True),
    )
    all_keys = gathered[0].reshape(sequence_count, BALANCED_TOKENS, local_key_value, HEAD_SIZE)
    all_values = gathered[1].reshape(sequence_count, BALANCED_TOKENS, local_key_value, HEAD_SIZE)
    rows_per = block_keys // sequence_count
    inner = 1
    outer = BALANCED_TOKENS // rows_per // inner
    query_rank = jnp.arange(BALANCED_TOKENS, dtype=jnp.int32) * sequence_count + my_index
    lse_t = lse_rows.transpose(1, 2, 0)
    delta_t = delta_rows.transpose(1, 2, 0)
    position = jnp.arange(sequence_count * rows_per, dtype=jnp.int32)

    def key_step(query_acc, row_start):
        key_blk = lax.dynamic_slice_in_dim(all_keys, row_start, rows_per, 1).reshape(
            sequence_count * rows_per, local_key_value, HEAD_SIZE
        )
        value_blk = lax.dynamic_slice_in_dim(all_values, row_start, rows_per, 1).reshape(
            sequence_count * rows_per, local_key_value, HEAD_SIZE
        )
        key_owner_rank = (row_start + position % rows_per) * sequence_count + position // rows_per
        mask = key_owner_rank[None, None, None, :] <= query_rank[None, None, :, None]
        scores = (
            jnp.einsum(
                "rgmc,kgc->gmrk", query_row_block, key_blk, preferred_element_type=jnp.float32
            )
            * scale
        )
        probs = jnp.where(mask, jnp.exp(scores - lse_t[..., None]), 0.0)
        dprob = jnp.einsum(
            "rgmc,kgc->gmrk", grad_rows, value_blk, preferred_element_type=jnp.float32
        )
        dscore = probs * (dprob - delta_t[..., None])
        probs_low = probs.astype(jnp.bfloat16)
        dscore_low = dscore.astype(jnp.bfloat16)
        query_acc = query_acc + scale * jnp.einsum(
            "gmrk,kgc->rgmc", dscore_low, key_blk, preferred_element_type=jnp.float32
        )
        key_part = scale * jnp.einsum(
            "gmrk,rgmc->kgc", dscore_low, query_row_block, preferred_element_type=jnp.float32
        )
        value_part = jnp.einsum(
            "gmrk,rgmc->kgc", probs_low, grad_rows, preferred_element_type=jnp.float32
        )
        return (
            query_acc,
            key_part.reshape(sequence_count, rows_per, local_key_value * HEAD_SIZE),
            value_part.reshape(sequence_count, rows_per, local_key_value * HEAD_SIZE),
        )

    def outer_step(query_acc, outer_index):

        def inner_step(query_inner, inner_index):
            row_start = (outer_index * inner + inner_index) * rows_per
            query_new, key_part, value_part = key_step(query_inner, row_start)
            return (query_new, (key_part, value_part))

        query_acc, (key_parts, value_parts) = lax.scan(
            inner_step, query_acc, jnp.arange(inner, dtype=jnp.int32)
        )
        key_parts = key_parts.transpose(1, 0, 2, 3).reshape(
            sequence_count, inner * rows_per, local_key_value * HEAD_SIZE
        )
        value_parts = value_parts.transpose(1, 0, 2, 3).reshape(
            sequence_count, inner * rows_per, local_key_value * HEAD_SIZE
        )
        received = (
            lax.all_to_all(key_parts, seq, split_axis=0, concat_axis=0, tiled=True),
            lax.all_to_all(value_parts, seq, split_axis=0, concat_axis=0, tiled=True),
        )
        return (query_acc, (jnp.sum(received[0], axis=0), jnp.sum(received[1], axis=0)))

    start_acc = jnp.zeros((BALANCED_TOKENS, local_key_value, group_size, HEAD_SIZE), jnp.float32)
    query_acc, (key_sums, value_sums) = lax.scan(
        outer_step, start_acc, jnp.arange(outer, dtype=jnp.int32)
    )
    query_done = query_acc.reshape(
        BALANCED_TOKENS, local_key_value * group_size * HEAD_SIZE
    ).astype(jnp.bfloat16)
    key_done = key_sums.reshape(BALANCED_TOKENS, local_key_value * HEAD_SIZE).astype(jnp.bfloat16)
    value_done = value_sums.reshape(BALANCED_TOKENS, local_key_value * HEAD_SIZE).astype(
        jnp.bfloat16
    )
    safe_rows = jnp.minimum(target_rank, BALANCED_TOKENS - 1)
    alive_flat = alive.reshape(-1)

    def collect(array):
        picked = jnp.where(alive_flat[:, None], array[safe_rows], jnp.zeros((), array.dtype))
        return picked.reshape(slots, sequence_count, array.shape[-1])

    returned = (
        lax.all_to_all(collect(query_done), seq, split_axis=1, concat_axis=1, tiled=True),
        lax.all_to_all(collect(key_done), seq, split_axis=1, concat_axis=1, tiled=True),
        lax.all_to_all(collect(value_done), seq, split_axis=1, concat_axis=1, tiled=True),
    )

    def to_home(array):
        unrolled = jnp.roll(array, -first_rank, axis=1)
        return unrolled.reshape(capacity, 1, array.shape[-1])

    homed = (
        lax.all_to_all(to_home(returned[0]), "head", split_axis=0, concat_axis=1, tiled=True),
        lax.all_to_all(to_home(returned[1]), "head", split_axis=0, concat_axis=1, tiled=True),
        lax.all_to_all(to_home(returned[2]), "head", split_axis=0, concat_axis=1, tiled=True),
    )
    query_grads = homed[0].reshape(home_rows, head_total * homed[0].shape[-1])
    key_gradient_output = homed[1].reshape(home_rows, head_total * homed[1].shape[-1])
    value_gradient = homed[2].reshape(home_rows, head_total * homed[2].shape[-1])
    return (query_grads, key_gradient_output, value_gradient)

LOG2E = 1.4426950408889634
KEY_TILE = 256
ROW_TILE = 128
INFO_ROWS = 16
AUX_LANES = 256
COUNT_ROW = 5
DELTA_ROW = 8
SMEM = pl.BlockSpec(memory_space=pltpu.SMEM)
VMEM = pl.BlockSpec(memory_space=pltpu.VMEM)
HBM = pl.BlockSpec(memory_space=pltpu.HBM)
GROUP = QUERY_HEADS // KEY_VALUE_HEADS
WIDTH = GROUP * HEAD_SIZE
CHIPS = (5, 4, 1)
CORE = 2
SHARD_TILES = 3
PASS_ROWS = (256, 512, 768)


def pack_pairs_kernel(limit, ranks_ref, lse_ref, k_ref, v_ref, do_ref, o_ref, out_ref, columns, lanes):
    home_rows = k_ref.shape[0]
    columns[...] = jnp.zeros_like(columns)
    for g in range(KEY_VALUE_HEADS):
        columns[:, 16 * g : 16 * g + GROUP] = lse_ref[:, g * GROUP : (g + 1) * GROUP].astype(
            jnp.float32
        )
    for h in range(QUERY_HEADS):
        head = slice(h * HEAD_SIZE, (h + 1) * HEAD_SIZE)
        product = do_ref[:, head].astype(jnp.float32) * o_ref[:, head].astype(jnp.float32)
        column = 16 * (h // GROUP) + DELTA_ROW + h % GROUP
        columns[:, column : column + 1] = jnp.sum(product, axis=1, keepdims=True)
    lanes[...] = jnp.zeros_like(lanes)
    lanes[:, :home_rows] = columns[...].T
    live = jnp.where(ranks_ref[...] < limit, 1.0, 0.0)
    count = jnp.sum(live, axis=1, keepdims=True)
    line = lax.broadcasted_iota(jnp.int32, (INFO_ROWS, 2 * HEAD_SIZE), 0)
    for g in range(KEY_VALUE_HEADS):
        head = slice(g * HEAD_SIZE, (g + 1) * HEAD_SIZE)
        out_ref[g, :home_rows, :HEAD_SIZE] = k_ref[:, head]
        out_ref[g, :home_rows, HEAD_SIZE:] = v_ref[:, head]
        info = jnp.where(line == COUNT_ROW, count, lanes[16 * g : 16 * g + INFO_ROWS, :])
        out_ref[g, home_rows:, :] = info.astype(out_ref.dtype)


def pack_pairs(limit, ranks, lse, keys, values, output_gradient, outputs):
    home_rows = keys.shape[0]
    return pl.pallas_call(
        functools.partial(pack_pairs_kernel, limit),
        out_shape=jax.ShapeDtypeStruct(
            (KEY_VALUE_HEADS, home_rows + INFO_ROWS, 2 * HEAD_SIZE), keys.dtype
        ),
        in_specs=[VMEM] * 6,
        out_specs=VMEM,
        scratch_shapes=[
            pltpu.VMEM((home_rows, HEAD_SIZE), jnp.float32),
            pltpu.VMEM((HEAD_SIZE, AUX_LANES), jnp.float32),
        ],
        compiler_params=pltpu.CompilerParams(vmem_limit_bytes=32 * 1024 * 1024),
        name="pack_pairs",
    )(ranks.reshape(1, home_rows), lse, keys, values, output_gradient, outputs)


def pack_rows_kernel(partners, me_ref, q_hbm, do_hbm, out, sems):
    copies = []
    for n, partner in enumerate(partners):
        start = pl.multiple_of((me_ref[0] ^ partner) * WIDTH, HEAD_SIZE)
        for m, source in enumerate((q_hbm, do_hbm)):
            copies.append(
                pltpu.make_async_copy(
                    source.at[:, pl.ds(start, WIDTH)],
                    out.at[n, :, pl.ds(m * WIDTH, WIDTH)],
                    sems.at[2 * n + m],
                )
            )
    for copy in copies:
        copy.start()
    for copy in copies:
        copy.wait()


def pack_rows(partners, me, queries, output_gradient):
    home_rows = queries.shape[0]
    return pl.pallas_call(
        functools.partial(pack_rows_kernel, partners),
        out_shape=jax.ShapeDtypeStruct((len(partners), home_rows, 2 * WIDTH), queries.dtype),
        in_specs=[SMEM, HBM, HBM],
        out_specs=VMEM,
        scratch_shapes=[pltpu.SemaphoreType.DMA((2 * len(partners),))],
        name="pack_rows",
    )(me, queries, output_gradient)


def compact_kernel(arrived, out, small, counts_ref):
    home_rows = arrived.shape[1] - INFO_ROWS
    capacity = out.shape[0] - INFO_ROWS
    row = lax.broadcasted_iota(jnp.int32, (capacity, home_rows), 0)
    within = lax.broadcasted_iota(jnp.int32, (capacity, home_rows), 1)
    total = jnp.int32(0)
    picked = []
    for block in range(KEY_VALUE_HEADS):
        info = arrived[block, home_rows:, :]
        small[block] = info
        count = jnp.max(info[COUNT_ROW : COUNT_ROW + 1].astype(jnp.float32)).astype(jnp.int32)
        counts_ref[block] = count
        hit = (row == within + total) & (within < count)
        picked.append(jnp.where(hit, 1.0, 0.0).astype(jnp.bfloat16))
        total = total + count
    acc = jnp.zeros((capacity, out.shape[1]), jnp.float32)
    for block in range(KEY_VALUE_HEADS):
        acc += jnp.dot(
            picked[block], arrived[block, :home_rows, :], preferred_element_type=jnp.float32
        )
    out[:capacity, :] = acc.astype(out.dtype)
    line = lax.broadcasted_iota(jnp.int32, (INFO_ROWS, out.shape[1]), 0)
    out[capacity:, :] = (
        jnp.where(line == 0, total // 64, jnp.where(line == 1, total % 64, 0))
        .astype(jnp.float32)
        .astype(out.dtype)
    )


def compact(arrived):
    blocks, rows, columns = arrived.shape
    capacity = blocks * (rows - INFO_ROWS) // 2
    return pl.pallas_call(
        compact_kernel,
        out_shape=(
            jax.ShapeDtypeStruct((capacity + INFO_ROWS, columns), arrived.dtype),
            jax.ShapeDtypeStruct((blocks, INFO_ROWS, columns), arrived.dtype),
            jax.ShapeDtypeStruct((blocks,), jnp.int32),
        ),
        in_specs=[VMEM],
        out_specs=(VMEM, VMEM, SMEM),
        compiler_params=pltpu.CompilerParams(vmem_limit_bytes=32 * 1024 * 1024),
        name="compact",
    )(arrived)


def load_rows(me, counts_ref, arrays, q_s, do_s, sems):
    home_rows = q_s.shape[0] // KEY_VALUE_HEADS
    q_hbm, do_hbm, beside, pairs, crossed = arrays
    column = pl.multiple_of(me * WIDTH, HEAD_SIZE)
    left, right = pl.ds(0, WIDTH), pl.ds(WIDTH, WIDTH)
    sources = [
        (0, q_hbm.at[:, pl.ds(column, WIDTH)], do_hbm.at[:, pl.ds(column, WIDTH)]),
        (CORE, beside.at[0, :, left], beside.at[0, :, right]),
    ]
    for chip, pair, cross in zip(CHIPS, pairs, crossed):
        sources.append((chip, pair.at[0, :, left], pair.at[0, :, right]))
        sources.append((chip ^ CORE, cross.at[0, :, left], cross.at[0, :, right]))
    plans = []
    for n, (partner, q, do) in enumerate(sources):
        source = me ^ partner
        rows = pl.ds(pl.multiple_of(source * home_rows, 64), home_rows)
        shard = counts_ref[source & ~1] + counts_ref[source | 1]
        needed = ((source & 1) == 0) | (shard > ROW_TILE)
        plans.append(
            (
                needed,
                [
                    pltpu.make_async_copy(q, q_s.at[rows, :], sems.at[2 * n]),
                    pltpu.make_async_copy(do, do_s.at[rows, :], sems.at[2 * n + 1]),
                ],
            )
        )

    def each(act):
        for needed, copies in plans:

            @pl.when(needed)
            def _():
                for copy in copies:
                    act(copy)

    return each


def list_tiles(counts_ref, tiles, starts):
    length = jnp.int32(0)
    total = jnp.int32(0)
    for shard in range(KEY_VALUE_HEADS // 2):
        count = counts_ref[2 * shard] + counts_ref[2 * shard + 1]
        starts[shard] = total
        total = total + count
        for t in range(SHARD_TILES):
            live = count > t * ROW_TILE

            @pl.when(live)
            def _():
                tiles[length] = SHARD_TILES * shard + t

            length = length + live.astype(jnp.int32)
    return length, total


def spread_lanes(aux_s, lse_s, delta_s):
    lane = lax.broadcasted_iota(jnp.int32, (INFO_ROWS, ROW_TILE), 1)
    for shard in range(KEY_VALUE_HEADS // 2):
        low = aux_s[2 * shard].astype(jnp.float32)
        high = aux_s[2 * shard + 1].astype(jnp.float32)
        half = ROW_TILE // 2
        middle = jnp.where(
            lane < half, low[:, ROW_TILE:], pltpu.roll(high[:, :ROW_TILE], half, axis=1)
        )
        last = pltpu.roll(high, AUX_LANES - half, axis=1)[:, :ROW_TILE]
        for t, rows in enumerate((low[:, :ROW_TILE], middle, last)):
            row = SHARD_TILES * shard + t
            for h in range(GROUP):
                columns = slice(h * ROW_TILE, (h + 1) * ROW_TILE)
                lse_s[row : row + 1, columns] = rows[h : h + 1] * LOG2E
                delta_s[row : row + 1, columns] = rows[DELTA_ROW + h : DELTA_ROW + 1 + h]


def row_tile(tile, q_s, do_s, lse_s, delta_s):
    def stack(ref):
        rows = ref[pl.ds(pl.multiple_of(tile * ROW_TILE, ROW_TILE), ROW_TILE), :]
        return jnp.concatenate(
            [rows[:, h * HEAD_SIZE : (h + 1) * HEAD_SIZE] for h in range(GROUP)], axis=0
        )

    return stack(q_s), stack(do_s), lse_s[pl.ds(tile, 1), :], delta_s[pl.ds(tile, 1), :]


def tile_step(key, value, key_t, rows, position, bound, acc_k, acc_v, add_dq):
    q, do, lse, delta = rows
    scale = HEAD_SIZE ** (-0.5)
    dims = (((1,), (1,)), ((), ()))
    scores = lax.dot_general(key, q, dims, preferred_element_type=jnp.float32)
    prob = jnp.where(position <= bound, jnp.exp2(scores * (scale * LOG2E) - lse), 0.0)
    dprob = lax.dot_general(value, do, dims, preferred_element_type=jnp.float32)
    dscore = (prob * (dprob - delta)).astype(jnp.bfloat16)
    acc_v[...] += jnp.dot(prob.astype(jnp.bfloat16), do, preferred_element_type=jnp.float32)
    acc_k[...] += jnp.dot(dscore, q, preferred_element_type=jnp.float32)
    add_dq(jnp.dot(key_t, dscore, preferred_element_type=jnp.float32))


def far_kernel(me_ref, counts_ref, *rest):
    aux_s, arrays, kvs, rest = rest[0], rest[1:10], rest[10:13], rest[13:]
    arrays = (*arrays[:3], arrays[3:6], arrays[6:9])
    downs, dqt_out, full_ref, rest = rest[:3], rest[3], rest[4], rest[5:]
    (
        q_s, do_s, lse_s, delta_s, dqt, kv_s, acc_k, acc_v, tiles, starts, limits, sems, kv_sem,
        down_sem, dq_sem, down_s,
    ) = rest
    capacity = downs[0].shape[0] - INFO_ROWS
    scale = HEAD_SIZE ** (-0.5)
    each = load_rows(me_ref[0], counts_ref, arrays, q_s, do_s, sems)
    each(lambda copy: copy.start())
    kv_copies = [
        pltpu.make_async_copy(kvs[n], kv_s.at[n], kv_sem.at[n])
        for n in range(3)
    ]
    for copy in kv_copies:
        copy.start()
    length, total = list_tiles(counts_ref, tiles, starts)

    def zero_tile(n, carry):
        dqt[tiles[n]] = jnp.zeros(dqt.shape[1:], jnp.float32)
        return carry

    lax.fori_loop(0, length, zero_tile, 0)
    spread_lanes(aux_s, lse_s, delta_s)
    for copy in kv_copies:
        copy.wait()
    most = total
    for n in range(3):
        info = kv_s[n, capacity:, :].astype(jnp.float32)
        limit = (jnp.max(info[0:1]) * 64.0 + jnp.max(info[1:2])).astype(jnp.int32)
        limits[n] = jnp.minimum(limit, capacity)
        most = jnp.maximum(most, limit)
    full = most > capacity
    full_ref[0] = full.astype(jnp.int32)
    for n in range(3):
        down_s[n, capacity:, :] = jnp.full(
            (INFO_ROWS, 2 * HEAD_SIZE), jnp.where(full, 1.0, 0.0)
        ).astype(jnp.bfloat16)
    each(lambda copy: copy.wait())
    lane = lax.broadcasted_iota(jnp.int32, (1, WIDTH), 1) % ROW_TILE

    def block_step(step, carry):
        index = 2 - step
        limit = limits[index]

        def run(rows):
            key = kv_s[index, :rows, :HEAD_SIZE]
            value = kv_s[index, :rows, HEAD_SIZE:]
            key_t = key.T
            acc_k[:rows] = jnp.zeros((rows, HEAD_SIZE), jnp.float32)
            acc_v[:rows] = jnp.zeros((rows, HEAD_SIZE), jnp.float32)
            position = lax.broadcasted_iota(jnp.int32, (rows, 1), 0)

            def row_step(n, inner):
                tile = tiles[n]
                shard = tile // SHARD_TILES
                count = counts_ref[2 * shard] + counts_ref[2 * shard + 1]
                alive = lane < count - (tile % SHARD_TILES) * ROW_TILE
                bound = jnp.where(alive, limit - 1, -1)

                def add_dq(part):
                    dqt[tile] += part

                tile_step(
                    key, value, key_t, row_tile(tile, q_s, do_s, lse_s, delta_s), position, bound,
                    acc_k.at[pl.ds(0, rows), :], acc_v.at[pl.ds(0, rows), :], add_dq,
                )
                return inner

            lax.fori_loop(0, length, row_step, 0)
            down_s[index, :rows, :HEAD_SIZE] = (acc_k[:rows] * scale).astype(jnp.bfloat16)
            down_s[index, :rows, HEAD_SIZE:] = acc_v[:rows].astype(jnp.bfloat16)
            if rows < capacity:
                down_s[index, rows:capacity, :] = jnp.zeros(
                    (capacity - rows, 2 * HEAD_SIZE), jnp.bfloat16
                )

        below = 0
        for rows in PASS_ROWS:

            @pl.when((limit > below) & (limit <= rows))
            def _():
                run(rows)

            below = rows

        @pl.when(limit == 0)
        def _():
            down_s[index, :capacity, :] = jnp.zeros((capacity, 2 * HEAD_SIZE), jnp.bfloat16)

        return carry

    lax.fori_loop(0, 3, block_step, 0)
    down_copies = [
        pltpu.make_async_copy(down_s.at[n], downs[n], down_sem.at[n]) for n in range(3)
    ]
    for copy in down_copies:
        copy.start()

    def dq_copy(n):
        tile = tiles[n]
        return pltpu.make_async_copy(dqt.at[tile], dqt_out.at[tile], dq_sem.at[n])

    def start_dq(n, carry):
        dq_copy(n).start()
        return carry

    def wait_dq(n, carry):
        dq_copy(n).wait()
        return carry

    lax.fori_loop(0, length, start_dq, 0)
    for copy in down_copies:
        copy.wait()
    lax.fori_loop(0, length, wait_dq, 0)


def own_kernel(me_ref, counts_ref, *rest):
    aux_s, arrays, kv, dqt_in, rest = rest[0], rest[1:10], rest[10], rest[11], rest[13:]
    arrays = (*arrays[:3], arrays[3:6], arrays[6:9])
    dq_out, own, rest = rest[0], rest[1], rest[2:]
    q_s, do_s, lse_s, delta_s, dqt, acc_k, acc_v, tiles, starts, sems, dq_sem, dq_s, out_sem = rest
    capacity = kv.shape[0] - INFO_ROWS
    home_rows = dq_out.shape[1]
    scale = HEAD_SIZE ** (-0.5)
    me = me_ref[0]
    each = load_rows(me, counts_ref, arrays, q_s, do_s, sems)
    each(lambda copy: copy.start())
    length, total = list_tiles(counts_ref, tiles, starts)
    limit = jnp.minimum(total, capacity)

    def dq_copy(n):
        tile = tiles[n]
        return pltpu.make_async_copy(dqt_in.at[tile], dqt.at[tile], dq_sem.at[n])

    def start_dq(n, carry):
        dq_copy(n).start()
        return carry

    def wait_dq(n, carry):
        dq_copy(n).wait()
        return carry

    lax.fori_loop(0, length, start_dq, 0)
    own[...] = jnp.zeros_like(own)
    spread_lanes(aux_s, lse_s, delta_s)
    each(lambda copy: copy.wait())
    lax.fori_loop(0, length, wait_dq, 0)
    lane = lax.broadcasted_iota(jnp.int32, (1, WIDTH), 1) % ROW_TILE

    def key_step(kt, carry):
        start = pl.multiple_of(kt * KEY_TILE, KEY_TILE)
        key = kv[pl.ds(start, KEY_TILE), :HEAD_SIZE]
        value = kv[pl.ds(start, KEY_TILE), HEAD_SIZE:]
        key_t = key.T
        acc_k[...] = jnp.zeros_like(acc_k)
        acc_v[...] = jnp.zeros_like(acc_v)
        position = start + lax.broadcasted_iota(jnp.int32, (KEY_TILE, 1), 0)

        def row_step(n, inner):
            tile = tiles[n]
            shard = tile // SHARD_TILES
            offset = (tile % SHARD_TILES) * ROW_TILE
            count = counts_ref[2 * shard] + counts_ref[2 * shard + 1]
            first = starts[shard] + offset

            @pl.when(first + ROW_TILE > start)
            def _():
                bound = jnp.where(lane < count - offset, first + lane, -1)

                def add_dq(part):
                    dqt[tile] += part

                tile_step(
                    key, value, key_t, row_tile(tile, q_s, do_s, lse_s, delta_s), position, bound,
                    acc_k, acc_v, add_dq,
                )

            return inner

        lax.fori_loop(0, length, row_step, 0)
        own[pl.ds(start, KEY_TILE), :HEAD_SIZE] = acc_k[...] * scale
        own[pl.ds(start, KEY_TILE), HEAD_SIZE:] = acc_v[...]
        return carry

    lax.fori_loop(0, (limit + KEY_TILE - 1) // KEY_TILE, key_step, 0)

    half = ROW_TILE // 2
    copies = []
    for block in range(KEY_VALUE_HEADS):
        shard = block // 2
        count = counts_ref[2 * shard] + counts_ref[2 * shard + 1]
        if block % 2 == 0:
            pieces = ((0, ROW_TILE, 0, 0), (ROW_TILE, half, 1, 0))
        else:
            pieces = ((0, half, 1, half), (half, ROW_TILE, 2, 0))
        for offset, size, t, first in pieces:
            live = count > t * ROW_TILE
            rows = slice(offset, offset + size)

            @pl.when(live)
            def _():
                for h in range(GROUP):
                    columns = slice(h * HEAD_SIZE, (h + 1) * HEAD_SIZE)
                    part = (dqt[SHARD_TILES * shard + t, :, columns] * scale).T
                    dq_s[block, rows, columns] = part[first : first + size].astype(jnp.bfloat16)

            @pl.when(jnp.logical_not(live))
            def _():
                dq_s[block, rows, :] = jnp.zeros((size, WIDTH), jnp.bfloat16)

        copy = pltpu.make_async_copy(dq_s.at[block], dq_out.at[block], out_sem.at[block])
        copy.start()
        copies.append(copy)
    for copy in copies:
        copy.wait()


def row_scratch(plane_rows):
    bf16, f32 = jnp.bfloat16, jnp.float32
    tile_count = plane_rows // ROW_TILE
    return [
        pltpu.VMEM((plane_rows, WIDTH), bf16),
        pltpu.VMEM((plane_rows, WIDTH), bf16),
        pltpu.VMEM((tile_count, WIDTH), f32),
        pltpu.VMEM((tile_count, WIDTH), f32),
        pltpu.VMEM((tile_count, HEAD_SIZE, WIDTH), f32),
    ]


def far_attention(me, counts, small, arrays, kvs):
    bf16, f32 = jnp.bfloat16, jnp.float32
    blocks = KEY_VALUE_HEADS
    rows = kvs[0].shape[0]
    columns = 2 * HEAD_SIZE
    plane_rows = 2 * (rows - INFO_ROWS)
    tile_count = plane_rows // ROW_TILE
    return pl.pallas_call(
        far_kernel,
        out_shape=(jax.ShapeDtypeStruct((rows, columns), bf16),) * 3
        + (
            jax.ShapeDtypeStruct((tile_count, HEAD_SIZE, WIDTH), f32),
            jax.ShapeDtypeStruct((1,), jnp.int32),
        ),
        in_specs=[SMEM] * 2 + [VMEM] + [HBM] * 12,
        out_specs=[HBM] * 4 + [SMEM],
        scratch_shapes=row_scratch(plane_rows)
        + [
            pltpu.VMEM((3, rows, columns), bf16),
            pltpu.VMEM((rows - INFO_ROWS, HEAD_SIZE), f32),
            pltpu.VMEM((rows - INFO_ROWS, HEAD_SIZE), f32),
            pltpu.SMEM((tile_count + 1,), jnp.int32),
            pltpu.SMEM((blocks,), jnp.int32),
            pltpu.SMEM((3,), jnp.int32),
            pltpu.SemaphoreType.DMA((2 * blocks,)),
            pltpu.SemaphoreType.DMA((3,)),
            pltpu.SemaphoreType.DMA((3,)),
            pltpu.SemaphoreType.DMA((tile_count,)),
            pltpu.VMEM((3, rows, columns), bf16),
        ],
        compiler_params=pltpu.CompilerParams(vmem_limit_bytes=48 * 1024 * 1024),
        cost_estimate=pl.CostEstimate(
            flops=10_000_000_000, bytes_accessed=12_000_000, transcendentals=8_000_000
        ),
        name="far_attention",
    )(me, counts, small, *arrays, *kvs)


def own_attention(me, counts, small, arrays, kv, dqt, note):
    bf16, f32 = jnp.bfloat16, jnp.float32
    blocks = KEY_VALUE_HEADS
    capacity = kv.shape[0] - INFO_ROWS
    plane_rows = 2 * capacity
    tile_count = plane_rows // ROW_TILE
    return pl.pallas_call(
        own_kernel,
        out_shape=(
            jax.ShapeDtypeStruct((blocks, plane_rows // blocks, WIDTH), bf16),
            jax.ShapeDtypeStruct((capacity, 2 * HEAD_SIZE), f32),
        ),
        in_specs=[SMEM] * 2 + [VMEM] + [HBM] * 9 + [VMEM, HBM, HBM],
        out_specs=[HBM, VMEM],
        scratch_shapes=row_scratch(plane_rows)
        + [
            pltpu.VMEM((KEY_TILE, HEAD_SIZE), f32),
            pltpu.VMEM((KEY_TILE, HEAD_SIZE), f32),
            pltpu.SMEM((tile_count + 1,), jnp.int32),
            pltpu.SMEM((blocks,), jnp.int32),
            pltpu.SemaphoreType.DMA((2 * blocks,)),
            pltpu.SemaphoreType.DMA((tile_count,)),
            pltpu.VMEM((blocks, plane_rows // blocks, WIDTH), bf16),
            pltpu.SemaphoreType.DMA((blocks,)),
        ],
        compiler_params=pltpu.CompilerParams(vmem_limit_bytes=48 * 1024 * 1024),
        cost_estimate=pl.CostEstimate(
            flops=1_000_000, bytes_accessed=100_000, transcendentals=1_000
        ),
        name="own_attention",
    )(me, counts, small, *arrays, kv, dqt, note)


def unpack_rows_kernel(parts, out):
    for g in range(KEY_VALUE_HEADS):
        out[:, g * WIDTH : (g + 1) * WIDTH] = parts[g]


def unpack_rows(parts):
    return pl.pallas_call(
        unpack_rows_kernel,
        out_shape=jax.ShapeDtypeStruct((parts.shape[1], KEY_VALUE_HEADS * WIDTH), parts.dtype),
        in_specs=[VMEM],
        out_specs=VMEM,
        name="unpack_rows",
    )(parts)


def combine_kernel(counts_ref, own, *rest):
    backs, out = rest[:3], rest[3]
    home_rows = out.shape[1]
    capacity = own.shape[0]
    total = own[...]
    for back in backs:
        total += back[:capacity, :].astype(jnp.float32)
    total = total.astype(jnp.bfloat16)
    within = lax.broadcasted_iota(jnp.int32, (home_rows, capacity), 0)
    place = lax.broadcasted_iota(jnp.int32, (home_rows, capacity), 1)
    start = jnp.int32(0)
    for block in range(KEY_VALUE_HEADS):
        count = counts_ref[block]
        hit = (place == within + start) & (within < count)
        out[block] = jnp.dot(
            jnp.where(hit, 1.0, 0.0).astype(jnp.bfloat16),
            total,
            preferred_element_type=jnp.float32,
        ).astype(jnp.bfloat16)
        start = start + count


def combine(counts, own, backs, home_rows):
    blocks = KEY_VALUE_HEADS
    return pl.pallas_call(
        combine_kernel,
        out_shape=jax.ShapeDtypeStruct((blocks, home_rows, own.shape[1]), jnp.bfloat16),
        in_specs=[SMEM] + [VMEM] * 4,
        out_specs=VMEM,
        compiler_params=pltpu.CompilerParams(vmem_limit_bytes=32 * 1024 * 1024),
        name="combine",
    )(counts, own, *backs)


def plane_device(queries, keys, values, outputs, output_gradient, lse, ranks):
    planes = lax.axis_size("outer")
    plane = ("inner", "head")
    blocks = KEY_VALUE_HEADS
    home_rows = queries.shape[0]
    plane_rows = blocks * home_rows
    capacity = plane_rows // 2
    surviving_tokens = BALANCED_TOKENS * planes * lax.axis_size("inner")
    bf16, f32 = jnp.bfloat16, jnp.float32
    me = lax.axis_index(plane).reshape(1).astype(jnp.int32)

    def swap(array, k):
        return lax.ppermute(array, plane, [(i, i ^ k) for i in range(blocks)])

    sent = pack_pairs(
        surviving_tokens, ranks, lse, keys, values, output_gradient, outputs
    )
    me, sent = lax.optimization_barrier((me, sent))
    arrived = lax.all_to_all(sent, plane, split_axis=0, concat_axis=0, tiled=True)
    pairs = [
        swap(pack_rows((chip, chip ^ CORE), me, queries, output_gradient), chip) for chip in CHIPS
    ]
    beside = swap(pack_rows((CORE,), me, queries, output_gradient), CORE)
    arrived, beside = lax.optimization_barrier((arrived, beside))
    mine, small, counts = compact(arrived)
    up = [lax.ppermute(mine, "outer", [(i, i + 1) for i in range(planes - 1)])]
    last = lax.ppermute(mine, "outer", [(0, planes - 1)])
    up.append(lax.ppermute(up[0], "outer", [(i, i + 1) for i in range(1, planes - 1)]))
    up.append(last)
    up[1], up[2], *pairs = lax.optimization_barrier((up[1], up[2], *pairs))
    crossed = [swap(pair[1:], CORE) for pair in pairs]
    arrays = [queries, output_gradient, beside, *pairs, *crossed]

    *down, dqt, full = far_attention(me, counts, small, arrays, up)
    note = swap(down[0][capacity:, :HEAD_SIZE], CORE)
    backs = [
        lax.ppermute(down[k - 1], "outer", [(i + k, i) for i in range(planes - k)])
        for k in (3, 2, 1)
    ]
    dq, own = own_attention(me, counts, small, arrays, mine, dqt, note)
    dq = lax.all_to_all(dq, plane, split_axis=0, concat_axis=0, tiled=True)
    dq, own = lax.optimization_barrier((dq, own))
    dq_home = unpack_rows(dq)
    kv_home = lax.all_to_all(
        combine(counts, own, backs, home_rows), plane, split_axis=0, concat_axis=0, tiled=True
    )
    full = full[0] > 0
    for back in backs:
        full = full | (back[capacity, 0] > 0)
    dk = kv_home[:, :, :HEAD_SIZE].transpose(1, 0, 2).reshape(home_rows, blocks * HEAD_SIZE)
    dv = kv_home[:, :, HEAD_SIZE:].transpose(1, 0, 2).reshape(home_rows, blocks * HEAD_SIZE)
    return (dq_home, dk, dv), full


def solution(mesh):
    spec = P(("seq", "head"), None)
    heads = mesh.shape["head"]
    inner = max(KEY_VALUE_HEADS // heads, 1)
    planes = mesh.shape["seq"] // inner
    if planes != 4 or inner * heads != KEY_VALUE_HEADS:
        return jax.shard_map(
            per_device,
            mesh=mesh,
            in_specs=(spec,) * 6 + (P(("seq", "head")),),
            out_specs=(spec,) * 3,
            check_vma=False,
        )
    axes = ("outer", "inner", "head")

    def device(*blocks):
        fast, full = plane_device(*blocks)
        return lax.cond(full, lambda: per_device(*blocks, seq=("outer", "inner")), lambda: fast)

    return jax.shard_map(
        device,
        mesh=Mesh(mesh.devices.reshape(planes, inner, heads), axes),
        in_specs=(P(axes, None),) * 6 + (P(axes),),
        out_specs=(P(axes, None),) * 3,
        check_vma=False,
    )
```

```python
import functools

import jax
import jax.numpy as jnp
from jax import lax
from jax.experimental import pallas as pl
from jax.experimental.pallas import tpu as pltpu
from jax.sharding import Mesh
from jax.sharding import PartitionSpec as P

QUERY_HEADS = 40
KEY_VALUE_HEADS = 8
HEAD_SIZE = 128
BALANCED_TOKENS = 128


block_keys = 512


def per_device(queries, keys, values, outputs, output_gradient, lse, ranks, seq="seq"):
    sequence_count = lax.axis_size(seq)
    head_total = lax.axis_size("head")
    home_rows = queries.shape[0]
    capacity = home_rows * head_total
    slots = capacity // sequence_count
    surviving_tokens = BALANCED_TOKENS * sequence_count
    group_size = QUERY_HEADS // KEY_VALUE_HEADS
    local_key_value = KEY_VALUE_HEADS // head_total
    scale = HEAD_SIZE ** (-0.5)

    def split_heads(array):
        return array.reshape(home_rows, head_total, array.shape[1] // head_total)

    moved = (
        lax.all_to_all(split_heads(queries), "head", split_axis=1, concat_axis=0, tiled=True),
        lax.all_to_all(split_heads(keys), "head", split_axis=1, concat_axis=0, tiled=True),
        lax.all_to_all(split_heads(values), "head", split_axis=1, concat_axis=0, tiled=True),
        lax.all_to_all(
            split_heads(output_gradient), "head", split_axis=1, concat_axis=0, tiled=True
        ),
        lax.all_to_all(split_heads(lse), "head", split_axis=1, concat_axis=0, tiled=True),
        lax.all_to_all(split_heads(outputs), "head", split_axis=1, concat_axis=0, tiled=True),
    )
    shard_rank_list = lax.all_gather(ranks, "head", axis=0, tiled=True)
    first_rank = shard_rank_list[0]
    living_count = jnp.sum((shard_rank_list < surviving_tokens).astype(jnp.int32))
    table = lax.all_gather(
        jnp.stack([first_rank, living_count])[None, :], seq, axis=0, tiled=True
    )

    def to_pairs(array):
        flat = array.reshape(slots, sequence_count, array.shape[-1])
        return jnp.roll(flat, first_rank, axis=1)

    arrived = (
        lax.all_to_all(to_pairs(moved[0]), seq, split_axis=1, concat_axis=1, tiled=True),
        lax.all_to_all(to_pairs(moved[1]), seq, split_axis=1, concat_axis=1, tiled=True),
        lax.all_to_all(to_pairs(moved[2]), seq, split_axis=1, concat_axis=1, tiled=True),
        lax.all_to_all(to_pairs(moved[3]), seq, split_axis=1, concat_axis=1, tiled=True),
        lax.all_to_all(to_pairs(moved[4]), seq, split_axis=1, concat_axis=1, tiled=True),
        lax.all_to_all(to_pairs(moved[5]), seq, split_axis=1, concat_axis=1, tiled=True),
    )
    my_index = lax.axis_index(seq)
    starts = table[:, 0]
    count_table = table[:, 1]
    offset = (my_index - starts) % sequence_count
    within = jnp.arange(slots, dtype=jnp.int32)[:, None] * sequence_count + offset[None, :]
    alive = within < count_table[None, :]
    target_rank = jnp.where(
        alive, (starts[None, :] + within) // sequence_count, BALANCED_TOKENS
    ).reshape(-1)

    def place(array):
        width = array.shape[-1]
        return (
            jnp.zeros((BALANCED_TOKENS, width), array.dtype)
            .at[target_rank]
            .set(array.reshape(slots * sequence_count, width), mode="drop")
        )

    query_row_block = place(arrived[0]).reshape(
        BALANCED_TOKENS, local_key_value, group_size, HEAD_SIZE
    )
    key_row_block = place(arrived[1]).reshape(BALANCED_TOKENS, local_key_value, HEAD_SIZE)
    value_row_block = place(arrived[2]).reshape(BALANCED_TOKENS, local_key_value, HEAD_SIZE)
    grad_rows = place(arrived[3]).reshape(BALANCED_TOKENS, local_key_value, group_size, HEAD_SIZE)
    lse_rows = (
        place(arrived[4]).astype(jnp.float32).reshape(BALANCED_TOKENS, local_key_value, group_size)
    )
    out_rows = (
        place(arrived[5])
        .astype(jnp.float32)
        .reshape(BALANCED_TOKENS, local_key_value, group_size, HEAD_SIZE)
    )
    delta_rows = (
        jnp.sum(grad_rows.astype(jnp.float32) * out_rows, axis=-1)
        .astype(jnp.bfloat16)
        .astype(jnp.float32)
    )
    gathered = (
        lax.all_gather(key_row_block, seq, axis=0, tiled=True),
        lax.all_gather(value_row_block, seq, axis=0, tiled=True),
    )
    all_keys = gathered[0].reshape(sequence_count, BALANCED_TOKENS, local_key_value, HEAD_SIZE)
    all_values = gathered[1].reshape(sequence_count, BALANCED_TOKENS, local_key_value, HEAD_SIZE)
    rows_per = block_keys // sequence_count
    inner = 1
    outer = BALANCED_TOKENS // rows_per // inner
    query_rank = jnp.arange(BALANCED_TOKENS, dtype=jnp.int32) * sequence_count + my_index
    lse_t = lse_rows.transpose(1, 2, 0)
    delta_t = delta_rows.transpose(1, 2, 0)
    position = jnp.arange(sequence_count * rows_per, dtype=jnp.int32)

    def key_step(query_acc, row_start):
        key_blk = lax.dynamic_slice_in_dim(all_keys, row_start, rows_per, 1).reshape(
            sequence_count * rows_per, local_key_value, HEAD_SIZE
        )
        value_blk = lax.dynamic_slice_in_dim(all_values, row_start, rows_per, 1).reshape(
            sequence_count * rows_per, local_key_value, HEAD_SIZE
        )
        key_owner_rank = (row_start + position % rows_per) * sequence_count + position // rows_per
        mask = key_owner_rank[None, None, None, :] <= query_rank[None, None, :, None]
        scores = (
            jnp.einsum(
                "rgmc,kgc->gmrk", query_row_block, key_blk, preferred_element_type=jnp.float32
            )
            * scale
        )
        probs = jnp.where(mask, jnp.exp(scores - lse_t[..., None]), 0.0)
        dprob = jnp.einsum(
            "rgmc,kgc->gmrk", grad_rows, value_blk, preferred_element_type=jnp.float32
        )
        dscore = probs * (dprob - delta_t[..., None])
        probs_low = probs.astype(jnp.bfloat16)
        dscore_low = dscore.astype(jnp.bfloat16)
        query_acc = query_acc + scale * jnp.einsum(
            "gmrk,kgc->rgmc", dscore_low, key_blk, preferred_element_type=jnp.float32
        )
        key_part = scale * jnp.einsum(
            "gmrk,rgmc->kgc", dscore_low, query_row_block, preferred_element_type=jnp.float32
        )
        value_part = jnp.einsum(
            "gmrk,rgmc->kgc", probs_low, grad_rows, preferred_element_type=jnp.float32
        )
        return (
            query_acc,
            key_part.reshape(sequence_count, rows_per, local_key_value * HEAD_SIZE),
            value_part.reshape(sequence_count, rows_per, local_key_value * HEAD_SIZE),
        )

    def outer_step(query_acc, outer_index):

        def inner_step(query_inner, inner_index):
            row_start = (outer_index * inner + inner_index) * rows_per
            query_new, key_part, value_part = key_step(query_inner, row_start)
            return (query_new, (key_part, value_part))

        query_acc, (key_parts, value_parts) = lax.scan(
            inner_step, query_acc, jnp.arange(inner, dtype=jnp.int32)
        )
        key_parts = key_parts.transpose(1, 0, 2, 3).reshape(
            sequence_count, inner * rows_per, local_key_value * HEAD_SIZE
        )
        value_parts = value_parts.transpose(1, 0, 2, 3).reshape(
            sequence_count, inner * rows_per, local_key_value * HEAD_SIZE
        )
        received = (
            lax.all_to_all(key_parts, seq, split_axis=0, concat_axis=0, tiled=True),
            lax.all_to_all(value_parts, seq, split_axis=0, concat_axis=0, tiled=True),
        )
        return (query_acc, (jnp.sum(received[0], axis=0), jnp.sum(received[1], axis=0)))

    start_acc = jnp.zeros((BALANCED_TOKENS, local_key_value, group_size, HEAD_SIZE), jnp.float32)
    query_acc, (key_sums, value_sums) = lax.scan(
        outer_step, start_acc, jnp.arange(outer, dtype=jnp.int32)
    )
    query_done = query_acc.reshape(
        BALANCED_TOKENS, local_key_value * group_size * HEAD_SIZE
    ).astype(jnp.bfloat16)
    key_done = key_sums.reshape(BALANCED_TOKENS, local_key_value * HEAD_SIZE).astype(jnp.bfloat16)
    value_done = value_sums.reshape(BALANCED_TOKENS, local_key_value * HEAD_SIZE).astype(
        jnp.bfloat16
    )
    safe_rows = jnp.minimum(target_rank, BALANCED_TOKENS - 1)
    alive_flat = alive.reshape(-1)

    def collect(array):
        picked = jnp.where(alive_flat[:, None], array[safe_rows], jnp.zeros((), array.dtype))
        return picked.reshape(slots, sequence_count, array.shape[-1])

    returned = (
        lax.all_to_all(collect(query_done), seq, split_axis=1, concat_axis=1, tiled=True),
        lax.all_to_all(collect(key_done), seq, split_axis=1, concat_axis=1, tiled=True),
        lax.all_to_all(collect(value_done), seq, split_axis=1, concat_axis=1, tiled=True),
    )

    def to_home(array):
        unrolled = jnp.roll(array, -first_rank, axis=1)
        return unrolled.reshape(capacity, 1, array.shape[-1])

    homed = (
        lax.all_to_all(to_home(returned[0]), "head", split_axis=0, concat_axis=1, tiled=True),
        lax.all_to_all(to_home(returned[1]), "head", split_axis=0, concat_axis=1, tiled=True),
        lax.all_to_all(to_home(returned[2]), "head", split_axis=0, concat_axis=1, tiled=True),
    )
    query_grads = homed[0].reshape(home_rows, head_total * homed[0].shape[-1])
    key_gradient_output = homed[1].reshape(home_rows, head_total * homed[1].shape[-1])
    value_gradient = homed[2].reshape(home_rows, head_total * homed[2].shape[-1])
    return (query_grads, key_gradient_output, value_gradient)

LOG2E = 1.4426950408889634
KEY_TILE = 256
ROW_TILE = 128
INFO_ROWS = 16
AUX_LANES = 256
COUNT_ROW = 5
DELTA_ROW = 8
SMEM = pl.BlockSpec(memory_space=pltpu.SMEM)
VMEM = pl.BlockSpec(memory_space=pltpu.VMEM)
HBM = pl.BlockSpec(memory_space=pltpu.HBM)
GROUP = QUERY_HEADS // KEY_VALUE_HEADS
WIDTH = GROUP * HEAD_SIZE
CHIPS = (5, 4, 1)
CORE = 2
SHARD_TILES = 3
PASS_ROWS = (256, 512, 768)


def pack_pairs_kernel(limit, ranks_ref, lse_ref, k_ref, v_ref, do_ref, o_ref, out_ref, columns, lanes):
    home_rows = k_ref.shape[0]
    columns[...] = jnp.zeros_like(columns)
    for g in range(KEY_VALUE_HEADS):
        columns[:, 16 * g : 16 * g + GROUP] = lse_ref[:, g * GROUP : (g + 1) * GROUP].astype(
            jnp.float32
        )
    for h in range(QUERY_HEADS):
        head = slice(h * HEAD_SIZE, (h + 1) * HEAD_SIZE)
        product = do_ref[:, head].astype(jnp.float32) * o_ref[:, head].astype(jnp.float32)
        column = 16 * (h // GROUP) + DELTA_ROW + h % GROUP
        columns[:, column : column + 1] = jnp.sum(product, axis=1, keepdims=True)
    lanes[...] = jnp.zeros_like(lanes)
    lanes[:, :home_rows] = columns[...].T
    live = jnp.where(ranks_ref[...] < limit, 1.0, 0.0)
    count = jnp.sum(live, axis=1, keepdims=True)
    line = lax.broadcasted_iota(jnp.int32, (INFO_ROWS, 2 * HEAD_SIZE), 0)
    for g in range(KEY_VALUE_HEADS):
        head = slice(g * HEAD_SIZE, (g + 1) * HEAD_SIZE)
        out_ref[g, :home_rows, :HEAD_SIZE] = k_ref[:, head]
        out_ref[g, :home_rows, HEAD_SIZE:] = v_ref[:, head]
        info = jnp.where(line == COUNT_ROW, count, lanes[16 * g : 16 * g + INFO_ROWS, :])
        out_ref[g, home_rows:, :] = info.astype(out_ref.dtype)


def pack_pairs(limit, ranks, lse, keys, values, output_gradient, outputs):
    home_rows = keys.shape[0]
    return pl.pallas_call(
        functools.partial(pack_pairs_kernel, limit),
        out_shape=jax.ShapeDtypeStruct(
            (KEY_VALUE_HEADS, home_rows + INFO_ROWS, 2 * HEAD_SIZE), keys.dtype
        ),
        in_specs=[VMEM] * 6,
        out_specs=VMEM,
        scratch_shapes=[
            pltpu.VMEM((home_rows, HEAD_SIZE), jnp.float32),
            pltpu.VMEM((HEAD_SIZE, AUX_LANES), jnp.float32),
        ],
        compiler_params=pltpu.CompilerParams(vmem_limit_bytes=32 * 1024 * 1024),
        name="pack_pairs",
    )(ranks.reshape(1, home_rows), lse, keys, values, output_gradient, outputs)


def pack_rows_kernel(partners, me_ref, q_hbm, do_hbm, out, sems):
    copies = []
    for n, partner in enumerate(partners):
        start = pl.multiple_of((me_ref[0] ^ partner) * WIDTH, HEAD_SIZE)
        for m, source in enumerate((q_hbm, do_hbm)):
            copies.append(
                pltpu.make_async_copy(
                    source.at[:, pl.ds(start, WIDTH)],
                    out.at[n, :, pl.ds(m * WIDTH, WIDTH)],
                    sems.at[2 * n + m],
                )
            )
    for copy in copies:
        copy.start()
    for copy in copies:
        copy.wait()


def pack_rows(partners, me, queries, output_gradient):
    home_rows = queries.shape[0]
    return pl.pallas_call(
        functools.partial(pack_rows_kernel, partners),
        out_shape=jax.ShapeDtypeStruct((len(partners), home_rows, 2 * WIDTH), queries.dtype),
        in_specs=[SMEM, HBM, HBM],
        out_specs=VMEM,
        scratch_shapes=[pltpu.SemaphoreType.DMA((2 * len(partners),))],
        name="pack_rows",
    )(me, queries, output_gradient)


def compact_kernel(arrived, out, small, counts_ref):
    home_rows = arrived.shape[1] - INFO_ROWS
    capacity = out.shape[0] - INFO_ROWS
    row = lax.broadcasted_iota(jnp.int32, (capacity, home_rows), 0)
    within = lax.broadcasted_iota(jnp.int32, (capacity, home_rows), 1)
    total = jnp.int32(0)
    picked = []
    for block in range(KEY_VALUE_HEADS):
        info = arrived[block, home_rows:, :]
        small[block] = info
        count = jnp.max(info[COUNT_ROW : COUNT_ROW + 1].astype(jnp.float32)).astype(jnp.int32)
        counts_ref[block] = count
        hit = (row == within + total) & (within < count)
        picked.append(jnp.where(hit, 1.0, 0.0).astype(jnp.bfloat16))
        total = total + count
    acc = jnp.zeros((capacity, out.shape[1]), jnp.float32)
    for block in range(KEY_VALUE_HEADS):
        acc += jnp.dot(
            picked[block], arrived[block, :home_rows, :], preferred_element_type=jnp.float32
        )
    out[:capacity, :] = acc.astype(out.dtype)
    line = lax.broadcasted_iota(jnp.int32, (INFO_ROWS, out.shape[1]), 0)
    out[capacity:, :] = (
        jnp.where(line == 0, total // 64, jnp.where(line == 1, total % 64, 0))
        .astype(jnp.float32)
        .astype(out.dtype)
    )


def compact(arrived):
    blocks, rows, columns = arrived.shape
    capacity = blocks * (rows - INFO_ROWS) // 2
    return pl.pallas_call(
        compact_kernel,
        out_shape=(
            jax.ShapeDtypeStruct((capacity + INFO_ROWS, columns), arrived.dtype),
            jax.ShapeDtypeStruct((blocks, INFO_ROWS, columns), arrived.dtype),
            jax.ShapeDtypeStruct((blocks,), jnp.int32),
        ),
        in_specs=[VMEM],
        out_specs=(VMEM, VMEM, SMEM),
        compiler_params=pltpu.CompilerParams(vmem_limit_bytes=32 * 1024 * 1024),
        name="compact",
    )(arrived)


def load_rows(me, counts_ref, arrays, q_s, do_s, sems):
    home_rows = q_s.shape[0] // KEY_VALUE_HEADS
    q_hbm, do_hbm, beside, pairs, crossed = arrays
    column = pl.multiple_of(me * WIDTH, HEAD_SIZE)
    left, right = pl.ds(0, WIDTH), pl.ds(WIDTH, WIDTH)
    sources = [
        (0, q_hbm.at[:, pl.ds(column, WIDTH)], do_hbm.at[:, pl.ds(column, WIDTH)]),
        (CORE, beside.at[0, :, left], beside.at[0, :, right]),
    ]
    for chip, pair, cross in zip(CHIPS, pairs, crossed):
        sources.append((chip, pair.at[0, :, left], pair.at[0, :, right]))
        sources.append((chip ^ CORE, cross.at[0, :, left], cross.at[0, :, right]))
    plans = []
    for n, (partner, q, do) in enumerate(sources):
        source = me ^ partner
        rows = pl.ds(pl.multiple_of(source * home_rows, 64), home_rows)
        shard = counts_ref[source & ~1] + counts_ref[source | 1]
        needed = ((source & 1) == 0) | (shard > ROW_TILE)
        plans.append(
            (
                needed,
                [
                    pltpu.make_async_copy(q, q_s.at[rows, :], sems.at[2 * n]),
                    pltpu.make_async_copy(do, do_s.at[rows, :], sems.at[2 * n + 1]),
                ],
            )
        )

    def each(act):
        for needed, copies in plans:

            @pl.when(needed)
            def _():
                for copy in copies:
                    act(copy)

    return each


def list_tiles(counts_ref, tiles, starts):
    length = jnp.int32(0)
    total = jnp.int32(0)
    for shard in range(KEY_VALUE_HEADS // 2):
        count = counts_ref[2 * shard] + counts_ref[2 * shard + 1]
        starts[shard] = total
        total = total + count
        for t in range(SHARD_TILES):
            live = count > t * ROW_TILE

            @pl.when(live)
            def _():
                tiles[length] = SHARD_TILES * shard + t

            length = length + live.astype(jnp.int32)
    return length, total


def spread_lanes(aux_s, lse_s, delta_s):
    lane = lax.broadcasted_iota(jnp.int32, (INFO_ROWS, ROW_TILE), 1)
    for shard in range(KEY_VALUE_HEADS // 2):
        low = aux_s[2 * shard].astype(jnp.float32)
        high = aux_s[2 * shard + 1].astype(jnp.float32)
        half = ROW_TILE // 2
        middle = jnp.where(
            lane < half, low[:, ROW_TILE:], pltpu.roll(high[:, :ROW_TILE], half, axis=1)
        )
        last = pltpu.roll(high, AUX_LANES - half, axis=1)[:, :ROW_TILE]
        for t, rows in enumerate((low[:, :ROW_TILE], middle, last)):
            row = SHARD_TILES * shard + t
            for h in range(GROUP):
                columns = slice(h * ROW_TILE, (h + 1) * ROW_TILE)
                lse_s[row : row + 1, columns] = rows[h : h + 1] * LOG2E
                delta_s[row : row + 1, columns] = rows[DELTA_ROW + h : DELTA_ROW + 1 + h]


def row_tile(tile, q_s, do_s, lse_s, delta_s):
    def stack(ref):
        rows = ref[pl.ds(pl.multiple_of(tile * ROW_TILE, ROW_TILE), ROW_TILE), :]
        return jnp.concatenate(
            [rows[:, h * HEAD_SIZE : (h + 1) * HEAD_SIZE] for h in range(GROUP)], axis=0
        )

    return stack(q_s), stack(do_s), lse_s[pl.ds(tile, 1), :], delta_s[pl.ds(tile, 1), :]


def tile_step(key, value, key_t, rows, position, bound, acc_k, acc_v, add_dq):
    q, do, lse, delta = rows
    scale = HEAD_SIZE ** (-0.5)
    dims = (((1,), (1,)), ((), ()))
    scores = lax.dot_general(key, q, dims, preferred_element_type=jnp.float32)
    prob = jnp.where(position <= bound, jnp.exp2(scores * (scale * LOG2E) - lse), 0.0)
    dprob = lax.dot_general(value, do, dims, preferred_element_type=jnp.float32)
    dscore = (prob * (dprob - delta)).astype(jnp.bfloat16)
    acc_v[...] += jnp.dot(prob.astype(jnp.bfloat16), do, preferred_element_type=jnp.float32)
    acc_k[...] += jnp.dot(dscore, q, preferred_element_type=jnp.float32)
    add_dq(jnp.dot(key_t, dscore, preferred_element_type=jnp.float32))


def attention_kernel(me_ref, counts_ref, *rest):
    aux_s, arrays, kv, kvs, rest = rest[0], rest[1:10], rest[10], rest[11:14], rest[14:]
    arrays = (*arrays[:3], arrays[3:6], arrays[6:9])
    downs, dq_out, own_out, full_ref, rest = rest[:3], rest[3], rest[4], rest[5], rest[6:]
    (
        q_s, do_s, lse_s, delta_s, dqt, kv_s, acc_k, acc_v, tiles, starts, limits, sems, kv_sem,
        down_sem, out_sem, down_s, dq_s, own,
    ) = rest
    capacity = downs[0].shape[0] - INFO_ROWS
    scale = HEAD_SIZE ** (-0.5)
    each = load_rows(me_ref[0], counts_ref, arrays, q_s, do_s, sems)
    each(lambda copy: copy.start())
    kv_copies = [
        pltpu.make_async_copy(source, kv_s.at[n], kv_sem.at[n])
        for n, source in enumerate((*kvs, kv))
    ]
    for copy in kv_copies:
        copy.start()
    length, total = list_tiles(counts_ref, tiles, starts)

    def zero_tile(n, carry):
        dqt[tiles[n]] = jnp.zeros(dqt.shape[1:], jnp.float32)
        return carry

    lax.fori_loop(0, length, zero_tile, 0)
    own[...] = jnp.zeros_like(own)
    spread_lanes(aux_s, lse_s, delta_s)
    for copy in kv_copies:
        copy.wait()
    most = total
    for n in range(3):
        info = kv_s[n, capacity:, :].astype(jnp.float32)
        limit = (jnp.max(info[0:1]) * 64.0 + jnp.max(info[1:2])).astype(jnp.int32)
        limits[n] = jnp.minimum(limit, capacity)
        most = jnp.maximum(most, limit)
    full = most > capacity
    full_ref[0] = full.astype(jnp.int32)
    for n in range(3):
        down_s[n, capacity:, :] = jnp.full(
            (INFO_ROWS, 2 * HEAD_SIZE), jnp.where(full, 1.0, 0.0)
        ).astype(jnp.bfloat16)
    each(lambda copy: copy.wait())
    lane = lax.broadcasted_iota(jnp.int32, (1, WIDTH), 1) % ROW_TILE

    def block_step(step, carry):
        index = 2 - step
        limit = limits[index]

        def run(rows):
            key = kv_s[index, :rows, :HEAD_SIZE]
            value = kv_s[index, :rows, HEAD_SIZE:]
            key_t = key.T
            acc_k[:rows] = jnp.zeros((rows, HEAD_SIZE), jnp.float32)
            acc_v[:rows] = jnp.zeros((rows, HEAD_SIZE), jnp.float32)
            position = lax.broadcasted_iota(jnp.int32, (rows, 1), 0)

            def row_step(n, inner):
                tile = tiles[n]
                shard = tile // SHARD_TILES
                count = counts_ref[2 * shard] + counts_ref[2 * shard + 1]
                alive = lane < count - (tile % SHARD_TILES) * ROW_TILE
                bound = jnp.where(alive, limit - 1, -1)

                def add_dq(part):
                    dqt[tile] += part

                tile_step(
                    key, value, key_t, row_tile(tile, q_s, do_s, lse_s, delta_s), position, bound,
                    acc_k.at[pl.ds(0, rows), :], acc_v.at[pl.ds(0, rows), :], add_dq,
                )
                return inner

            lax.fori_loop(0, length, row_step, 0)
            down_s[index, :rows, :HEAD_SIZE] = (acc_k[:rows] * scale).astype(jnp.bfloat16)
            down_s[index, :rows, HEAD_SIZE:] = acc_v[:rows].astype(jnp.bfloat16)
            if rows < capacity:
                down_s[index, rows:capacity, :] = jnp.zeros(
                    (capacity - rows, 2 * HEAD_SIZE), jnp.bfloat16
                )

        below = 0
        for rows in PASS_ROWS:

            @pl.when((limit > below) & (limit <= rows))
            def _():
                run(rows)

            below = rows

        @pl.when(limit == 0)
        def _():
            down_s[index, :capacity, :] = jnp.zeros((capacity, 2 * HEAD_SIZE), jnp.bfloat16)

        return carry

    lax.fori_loop(0, 3, block_step, 0)
    down_copies = [
        pltpu.make_async_copy(down_s.at[n], downs[n], down_sem.at[n]) for n in range(3)
    ]
    for copy in down_copies:
        copy.start()

    limit = jnp.minimum(total, capacity)

    def key_step(kt, carry):
        start = pl.multiple_of(kt * KEY_TILE, KEY_TILE)
        key = kv_s[3, pl.ds(start, KEY_TILE), :HEAD_SIZE]
        value = kv_s[3, pl.ds(start, KEY_TILE), HEAD_SIZE:]
        key_t = key.T
        own_k = acc_k.at[pl.ds(0, KEY_TILE), :]
        own_v = acc_v.at[pl.ds(0, KEY_TILE), :]
        own_k[...] = jnp.zeros_like(own_k)
        own_v[...] = jnp.zeros_like(own_v)
        position = start + lax.broadcasted_iota(jnp.int32, (KEY_TILE, 1), 0)

        def row_step(n, inner):
            tile = tiles[n]
            shard = tile // SHARD_TILES
            offset = (tile % SHARD_TILES) * ROW_TILE
            count = counts_ref[2 * shard] + counts_ref[2 * shard + 1]
            first = starts[shard] + offset

            @pl.when(first + ROW_TILE > start)
            def _():
                bound = jnp.where(lane < count - offset, first + lane, -1)

                def add_dq(part):
                    dqt[tile] += part

                tile_step(
                    key, value, key_t, row_tile(tile, q_s, do_s, lse_s, delta_s), position, bound,
                    own_k, own_v, add_dq,
                )

            return inner

        lax.fori_loop(0, length, row_step, 0)
        own[pl.ds(start, KEY_TILE), :HEAD_SIZE] = own_k[...] * scale
        own[pl.ds(start, KEY_TILE), HEAD_SIZE:] = own_v[...]
        return carry

    lax.fori_loop(0, (limit + KEY_TILE - 1) // KEY_TILE, key_step, 0)
    own_copy = pltpu.make_async_copy(own, own_out, down_sem.at[3])
    own_copy.start()

    half = ROW_TILE // 2
    copies = []
    for block in range(KEY_VALUE_HEADS):
        shard = block // 2
        count = counts_ref[2 * shard] + counts_ref[2 * shard + 1]
        if block % 2 == 0:
            pieces = ((0, ROW_TILE, 0, 0), (ROW_TILE, half, 1, 0))
        else:
            pieces = ((0, half, 1, half), (half, ROW_TILE, 2, 0))
        for offset, size, t, first in pieces:
            live = count > t * ROW_TILE
            rows = slice(offset, offset + size)

            @pl.when(live)
            def _():
                for h in range(GROUP):
                    columns = slice(h * HEAD_SIZE, (h + 1) * HEAD_SIZE)
                    part = (dqt[SHARD_TILES * shard + t, :, columns] * scale).T
                    dq_s[block, rows, columns] = part[first : first + size].astype(jnp.bfloat16)

            @pl.when(jnp.logical_not(live))
            def _():
                dq_s[block, rows, :] = jnp.zeros((size, WIDTH), jnp.bfloat16)

        copy = pltpu.make_async_copy(dq_s.at[block], dq_out.at[block], out_sem.at[block])
        copy.start()
        copies.append(copy)
    for copy in (*copies, *down_copies, own_copy):
        copy.wait()


def row_scratch(plane_rows):
    bf16, f32 = jnp.bfloat16, jnp.float32
    tile_count = plane_rows // ROW_TILE
    return [
        pltpu.VMEM((plane_rows, WIDTH), bf16),
        pltpu.VMEM((plane_rows, WIDTH), bf16),
        pltpu.VMEM((tile_count, WIDTH), f32),
        pltpu.VMEM((tile_count, WIDTH), f32),
        pltpu.VMEM((tile_count, HEAD_SIZE, WIDTH), f32),
    ]


def attention(me, counts, small, arrays, kv, kvs):
    bf16, f32 = jnp.bfloat16, jnp.float32
    blocks = KEY_VALUE_HEADS
    rows = kv.shape[0]
    capacity = rows - INFO_ROWS
    columns = 2 * HEAD_SIZE
    plane_rows = 2 * capacity
    tile_count = plane_rows // ROW_TILE
    dq = (blocks, plane_rows // blocks, WIDTH)
    return pl.pallas_call(
        attention_kernel,
        out_shape=(jax.ShapeDtypeStruct((rows, columns), bf16),) * 3
        + (
            jax.ShapeDtypeStruct(dq, bf16),
            jax.ShapeDtypeStruct((capacity, columns), f32),
            jax.ShapeDtypeStruct((1,), jnp.int32),
        ),
        in_specs=[SMEM] * 2 + [VMEM] + [HBM] * 13,
        out_specs=[HBM] * 5 + [SMEM],
        scratch_shapes=[
            pltpu.VMEM((plane_rows, WIDTH), bf16),
            pltpu.VMEM((plane_rows, WIDTH), bf16),
            pltpu.VMEM((tile_count, WIDTH), f32),
            pltpu.VMEM((tile_count, WIDTH), f32),
            pltpu.VMEM((tile_count, HEAD_SIZE, WIDTH), f32),
            pltpu.VMEM((4, rows, columns), bf16),
            pltpu.VMEM((capacity, HEAD_SIZE), f32),
            pltpu.VMEM((capacity, HEAD_SIZE), f32),
            pltpu.SMEM((tile_count + 1,), jnp.int32),
            pltpu.SMEM((blocks,), jnp.int32),
            pltpu.SMEM((3,), jnp.int32),
            pltpu.SemaphoreType.DMA((2 * blocks,)),
            pltpu.SemaphoreType.DMA((4,)),
            pltpu.SemaphoreType.DMA((4,)),
            pltpu.SemaphoreType.DMA((blocks,)),
            pltpu.VMEM((3, rows, columns), bf16),
            pltpu.VMEM(dq, bf16),
            pltpu.VMEM((capacity, columns), f32),
        ],
        compiler_params=pltpu.CompilerParams(vmem_limit_bytes=48 * 1024 * 1024),
        cost_estimate=pl.CostEstimate(
            flops=10_000_000_000, bytes_accessed=12_000_000, transcendentals=8_000_000
        ),
        name="attention",
    )(me, counts, small, *arrays, kv, *kvs)


def unpack_rows_kernel(parts, out):
    for g in range(KEY_VALUE_HEADS):
        out[:, g * WIDTH : (g + 1) * WIDTH] = parts[g]


def unpack_rows(parts):
    return pl.pallas_call(
        unpack_rows_kernel,
        out_shape=jax.ShapeDtypeStruct((parts.shape[1], KEY_VALUE_HEADS * WIDTH), parts.dtype),
        in_specs=[VMEM],
        out_specs=VMEM,
        name="unpack_rows",
    )(parts)


def combine_kernel(counts_ref, own, *rest):
    backs, out = rest[:3], rest[3]
    home_rows = out.shape[1]
    capacity = own.shape[0]
    total = own[...]
    for back in backs:
        total += back[:capacity, :].astype(jnp.float32)
    total = total.astype(jnp.bfloat16)
    within = lax.broadcasted_iota(jnp.int32, (home_rows, capacity), 0)
    place = lax.broadcasted_iota(jnp.int32, (home_rows, capacity), 1)
    start = jnp.int32(0)
    for block in range(KEY_VALUE_HEADS):
        count = counts_ref[block]
        hit = (place == within + start) & (within < count)
        out[block] = jnp.dot(
            jnp.where(hit, 1.0, 0.0).astype(jnp.bfloat16),
            total,
            preferred_element_type=jnp.float32,
        ).astype(jnp.bfloat16)
        start = start + count


def combine(counts, own, backs, home_rows):
    blocks = KEY_VALUE_HEADS
    return pl.pallas_call(
        combine_kernel,
        out_shape=jax.ShapeDtypeStruct((blocks, home_rows, own.shape[1]), jnp.bfloat16),
        in_specs=[SMEM] + [VMEM] * 4,
        out_specs=VMEM,
        compiler_params=pltpu.CompilerParams(vmem_limit_bytes=32 * 1024 * 1024),
        name="combine",
    )(counts, own, *backs)


def plane_device(queries, keys, values, outputs, output_gradient, lse, ranks):
    planes = lax.axis_size("outer")
    plane = ("inner", "head")
    blocks = KEY_VALUE_HEADS
    home_rows = queries.shape[0]
    plane_rows = blocks * home_rows
    capacity = plane_rows // 2
    surviving_tokens = BALANCED_TOKENS * planes * lax.axis_size("inner")
    bf16, f32 = jnp.bfloat16, jnp.float32
    me = lax.axis_index(plane).reshape(1).astype(jnp.int32)

    def swap(array, k):
        return lax.ppermute(array, plane, [(i, i ^ k) for i in range(blocks)])

    sent = pack_pairs(
        surviving_tokens, ranks, lse, keys, values, output_gradient, outputs
    )
    me, sent = lax.optimization_barrier((me, sent))
    arrived = lax.all_to_all(sent, plane, split_axis=0, concat_axis=0, tiled=True)
    packed = [pack_rows((chip, chip ^ CORE), me, queries, output_gradient) for chip in CHIPS]
    me, packed[-1] = lax.optimization_barrier((me, packed[-1]))
    pairs = [swap(rows, chip) for rows, chip in zip(packed, CHIPS)]
    beside = swap(pack_rows((CORE,), me, queries, output_gradient), CORE)
    arrived, beside = lax.optimization_barrier((arrived, beside))
    mine, small, counts = compact(arrived)
    up = [lax.ppermute(mine, "outer", [(i, i + 1) for i in range(planes - 1)])]
    last = lax.ppermute(mine, "outer", [(0, planes - 1)])
    up.append(lax.ppermute(up[0], "outer", [(i, i + 1) for i in range(1, planes - 1)]))
    up.append(last)
    up[1], up[2], *pairs = lax.optimization_barrier((up[1], up[2], *pairs))
    crossed = [swap(pair[1:], CORE) for pair in pairs]
    arrays = [queries, output_gradient, beside, *pairs, *crossed]

    *down, dq, own, full = attention(me, counts, small, arrays, mine, up)
    backs = [
        lax.ppermute(down[k - 1], "outer", [(i + k, i) for i in range(planes - k)])
        for k in (3, 2, 1)
    ]
    dq = lax.all_to_all(dq, plane, split_axis=0, concat_axis=0, tiled=True)
    dq, own = lax.optimization_barrier((dq, own))
    dq_home = unpack_rows(dq)
    kv_home = lax.all_to_all(
        combine(counts, own, backs, home_rows), plane, split_axis=0, concat_axis=0, tiled=True
    )
    full = full[0] > 0
    for back in backs:
        full = full | (back[capacity, 0] > 0)
    dk = kv_home[:, :, :HEAD_SIZE].transpose(1, 0, 2).reshape(home_rows, blocks * HEAD_SIZE)
    dv = kv_home[:, :, HEAD_SIZE:].transpose(1, 0, 2).reshape(home_rows, blocks * HEAD_SIZE)
    return (dq_home, dk, dv), full


def solution(mesh):
    spec = P(("seq", "head"), None)
    heads = mesh.shape["head"]
    inner = max(KEY_VALUE_HEADS // heads, 1)
    planes = mesh.shape["seq"] // inner
    if planes != 4 or inner * heads != KEY_VALUE_HEADS:
        return jax.shard_map(
            per_device,
            mesh=mesh,
            in_specs=(spec,) * 6 + (P(("seq", "head")),),
            out_specs=(spec,) * 3,
            check_vma=False,
        )
    axes = ("outer", "inner", "head")

    def device(*blocks):
        fast, full = plane_device(*blocks)
        return lax.cond(full, lambda: per_device(*blocks, seq=("outer", "inner")), lambda: fast)

    return jax.shard_map(
        device,
        mesh=Mesh(mesh.devices.reshape(planes, inner, heads), axes),
        in_specs=(P(axes, None),) * 6 + (P(axes),),
        out_specs=(P(axes, None),) * 3,
        check_vma=False,
    )
```

```python
import functools

import jax
import jax.numpy as jnp
from jax import lax
from jax.experimental import pallas as pl
from jax.experimental.pallas import tpu as pltpu
from jax.sharding import Mesh
from jax.sharding import PartitionSpec as P

QUERY_HEADS = 40
KEY_VALUE_HEADS = 8
HEAD_SIZE = 128
BALANCED_TOKENS = 128


block_keys = 512


def per_device(queries, keys, values, outputs, output_gradient, lse, ranks, seq="seq"):
    sequence_count = lax.axis_size(seq)
    head_total = lax.axis_size("head")
    home_rows = queries.shape[0]
    capacity = home_rows * head_total
    slots = capacity // sequence_count
    surviving_tokens = BALANCED_TOKENS * sequence_count
    group_size = QUERY_HEADS // KEY_VALUE_HEADS
    local_key_value = KEY_VALUE_HEADS // head_total
    scale = HEAD_SIZE ** (-0.5)

    def split_heads(array):
        return array.reshape(home_rows, head_total, array.shape[1] // head_total)

    moved = (
        lax.all_to_all(split_heads(queries), "head", split_axis=1, concat_axis=0, tiled=True),
        lax.all_to_all(split_heads(keys), "head", split_axis=1, concat_axis=0, tiled=True),
        lax.all_to_all(split_heads(values), "head", split_axis=1, concat_axis=0, tiled=True),
        lax.all_to_all(
            split_heads(output_gradient), "head", split_axis=1, concat_axis=0, tiled=True
        ),
        lax.all_to_all(split_heads(lse), "head", split_axis=1, concat_axis=0, tiled=True),
        lax.all_to_all(split_heads(outputs), "head", split_axis=1, concat_axis=0, tiled=True),
    )
    shard_rank_list = lax.all_gather(ranks, "head", axis=0, tiled=True)
    first_rank = shard_rank_list[0]
    living_count = jnp.sum((shard_rank_list < surviving_tokens).astype(jnp.int32))
    table = lax.all_gather(
        jnp.stack([first_rank, living_count])[None, :], seq, axis=0, tiled=True
    )

    def to_pairs(array):
        flat = array.reshape(slots, sequence_count, array.shape[-1])
        return jnp.roll(flat, first_rank, axis=1)

    arrived = (
        lax.all_to_all(to_pairs(moved[0]), seq, split_axis=1, concat_axis=1, tiled=True),
        lax.all_to_all(to_pairs(moved[1]), seq, split_axis=1, concat_axis=1, tiled=True),
        lax.all_to_all(to_pairs(moved[2]), seq, split_axis=1, concat_axis=1, tiled=True),
        lax.all_to_all(to_pairs(moved[3]), seq, split_axis=1, concat_axis=1, tiled=True),
        lax.all_to_all(to_pairs(moved[4]), seq, split_axis=1, concat_axis=1, tiled=True),
        lax.all_to_all(to_pairs(moved[5]), seq, split_axis=1, concat_axis=1, tiled=True),
    )
    my_index = lax.axis_index(seq)
    starts = table[:, 0]
    count_table = table[:, 1]
    offset = (my_index - starts) % sequence_count
    within = jnp.arange(slots, dtype=jnp.int32)[:, None] * sequence_count + offset[None, :]
    alive = within < count_table[None, :]
    target_rank = jnp.where(
        alive, (starts[None, :] + within) // sequence_count, BALANCED_TOKENS
    ).reshape(-1)

    def place(array):
        width = array.shape[-1]
        return (
            jnp.zeros((BALANCED_TOKENS, width), array.dtype)
            .at[target_rank]
            .set(array.reshape(slots * sequence_count, width), mode="drop")
        )

    query_row_block = place(arrived[0]).reshape(
        BALANCED_TOKENS, local_key_value, group_size, HEAD_SIZE
    )
    key_row_block = place(arrived[1]).reshape(BALANCED_TOKENS, local_key_value, HEAD_SIZE)
    value_row_block = place(arrived[2]).reshape(BALANCED_TOKENS, local_key_value, HEAD_SIZE)
    grad_rows = place(arrived[3]).reshape(BALANCED_TOKENS, local_key_value, group_size, HEAD_SIZE)
    lse_rows = (
        place(arrived[4]).astype(jnp.float32).reshape(BALANCED_TOKENS, local_key_value, group_size)
    )
    out_rows = (
        place(arrived[5])
        .astype(jnp.float32)
        .reshape(BALANCED_TOKENS, local_key_value, group_size, HEAD_SIZE)
    )
    delta_rows = (
        jnp.sum(grad_rows.astype(jnp.float32) * out_rows, axis=-1)
        .astype(jnp.bfloat16)
        .astype(jnp.float32)
    )
    gathered = (
        lax.all_gather(key_row_block, seq, axis=0, tiled=True),
        lax.all_gather(value_row_block, seq, axis=0, tiled=True),
    )
    all_keys = gathered[0].reshape(sequence_count, BALANCED_TOKENS, local_key_value, HEAD_SIZE)
    all_values = gathered[1].reshape(sequence_count, BALANCED_TOKENS, local_key_value, HEAD_SIZE)
    rows_per = block_keys // sequence_count
    inner = 1
    outer = BALANCED_TOKENS // rows_per // inner
    query_rank = jnp.arange(BALANCED_TOKENS, dtype=jnp.int32) * sequence_count + my_index
    lse_t = lse_rows.transpose(1, 2, 0)
    delta_t = delta_rows.transpose(1, 2, 0)
    position = jnp.arange(sequence_count * rows_per, dtype=jnp.int32)

    def key_step(query_acc, row_start):
        key_blk = lax.dynamic_slice_in_dim(all_keys, row_start, rows_per, 1).reshape(
            sequence_count * rows_per, local_key_value, HEAD_SIZE
        )
        value_blk = lax.dynamic_slice_in_dim(all_values, row_start, rows_per, 1).reshape(
            sequence_count * rows_per, local_key_value, HEAD_SIZE
        )
        key_owner_rank = (row_start + position % rows_per) * sequence_count + position // rows_per
        mask = key_owner_rank[None, None, None, :] <= query_rank[None, None, :, None]
        scores = (
            jnp.einsum(
                "rgmc,kgc->gmrk", query_row_block, key_blk, preferred_element_type=jnp.float32
            )
            * scale
        )
        probs = jnp.where(mask, jnp.exp(scores - lse_t[..., None]), 0.0)
        dprob = jnp.einsum(
            "rgmc,kgc->gmrk", grad_rows, value_blk, preferred_element_type=jnp.float32
        )
        dscore = probs * (dprob - delta_t[..., None])
        probs_low = probs.astype(jnp.bfloat16)
        dscore_low = dscore.astype(jnp.bfloat16)
        query_acc = query_acc + scale * jnp.einsum(
            "gmrk,kgc->rgmc", dscore_low, key_blk, preferred_element_type=jnp.float32
        )
        key_part = scale * jnp.einsum(
            "gmrk,rgmc->kgc", dscore_low, query_row_block, preferred_element_type=jnp.float32
        )
        value_part = jnp.einsum(
            "gmrk,rgmc->kgc", probs_low, grad_rows, preferred_element_type=jnp.float32
        )
        return (
            query_acc,
            key_part.reshape(sequence_count, rows_per, local_key_value * HEAD_SIZE),
            value_part.reshape(sequence_count, rows_per, local_key_value * HEAD_SIZE),
        )

    def outer_step(query_acc, outer_index):

        def inner_step(query_inner, inner_index):
            row_start = (outer_index * inner + inner_index) * rows_per
            query_new, key_part, value_part = key_step(query_inner, row_start)
            return (query_new, (key_part, value_part))

        query_acc, (key_parts, value_parts) = lax.scan(
            inner_step, query_acc, jnp.arange(inner, dtype=jnp.int32)
        )
        key_parts = key_parts.transpose(1, 0, 2, 3).reshape(
            sequence_count, inner * rows_per, local_key_value * HEAD_SIZE
        )
        value_parts = value_parts.transpose(1, 0, 2, 3).reshape(
            sequence_count, inner * rows_per, local_key_value * HEAD_SIZE
        )
        received = (
            lax.all_to_all(key_parts, seq, split_axis=0, concat_axis=0, tiled=True),
            lax.all_to_all(value_parts, seq, split_axis=0, concat_axis=0, tiled=True),
        )
        return (query_acc, (jnp.sum(received[0], axis=0), jnp.sum(received[1], axis=0)))

    start_acc = jnp.zeros((BALANCED_TOKENS, local_key_value, group_size, HEAD_SIZE), jnp.float32)
    query_acc, (key_sums, value_sums) = lax.scan(
        outer_step, start_acc, jnp.arange(outer, dtype=jnp.int32)
    )
    query_done = query_acc.reshape(
        BALANCED_TOKENS, local_key_value * group_size * HEAD_SIZE
    ).astype(jnp.bfloat16)
    key_done = key_sums.reshape(BALANCED_TOKENS, local_key_value * HEAD_SIZE).astype(jnp.bfloat16)
    value_done = value_sums.reshape(BALANCED_TOKENS, local_key_value * HEAD_SIZE).astype(
        jnp.bfloat16
    )
    safe_rows = jnp.minimum(target_rank, BALANCED_TOKENS - 1)
    alive_flat = alive.reshape(-1)

    def collect(array):
        picked = jnp.where(alive_flat[:, None], array[safe_rows], jnp.zeros((), array.dtype))
        return picked.reshape(slots, sequence_count, array.shape[-1])

    returned = (
        lax.all_to_all(collect(query_done), seq, split_axis=1, concat_axis=1, tiled=True),
        lax.all_to_all(collect(key_done), seq, split_axis=1, concat_axis=1, tiled=True),
        lax.all_to_all(collect(value_done), seq, split_axis=1, concat_axis=1, tiled=True),
    )

    def to_home(array):
        unrolled = jnp.roll(array, -first_rank, axis=1)
        return unrolled.reshape(capacity, 1, array.shape[-1])

    homed = (
        lax.all_to_all(to_home(returned[0]), "head", split_axis=0, concat_axis=1, tiled=True),
        lax.all_to_all(to_home(returned[1]), "head", split_axis=0, concat_axis=1, tiled=True),
        lax.all_to_all(to_home(returned[2]), "head", split_axis=0, concat_axis=1, tiled=True),
    )
    query_grads = homed[0].reshape(home_rows, head_total * homed[0].shape[-1])
    key_gradient_output = homed[1].reshape(home_rows, head_total * homed[1].shape[-1])
    value_gradient = homed[2].reshape(home_rows, head_total * homed[2].shape[-1])
    return (query_grads, key_gradient_output, value_gradient)

LOG2E = 1.4426950408889634
KEY_TILE = 256
ROW_TILE = 128
INFO_ROWS = 16
AUX_LANES = 256
COUNT_ROW = 5
DELTA_ROW = 8
SMEM = pl.BlockSpec(memory_space=pltpu.SMEM)
VMEM = pl.BlockSpec(memory_space=pltpu.VMEM)
HBM = pl.BlockSpec(memory_space=pltpu.HBM)
GROUP = QUERY_HEADS // KEY_VALUE_HEADS
WIDTH = GROUP * HEAD_SIZE
CHIPS = (5, 4, 1)
CORE = 2
SHARD_TILES = 3
PASS_ROWS = (256, 512, 768)


def pack_pairs_kernel(limit, ranks_ref, lse_ref, k_ref, v_ref, do_ref, o_ref, out_ref, columns, lanes):
    home_rows = k_ref.shape[0]
    columns[...] = jnp.zeros_like(columns)
    for g in range(KEY_VALUE_HEADS):
        columns[:, 16 * g : 16 * g + GROUP] = lse_ref[:, g * GROUP : (g + 1) * GROUP].astype(
            jnp.float32
        )
    for h in range(QUERY_HEADS):
        head = slice(h * HEAD_SIZE, (h + 1) * HEAD_SIZE)
        product = do_ref[:, head].astype(jnp.float32) * o_ref[:, head].astype(jnp.float32)
        column = 16 * (h // GROUP) + DELTA_ROW + h % GROUP
        columns[:, column : column + 1] = jnp.sum(product, axis=1, keepdims=True)
    lanes[...] = jnp.zeros_like(lanes)
    lanes[:, :home_rows] = columns[...].T
    live = jnp.where(ranks_ref[...] < limit, 1.0, 0.0)
    count = jnp.sum(live, axis=1, keepdims=True)
    line = lax.broadcasted_iota(jnp.int32, (INFO_ROWS, 2 * HEAD_SIZE), 0)
    for g in range(KEY_VALUE_HEADS):
        head = slice(g * HEAD_SIZE, (g + 1) * HEAD_SIZE)
        out_ref[g, :home_rows, :HEAD_SIZE] = k_ref[:, head]
        out_ref[g, :home_rows, HEAD_SIZE:] = v_ref[:, head]
        info = jnp.where(line == COUNT_ROW, count, lanes[16 * g : 16 * g + INFO_ROWS, :])
        out_ref[g, home_rows:, :] = info.astype(out_ref.dtype)


def pack_pairs(limit, ranks, lse, keys, values, output_gradient, outputs):
    home_rows = keys.shape[0]
    return pl.pallas_call(
        functools.partial(pack_pairs_kernel, limit),
        out_shape=jax.ShapeDtypeStruct(
            (KEY_VALUE_HEADS, home_rows + INFO_ROWS, 2 * HEAD_SIZE), keys.dtype
        ),
        in_specs=[VMEM] * 6,
        out_specs=VMEM,
        scratch_shapes=[
            pltpu.VMEM((home_rows, HEAD_SIZE), jnp.float32),
            pltpu.VMEM((HEAD_SIZE, AUX_LANES), jnp.float32),
        ],
        compiler_params=pltpu.CompilerParams(vmem_limit_bytes=32 * 1024 * 1024),
        name="pack_pairs",
    )(ranks.reshape(1, home_rows), lse, keys, values, output_gradient, outputs)


def pack_rows_kernel(partners, me_ref, q_hbm, do_hbm, out, sems):
    copies = []
    for n, partner in enumerate(partners):
        start = pl.multiple_of((me_ref[0] ^ partner) * WIDTH, HEAD_SIZE)
        for m, source in enumerate((q_hbm, do_hbm)):
            copies.append(
                pltpu.make_async_copy(
                    source.at[:, pl.ds(start, WIDTH)],
                    out.at[n, :, pl.ds(m * WIDTH, WIDTH)],
                    sems.at[2 * n + m],
                )
            )
    for copy in copies:
        copy.start()
    for copy in copies:
        copy.wait()


def pack_rows(partners, me, queries, output_gradient):
    home_rows = queries.shape[0]
    return pl.pallas_call(
        functools.partial(pack_rows_kernel, partners),
        out_shape=jax.ShapeDtypeStruct((len(partners), home_rows, 2 * WIDTH), queries.dtype),
        in_specs=[SMEM, HBM, HBM],
        out_specs=VMEM,
        scratch_shapes=[pltpu.SemaphoreType.DMA((2 * len(partners),))],
        name="pack_rows",
    )(me, queries, output_gradient)


def compact_kernel(arrived, out, small, counts_ref):
    home_rows = arrived.shape[1] - INFO_ROWS
    capacity = out.shape[0] - INFO_ROWS
    row = lax.broadcasted_iota(jnp.int32, (capacity, home_rows), 0)
    within = lax.broadcasted_iota(jnp.int32, (capacity, home_rows), 1)
    total = jnp.int32(0)
    picked = []
    for block in range(KEY_VALUE_HEADS):
        info = arrived[block, home_rows:, :]
        small[block] = info
        count = jnp.max(info[COUNT_ROW : COUNT_ROW + 1].astype(jnp.float32)).astype(jnp.int32)
        counts_ref[block] = count
        hit = (row == within + total) & (within < count)
        picked.append(jnp.where(hit, 1.0, 0.0).astype(jnp.bfloat16))
        total = total + count
    acc = jnp.zeros((capacity, out.shape[1]), jnp.float32)
    for block in range(KEY_VALUE_HEADS):
        acc += jnp.dot(
            picked[block], arrived[block, :home_rows, :], preferred_element_type=jnp.float32
        )
    out[:capacity, :] = acc.astype(out.dtype)
    line = lax.broadcasted_iota(jnp.int32, (INFO_ROWS, out.shape[1]), 0)
    out[capacity:, :] = (
        jnp.where(line == 0, total // 64, jnp.where(line == 1, total % 64, 0))
        .astype(jnp.float32)
        .astype(out.dtype)
    )


def compact(arrived):
    blocks, rows, columns = arrived.shape
    capacity = blocks * (rows - INFO_ROWS) // 2
    return pl.pallas_call(
        compact_kernel,
        out_shape=(
            jax.ShapeDtypeStruct((capacity + INFO_ROWS, columns), arrived.dtype),
            jax.ShapeDtypeStruct((blocks, INFO_ROWS, columns), arrived.dtype),
            jax.ShapeDtypeStruct((blocks,), jnp.int32),
        ),
        in_specs=[VMEM],
        out_specs=(VMEM, VMEM, SMEM),
        compiler_params=pltpu.CompilerParams(vmem_limit_bytes=32 * 1024 * 1024),
        name="compact",
    )(arrived)


def load_rows(me, counts_ref, arrays, q_s, do_s, sems):
    home_rows = q_s.shape[0] // KEY_VALUE_HEADS
    q_hbm, do_hbm, beside, pairs, crossed = arrays
    column = pl.multiple_of(me * WIDTH, HEAD_SIZE)
    left, right = pl.ds(0, WIDTH), pl.ds(WIDTH, WIDTH)
    sources = [
        (0, q_hbm.at[:, pl.ds(column, WIDTH)], do_hbm.at[:, pl.ds(column, WIDTH)]),
        (CORE, beside.at[0, :, left], beside.at[0, :, right]),
    ]
    for chip, pair, cross in zip(CHIPS, pairs, crossed):
        sources.append((chip, pair.at[0, :, left], pair.at[0, :, right]))
        sources.append((chip ^ CORE, cross.at[0, :, left], cross.at[0, :, right]))
    plans = []
    for n, (partner, q, do) in enumerate(sources):
        source = me ^ partner
        rows = pl.ds(pl.multiple_of(source * home_rows, 64), home_rows)
        shard = counts_ref[source & ~1] + counts_ref[source | 1]
        needed = ((source & 1) == 0) | (shard > ROW_TILE)
        plans.append(
            (
                needed,
                [
                    pltpu.make_async_copy(q, q_s.at[rows, :], sems.at[2 * n]),
                    pltpu.make_async_copy(do, do_s.at[rows, :], sems.at[2 * n + 1]),
                ],
            )
        )

    def each(act):
        for needed, copies in plans:

            @pl.when(needed)
            def _():
                for copy in copies:
                    act(copy)

    return each


def list_tiles(counts_ref, tiles, starts):
    length = jnp.int32(0)
    total = jnp.int32(0)
    for shard in range(KEY_VALUE_HEADS // 2):
        count = counts_ref[2 * shard] + counts_ref[2 * shard + 1]
        starts[shard] = total
        total = total + count
        for t in range(SHARD_TILES):
            live = count > t * ROW_TILE

            @pl.when(live)
            def _():
                tiles[length] = SHARD_TILES * shard + t

            length = length + live.astype(jnp.int32)
    return length, total


def spread_lanes(aux_s, lse_s, delta_s):
    lane = lax.broadcasted_iota(jnp.int32, (INFO_ROWS, ROW_TILE), 1)
    for shard in range(KEY_VALUE_HEADS // 2):
        low = aux_s[2 * shard].astype(jnp.float32)
        high = aux_s[2 * shard + 1].astype(jnp.float32)
        half = ROW_TILE // 2
        middle = jnp.where(
            lane < half, low[:, ROW_TILE:], pltpu.roll(high[:, :ROW_TILE], half, axis=1)
        )
        last = pltpu.roll(high, AUX_LANES - half, axis=1)[:, :ROW_TILE]
        for t, rows in enumerate((low[:, :ROW_TILE], middle, last)):
            row = SHARD_TILES * shard + t
            for h in range(GROUP):
                columns = slice(h * ROW_TILE, (h + 1) * ROW_TILE)
                lse_s[row : row + 1, columns] = rows[h : h + 1] * LOG2E
                delta_s[row : row + 1, columns] = rows[DELTA_ROW + h : DELTA_ROW + 1 + h]


def row_tile(tile, q_s, do_s, lse_s, delta_s):
    def stack(ref):
        rows = ref[pl.ds(pl.multiple_of(tile * ROW_TILE, ROW_TILE), ROW_TILE), :]
        return jnp.concatenate(
            [rows[:, h * HEAD_SIZE : (h + 1) * HEAD_SIZE] for h in range(GROUP)], axis=0
        )

    return stack(q_s), stack(do_s), lse_s[pl.ds(tile, 1), :], delta_s[pl.ds(tile, 1), :]


def tile_step(key, value, key_t, rows, position, bound, acc_k, acc_v, add_dq):
    q, do, lse, delta = rows
    scale = HEAD_SIZE ** (-0.5)
    dims = (((1,), (1,)), ((), ()))
    scores = lax.dot_general(key, q, dims, preferred_element_type=jnp.float32)
    prob = jnp.where(position <= bound, jnp.exp2(scores * (scale * LOG2E) - lse), 0.0)
    dprob = lax.dot_general(value, do, dims, preferred_element_type=jnp.float32)
    dscore = (prob * (dprob - delta)).astype(jnp.bfloat16)
    acc_v[...] += jnp.dot(prob.astype(jnp.bfloat16), do, preferred_element_type=jnp.float32)
    acc_k[...] += jnp.dot(dscore, q, preferred_element_type=jnp.float32)
    add_dq(jnp.dot(key_t, dscore, preferred_element_type=jnp.float32))


def attention_kernel(first, me_ref, counts_ref, *rest):
    aux_s, arrays, kvs, rest = rest[0], rest[1:10], rest[10:12], rest[12:]
    arrays = (*arrays[:3], arrays[3:6], arrays[6:9])
    if first:
        far, downs, dqt_out, full_ref, rest = 2, rest[:2], rest[2], rest[3], rest[4:]
    else:
        dqt_in, far, downs, rest = rest[0], 1, rest[1:2], rest[2:]
        dq_out, own_out, full_ref, rest = rest[0], rest[1], rest[2], rest[3:]
    (
        q_s, do_s, lse_s, delta_s, dqt, kv_s, acc_k, acc_v, tiles, starts, limits, sems, kv_sem,
        down_sem, dqt_sem, down_s,
    ) = rest[:16]
    if not first:
        out_sem, dq_s, own = rest[16:]
    capacity = downs[0].shape[0] - INFO_ROWS
    scale = HEAD_SIZE ** (-0.5)
    each = load_rows(me_ref[0], counts_ref, arrays, q_s, do_s, sems)
    each(lambda copy: copy.start())
    kv_copies = [
        pltpu.make_async_copy(source, kv_s.at[n], kv_sem.at[n])
        for n, source in enumerate(kvs)
    ]
    for copy in kv_copies:
        copy.start()
    length, total = list_tiles(counts_ref, tiles, starts)

    def each_tile(act):
        def step(n, carry):
            act(n, tiles[n])
            return carry

        lax.fori_loop(0, length, step, 0)

    if first:

        def zero_tile(n, tile):
            dqt[tile] = jnp.zeros(dqt.shape[1:], jnp.float32)

        each_tile(zero_tile)
    else:

        def load(n, tile):
            return pltpu.make_async_copy(dqt_in.at[tile], dqt.at[tile], dqt_sem.at[n])

        each_tile(lambda n, tile: load(n, tile).start())
        own[...] = jnp.zeros_like(own)
    spread_lanes(aux_s, lse_s, delta_s)
    for copy in kv_copies:
        copy.wait()
    most = total
    for n in range(far):
        info = kv_s[n, capacity:, :].astype(jnp.float32)
        limit = (jnp.max(info[0:1]) * 64.0 + jnp.max(info[1:2])).astype(jnp.int32)
        limits[n] = jnp.minimum(limit, capacity)
        most = jnp.maximum(most, limit)
    full_ref[0] = (most > capacity).astype(jnp.int32)
    for n in range(far):
        down_s[n, capacity:, :] = jnp.full(
            (INFO_ROWS, 2 * HEAD_SIZE), jnp.where(most > capacity, 1.0, 0.0)
        ).astype(jnp.bfloat16)
    each(lambda copy: copy.wait())
    if not first:
        each_tile(lambda n, tile: load(n, tile).wait())
    lane = lax.broadcasted_iota(jnp.int32, (1, WIDTH), 1) % ROW_TILE

    def block_step(step, carry):
        index = far - 1 - step
        limit = limits[index]

        def run(rows):
            key = kv_s[index, :rows, :HEAD_SIZE]
            value = kv_s[index, :rows, HEAD_SIZE:]
            key_t = key.T
            acc_k[:rows] = jnp.zeros((rows, HEAD_SIZE), jnp.float32)
            acc_v[:rows] = jnp.zeros((rows, HEAD_SIZE), jnp.float32)
            position = lax.broadcasted_iota(jnp.int32, (rows, 1), 0)

            def row_step(n, inner):
                tile = tiles[n]
                shard = tile // SHARD_TILES
                count = counts_ref[2 * shard] + counts_ref[2 * shard + 1]
                alive = lane < count - (tile % SHARD_TILES) * ROW_TILE
                bound = jnp.where(alive, limit - 1, -1)

                def add_dq(part):
                    dqt[tile] += part

                tile_step(
                    key, value, key_t, row_tile(tile, q_s, do_s, lse_s, delta_s), position, bound,
                    acc_k.at[pl.ds(0, rows), :], acc_v.at[pl.ds(0, rows), :], add_dq,
                )
                return inner

            lax.fori_loop(0, length, row_step, 0)
            down_s[index, :rows, :HEAD_SIZE] = (acc_k[:rows] * scale).astype(jnp.bfloat16)
            down_s[index, :rows, HEAD_SIZE:] = acc_v[:rows].astype(jnp.bfloat16)
            if rows < capacity:
                down_s[index, rows:capacity, :] = jnp.zeros(
                    (capacity - rows, 2 * HEAD_SIZE), jnp.bfloat16
                )

        below = 0
        for rows in PASS_ROWS:

            @pl.when((limit > below) & (limit <= rows))
            def _():
                run(rows)

            below = rows

        @pl.when(limit == 0)
        def _():
            down_s[index, :capacity, :] = jnp.zeros((capacity, 2 * HEAD_SIZE), jnp.bfloat16)

        return carry

    lax.fori_loop(0, far, block_step, 0)
    down_copies = [
        pltpu.make_async_copy(down_s.at[n], downs[n], down_sem.at[n]) for n in range(far)
    ]
    for copy in down_copies:
        copy.start()

    if first:

        def save(n, tile):
            return pltpu.make_async_copy(dqt.at[tile], dqt_out.at[tile], dqt_sem.at[n])

        each_tile(lambda n, tile: save(n, tile).start())
        for copy in down_copies:
            copy.wait()
        each_tile(lambda n, tile: save(n, tile).wait())
        return

    limit = jnp.minimum(total, capacity)

    def key_step(kt, carry):
        start = pl.multiple_of(kt * KEY_TILE, KEY_TILE)
        key = kv_s[1, pl.ds(start, KEY_TILE), :HEAD_SIZE]
        value = kv_s[1, pl.ds(start, KEY_TILE), HEAD_SIZE:]
        key_t = key.T
        own_k = acc_k.at[pl.ds(0, KEY_TILE), :]
        own_v = acc_v.at[pl.ds(0, KEY_TILE), :]
        own_k[...] = jnp.zeros_like(own_k)
        own_v[...] = jnp.zeros_like(own_v)
        position = start + lax.broadcasted_iota(jnp.int32, (KEY_TILE, 1), 0)

        def row_step(n, inner):
            tile = tiles[n]
            shard = tile // SHARD_TILES
            offset = (tile % SHARD_TILES) * ROW_TILE
            count = counts_ref[2 * shard] + counts_ref[2 * shard + 1]
            first = starts[shard] + offset

            @pl.when(first + ROW_TILE > start)
            def _():
                bound = jnp.where(lane < count - offset, first + lane, -1)

                def add_dq(part):
                    dqt[tile] += part

                tile_step(
                    key, value, key_t, row_tile(tile, q_s, do_s, lse_s, delta_s), position, bound,
                    own_k, own_v, add_dq,
                )

            return inner

        lax.fori_loop(0, length, row_step, 0)
        own[pl.ds(start, KEY_TILE), :HEAD_SIZE] = own_k[...] * scale
        own[pl.ds(start, KEY_TILE), HEAD_SIZE:] = own_v[...]
        return carry

    lax.fori_loop(0, (limit + KEY_TILE - 1) // KEY_TILE, key_step, 0)
    own_copy = pltpu.make_async_copy(own, own_out, down_sem.at[1])
    own_copy.start()

    half = ROW_TILE // 2
    copies = []
    for block in range(KEY_VALUE_HEADS):
        shard = block // 2
        count = counts_ref[2 * shard] + counts_ref[2 * shard + 1]
        if block % 2 == 0:
            pieces = ((0, ROW_TILE, 0, 0), (ROW_TILE, half, 1, 0))
        else:
            pieces = ((0, half, 1, half), (half, ROW_TILE, 2, 0))
        for offset, size, t, first in pieces:
            live = count > t * ROW_TILE
            rows = slice(offset, offset + size)

            @pl.when(live)
            def _():
                for h in range(GROUP):
                    columns = slice(h * HEAD_SIZE, (h + 1) * HEAD_SIZE)
                    part = (dqt[SHARD_TILES * shard + t, :, columns] * scale).T
                    dq_s[block, rows, columns] = part[first : first + size].astype(jnp.bfloat16)

            @pl.when(jnp.logical_not(live))
            def _():
                dq_s[block, rows, :] = jnp.zeros((size, WIDTH), jnp.bfloat16)

        copy = pltpu.make_async_copy(dq_s.at[block], dq_out.at[block], out_sem.at[block])
        copy.start()
        copies.append(copy)
    for copy in (*copies, *down_copies, own_copy):
        copy.wait()


def row_scratch(plane_rows):
    bf16, f32 = jnp.bfloat16, jnp.float32
    tile_count = plane_rows // ROW_TILE
    return [
        pltpu.VMEM((plane_rows, WIDTH), bf16),
        pltpu.VMEM((plane_rows, WIDTH), bf16),
        pltpu.VMEM((tile_count, WIDTH), f32),
        pltpu.VMEM((tile_count, WIDTH), f32),
        pltpu.VMEM((tile_count, HEAD_SIZE, WIDTH), f32),
    ]


def attention(first, me, counts, small, arrays, kvs, *before):
    bf16, f32 = jnp.bfloat16, jnp.float32
    blocks = KEY_VALUE_HEADS
    rows = kvs[0].shape[0]
    capacity = rows - INFO_ROWS
    columns = 2 * HEAD_SIZE
    plane_rows = 2 * capacity
    tile_count = plane_rows // ROW_TILE
    dq = (blocks, plane_rows // blocks, WIDTH)
    dqt = (tile_count, HEAD_SIZE, WIDTH)
    down = jax.ShapeDtypeStruct((rows, columns), bf16)
    flag = jax.ShapeDtypeStruct((1,), jnp.int32)
    if first:
        outs = (down, down, jax.ShapeDtypeStruct(dqt, f32), flag)
        more = []
    else:
        own = jax.ShapeDtypeStruct((capacity, columns), f32)
        outs = (down, jax.ShapeDtypeStruct(dq, bf16), own, flag)
        more = [
            pltpu.SemaphoreType.DMA((blocks,)),
            pltpu.VMEM(dq, bf16),
            pltpu.VMEM((capacity, columns), f32),
        ]
    return pl.pallas_call(
        functools.partial(attention_kernel, first),
        out_shape=outs,
        in_specs=[SMEM] * 2 + [VMEM] + [HBM] * (11 + len(before)),
        out_specs=[HBM] * 3 + [SMEM],
        scratch_shapes=[
            pltpu.VMEM((plane_rows, WIDTH), bf16),
            pltpu.VMEM((plane_rows, WIDTH), bf16),
            pltpu.VMEM((tile_count, WIDTH), f32),
            pltpu.VMEM((tile_count, WIDTH), f32),
            pltpu.VMEM(dqt, f32),
            pltpu.VMEM((2, rows, columns), bf16),
            pltpu.VMEM((capacity, HEAD_SIZE), f32),
            pltpu.VMEM((capacity, HEAD_SIZE), f32),
            pltpu.SMEM((tile_count + 1,), jnp.int32),
            pltpu.SMEM((blocks,), jnp.int32),
            pltpu.SMEM((2,), jnp.int32),
            pltpu.SemaphoreType.DMA((2 * blocks,)),
            pltpu.SemaphoreType.DMA((2,)),
            pltpu.SemaphoreType.DMA((2,)),
            pltpu.SemaphoreType.DMA((tile_count,)),
            pltpu.VMEM((2, rows, columns), bf16),
            *more,
        ],
        compiler_params=pltpu.CompilerParams(vmem_limit_bytes=48 * 1024 * 1024),
        cost_estimate=pl.CostEstimate(
            flops=5_000_000_000, bytes_accessed=12_000_000, transcendentals=4_000_000
        ),
        name="attention",
    )(me, counts, small, *arrays, *kvs, *before)


def unpack_rows_kernel(parts, out):
    for g in range(KEY_VALUE_HEADS):
        out[:, g * WIDTH : (g + 1) * WIDTH] = parts[g]


def unpack_rows(parts):
    return pl.pallas_call(
        unpack_rows_kernel,
        out_shape=jax.ShapeDtypeStruct((parts.shape[1], KEY_VALUE_HEADS * WIDTH), parts.dtype),
        in_specs=[VMEM],
        out_specs=VMEM,
        name="unpack_rows",
    )(parts)


def combine_kernel(counts_ref, own, *rest):
    backs, out = rest[:3], rest[3]
    home_rows = out.shape[1]
    capacity = own.shape[0]
    total = own[...]
    for back in backs:
        total += back[:capacity, :].astype(jnp.float32)
    total = total.astype(jnp.bfloat16)
    within = lax.broadcasted_iota(jnp.int32, (home_rows, capacity), 0)
    place = lax.broadcasted_iota(jnp.int32, (home_rows, capacity), 1)
    start = jnp.int32(0)
    for block in range(KEY_VALUE_HEADS):
        count = counts_ref[block]
        hit = (place == within + start) & (within < count)
        out[block] = jnp.dot(
            jnp.where(hit, 1.0, 0.0).astype(jnp.bfloat16),
            total,
            preferred_element_type=jnp.float32,
        ).astype(jnp.bfloat16)
        start = start + count


def combine(counts, own, backs, home_rows):
    blocks = KEY_VALUE_HEADS
    return pl.pallas_call(
        combine_kernel,
        out_shape=jax.ShapeDtypeStruct((blocks, home_rows, own.shape[1]), jnp.bfloat16),
        in_specs=[SMEM] + [VMEM] * 4,
        out_specs=VMEM,
        compiler_params=pltpu.CompilerParams(vmem_limit_bytes=32 * 1024 * 1024),
        name="combine",
    )(counts, own, *backs)


def plane_device(queries, keys, values, outputs, output_gradient, lse, ranks):
    planes = lax.axis_size("outer")
    plane = ("inner", "head")
    blocks = KEY_VALUE_HEADS
    home_rows = queries.shape[0]
    plane_rows = blocks * home_rows
    capacity = plane_rows // 2
    surviving_tokens = BALANCED_TOKENS * planes * lax.axis_size("inner")
    bf16, f32 = jnp.bfloat16, jnp.float32
    me = lax.axis_index(plane).reshape(1).astype(jnp.int32)

    def swap(array, k):
        return lax.ppermute(array, plane, [(i, i ^ k) for i in range(blocks)])

    sent = pack_pairs(
        surviving_tokens, ranks, lse, keys, values, output_gradient, outputs
    )
    me, sent = lax.optimization_barrier((me, sent))
    arrived = lax.all_to_all(sent, plane, split_axis=0, concat_axis=0, tiled=True)
    packed = [pack_rows((chip, chip ^ CORE), me, queries, output_gradient) for chip in CHIPS]
    me, packed[-1] = lax.optimization_barrier((me, packed[-1]))
    pairs = [swap(rows, chip) for rows, chip in zip(packed, CHIPS)]
    beside = swap(pack_rows((CORE,), me, queries, output_gradient), CORE)
    arrived, beside = lax.optimization_barrier((arrived, beside))
    mine, small, counts = compact(arrived)
    up = [lax.ppermute(mine, "outer", [(i, i + 1) for i in range(planes - 1)])]
    last = lax.ppermute(mine, "outer", [(0, planes - 1)])
    up.append(lax.ppermute(up[0], "outer", [(i, i + 1) for i in range(1, planes - 1)]))
    up.append(last)
    up[1], up[2], *pairs = lax.optimization_barrier((up[1], up[2], *pairs))
    crossed = [swap(pair[1:], CORE) for pair in pairs]
    arrays = [queries, output_gradient, beside, *pairs, *crossed]

    def lower(rows, k):
        return lax.ppermute(rows, "outer", [(i + k, i) for i in range(planes - k)])

    down2, down3, dqt, full1 = attention(True, me, counts, small, arrays, [up[1], up[2]])
    back2 = lower(down2, 2)
    down1, dq, own, full2 = attention(False, me, counts, small, arrays, [up[0], mine], dqt)
    dq, back2 = lax.optimization_barrier((dq, back2))
    backs = [lower(down3, 3), back2, lower(down1, 1)]
    dq = lax.all_to_all(dq, plane, split_axis=0, concat_axis=0, tiled=True)
    dq, own = lax.optimization_barrier((dq, own))
    dq_home = unpack_rows(dq)
    kv_home = lax.all_to_all(
        combine(counts, own, backs, home_rows), plane, split_axis=0, concat_axis=0, tiled=True
    )
    full = (full1[0] + full2[0]) > 0
    for back in backs:
        full = full | (back[capacity, 0] > 0)
    dk = kv_home[:, :, :HEAD_SIZE].transpose(1, 0, 2).reshape(home_rows, blocks * HEAD_SIZE)
    dv = kv_home[:, :, HEAD_SIZE:].transpose(1, 0, 2).reshape(home_rows, blocks * HEAD_SIZE)
    return (dq_home, dk, dv), full


def solution(mesh):
    spec = P(("seq", "head"), None)
    heads = mesh.shape["head"]
    inner = max(KEY_VALUE_HEADS // heads, 1)
    planes = mesh.shape["seq"] // inner
    if planes != 4 or inner * heads != KEY_VALUE_HEADS:
        return jax.shard_map(
            per_device,
            mesh=mesh,
            in_specs=(spec,) * 6 + (P(("seq", "head")),),
            out_specs=(spec,) * 3,
            check_vma=False,
        )
    axes = ("outer", "inner", "head")

    def device(*blocks):
        fast, full = plane_device(*blocks)
        return lax.cond(full, lambda: per_device(*blocks, seq=("outer", "inner")), lambda: fast)

    return jax.shard_map(
        device,
        mesh=Mesh(mesh.devices.reshape(planes, inner, heads), axes),
        in_specs=(P(axes, None),) * 6 + (P(axes),),
        out_specs=(P(axes, None),) * 3,
        check_vma=False,
    )
```

```python
import functools

import jax
import jax.numpy as jnp
from jax import lax
from jax.experimental import pallas as pl
from jax.experimental.pallas import tpu as pltpu
from jax.sharding import Mesh
from jax.sharding import PartitionSpec as P

QUERY_HEADS = 40
KEY_VALUE_HEADS = 8
HEAD_SIZE = 128
BALANCED_TOKENS = 128


block_keys = 512


def per_device(queries, keys, values, outputs, output_gradient, lse, ranks, seq="seq"):
    sequence_count = lax.axis_size(seq)
    head_total = lax.axis_size("head")
    home_rows = queries.shape[0]
    capacity = home_rows * head_total
    slots = capacity // sequence_count
    surviving_tokens = BALANCED_TOKENS * sequence_count
    group_size = QUERY_HEADS // KEY_VALUE_HEADS
    local_key_value = KEY_VALUE_HEADS // head_total
    scale = HEAD_SIZE ** (-0.5)

    def split_heads(array):
        return array.reshape(home_rows, head_total, array.shape[1] // head_total)

    moved = (
        lax.all_to_all(split_heads(queries), "head", split_axis=1, concat_axis=0, tiled=True),
        lax.all_to_all(split_heads(keys), "head", split_axis=1, concat_axis=0, tiled=True),
        lax.all_to_all(split_heads(values), "head", split_axis=1, concat_axis=0, tiled=True),
        lax.all_to_all(
            split_heads(output_gradient), "head", split_axis=1, concat_axis=0, tiled=True
        ),
        lax.all_to_all(split_heads(lse), "head", split_axis=1, concat_axis=0, tiled=True),
        lax.all_to_all(split_heads(outputs), "head", split_axis=1, concat_axis=0, tiled=True),
    )
    shard_rank_list = lax.all_gather(ranks, "head", axis=0, tiled=True)
    first_rank = shard_rank_list[0]
    living_count = jnp.sum((shard_rank_list < surviving_tokens).astype(jnp.int32))
    table = lax.all_gather(
        jnp.stack([first_rank, living_count])[None, :], seq, axis=0, tiled=True
    )

    def to_pairs(array):
        flat = array.reshape(slots, sequence_count, array.shape[-1])
        return jnp.roll(flat, first_rank, axis=1)

    arrived = (
        lax.all_to_all(to_pairs(moved[0]), seq, split_axis=1, concat_axis=1, tiled=True),
        lax.all_to_all(to_pairs(moved[1]), seq, split_axis=1, concat_axis=1, tiled=True),
        lax.all_to_all(to_pairs(moved[2]), seq, split_axis=1, concat_axis=1, tiled=True),
        lax.all_to_all(to_pairs(moved[3]), seq, split_axis=1, concat_axis=1, tiled=True),
        lax.all_to_all(to_pairs(moved[4]), seq, split_axis=1, concat_axis=1, tiled=True),
        lax.all_to_all(to_pairs(moved[5]), seq, split_axis=1, concat_axis=1, tiled=True),
    )
    my_index = lax.axis_index(seq)
    starts = table[:, 0]
    count_table = table[:, 1]
    offset = (my_index - starts) % sequence_count
    within = jnp.arange(slots, dtype=jnp.int32)[:, None] * sequence_count + offset[None, :]
    alive = within < count_table[None, :]
    target_rank = jnp.where(
        alive, (starts[None, :] + within) // sequence_count, BALANCED_TOKENS
    ).reshape(-1)

    def place(array):
        width = array.shape[-1]
        return (
            jnp.zeros((BALANCED_TOKENS, width), array.dtype)
            .at[target_rank]
            .set(array.reshape(slots * sequence_count, width), mode="drop")
        )

    query_row_block = place(arrived[0]).reshape(
        BALANCED_TOKENS, local_key_value, group_size, HEAD_SIZE
    )
    key_row_block = place(arrived[1]).reshape(BALANCED_TOKENS, local_key_value, HEAD_SIZE)
    value_row_block = place(arrived[2]).reshape(BALANCED_TOKENS, local_key_value, HEAD_SIZE)
    grad_rows = place(arrived[3]).reshape(BALANCED_TOKENS, local_key_value, group_size, HEAD_SIZE)
    lse_rows = (
        place(arrived[4]).astype(jnp.float32).reshape(BALANCED_TOKENS, local_key_value, group_size)
    )
    out_rows = (
        place(arrived[5])
        .astype(jnp.float32)
        .reshape(BALANCED_TOKENS, local_key_value, group_size, HEAD_SIZE)
    )
    delta_rows = (
        jnp.sum(grad_rows.astype(jnp.float32) * out_rows, axis=-1)
        .astype(jnp.bfloat16)
        .astype(jnp.float32)
    )
    gathered = (
        lax.all_gather(key_row_block, seq, axis=0, tiled=True),
        lax.all_gather(value_row_block, seq, axis=0, tiled=True),
    )
    all_keys = gathered[0].reshape(sequence_count, BALANCED_TOKENS, local_key_value, HEAD_SIZE)
    all_values = gathered[1].reshape(sequence_count, BALANCED_TOKENS, local_key_value, HEAD_SIZE)
    rows_per = block_keys // sequence_count
    inner = 1
    outer = BALANCED_TOKENS // rows_per // inner
    query_rank = jnp.arange(BALANCED_TOKENS, dtype=jnp.int32) * sequence_count + my_index
    lse_t = lse_rows.transpose(1, 2, 0)
    delta_t = delta_rows.transpose(1, 2, 0)
    position = jnp.arange(sequence_count * rows_per, dtype=jnp.int32)

    def key_step(query_acc, row_start):
        key_blk = lax.dynamic_slice_in_dim(all_keys, row_start, rows_per, 1).reshape(
            sequence_count * rows_per, local_key_value, HEAD_SIZE
        )
        value_blk = lax.dynamic_slice_in_dim(all_values, row_start, rows_per, 1).reshape(
            sequence_count * rows_per, local_key_value, HEAD_SIZE
        )
        key_owner_rank = (row_start + position % rows_per) * sequence_count + position // rows_per
        mask = key_owner_rank[None, None, None, :] <= query_rank[None, None, :, None]
        scores = (
            jnp.einsum(
                "rgmc,kgc->gmrk", query_row_block, key_blk, preferred_element_type=jnp.float32
            )
            * scale
        )
        probs = jnp.where(mask, jnp.exp(scores - lse_t[..., None]), 0.0)
        dprob = jnp.einsum(
            "rgmc,kgc->gmrk", grad_rows, value_blk, preferred_element_type=jnp.float32
        )
        dscore = probs * (dprob - delta_t[..., None])
        probs_low = probs.astype(jnp.bfloat16)
        dscore_low = dscore.astype(jnp.bfloat16)
        query_acc = query_acc + scale * jnp.einsum(
            "gmrk,kgc->rgmc", dscore_low, key_blk, preferred_element_type=jnp.float32
        )
        key_part = scale * jnp.einsum(
            "gmrk,rgmc->kgc", dscore_low, query_row_block, preferred_element_type=jnp.float32
        )
        value_part = jnp.einsum(
            "gmrk,rgmc->kgc", probs_low, grad_rows, preferred_element_type=jnp.float32
        )
        return (
            query_acc,
            key_part.reshape(sequence_count, rows_per, local_key_value * HEAD_SIZE),
            value_part.reshape(sequence_count, rows_per, local_key_value * HEAD_SIZE),
        )

    def outer_step(query_acc, outer_index):

        def inner_step(query_inner, inner_index):
            row_start = (outer_index * inner + inner_index) * rows_per
            query_new, key_part, value_part = key_step(query_inner, row_start)
            return (query_new, (key_part, value_part))

        query_acc, (key_parts, value_parts) = lax.scan(
            inner_step, query_acc, jnp.arange(inner, dtype=jnp.int32)
        )
        key_parts = key_parts.transpose(1, 0, 2, 3).reshape(
            sequence_count, inner * rows_per, local_key_value * HEAD_SIZE
        )
        value_parts = value_parts.transpose(1, 0, 2, 3).reshape(
            sequence_count, inner * rows_per, local_key_value * HEAD_SIZE
        )
        received = (
            lax.all_to_all(key_parts, seq, split_axis=0, concat_axis=0, tiled=True),
            lax.all_to_all(value_parts, seq, split_axis=0, concat_axis=0, tiled=True),
        )
        return (query_acc, (jnp.sum(received[0], axis=0), jnp.sum(received[1], axis=0)))

    start_acc = jnp.zeros((BALANCED_TOKENS, local_key_value, group_size, HEAD_SIZE), jnp.float32)
    query_acc, (key_sums, value_sums) = lax.scan(
        outer_step, start_acc, jnp.arange(outer, dtype=jnp.int32)
    )
    query_done = query_acc.reshape(
        BALANCED_TOKENS, local_key_value * group_size * HEAD_SIZE
    ).astype(jnp.bfloat16)
    key_done = key_sums.reshape(BALANCED_TOKENS, local_key_value * HEAD_SIZE).astype(jnp.bfloat16)
    value_done = value_sums.reshape(BALANCED_TOKENS, local_key_value * HEAD_SIZE).astype(
        jnp.bfloat16
    )
    safe_rows = jnp.minimum(target_rank, BALANCED_TOKENS - 1)
    alive_flat = alive.reshape(-1)

    def collect(array):
        picked = jnp.where(alive_flat[:, None], array[safe_rows], jnp.zeros((), array.dtype))
        return picked.reshape(slots, sequence_count, array.shape[-1])

    returned = (
        lax.all_to_all(collect(query_done), seq, split_axis=1, concat_axis=1, tiled=True),
        lax.all_to_all(collect(key_done), seq, split_axis=1, concat_axis=1, tiled=True),
        lax.all_to_all(collect(value_done), seq, split_axis=1, concat_axis=1, tiled=True),
    )

    def to_home(array):
        unrolled = jnp.roll(array, -first_rank, axis=1)
        return unrolled.reshape(capacity, 1, array.shape[-1])

    homed = (
        lax.all_to_all(to_home(returned[0]), "head", split_axis=0, concat_axis=1, tiled=True),
        lax.all_to_all(to_home(returned[1]), "head", split_axis=0, concat_axis=1, tiled=True),
        lax.all_to_all(to_home(returned[2]), "head", split_axis=0, concat_axis=1, tiled=True),
    )
    query_grads = homed[0].reshape(home_rows, head_total * homed[0].shape[-1])
    key_gradient_output = homed[1].reshape(home_rows, head_total * homed[1].shape[-1])
    value_gradient = homed[2].reshape(home_rows, head_total * homed[2].shape[-1])
    return (query_grads, key_gradient_output, value_gradient)

LOG2E = 1.4426950408889634
KEY_TILE = 256
ROW_TILE = 128
INFO_ROWS = 16
AUX_LANES = 256
DELTA_ROW = 8
SMEM = pl.BlockSpec(memory_space=pltpu.SMEM)
VMEM = pl.BlockSpec(memory_space=pltpu.VMEM)
HBM = pl.BlockSpec(memory_space=pltpu.HBM)
GROUP = QUERY_HEADS // KEY_VALUE_HEADS
WIDTH = GROUP * HEAD_SIZE
CHIPS = (5, 4, 1)
CORE = 2
SHARD_TILES = 3
PASS_ROWS = (256, 512, 768)


def pack_pairs_kernel(limit, ranks_ref, k_ref, v_ref, out_ref):
    home_rows = k_ref.shape[0]
    live = jnp.where(ranks_ref[...] < limit, 1.0, 0.0)
    info = jnp.broadcast_to(
        jnp.sum(live, axis=1, keepdims=True), (INFO_ROWS, 2 * HEAD_SIZE)
    ).astype(out_ref.dtype)
    for g in range(KEY_VALUE_HEADS):
        head = slice(g * HEAD_SIZE, (g + 1) * HEAD_SIZE)
        out_ref[g, :home_rows, :HEAD_SIZE] = k_ref[:, head]
        out_ref[g, :home_rows, HEAD_SIZE:] = v_ref[:, head]
        out_ref[g, home_rows:, :] = info


def pack_pairs(limit, ranks, keys, values):
    home_rows = keys.shape[0]
    return pl.pallas_call(
        functools.partial(pack_pairs_kernel, limit),
        out_shape=jax.ShapeDtypeStruct(
            (KEY_VALUE_HEADS, home_rows + INFO_ROWS, 2 * HEAD_SIZE), keys.dtype
        ),
        in_specs=[VMEM] * 3,
        out_specs=VMEM,
        name="pack_pairs",
    )(ranks.reshape(1, home_rows), keys, values)


def pack_rows_kernel(me_ref, lse_ref, q_ref, do_ref, o_ref, *rest):
    outs, small_ref, columns, lanes = rest[:4], rest[4], rest[5], rest[6]
    home_rows = q_ref.shape[0]
    me = me_ref[0]
    columns[...] = jnp.zeros_like(columns)
    for h in range(QUERY_HEADS):
        head = slice(h * HEAD_SIZE, (h + 1) * HEAD_SIZE)
        product = do_ref[:, head].astype(jnp.float32) * o_ref[:, head].astype(jnp.float32)
        column = INFO_ROWS * (h // GROUP) + DELTA_ROW + h % GROUP
        columns[:, column : column + 1] = jnp.sum(product, axis=1, keepdims=True)
    lanes[...] = jnp.zeros_like(lanes)
    lanes[:, :home_rows] = columns[...].T
    lse = lse_ref[...].astype(jnp.float32)
    for g in range(KEY_VALUE_HEADS):
        lanes[INFO_ROWS * g : INFO_ROWS * g + GROUP, :home_rows] = lse[g * GROUP : (g + 1) * GROUP]

    def small(to):
        rows = pl.ds(pl.multiple_of(to * INFO_ROWS, INFO_ROWS), INFO_ROWS)
        return lanes[rows, :].astype(jnp.bfloat16)

    small_ref[...] = small(me)
    for out, partners in zip(outs, [(chip, chip ^ CORE) for chip in CHIPS] + [(CORE,)]):
        for n, partner in enumerate(partners):
            to = me ^ partner
            start = pl.multiple_of(to * WIDTH, HEAD_SIZE)
            out[n, :home_rows, :WIDTH] = q_ref[:, pl.ds(start, WIDTH)]
            out[n, :home_rows, WIDTH:] = do_ref[:, pl.ds(start, WIDTH)]
            out[n, home_rows:, :AUX_LANES] = small(to)


def pack_rows(me, lse, queries, output_gradient, outputs):
    home_rows = queries.shape[0]
    bf16, f32 = jnp.bfloat16, jnp.float32
    pair = jax.ShapeDtypeStruct((2, home_rows + INFO_ROWS, 2 * WIDTH), bf16)
    beside = jax.ShapeDtypeStruct((1, home_rows + INFO_ROWS, 2 * WIDTH), bf16)
    return pl.pallas_call(
        pack_rows_kernel,
        out_shape=(pair, pair, pair, beside, jax.ShapeDtypeStruct((INFO_ROWS, AUX_LANES), bf16)),
        in_specs=[SMEM] + [VMEM] * 4,
        out_specs=[VMEM] * 5,
        scratch_shapes=[
            pltpu.VMEM((home_rows, HEAD_SIZE), f32),
            pltpu.VMEM((HEAD_SIZE, AUX_LANES), f32),
        ],
        compiler_params=pltpu.CompilerParams(vmem_limit_bytes=32 * 1024 * 1024),
        name="pack_rows",
    )(me, lse.T, queries, output_gradient, outputs)


def compact_kernel(arrived, out, counts_ref):
    home_rows = arrived.shape[1] - INFO_ROWS
    capacity = out.shape[0] - INFO_ROWS
    row = lax.broadcasted_iota(jnp.int32, (capacity, home_rows), 0)
    within = lax.broadcasted_iota(jnp.int32, (capacity, home_rows), 1)
    total = jnp.int32(0)
    picked = []
    for block in range(KEY_VALUE_HEADS):
        info = arrived[block, home_rows:, :].astype(jnp.float32)
        count = jnp.max(info[0:8]).astype(jnp.int32)
        counts_ref[block] = count
        hit = (row == within + total) & (within < count)
        picked.append(jnp.where(hit, 1.0, 0.0).astype(jnp.bfloat16))
        total = total + count
    acc = jnp.zeros((capacity, out.shape[1]), jnp.float32)
    for block in range(KEY_VALUE_HEADS):
        acc += jnp.dot(
            picked[block], arrived[block, :home_rows, :], preferred_element_type=jnp.float32
        )
    out[:capacity, :] = acc.astype(out.dtype)
    line = lax.broadcasted_iota(jnp.int32, (INFO_ROWS, out.shape[1]), 0)
    out[capacity:, :] = (
        jnp.where(line == 0, total // 64, jnp.where(line == 1, total % 64, 0))
        .astype(jnp.float32)
        .astype(out.dtype)
    )


def compact(arrived):
    blocks, rows, columns = arrived.shape
    capacity = blocks * (rows - INFO_ROWS) // 2
    return pl.pallas_call(
        compact_kernel,
        out_shape=(
            jax.ShapeDtypeStruct((capacity + INFO_ROWS, columns), arrived.dtype),
            jax.ShapeDtypeStruct((blocks,), jnp.int32),
        ),
        in_specs=[VMEM],
        out_specs=(VMEM, SMEM),
        compiler_params=pltpu.CompilerParams(vmem_limit_bytes=32 * 1024 * 1024),
        name="compact",
    )(arrived)


def load_rows(me, counts_ref, arrays, q_s, do_s, aux_s, sems):
    home_rows = q_s.shape[0] // KEY_VALUE_HEADS
    q_hbm, do_hbm, small, beside, pairs, crossed = arrays
    column = pl.ds(pl.multiple_of(me * WIDTH, HEAD_SIZE), WIDTH)

    def parts(partner, payload):
        rows = pl.ds(0, home_rows)
        return (
            partner,
            payload.at[0, rows, pl.ds(0, WIDTH)],
            payload.at[0, rows, pl.ds(WIDTH, WIDTH)],
            payload.at[0, pl.ds(home_rows, INFO_ROWS), pl.ds(0, AUX_LANES)],
        )

    sources = [(0, q_hbm.at[:, column], do_hbm.at[:, column], small), parts(CORE, beside)]
    for chip, pair, cross in zip(CHIPS, pairs, crossed):
        sources += [parts(chip, pair), parts(chip ^ CORE, cross)]
    plans = []
    for n, (partner, q, do, lanes) in enumerate(sources):
        source = me ^ partner
        rows = pl.ds(pl.multiple_of(source * home_rows, 64), home_rows)
        shard = counts_ref[source & ~1] + counts_ref[source | 1]
        needed = ((source & 1) == 0) | (shard > ROW_TILE)
        plans.append(
            (
                needed,
                [
                    pltpu.make_async_copy(q, q_s.at[rows, :], sems.at[3 * n]),
                    pltpu.make_async_copy(do, do_s.at[rows, :], sems.at[3 * n + 1]),
                    pltpu.make_async_copy(lanes, aux_s.at[source], sems.at[3 * n + 2]),
                ],
            )
        )

    def each(act):
        for needed, copies in plans:

            @pl.when(needed)
            def _():
                for copy in copies:
                    act(copy)

    return each


def list_tiles(counts_ref, tiles, starts):
    length = jnp.int32(0)
    total = jnp.int32(0)
    for shard in range(KEY_VALUE_HEADS // 2):
        count = counts_ref[2 * shard] + counts_ref[2 * shard + 1]
        starts[shard] = total
        total = total + count
        for t in range(SHARD_TILES):
            live = count > t * ROW_TILE

            @pl.when(live)
            def _():
                tiles[length] = SHARD_TILES * shard + t

            length = length + live.astype(jnp.int32)
    return length, total


def spread_lanes(aux_s, lse_s, delta_s):
    lane = lax.broadcasted_iota(jnp.int32, (INFO_ROWS, ROW_TILE), 1)
    for shard in range(KEY_VALUE_HEADS // 2):
        low = aux_s[2 * shard].astype(jnp.float32)
        high = aux_s[2 * shard + 1].astype(jnp.float32)
        half = ROW_TILE // 2
        middle = jnp.where(
            lane < half, low[:, ROW_TILE:], pltpu.roll(high[:, :ROW_TILE], half, axis=1)
        )
        last = pltpu.roll(high, AUX_LANES - half, axis=1)[:, :ROW_TILE]
        for t, rows in enumerate((low[:, :ROW_TILE], middle, last)):
            row = SHARD_TILES * shard + t
            for h in range(GROUP):
                columns = slice(h * ROW_TILE, (h + 1) * ROW_TILE)
                lse_s[row : row + 1, columns] = rows[h : h + 1] * LOG2E
                delta_s[row : row + 1, columns] = rows[DELTA_ROW + h : DELTA_ROW + 1 + h]


def row_tile(tile, q_s, do_s, lse_s, delta_s):
    def stack(ref):
        rows = ref[pl.ds(pl.multiple_of(tile * ROW_TILE, ROW_TILE), ROW_TILE), :]
        return jnp.concatenate(
            [rows[:, h * HEAD_SIZE : (h + 1) * HEAD_SIZE] for h in range(GROUP)], axis=0
        )

    return stack(q_s), stack(do_s), lse_s[pl.ds(tile, 1), :], delta_s[pl.ds(tile, 1), :]


def tile_step(key, value, key_t, rows, position, bound, acc_k, acc_v, add_dq):
    q, do, lse, delta = rows
    scale = HEAD_SIZE ** (-0.5)
    dims = (((1,), (1,)), ((), ()))
    scores = lax.dot_general(key, q, dims, preferred_element_type=jnp.float32)
    prob = jnp.where(position <= bound, jnp.exp2(scores * (scale * LOG2E) - lse), 0.0)
    dprob = lax.dot_general(value, do, dims, preferred_element_type=jnp.float32)
    dscore = (prob * (dprob - delta)).astype(jnp.bfloat16)
    acc_v[...] += jnp.dot(prob.astype(jnp.bfloat16), do, preferred_element_type=jnp.float32)
    acc_k[...] += jnp.dot(dscore, q, preferred_element_type=jnp.float32)
    add_dq(jnp.dot(key_t, dscore, preferred_element_type=jnp.float32))


def attention_kernel(first, me_ref, counts_ref, *rest):
    arrays, kvs, rest = rest[:10], rest[10:12], rest[12:]
    arrays = (*arrays[:4], arrays[4:7], arrays[7:10])
    if first:
        far, downs, dqt_out, full_ref, rest = 2, rest[:2], rest[2], rest[3], rest[4:]
    else:
        dqt_in, far, downs, rest = rest[0], 1, rest[1:2], rest[2:]
        dq_out, own_out, full_ref, rest = rest[0], rest[1], rest[2], rest[3:]
    (
        q_s, do_s, aux_s, lse_s, delta_s, dqt, kv_s, acc_k, acc_v, tiles, starts, limits, sems,
        kv_sem, down_sem, dqt_sem, down_s,
    ) = rest[:17]
    if not first:
        out_sem, dq_s, own, before = rest[17:]
    capacity = downs[0].shape[0] - INFO_ROWS
    scale = HEAD_SIZE ** (-0.5)
    each = load_rows(me_ref[0], counts_ref, arrays, q_s, do_s, aux_s, sems)
    each(lambda copy: copy.start())
    kv_copies = [
        pltpu.make_async_copy(source, kv_s.at[n], kv_sem.at[n])
        for n, source in enumerate(kvs)
    ]
    for copy in kv_copies:
        copy.start()
    length, total = list_tiles(counts_ref, tiles, starts)

    def each_tile(act):
        def step(n, carry):
            act(n, tiles[n])
            return carry

        lax.fori_loop(0, length, step, 0)

    def zero_tile(n, tile):
        dqt[tile] = jnp.zeros(dqt.shape[1:], jnp.float32)

    each_tile(zero_tile)
    if not first:

        def load(n, tile):
            return pltpu.make_async_copy(dqt_in.at[tile], before.at[tile], dqt_sem.at[n])

        each_tile(lambda n, tile: load(n, tile).start())
        own[...] = jnp.zeros_like(own)
    for copy in kv_copies:
        copy.wait()
    most = total
    for n in range(far):
        info = kv_s[n, capacity:, :].astype(jnp.float32)
        limit = (jnp.max(info[0:1]) * 64.0 + jnp.max(info[1:2])).astype(jnp.int32)
        limits[n] = jnp.minimum(limit, capacity)
        most = jnp.maximum(most, limit)
    full_ref[0] = (most > capacity).astype(jnp.int32)
    for n in range(far):
        down_s[n, capacity:, :] = jnp.full(
            (INFO_ROWS, 2 * HEAD_SIZE), jnp.where(most > capacity, 1.0, 0.0)
        ).astype(jnp.bfloat16)
    each(lambda copy: copy.wait())
    spread_lanes(aux_s, lse_s, delta_s)
    lane = lax.broadcasted_iota(jnp.int32, (1, WIDTH), 1) % ROW_TILE

    def block_step(step, carry):
        index = far - 1 - step
        limit = limits[index]

        def run(rows):
            key = kv_s[index, :rows, :HEAD_SIZE]
            value = kv_s[index, :rows, HEAD_SIZE:]
            key_t = key.T
            acc_k[:rows] = jnp.zeros((rows, HEAD_SIZE), jnp.float32)
            acc_v[:rows] = jnp.zeros((rows, HEAD_SIZE), jnp.float32)
            position = lax.broadcasted_iota(jnp.int32, (rows, 1), 0)

            def row_step(n, inner):
                tile = tiles[n]
                shard = tile // SHARD_TILES
                count = counts_ref[2 * shard] + counts_ref[2 * shard + 1]
                alive = lane < count - (tile % SHARD_TILES) * ROW_TILE
                bound = jnp.where(alive, limit - 1, -1)

                def add_dq(part):
                    dqt[tile] += part

                tile_step(
                    key, value, key_t, row_tile(tile, q_s, do_s, lse_s, delta_s), position, bound,
                    acc_k.at[pl.ds(0, rows), :], acc_v.at[pl.ds(0, rows), :], add_dq,
                )
                return inner

            lax.fori_loop(0, length, row_step, 0)
            down_s[index, :rows, :HEAD_SIZE] = (acc_k[:rows] * scale).astype(jnp.bfloat16)
            down_s[index, :rows, HEAD_SIZE:] = acc_v[:rows].astype(jnp.bfloat16)
            if rows < capacity:
                down_s[index, rows:capacity, :] = jnp.zeros(
                    (capacity - rows, 2 * HEAD_SIZE), jnp.bfloat16
                )

        below = 0
        for rows in PASS_ROWS:

            @pl.when((limit > below) & (limit <= rows))
            def _():
                run(rows)

            below = rows

        @pl.when(limit == 0)
        def _():
            down_s[index, :capacity, :] = jnp.zeros((capacity, 2 * HEAD_SIZE), jnp.bfloat16)

        return carry

    lax.fori_loop(0, far, block_step, 0)
    down_copies = [
        pltpu.make_async_copy(down_s.at[n], downs[n], down_sem.at[n]) for n in range(far)
    ]
    for copy in down_copies:
        copy.start()

    if first:

        def save(n, tile):
            return pltpu.make_async_copy(dqt.at[tile], dqt_out.at[tile], dqt_sem.at[n])

        each_tile(lambda n, tile: save(n, tile).start())
        for copy in down_copies:
            copy.wait()
        each_tile(lambda n, tile: save(n, tile).wait())
        return

    limit = jnp.minimum(total, capacity)

    def key_step(kt, carry):
        start = pl.multiple_of(kt * KEY_TILE, KEY_TILE)
        key = kv_s[1, pl.ds(start, KEY_TILE), :HEAD_SIZE]
        value = kv_s[1, pl.ds(start, KEY_TILE), HEAD_SIZE:]
        key_t = key.T
        own_k = acc_k.at[pl.ds(0, KEY_TILE), :]
        own_v = acc_v.at[pl.ds(0, KEY_TILE), :]
        own_k[...] = jnp.zeros_like(own_k)
        own_v[...] = jnp.zeros_like(own_v)
        position = start + lax.broadcasted_iota(jnp.int32, (KEY_TILE, 1), 0)

        def row_step(n, inner):
            tile = tiles[n]
            shard = tile // SHARD_TILES
            offset = (tile % SHARD_TILES) * ROW_TILE
            count = counts_ref[2 * shard] + counts_ref[2 * shard + 1]
            first = starts[shard] + offset

            @pl.when(first + ROW_TILE > start)
            def _():
                bound = jnp.where(lane < count - offset, first + lane, -1)

                def add_dq(part):
                    dqt[tile] += part

                tile_step(
                    key, value, key_t, row_tile(tile, q_s, do_s, lse_s, delta_s), position, bound,
                    own_k, own_v, add_dq,
                )

            return inner

        lax.fori_loop(0, length, row_step, 0)
        own[pl.ds(start, KEY_TILE), :HEAD_SIZE] = own_k[...] * scale
        own[pl.ds(start, KEY_TILE), HEAD_SIZE:] = own_v[...]
        return carry

    lax.fori_loop(0, (limit + KEY_TILE - 1) // KEY_TILE, key_step, 0)
    own_copy = pltpu.make_async_copy(own, own_out, down_sem.at[1])
    own_copy.start()
    each_tile(lambda n, tile: load(n, tile).wait())

    half = ROW_TILE // 2
    copies = []
    for block in range(KEY_VALUE_HEADS):
        shard = block // 2
        count = counts_ref[2 * shard] + counts_ref[2 * shard + 1]
        if block % 2 == 0:
            pieces = ((0, ROW_TILE, 0, 0), (ROW_TILE, half, 1, 0))
        else:
            pieces = ((0, half, 1, half), (half, ROW_TILE, 2, 0))
        for offset, size, t, first in pieces:
            live = count > t * ROW_TILE
            rows = slice(offset, offset + size)

            @pl.when(live)
            def _():
                for h in range(GROUP):
                    columns = slice(h * HEAD_SIZE, (h + 1) * HEAD_SIZE)
                    tile = SHARD_TILES * shard + t
                    part = ((dqt[tile, :, columns] + before[tile, :, columns]) * scale).T
                    dq_s[block, rows, columns] = part[first : first + size].astype(jnp.bfloat16)

            @pl.when(jnp.logical_not(live))
            def _():
                dq_s[block, rows, :] = jnp.zeros((size, WIDTH), jnp.bfloat16)

        copy = pltpu.make_async_copy(dq_s.at[block], dq_out.at[block], out_sem.at[block])
        copy.start()
        copies.append(copy)
    for copy in (*copies, *down_copies, own_copy):
        copy.wait()


def row_scratch(plane_rows):
    bf16, f32 = jnp.bfloat16, jnp.float32
    tile_count = plane_rows // ROW_TILE
    return [
        pltpu.VMEM((plane_rows, WIDTH), bf16),
        pltpu.VMEM((plane_rows, WIDTH), bf16),
        pltpu.VMEM((tile_count, WIDTH), f32),
        pltpu.VMEM((tile_count, WIDTH), f32),
        pltpu.VMEM((tile_count, HEAD_SIZE, WIDTH), f32),
    ]


def attention(first, me, counts, arrays, kvs, *before):
    bf16, f32 = jnp.bfloat16, jnp.float32
    blocks = KEY_VALUE_HEADS
    rows = kvs[0].shape[0]
    capacity = rows - INFO_ROWS
    columns = 2 * HEAD_SIZE
    plane_rows = 2 * capacity
    tile_count = plane_rows // ROW_TILE
    dq = (blocks, plane_rows // blocks, WIDTH)
    dqt = (tile_count, HEAD_SIZE, WIDTH)
    down = jax.ShapeDtypeStruct((rows, columns), bf16)
    flag = jax.ShapeDtypeStruct((1,), jnp.int32)
    if first:
        outs = (down, down, jax.ShapeDtypeStruct(dqt, f32), flag)
        more = []
    else:
        own = jax.ShapeDtypeStruct((capacity, columns), f32)
        outs = (down, jax.ShapeDtypeStruct(dq, bf16), own, flag)
        more = [
            pltpu.SemaphoreType.DMA((blocks,)),
            pltpu.VMEM(dq, bf16),
            pltpu.VMEM((capacity, columns), f32),
            pltpu.VMEM(dqt, f32),
        ]
    return pl.pallas_call(
        functools.partial(attention_kernel, first),
        out_shape=outs,
        in_specs=[SMEM] * 2 + [HBM] * (12 + len(before)),
        out_specs=[HBM] * 3 + [SMEM],
        scratch_shapes=[
            pltpu.VMEM((plane_rows, WIDTH), bf16),
            pltpu.VMEM((plane_rows, WIDTH), bf16),
            pltpu.VMEM((blocks, INFO_ROWS, AUX_LANES), bf16),
            pltpu.VMEM((tile_count, WIDTH), f32),
            pltpu.VMEM((tile_count, WIDTH), f32),
            pltpu.VMEM(dqt, f32),
            pltpu.VMEM((2, rows, columns), bf16),
            pltpu.VMEM((capacity, HEAD_SIZE), f32),
            pltpu.VMEM((capacity, HEAD_SIZE), f32),
            pltpu.SMEM((tile_count + 1,), jnp.int32),
            pltpu.SMEM((blocks,), jnp.int32),
            pltpu.SMEM((2,), jnp.int32),
            pltpu.SemaphoreType.DMA((3 * blocks,)),
            pltpu.SemaphoreType.DMA((2,)),
            pltpu.SemaphoreType.DMA((2,)),
            pltpu.SemaphoreType.DMA((tile_count,)),
            pltpu.VMEM((2, rows, columns), bf16),
            *more,
        ],
        compiler_params=pltpu.CompilerParams(vmem_limit_bytes=48 * 1024 * 1024),
        cost_estimate=pl.CostEstimate(
            flops=5_000_000_000, bytes_accessed=12_000_000, transcendentals=4_000_000
        ),
        name="attention",
    )(me, counts, *arrays, *kvs, *before)


def unpack_rows_kernel(parts, out):
    for g in range(KEY_VALUE_HEADS):
        out[:, g * WIDTH : (g + 1) * WIDTH] = parts[g]


def unpack_rows(parts):
    return pl.pallas_call(
        unpack_rows_kernel,
        out_shape=jax.ShapeDtypeStruct((parts.shape[1], KEY_VALUE_HEADS * WIDTH), parts.dtype),
        in_specs=[VMEM],
        out_specs=VMEM,
        name="unpack_rows",
    )(parts)


def combine_kernel(counts_ref, own, *rest):
    backs, out = rest[:3], rest[3]
    home_rows = out.shape[1]
    capacity = own.shape[0]
    total = own[...]
    for back in backs:
        total += back[:capacity, :].astype(jnp.float32)
    total = total.astype(jnp.bfloat16)
    within = lax.broadcasted_iota(jnp.int32, (home_rows, capacity), 0)
    place = lax.broadcasted_iota(jnp.int32, (home_rows, capacity), 1)
    start = jnp.int32(0)
    for block in range(KEY_VALUE_HEADS):
        count = counts_ref[block]
        hit = (place == within + start) & (within < count)
        out[block] = jnp.dot(
            jnp.where(hit, 1.0, 0.0).astype(jnp.bfloat16),
            total,
            preferred_element_type=jnp.float32,
        ).astype(jnp.bfloat16)
        start = start + count


def combine(counts, own, backs, home_rows):
    blocks = KEY_VALUE_HEADS
    return pl.pallas_call(
        combine_kernel,
        out_shape=jax.ShapeDtypeStruct((blocks, home_rows, own.shape[1]), jnp.bfloat16),
        in_specs=[SMEM] + [VMEM] * 4,
        out_specs=VMEM,
        compiler_params=pltpu.CompilerParams(vmem_limit_bytes=32 * 1024 * 1024),
        name="combine",
    )(counts, own, *backs)


def plane_device(queries, keys, values, outputs, output_gradient, lse, ranks):
    planes = lax.axis_size("outer")
    plane = ("inner", "head")
    blocks = KEY_VALUE_HEADS
    home_rows = queries.shape[0]
    plane_rows = blocks * home_rows
    capacity = plane_rows // 2
    surviving_tokens = BALANCED_TOKENS * planes * lax.axis_size("inner")
    bf16, f32 = jnp.bfloat16, jnp.float32
    me = lax.axis_index(plane).reshape(1).astype(jnp.int32)

    def swap(array, k):
        return lax.ppermute(array, plane, [(i, i ^ k) for i in range(blocks)])

    sent = pack_pairs(surviving_tokens, ranks, keys, values)
    me, sent = lax.optimization_barrier((me, sent))
    arrived = lax.all_to_all(sent, plane, split_axis=0, concat_axis=0, tiled=True)
    *packed, beside, small = pack_rows(me, lse, queries, output_gradient, outputs)
    pairs = [swap(rows, chip) for rows, chip in zip(packed, CHIPS)]
    beside = swap(beside, CORE)
    arrived, beside = lax.optimization_barrier((arrived, beside))
    mine, counts = compact(arrived)
    up = [lax.ppermute(mine, "outer", [(i, i + 1) for i in range(planes - 1)])]
    last = lax.ppermute(mine, "outer", [(0, planes - 1)])
    up.append(lax.ppermute(up[0], "outer", [(i, i + 1) for i in range(1, planes - 1)]))
    up.append(last)
    up[1], up[2], *pairs = lax.optimization_barrier((up[1], up[2], *pairs))
    crossed = [swap(pair[1:], CORE) for pair in pairs]
    arrays = [queries, output_gradient, small, beside, *pairs, *crossed]

    def lower(rows, k):
        return lax.ppermute(rows, "outer", [(i + k, i) for i in range(planes - k)])

    down2, down3, dqt, full1 = attention(True, me, counts, arrays, [up[1], up[2]])
    back2 = lower(down2, 2)
    down1, dq, own, full2 = attention(False, me, counts, arrays, [up[0], mine], dqt)
    dq, back2 = lax.optimization_barrier((dq, back2))
    backs = [lower(down3, 3), back2, lower(down1, 1)]
    dq = lax.all_to_all(dq, plane, split_axis=0, concat_axis=0, tiled=True)
    spread = combine(counts, own, backs, home_rows)
    dq, spread = lax.optimization_barrier((dq, spread))
    dq_home = unpack_rows(dq)
    kv_home = lax.all_to_all(spread, plane, split_axis=0, concat_axis=0, tiled=True)
    full = (full1[0] + full2[0]) > 0
    for back in backs:
        full = full | (back[capacity, 0] > 0)
    dk = kv_home[:, :, :HEAD_SIZE].transpose(1, 0, 2).reshape(home_rows, blocks * HEAD_SIZE)
    dv = kv_home[:, :, HEAD_SIZE:].transpose(1, 0, 2).reshape(home_rows, blocks * HEAD_SIZE)
    return (dq_home, dk, dv), full


def solution(mesh):
    spec = P(("seq", "head"), None)
    heads = mesh.shape["head"]
    inner = max(KEY_VALUE_HEADS // heads, 1)
    planes = mesh.shape["seq"] // inner
    if planes != 4 or inner * heads != KEY_VALUE_HEADS:
        return jax.shard_map(
            per_device,
            mesh=mesh,
            in_specs=(spec,) * 6 + (P(("seq", "head")),),
            out_specs=(spec,) * 3,
            check_vma=False,
        )
    axes = ("outer", "inner", "head")

    def device(*blocks):
        fast, full = plane_device(*blocks)
        return lax.cond(full, lambda: per_device(*blocks, seq=("outer", "inner")), lambda: fast)

    return jax.shard_map(
        device,
        mesh=Mesh(mesh.devices.reshape(planes, inner, heads), axes),
        in_specs=(P(axes, None),) * 6 + (P(axes),),
        out_specs=(P(axes, None),) * 3,
        check_vma=False,
    )
```

```python
import functools

import jax
import jax.numpy as jnp
from jax import lax
from jax.experimental import pallas as pl
from jax.experimental.pallas import tpu as pltpu
from jax.sharding import Mesh
from jax.sharding import PartitionSpec as P

QUERY_HEADS = 40
KEY_VALUE_HEADS = 8
HEAD_SIZE = 128
BALANCED_TOKENS = 128


block_keys = 512


def per_device(queries, keys, values, outputs, output_gradient, lse, ranks, seq="seq"):
    sequence_count = lax.axis_size(seq)
    head_total = lax.axis_size("head")
    home_rows = queries.shape[0]
    capacity = home_rows * head_total
    slots = capacity // sequence_count
    surviving_tokens = BALANCED_TOKENS * sequence_count
    group_size = QUERY_HEADS // KEY_VALUE_HEADS
    local_key_value = KEY_VALUE_HEADS // head_total
    scale = HEAD_SIZE ** (-0.5)

    def split_heads(array):
        return array.reshape(home_rows, head_total, array.shape[1] // head_total)

    moved = (
        lax.all_to_all(split_heads(queries), "head", split_axis=1, concat_axis=0, tiled=True),
        lax.all_to_all(split_heads(keys), "head", split_axis=1, concat_axis=0, tiled=True),
        lax.all_to_all(split_heads(values), "head", split_axis=1, concat_axis=0, tiled=True),
        lax.all_to_all(
            split_heads(output_gradient), "head", split_axis=1, concat_axis=0, tiled=True
        ),
        lax.all_to_all(split_heads(lse), "head", split_axis=1, concat_axis=0, tiled=True),
        lax.all_to_all(split_heads(outputs), "head", split_axis=1, concat_axis=0, tiled=True),
    )
    shard_rank_list = lax.all_gather(ranks, "head", axis=0, tiled=True)
    first_rank = shard_rank_list[0]
    living_count = jnp.sum((shard_rank_list < surviving_tokens).astype(jnp.int32))
    table = lax.all_gather(
        jnp.stack([first_rank, living_count])[None, :], seq, axis=0, tiled=True
    )

    def to_pairs(array):
        flat = array.reshape(slots, sequence_count, array.shape[-1])
        return jnp.roll(flat, first_rank, axis=1)

    arrived = (
        lax.all_to_all(to_pairs(moved[0]), seq, split_axis=1, concat_axis=1, tiled=True),
        lax.all_to_all(to_pairs(moved[1]), seq, split_axis=1, concat_axis=1, tiled=True),
        lax.all_to_all(to_pairs(moved[2]), seq, split_axis=1, concat_axis=1, tiled=True),
        lax.all_to_all(to_pairs(moved[3]), seq, split_axis=1, concat_axis=1, tiled=True),
        lax.all_to_all(to_pairs(moved[4]), seq, split_axis=1, concat_axis=1, tiled=True),
        lax.all_to_all(to_pairs(moved[5]), seq, split_axis=1, concat_axis=1, tiled=True),
    )
    my_index = lax.axis_index(seq)
    starts = table[:, 0]
    count_table = table[:, 1]
    offset = (my_index - starts) % sequence_count
    within = jnp.arange(slots, dtype=jnp.int32)[:, None] * sequence_count + offset[None, :]
    alive = within < count_table[None, :]
    target_rank = jnp.where(
        alive, (starts[None, :] + within) // sequence_count, BALANCED_TOKENS
    ).reshape(-1)

    def place(array):
        width = array.shape[-1]
        return (
            jnp.zeros((BALANCED_TOKENS, width), array.dtype)
            .at[target_rank]
            .set(array.reshape(slots * sequence_count, width), mode="drop")
        )

    query_row_block = place(arrived[0]).reshape(
        BALANCED_TOKENS, local_key_value, group_size, HEAD_SIZE
    )
    key_row_block = place(arrived[1]).reshape(BALANCED_TOKENS, local_key_value, HEAD_SIZE)
    value_row_block = place(arrived[2]).reshape(BALANCED_TOKENS, local_key_value, HEAD_SIZE)
    grad_rows = place(arrived[3]).reshape(BALANCED_TOKENS, local_key_value, group_size, HEAD_SIZE)
    lse_rows = (
        place(arrived[4]).astype(jnp.float32).reshape(BALANCED_TOKENS, local_key_value, group_size)
    )
    out_rows = (
        place(arrived[5])
        .astype(jnp.float32)
        .reshape(BALANCED_TOKENS, local_key_value, group_size, HEAD_SIZE)
    )
    delta_rows = (
        jnp.sum(grad_rows.astype(jnp.float32) * out_rows, axis=-1)
        .astype(jnp.bfloat16)
        .astype(jnp.float32)
    )
    gathered = (
        lax.all_gather(key_row_block, seq, axis=0, tiled=True),
        lax.all_gather(value_row_block, seq, axis=0, tiled=True),
    )
    all_keys = gathered[0].reshape(sequence_count, BALANCED_TOKENS, local_key_value, HEAD_SIZE)
    all_values = gathered[1].reshape(sequence_count, BALANCED_TOKENS, local_key_value, HEAD_SIZE)
    rows_per = block_keys // sequence_count
    inner = 1
    outer = BALANCED_TOKENS // rows_per // inner
    query_rank = jnp.arange(BALANCED_TOKENS, dtype=jnp.int32) * sequence_count + my_index
    lse_t = lse_rows.transpose(1, 2, 0)
    delta_t = delta_rows.transpose(1, 2, 0)
    position = jnp.arange(sequence_count * rows_per, dtype=jnp.int32)

    def key_step(query_acc, row_start):
        key_blk = lax.dynamic_slice_in_dim(all_keys, row_start, rows_per, 1).reshape(
            sequence_count * rows_per, local_key_value, HEAD_SIZE
        )
        value_blk = lax.dynamic_slice_in_dim(all_values, row_start, rows_per, 1).reshape(
            sequence_count * rows_per, local_key_value, HEAD_SIZE
        )
        key_owner_rank = (row_start + position % rows_per) * sequence_count + position // rows_per
        mask = key_owner_rank[None, None, None, :] <= query_rank[None, None, :, None]
        scores = (
            jnp.einsum(
                "rgmc,kgc->gmrk", query_row_block, key_blk, preferred_element_type=jnp.float32
            )
            * scale
        )
        probs = jnp.where(mask, jnp.exp(scores - lse_t[..., None]), 0.0)
        dprob = jnp.einsum(
            "rgmc,kgc->gmrk", grad_rows, value_blk, preferred_element_type=jnp.float32
        )
        dscore = probs * (dprob - delta_t[..., None])
        probs_low = probs.astype(jnp.bfloat16)
        dscore_low = dscore.astype(jnp.bfloat16)
        query_acc = query_acc + scale * jnp.einsum(
            "gmrk,kgc->rgmc", dscore_low, key_blk, preferred_element_type=jnp.float32
        )
        key_part = scale * jnp.einsum(
            "gmrk,rgmc->kgc", dscore_low, query_row_block, preferred_element_type=jnp.float32
        )
        value_part = jnp.einsum(
            "gmrk,rgmc->kgc", probs_low, grad_rows, preferred_element_type=jnp.float32
        )
        return (
            query_acc,
            key_part.reshape(sequence_count, rows_per, local_key_value * HEAD_SIZE),
            value_part.reshape(sequence_count, rows_per, local_key_value * HEAD_SIZE),
        )

    def outer_step(query_acc, outer_index):

        def inner_step(query_inner, inner_index):
            row_start = (outer_index * inner + inner_index) * rows_per
            query_new, key_part, value_part = key_step(query_inner, row_start)
            return (query_new, (key_part, value_part))

        query_acc, (key_parts, value_parts) = lax.scan(
            inner_step, query_acc, jnp.arange(inner, dtype=jnp.int32)
        )
        key_parts = key_parts.transpose(1, 0, 2, 3).reshape(
            sequence_count, inner * rows_per, local_key_value * HEAD_SIZE
        )
        value_parts = value_parts.transpose(1, 0, 2, 3).reshape(
            sequence_count, inner * rows_per, local_key_value * HEAD_SIZE
        )
        received = (
            lax.all_to_all(key_parts, seq, split_axis=0, concat_axis=0, tiled=True),
            lax.all_to_all(value_parts, seq, split_axis=0, concat_axis=0, tiled=True),
        )
        return (query_acc, (jnp.sum(received[0], axis=0), jnp.sum(received[1], axis=0)))

    start_acc = jnp.zeros((BALANCED_TOKENS, local_key_value, group_size, HEAD_SIZE), jnp.float32)
    query_acc, (key_sums, value_sums) = lax.scan(
        outer_step, start_acc, jnp.arange(outer, dtype=jnp.int32)
    )
    query_done = query_acc.reshape(
        BALANCED_TOKENS, local_key_value * group_size * HEAD_SIZE
    ).astype(jnp.bfloat16)
    key_done = key_sums.reshape(BALANCED_TOKENS, local_key_value * HEAD_SIZE).astype(jnp.bfloat16)
    value_done = value_sums.reshape(BALANCED_TOKENS, local_key_value * HEAD_SIZE).astype(
        jnp.bfloat16
    )
    safe_rows = jnp.minimum(target_rank, BALANCED_TOKENS - 1)
    alive_flat = alive.reshape(-1)

    def collect(array):
        picked = jnp.where(alive_flat[:, None], array[safe_rows], jnp.zeros((), array.dtype))
        return picked.reshape(slots, sequence_count, array.shape[-1])

    returned = (
        lax.all_to_all(collect(query_done), seq, split_axis=1, concat_axis=1, tiled=True),
        lax.all_to_all(collect(key_done), seq, split_axis=1, concat_axis=1, tiled=True),
        lax.all_to_all(collect(value_done), seq, split_axis=1, concat_axis=1, tiled=True),
    )

    def to_home(array):
        unrolled = jnp.roll(array, -first_rank, axis=1)
        return unrolled.reshape(capacity, 1, array.shape[-1])

    homed = (
        lax.all_to_all(to_home(returned[0]), "head", split_axis=0, concat_axis=1, tiled=True),
        lax.all_to_all(to_home(returned[1]), "head", split_axis=0, concat_axis=1, tiled=True),
        lax.all_to_all(to_home(returned[2]), "head", split_axis=0, concat_axis=1, tiled=True),
    )
    query_grads = homed[0].reshape(home_rows, head_total * homed[0].shape[-1])
    key_gradient_output = homed[1].reshape(home_rows, head_total * homed[1].shape[-1])
    value_gradient = homed[2].reshape(home_rows, head_total * homed[2].shape[-1])
    return (query_grads, key_gradient_output, value_gradient)

LOG2E = 1.4426950408889634
KEY_TILE = 256
ROW_TILE = 128
INFO_ROWS = 16
AUX_LANES = 256
DELTA_ROW = 8
SMEM = pl.BlockSpec(memory_space=pltpu.SMEM)
VMEM = pl.BlockSpec(memory_space=pltpu.VMEM)
HBM = pl.BlockSpec(memory_space=pltpu.HBM)
GROUP = QUERY_HEADS // KEY_VALUE_HEADS
WIDTH = GROUP * HEAD_SIZE
CHIPS = (5, 4, 1)
CORE = 2
SHARD_TILES = 3
PASS_ROWS = (256, 512, 768)


def pack_pairs_kernel(limit, ranks_ref, lse_ref, k_ref, v_ref, do_ref, o_ref, out_ref, columns):
    home_rows = k_ref.shape[0]
    columns[...] = jnp.zeros_like(columns)
    for h in range(QUERY_HEADS):
        head = slice(h * HEAD_SIZE, (h + 1) * HEAD_SIZE)
        product = do_ref[:, head].astype(jnp.float32) * o_ref[:, head].astype(jnp.float32)
        column = 8 * (h // GROUP) + h % GROUP
        columns[:, column : column + 1] = jnp.sum(product, axis=1, keepdims=True)
    delta = columns[...].T
    lse = lse_ref[...].astype(jnp.float32)
    live = jnp.where(ranks_ref[...] < limit, 1.0, 0.0)
    count = jnp.broadcast_to(jnp.sum(live, axis=1, keepdims=True), (8 - GROUP, home_rows))
    for g in range(KEY_VALUE_HEADS):
        head = slice(g * HEAD_SIZE, (g + 1) * HEAD_SIZE)
        out_ref[g, :home_rows, :HEAD_SIZE] = k_ref[:, head]
        out_ref[g, :home_rows, HEAD_SIZE:] = v_ref[:, head]
        info = jnp.concatenate(
            [lse[g * GROUP : (g + 1) * GROUP], count, delta[8 * g : 8 * g + 8]], axis=0
        )
        out_ref[g, home_rows:, :home_rows] = info.astype(out_ref.dtype)


def pack_pairs(limit, ranks, lse, keys, values, output_gradient, outputs):
    home_rows = keys.shape[0]
    return pl.pallas_call(
        functools.partial(pack_pairs_kernel, limit),
        out_shape=jax.ShapeDtypeStruct(
            (KEY_VALUE_HEADS, home_rows + INFO_ROWS, 2 * HEAD_SIZE), keys.dtype
        ),
        in_specs=[VMEM] * 6,
        out_specs=VMEM,
        scratch_shapes=[pltpu.VMEM((home_rows, HEAD_SIZE), jnp.float32)],
        compiler_params=pltpu.CompilerParams(vmem_limit_bytes=32 * 1024 * 1024),
        name="pack_pairs",
    )(ranks.reshape(1, home_rows), lse.T, keys, values, output_gradient, outputs)


def pack_rows_kernel(me_ref, q_ref, do_ref, *outs):
    me = me_ref[0]
    for out, partners in zip(outs, [(chip, chip ^ CORE) for chip in CHIPS] + [(CORE,)]):
        for n, partner in enumerate(partners):
            start = pl.multiple_of((me ^ partner) * WIDTH, HEAD_SIZE)
            out[n, :, :WIDTH] = q_ref[:, pl.ds(start, WIDTH)]
            out[n, :, WIDTH:] = do_ref[:, pl.ds(start, WIDTH)]


def pack_rows(me, queries, output_gradient):
    home_rows = queries.shape[0]
    pair = jax.ShapeDtypeStruct((2, home_rows, 2 * WIDTH), queries.dtype)
    beside = jax.ShapeDtypeStruct((1, home_rows, 2 * WIDTH), queries.dtype)
    return pl.pallas_call(
        pack_rows_kernel,
        out_shape=(pair, pair, pair, beside),
        in_specs=[SMEM] + [VMEM] * 2,
        out_specs=[VMEM] * 4,
        compiler_params=pltpu.CompilerParams(vmem_limit_bytes=32 * 1024 * 1024),
        name="pack_rows",
    )(me, queries, output_gradient)


def compact_kernel(arrived, out, small, counts_ref):
    home_rows = arrived.shape[1] - INFO_ROWS
    capacity = out.shape[0] - INFO_ROWS
    row = lax.broadcasted_iota(jnp.int32, (capacity, home_rows), 0)
    within = lax.broadcasted_iota(jnp.int32, (capacity, home_rows), 1)
    total = jnp.int32(0)
    picked = []
    for block in range(KEY_VALUE_HEADS):
        info = arrived[block, home_rows:, :]
        small[block] = info
        count = jnp.max(info.astype(jnp.float32)[GROUP : GROUP + 1, :home_rows]).astype(jnp.int32)
        counts_ref[block] = count
        hit = (row == within + total) & (within < count)
        picked.append(jnp.where(hit, 1.0, 0.0).astype(jnp.bfloat16))
        total = total + count
    acc = jnp.zeros((capacity, out.shape[1]), jnp.float32)
    for block in range(KEY_VALUE_HEADS):
        acc += jnp.dot(
            picked[block], arrived[block, :home_rows, :], preferred_element_type=jnp.float32
        )
    out[:capacity, :] = acc.astype(out.dtype)
    line = lax.broadcasted_iota(jnp.int32, (INFO_ROWS, out.shape[1]), 0)
    out[capacity:, :] = (
        jnp.where(line == 0, total // 64, jnp.where(line == 1, total % 64, 0))
        .astype(jnp.float32)
        .astype(out.dtype)
    )


def compact(arrived):
    blocks, rows, columns = arrived.shape
    capacity = blocks * (rows - INFO_ROWS) // 2
    return pl.pallas_call(
        compact_kernel,
        out_shape=(
            jax.ShapeDtypeStruct((capacity + INFO_ROWS, columns), arrived.dtype),
            jax.ShapeDtypeStruct((blocks, INFO_ROWS, columns), arrived.dtype),
            jax.ShapeDtypeStruct((blocks,), jnp.int32),
        ),
        in_specs=[VMEM],
        out_specs=(VMEM, VMEM, SMEM),
        compiler_params=pltpu.CompilerParams(vmem_limit_bytes=32 * 1024 * 1024),
        name="compact",
    )(arrived)


def load_rows(me, counts_ref, arrays, q_s, do_s, sems):
    home_rows = q_s.shape[0] // KEY_VALUE_HEADS
    q_hbm, do_hbm, beside, pairs, crossed = arrays
    column = pl.ds(pl.multiple_of(me * WIDTH, HEAD_SIZE), WIDTH)
    left, right = pl.ds(0, WIDTH), pl.ds(WIDTH, WIDTH)
    sources = [
        (0, q_hbm.at[:, column], do_hbm.at[:, column]),
        (CORE, beside.at[0, :, left], beside.at[0, :, right]),
    ]
    for chip, pair, cross in zip(CHIPS, pairs, crossed):
        sources.append((chip, pair.at[0, :, left], pair.at[0, :, right]))
        sources.append((chip ^ CORE, cross.at[0, :, left], cross.at[0, :, right]))
    plans = []
    for n, (partner, q, do) in enumerate(sources):
        source = me ^ partner
        rows = pl.ds(pl.multiple_of(source * home_rows, 64), home_rows)
        shard = counts_ref[source & ~1] + counts_ref[source | 1]
        needed = ((source & 1) == 0) | (shard > ROW_TILE)
        plans.append(
            (
                needed,
                [
                    pltpu.make_async_copy(q, q_s.at[rows, :], sems.at[2 * n]),
                    pltpu.make_async_copy(do, do_s.at[rows, :], sems.at[2 * n + 1]),
                ],
            )
        )

    def each(act):
        for needed, copies in plans:

            @pl.when(needed)
            def _():
                for copy in copies:
                    act(copy)

    return each


def list_tiles(counts_ref, tiles, starts):
    length = jnp.int32(0)
    total = jnp.int32(0)
    for shard in range(KEY_VALUE_HEADS // 2):
        count = counts_ref[2 * shard] + counts_ref[2 * shard + 1]
        starts[shard] = total
        total = total + count
        for t in range(SHARD_TILES):
            live = count > t * ROW_TILE

            @pl.when(live)
            def _():
                tiles[length] = SHARD_TILES * shard + t

            length = length + live.astype(jnp.int32)
    return length, total


def spread_lanes(aux_s, lse_s, delta_s):
    lane = lax.broadcasted_iota(jnp.int32, (INFO_ROWS, ROW_TILE), 1)
    for shard in range(KEY_VALUE_HEADS // 2):
        low = aux_s[2 * shard].astype(jnp.float32)
        high = aux_s[2 * shard + 1].astype(jnp.float32)
        half = ROW_TILE // 2
        middle = jnp.where(
            lane < half, low[:, ROW_TILE:], pltpu.roll(high[:, :ROW_TILE], half, axis=1)
        )
        last = pltpu.roll(high, AUX_LANES - half, axis=1)[:, :ROW_TILE]
        for t, rows in enumerate((low[:, :ROW_TILE], middle, last)):
            row = SHARD_TILES * shard + t
            for h in range(GROUP):
                columns = slice(h * ROW_TILE, (h + 1) * ROW_TILE)
                lse_s[row : row + 1, columns] = rows[h : h + 1] * LOG2E
                delta_s[row : row + 1, columns] = rows[DELTA_ROW + h : DELTA_ROW + 1 + h]


def row_tile(tile, q_s, do_s, lse_s, delta_s):
    def stack(ref):
        rows = ref[pl.ds(pl.multiple_of(tile * ROW_TILE, ROW_TILE), ROW_TILE), :]
        return jnp.concatenate(
            [rows[:, h * HEAD_SIZE : (h + 1) * HEAD_SIZE] for h in range(GROUP)], axis=0
        )

    return stack(q_s), stack(do_s), lse_s[pl.ds(tile, 1), :], delta_s[pl.ds(tile, 1), :]


def tile_step(key, value, key_t, rows, position, bound, acc_k, acc_v, add_dq):
    q, do, lse, delta = rows
    scale = HEAD_SIZE ** (-0.5)
    dims = (((1,), (1,)), ((), ()))
    scores = lax.dot_general(key, q, dims, preferred_element_type=jnp.float32)
    prob = jnp.where(position <= bound, jnp.exp2(scores * (scale * LOG2E) - lse), 0.0)
    dprob = lax.dot_general(value, do, dims, preferred_element_type=jnp.float32)
    dscore = (prob * (dprob - delta)).astype(jnp.bfloat16)
    acc_v[...] += jnp.dot(prob.astype(jnp.bfloat16), do, preferred_element_type=jnp.float32)
    acc_k[...] += jnp.dot(dscore, q, preferred_element_type=jnp.float32)
    add_dq(jnp.dot(key_t, dscore, preferred_element_type=jnp.float32))


def attention_kernel(first, me_ref, counts_ref, *rest):
    aux_s, arrays, kvs, rest = rest[0], rest[1:10], rest[10:12], rest[12:]
    arrays = (*arrays[:3], arrays[3:6], arrays[6:9])
    if first:
        far, downs, dqt_out, full_ref, rest = 2, rest[:2], rest[2], rest[3], rest[4:]
    else:
        dqt_in, far, downs, rest = rest[0], 1, rest[1:2], rest[2:]
        dq_out, own_out, full_ref, rest = rest[0], rest[1], rest[2], rest[3:]
    (
        q_s, do_s, lse_s, delta_s, dqt, kv_s, acc_k, acc_v, tiles, starts, limits, sems,
        kv_sem, down_sem, dqt_sem, down_s,
    ) = rest[:16]
    if not first:
        out_sem, dq_s, own, before = rest[16:]
    capacity = downs[0].shape[0] - INFO_ROWS
    scale = HEAD_SIZE ** (-0.5)
    each = load_rows(me_ref[0], counts_ref, arrays, q_s, do_s, sems)
    each(lambda copy: copy.start())
    kv_copies = [
        pltpu.make_async_copy(source, kv_s.at[n], kv_sem.at[n])
        for n, source in enumerate(kvs)
    ]
    for copy in kv_copies:
        copy.start()
    length, total = list_tiles(counts_ref, tiles, starts)

    def each_tile(act):
        def step(n, carry):
            act(n, tiles[n])
            return carry

        lax.fori_loop(0, length, step, 0)

    def zero_tile(n, tile):
        dqt[tile] = jnp.zeros(dqt.shape[1:], jnp.float32)

    each_tile(zero_tile)
    spread_lanes(aux_s, lse_s, delta_s)
    if not first:

        def load(n, tile):
            return pltpu.make_async_copy(dqt_in.at[tile], before.at[tile], dqt_sem.at[n])

        each_tile(lambda n, tile: load(n, tile).start())
        own[...] = jnp.zeros_like(own)
    for copy in kv_copies:
        copy.wait()
    most = total
    for n in range(far):
        info = kv_s[n, capacity:, :].astype(jnp.float32)
        limit = (jnp.max(info[0:1]) * 64.0 + jnp.max(info[1:2])).astype(jnp.int32)
        limits[n] = jnp.minimum(limit, capacity)
        most = jnp.maximum(most, limit)
    full_ref[0] = (most > capacity).astype(jnp.int32)
    for n in range(far):
        down_s[n, capacity:, :] = jnp.full(
            (INFO_ROWS, 2 * HEAD_SIZE), jnp.where(most > capacity, 1.0, 0.0)
        ).astype(jnp.bfloat16)
    each(lambda copy: copy.wait())
    lane = lax.broadcasted_iota(jnp.int32, (1, WIDTH), 1) % ROW_TILE

    def block_step(step, carry):
        index = far - 1 - step
        limit = limits[index]

        def run(rows):
            key = kv_s[index, :rows, :HEAD_SIZE]
            value = kv_s[index, :rows, HEAD_SIZE:]
            key_t = key.T
            acc_k[:rows] = jnp.zeros((rows, HEAD_SIZE), jnp.float32)
            acc_v[:rows] = jnp.zeros((rows, HEAD_SIZE), jnp.float32)
            position = lax.broadcasted_iota(jnp.int32, (rows, 1), 0)

            def row_step(n, inner):
                tile = tiles[n]
                shard = tile // SHARD_TILES
                count = counts_ref[2 * shard] + counts_ref[2 * shard + 1]
                alive = lane < count - (tile % SHARD_TILES) * ROW_TILE
                bound = jnp.where(alive, limit - 1, -1)

                def add_dq(part):
                    dqt[tile] += part

                tile_step(
                    key, value, key_t, row_tile(tile, q_s, do_s, lse_s, delta_s), position, bound,
                    acc_k.at[pl.ds(0, rows), :], acc_v.at[pl.ds(0, rows), :], add_dq,
                )
                return inner

            lax.fori_loop(0, length, row_step, 0)
            down_s[index, :rows, :HEAD_SIZE] = (acc_k[:rows] * scale).astype(jnp.bfloat16)
            down_s[index, :rows, HEAD_SIZE:] = acc_v[:rows].astype(jnp.bfloat16)
            if rows < capacity:
                down_s[index, rows:capacity, :] = jnp.zeros(
                    (capacity - rows, 2 * HEAD_SIZE), jnp.bfloat16
                )

        below = 0
        for rows in PASS_ROWS:

            @pl.when((limit > below) & (limit <= rows))
            def _():
                run(rows)

            below = rows

        @pl.when(limit == 0)
        def _():
            down_s[index, :capacity, :] = jnp.zeros((capacity, 2 * HEAD_SIZE), jnp.bfloat16)

        return carry

    lax.fori_loop(0, far, block_step, 0)
    down_copies = [
        pltpu.make_async_copy(down_s.at[n], downs[n], down_sem.at[n]) for n in range(far)
    ]
    for copy in down_copies:
        copy.start()

    if first:

        def save(n, tile):
            return pltpu.make_async_copy(dqt.at[tile], dqt_out.at[tile], dqt_sem.at[n])

        each_tile(lambda n, tile: save(n, tile).start())
        for copy in down_copies:
            copy.wait()
        each_tile(lambda n, tile: save(n, tile).wait())
        return

    limit = jnp.minimum(total, capacity)

    def key_step(kt, carry):
        start = pl.multiple_of(kt * KEY_TILE, KEY_TILE)
        key = kv_s[1, pl.ds(start, KEY_TILE), :HEAD_SIZE]
        value = kv_s[1, pl.ds(start, KEY_TILE), HEAD_SIZE:]
        key_t = key.T
        own_k = acc_k.at[pl.ds(0, KEY_TILE), :]
        own_v = acc_v.at[pl.ds(0, KEY_TILE), :]
        own_k[...] = jnp.zeros_like(own_k)
        own_v[...] = jnp.zeros_like(own_v)
        position = start + lax.broadcasted_iota(jnp.int32, (KEY_TILE, 1), 0)

        def row_step(n, inner):
            tile = tiles[n]
            shard = tile // SHARD_TILES
            offset = (tile % SHARD_TILES) * ROW_TILE
            count = counts_ref[2 * shard] + counts_ref[2 * shard + 1]
            first = starts[shard] + offset

            @pl.when(first + ROW_TILE > start)
            def _():
                bound = jnp.where(lane < count - offset, first + lane, -1)

                def add_dq(part):
                    dqt[tile] += part

                tile_step(
                    key, value, key_t, row_tile(tile, q_s, do_s, lse_s, delta_s), position, bound,
                    own_k, own_v, add_dq,
                )

            return inner

        lax.fori_loop(0, length, row_step, 0)
        own[pl.ds(start, KEY_TILE), :HEAD_SIZE] = own_k[...] * scale
        own[pl.ds(start, KEY_TILE), HEAD_SIZE:] = own_v[...]
        return carry

    lax.fori_loop(0, (limit + KEY_TILE - 1) // KEY_TILE, key_step, 0)
    own_copy = pltpu.make_async_copy(own, own_out, down_sem.at[1])
    own_copy.start()
    each_tile(lambda n, tile: load(n, tile).wait())

    half = ROW_TILE // 2
    copies = []
    for block in range(KEY_VALUE_HEADS):
        shard = block // 2
        count = counts_ref[2 * shard] + counts_ref[2 * shard + 1]
        if block % 2 == 0:
            pieces = ((0, ROW_TILE, 0, 0), (ROW_TILE, half, 1, 0))
        else:
            pieces = ((0, half, 1, half), (half, ROW_TILE, 2, 0))
        for offset, size, t, first in pieces:
            live = count > t * ROW_TILE
            rows = slice(offset, offset + size)

            @pl.when(live)
            def _():
                for h in range(GROUP):
                    columns = slice(h * HEAD_SIZE, (h + 1) * HEAD_SIZE)
                    tile = SHARD_TILES * shard + t
                    part = ((dqt[tile, :, columns] + before[tile, :, columns]) * scale).T
                    dq_s[block, rows, columns] = part[first : first + size].astype(jnp.bfloat16)

            @pl.when(jnp.logical_not(live))
            def _():
                dq_s[block, rows, :] = jnp.zeros((size, WIDTH), jnp.bfloat16)

        copy = pltpu.make_async_copy(dq_s.at[block], dq_out.at[block], out_sem.at[block])
        copy.start()
        copies.append(copy)
    for copy in (*copies, *down_copies, own_copy):
        copy.wait()


def row_scratch(plane_rows):
    bf16, f32 = jnp.bfloat16, jnp.float32
    tile_count = plane_rows // ROW_TILE
    return [
        pltpu.VMEM((plane_rows, WIDTH), bf16),
        pltpu.VMEM((plane_rows, WIDTH), bf16),
        pltpu.VMEM((tile_count, WIDTH), f32),
        pltpu.VMEM((tile_count, WIDTH), f32),
        pltpu.VMEM((tile_count, HEAD_SIZE, WIDTH), f32),
    ]


def attention(first, me, counts, small, arrays, kvs, *before):
    bf16, f32 = jnp.bfloat16, jnp.float32
    blocks = KEY_VALUE_HEADS
    rows = kvs[0].shape[0]
    capacity = rows - INFO_ROWS
    columns = 2 * HEAD_SIZE
    plane_rows = 2 * capacity
    tile_count = plane_rows // ROW_TILE
    dq = (blocks, plane_rows // blocks, WIDTH)
    dqt = (tile_count, HEAD_SIZE, WIDTH)
    down = jax.ShapeDtypeStruct((rows, columns), bf16)
    flag = jax.ShapeDtypeStruct((1,), jnp.int32)
    if first:
        outs = (down, down, jax.ShapeDtypeStruct(dqt, f32), flag)
        more = []
    else:
        own = jax.ShapeDtypeStruct((capacity, columns), f32)
        outs = (down, jax.ShapeDtypeStruct(dq, bf16), own, flag)
        more = [
            pltpu.SemaphoreType.DMA((blocks,)),
            pltpu.VMEM(dq, bf16),
            pltpu.VMEM((capacity, columns), f32),
            pltpu.VMEM(dqt, f32),
        ]
    return pl.pallas_call(
        functools.partial(attention_kernel, first),
        out_shape=outs,
        in_specs=[SMEM] * 2 + [VMEM] + [HBM] * (11 + len(before)),
        out_specs=[HBM] * 3 + [SMEM],
        scratch_shapes=[
            pltpu.VMEM((plane_rows, WIDTH), bf16),
            pltpu.VMEM((plane_rows, WIDTH), bf16),
            pltpu.VMEM((tile_count, WIDTH), f32),
            pltpu.VMEM((tile_count, WIDTH), f32),
            pltpu.VMEM(dqt, f32),
            pltpu.VMEM((2, rows, columns), bf16),
            pltpu.VMEM((capacity, HEAD_SIZE), f32),
            pltpu.VMEM((capacity, HEAD_SIZE), f32),
            pltpu.SMEM((tile_count + 1,), jnp.int32),
            pltpu.SMEM((blocks,), jnp.int32),
            pltpu.SMEM((2,), jnp.int32),
            pltpu.SemaphoreType.DMA((2 * blocks,)),
            pltpu.SemaphoreType.DMA((2,)),
            pltpu.SemaphoreType.DMA((2,)),
            pltpu.SemaphoreType.DMA((tile_count,)),
            pltpu.VMEM((2, rows, columns), bf16),
            *more,
        ],
        compiler_params=pltpu.CompilerParams(vmem_limit_bytes=48 * 1024 * 1024),
        cost_estimate=pl.CostEstimate(
            flops=5_000_000_000, bytes_accessed=12_000_000, transcendentals=4_000_000
        ),
        name="attention",
    )(me, counts, small, *arrays, *kvs, *before)


def unpack_rows_kernel(parts, out):
    for g in range(KEY_VALUE_HEADS):
        out[:, g * WIDTH : (g + 1) * WIDTH] = parts[g]


def unpack_rows(parts):
    return pl.pallas_call(
        unpack_rows_kernel,
        out_shape=jax.ShapeDtypeStruct((parts.shape[1], KEY_VALUE_HEADS * WIDTH), parts.dtype),
        in_specs=[VMEM],
        out_specs=VMEM,
        name="unpack_rows",
    )(parts)


def combine_kernel(counts_ref, own, *rest):
    backs, out = rest[:3], rest[3]
    home_rows = out.shape[1]
    capacity = own.shape[0]
    total = own[...]
    for back in backs:
        total += back[:capacity, :].astype(jnp.float32)
    total = total.astype(jnp.bfloat16)
    within = lax.broadcasted_iota(jnp.int32, (home_rows, capacity), 0)
    place = lax.broadcasted_iota(jnp.int32, (home_rows, capacity), 1)
    start = jnp.int32(0)
    for block in range(KEY_VALUE_HEADS):
        count = counts_ref[block]
        hit = (place == within + start) & (within < count)
        out[block] = jnp.dot(
            jnp.where(hit, 1.0, 0.0).astype(jnp.bfloat16),
            total,
            preferred_element_type=jnp.float32,
        ).astype(jnp.bfloat16)
        start = start + count


def combine(counts, own, backs, home_rows):
    blocks = KEY_VALUE_HEADS
    return pl.pallas_call(
        combine_kernel,
        out_shape=jax.ShapeDtypeStruct((blocks, home_rows, own.shape[1]), jnp.bfloat16),
        in_specs=[SMEM] + [VMEM] * 4,
        out_specs=VMEM,
        compiler_params=pltpu.CompilerParams(vmem_limit_bytes=32 * 1024 * 1024),
        name="combine",
    )(counts, own, *backs)


def plane_device(queries, keys, values, outputs, output_gradient, lse, ranks):
    planes = lax.axis_size("outer")
    plane = ("inner", "head")
    blocks = KEY_VALUE_HEADS
    home_rows = queries.shape[0]
    plane_rows = blocks * home_rows
    capacity = plane_rows // 2
    surviving_tokens = BALANCED_TOKENS * planes * lax.axis_size("inner")
    bf16, f32 = jnp.bfloat16, jnp.float32
    me = lax.axis_index(plane).reshape(1).astype(jnp.int32)

    def swap(array, k):
        return lax.ppermute(array, plane, [(i, i ^ k) for i in range(blocks)])

    sent = pack_pairs(
        surviving_tokens, ranks, lse, keys, values, output_gradient, outputs
    )
    me, sent = lax.optimization_barrier((me, sent))
    arrived = lax.all_to_all(sent, plane, split_axis=0, concat_axis=0, tiled=True)
    *packed, beside = pack_rows(me, queries, output_gradient)
    pairs = [swap(rows, chip) for rows, chip in zip(packed, CHIPS)]
    beside = swap(beside, CORE)
    arrived, beside = lax.optimization_barrier((arrived, beside))
    mine, small, counts = compact(arrived)
    up = [lax.ppermute(mine, "outer", [(i, i + 1) for i in range(planes - 1)])]
    last = lax.ppermute(mine, "outer", [(0, planes - 1)])
    up.append(lax.ppermute(up[0], "outer", [(i, i + 1) for i in range(1, planes - 1)]))
    up.append(last)
    up[1], up[2], *pairs = lax.optimization_barrier((up[1], up[2], *pairs))
    crossed = [swap(pair[1:], CORE) for pair in pairs]
    arrays = [queries, output_gradient, beside, *pairs, *crossed]

    def lower(rows, k):
        return lax.ppermute(rows, "outer", [(i + k, i) for i in range(planes - k)])

    down2, down3, dqt, full1 = attention(True, me, counts, small, arrays, [up[1], up[2]])
    back2 = lower(down2, 2)
    down1, dq, own, full2 = attention(False, me, counts, small, arrays, [up[0], mine], dqt)
    dq, back2 = lax.optimization_barrier((dq, back2))
    backs = [lower(down3, 3), back2, lower(down1, 1)]
    dq = lax.all_to_all(dq, plane, split_axis=0, concat_axis=0, tiled=True)
    spread = combine(counts, own, backs, home_rows)
    dq, spread = lax.optimization_barrier((dq, spread))
    dq_home = unpack_rows(dq)
    kv_home = lax.all_to_all(spread, plane, split_axis=0, concat_axis=0, tiled=True)
    full = (full1[0] + full2[0]) > 0
    for back in backs:
        full = full | (back[capacity, 0] > 0)
    dk = kv_home[:, :, :HEAD_SIZE].transpose(1, 0, 2).reshape(home_rows, blocks * HEAD_SIZE)
    dv = kv_home[:, :, HEAD_SIZE:].transpose(1, 0, 2).reshape(home_rows, blocks * HEAD_SIZE)
    return (dq_home, dk, dv), full


def solution(mesh):
    spec = P(("seq", "head"), None)
    heads = mesh.shape["head"]
    inner = max(KEY_VALUE_HEADS // heads, 1)
    planes = mesh.shape["seq"] // inner
    if planes != 4 or inner * heads != KEY_VALUE_HEADS:
        return jax.shard_map(
            per_device,
            mesh=mesh,
            in_specs=(spec,) * 6 + (P(("seq", "head")),),
            out_specs=(spec,) * 3,
            check_vma=False,
        )
    axes = ("outer", "inner", "head")

    def device(*blocks):
        fast, full = plane_device(*blocks)
        return lax.cond(full, lambda: per_device(*blocks, seq=("outer", "inner")), lambda: fast)

    return jax.shard_map(
        device,
        mesh=Mesh(mesh.devices.reshape(planes, inner, heads), axes),
        in_specs=(P(axes, None),) * 6 + (P(axes),),
        out_specs=(P(axes, None),) * 3,
        check_vma=False,
    )
```

```python
import functools

import jax
import jax.numpy as jnp
from jax import lax
from jax.experimental import pallas as pl
from jax.experimental.pallas import tpu as pltpu
from jax.sharding import Mesh
from jax.sharding import PartitionSpec as P

QUERY_HEADS = 40
KEY_VALUE_HEADS = 8
HEAD_SIZE = 128
BALANCED_TOKENS = 128


block_keys = 512


def gather(array, axis):
    count = lax.axis_size(axis)
    copies = jnp.broadcast_to(array[None], (count, *array.shape))
    got = lax.all_to_all(copies, axis, split_axis=0, concat_axis=0, tiled=True)
    return got.reshape(count * array.shape[0], *array.shape[1:])


def per_device(queries, keys, values, outputs, output_gradient, lse, ranks, seq="seq"):
    sequence_count = lax.axis_size(seq)
    head_total = lax.axis_size("head")
    home_rows = queries.shape[0]
    capacity = home_rows * head_total
    slots = capacity // sequence_count
    surviving_tokens = BALANCED_TOKENS * sequence_count
    group_size = QUERY_HEADS // KEY_VALUE_HEADS
    local_key_value = KEY_VALUE_HEADS // head_total
    scale = HEAD_SIZE ** (-0.5)

    def split_heads(array):
        return array.reshape(home_rows, head_total, array.shape[1] // head_total)

    moved = (
        lax.all_to_all(split_heads(queries), "head", split_axis=1, concat_axis=0, tiled=True),
        lax.all_to_all(split_heads(keys), "head", split_axis=1, concat_axis=0, tiled=True),
        lax.all_to_all(split_heads(values), "head", split_axis=1, concat_axis=0, tiled=True),
        lax.all_to_all(
            split_heads(output_gradient), "head", split_axis=1, concat_axis=0, tiled=True
        ),
        lax.all_to_all(split_heads(lse), "head", split_axis=1, concat_axis=0, tiled=True),
        lax.all_to_all(split_heads(outputs), "head", split_axis=1, concat_axis=0, tiled=True),
    )
    shard_rank_list = gather(ranks, "head")
    first_rank = shard_rank_list[0]
    living_count = jnp.sum((shard_rank_list < surviving_tokens).astype(jnp.int32))
    table = gather(jnp.stack([first_rank, living_count])[None, :], seq)

    def to_pairs(array):
        flat = array.reshape(slots, sequence_count, array.shape[-1])
        return jnp.roll(flat, first_rank, axis=1)

    arrived = (
        lax.all_to_all(to_pairs(moved[0]), seq, split_axis=1, concat_axis=1, tiled=True),
        lax.all_to_all(to_pairs(moved[1]), seq, split_axis=1, concat_axis=1, tiled=True),
        lax.all_to_all(to_pairs(moved[2]), seq, split_axis=1, concat_axis=1, tiled=True),
        lax.all_to_all(to_pairs(moved[3]), seq, split_axis=1, concat_axis=1, tiled=True),
        lax.all_to_all(to_pairs(moved[4]), seq, split_axis=1, concat_axis=1, tiled=True),
        lax.all_to_all(to_pairs(moved[5]), seq, split_axis=1, concat_axis=1, tiled=True),
    )
    my_index = lax.axis_index(seq)
    starts = table[:, 0]
    count_table = table[:, 1]
    offset = (my_index - starts) % sequence_count
    within = jnp.arange(slots, dtype=jnp.int32)[:, None] * sequence_count + offset[None, :]
    alive = within < count_table[None, :]
    target_rank = jnp.where(
        alive, (starts[None, :] + within) // sequence_count, BALANCED_TOKENS
    ).reshape(-1)

    def place(array):
        width = array.shape[-1]
        return (
            jnp.zeros((BALANCED_TOKENS, width), array.dtype)
            .at[target_rank]
            .set(array.reshape(slots * sequence_count, width), mode="drop")
        )

    query_row_block = place(arrived[0]).reshape(
        BALANCED_TOKENS, local_key_value, group_size, HEAD_SIZE
    )
    key_row_block = place(arrived[1]).reshape(BALANCED_TOKENS, local_key_value, HEAD_SIZE)
    value_row_block = place(arrived[2]).reshape(BALANCED_TOKENS, local_key_value, HEAD_SIZE)
    grad_rows = place(arrived[3]).reshape(BALANCED_TOKENS, local_key_value, group_size, HEAD_SIZE)
    lse_rows = (
        place(arrived[4]).astype(jnp.float32).reshape(BALANCED_TOKENS, local_key_value, group_size)
    )
    out_rows = (
        place(arrived[5])
        .astype(jnp.float32)
        .reshape(BALANCED_TOKENS, local_key_value, group_size, HEAD_SIZE)
    )
    delta_rows = (
        jnp.sum(grad_rows.astype(jnp.float32) * out_rows, axis=-1)
        .astype(jnp.bfloat16)
        .astype(jnp.float32)
    )
    gathered = (
        gather(key_row_block, seq),
        gather(value_row_block, seq),
    )
    all_keys = gathered[0].reshape(sequence_count, BALANCED_TOKENS, local_key_value, HEAD_SIZE)
    all_values = gathered[1].reshape(sequence_count, BALANCED_TOKENS, local_key_value, HEAD_SIZE)
    rows_per = block_keys // sequence_count
    inner = 1
    outer = BALANCED_TOKENS // rows_per // inner
    query_rank = jnp.arange(BALANCED_TOKENS, dtype=jnp.int32) * sequence_count + my_index
    lse_t = lse_rows.transpose(1, 2, 0)
    delta_t = delta_rows.transpose(1, 2, 0)
    position = jnp.arange(sequence_count * rows_per, dtype=jnp.int32)

    def key_step(query_acc, row_start):
        key_blk = lax.dynamic_slice_in_dim(all_keys, row_start, rows_per, 1).reshape(
            sequence_count * rows_per, local_key_value, HEAD_SIZE
        )
        value_blk = lax.dynamic_slice_in_dim(all_values, row_start, rows_per, 1).reshape(
            sequence_count * rows_per, local_key_value, HEAD_SIZE
        )
        key_owner_rank = (row_start + position % rows_per) * sequence_count + position // rows_per
        mask = key_owner_rank[None, None, None, :] <= query_rank[None, None, :, None]
        scores = (
            jnp.einsum(
                "rgmc,kgc->gmrk", query_row_block, key_blk, preferred_element_type=jnp.float32
            )
            * scale
        )
        probs = jnp.where(mask, jnp.exp(scores - lse_t[..., None]), 0.0)
        dprob = jnp.einsum(
            "rgmc,kgc->gmrk", grad_rows, value_blk, preferred_element_type=jnp.float32
        )
        dscore = probs * (dprob - delta_t[..., None])
        probs_low = probs.astype(jnp.bfloat16)
        dscore_low = dscore.astype(jnp.bfloat16)
        query_acc = query_acc + scale * jnp.einsum(
            "gmrk,kgc->rgmc", dscore_low, key_blk, preferred_element_type=jnp.float32
        )
        key_part = scale * jnp.einsum(
            "gmrk,rgmc->kgc", dscore_low, query_row_block, preferred_element_type=jnp.float32
        )
        value_part = jnp.einsum(
            "gmrk,rgmc->kgc", probs_low, grad_rows, preferred_element_type=jnp.float32
        )
        return (
            query_acc,
            key_part.reshape(sequence_count, rows_per, local_key_value * HEAD_SIZE),
            value_part.reshape(sequence_count, rows_per, local_key_value * HEAD_SIZE),
        )

    def outer_step(query_acc, outer_index):

        def inner_step(query_inner, inner_index):
            row_start = (outer_index * inner + inner_index) * rows_per
            query_new, key_part, value_part = key_step(query_inner, row_start)
            return (query_new, (key_part, value_part))

        query_acc, (key_parts, value_parts) = lax.scan(
            inner_step, query_acc, jnp.arange(inner, dtype=jnp.int32)
        )
        key_parts = key_parts.transpose(1, 0, 2, 3).reshape(
            sequence_count, inner * rows_per, local_key_value * HEAD_SIZE
        )
        value_parts = value_parts.transpose(1, 0, 2, 3).reshape(
            sequence_count, inner * rows_per, local_key_value * HEAD_SIZE
        )
        received = (
            lax.all_to_all(key_parts, seq, split_axis=0, concat_axis=0, tiled=True),
            lax.all_to_all(value_parts, seq, split_axis=0, concat_axis=0, tiled=True),
        )
        return (query_acc, (jnp.sum(received[0], axis=0), jnp.sum(received[1], axis=0)))

    start_acc = jnp.zeros((BALANCED_TOKENS, local_key_value, group_size, HEAD_SIZE), jnp.float32)
    query_acc, (key_sums, value_sums) = lax.scan(
        outer_step, start_acc, jnp.arange(outer, dtype=jnp.int32)
    )
    query_done = query_acc.reshape(
        BALANCED_TOKENS, local_key_value * group_size * HEAD_SIZE
    ).astype(jnp.bfloat16)
    key_done = key_sums.reshape(BALANCED_TOKENS, local_key_value * HEAD_SIZE).astype(jnp.bfloat16)
    value_done = value_sums.reshape(BALANCED_TOKENS, local_key_value * HEAD_SIZE).astype(
        jnp.bfloat16
    )
    safe_rows = jnp.minimum(target_rank, BALANCED_TOKENS - 1)
    alive_flat = alive.reshape(-1)

    def collect(array):
        picked = jnp.where(alive_flat[:, None], array[safe_rows], jnp.zeros((), array.dtype))
        return picked.reshape(slots, sequence_count, array.shape[-1])

    returned = (
        lax.all_to_all(collect(query_done), seq, split_axis=1, concat_axis=1, tiled=True),
        lax.all_to_all(collect(key_done), seq, split_axis=1, concat_axis=1, tiled=True),
        lax.all_to_all(collect(value_done), seq, split_axis=1, concat_axis=1, tiled=True),
    )

    def to_home(array):
        unrolled = jnp.roll(array, -first_rank, axis=1)
        return unrolled.reshape(capacity, 1, array.shape[-1])

    homed = (
        lax.all_to_all(to_home(returned[0]), "head", split_axis=0, concat_axis=1, tiled=True),
        lax.all_to_all(to_home(returned[1]), "head", split_axis=0, concat_axis=1, tiled=True),
        lax.all_to_all(to_home(returned[2]), "head", split_axis=0, concat_axis=1, tiled=True),
    )
    query_grads = homed[0].reshape(home_rows, head_total * homed[0].shape[-1])
    key_gradient_output = homed[1].reshape(home_rows, head_total * homed[1].shape[-1])
    value_gradient = homed[2].reshape(home_rows, head_total * homed[2].shape[-1])
    return (query_grads, key_gradient_output, value_gradient)

LOG2E = 1.4426950408889634
KEY_TILE = 256
ROW_TILE = 128
INFO_ROWS = 16
AUX_LANES = 256
DELTA_ROW = 8
SMEM = pl.BlockSpec(memory_space=pltpu.SMEM)
VMEM = pl.BlockSpec(memory_space=pltpu.VMEM)
HBM = pl.BlockSpec(memory_space=pltpu.HBM)
GROUP = QUERY_HEADS // KEY_VALUE_HEADS
WIDTH = GROUP * HEAD_SIZE
CHIPS = (5, 4, 1)
CORE = 2
SHARD_TILES = 3
PASS_ROWS = (256, 512, 768)


def pack_pairs_kernel(limit, ranks_ref, lse_ref, k_ref, v_ref, do_ref, o_ref, out_ref, columns):
    home_rows = k_ref.shape[0]
    columns[...] = jnp.zeros_like(columns)
    for h in range(QUERY_HEADS):
        head = slice(h * HEAD_SIZE, (h + 1) * HEAD_SIZE)
        product = do_ref[:, head].astype(jnp.float32) * o_ref[:, head].astype(jnp.float32)
        column = 8 * (h // GROUP) + h % GROUP
        columns[:, column : column + 1] = jnp.sum(product, axis=1, keepdims=True)
    delta = columns[...].T
    lse = lse_ref[...].astype(jnp.float32)
    live = jnp.where(ranks_ref[...] < limit, 1.0, 0.0)
    count = jnp.broadcast_to(jnp.sum(live, axis=1, keepdims=True), (8 - GROUP, home_rows))
    for g in range(KEY_VALUE_HEADS):
        head = slice(g * HEAD_SIZE, (g + 1) * HEAD_SIZE)
        out_ref[g, :home_rows, :HEAD_SIZE] = k_ref[:, head]
        out_ref[g, :home_rows, HEAD_SIZE:] = v_ref[:, head]
        info = jnp.concatenate(
            [lse[g * GROUP : (g + 1) * GROUP], count, delta[8 * g : 8 * g + 8]], axis=0
        )
        out_ref[g, home_rows:, :home_rows] = info.astype(out_ref.dtype)


def pack_pairs(limit, ranks, lse, keys, values, output_gradient, outputs):
    home_rows = keys.shape[0]
    return pl.pallas_call(
        functools.partial(pack_pairs_kernel, limit),
        out_shape=jax.ShapeDtypeStruct(
            (KEY_VALUE_HEADS, home_rows + INFO_ROWS, 2 * HEAD_SIZE), keys.dtype
        ),
        in_specs=[VMEM] * 6,
        out_specs=VMEM,
        scratch_shapes=[pltpu.VMEM((home_rows, HEAD_SIZE), jnp.float32)],
        compiler_params=pltpu.CompilerParams(vmem_limit_bytes=32 * 1024 * 1024),
        name="pack_pairs",
    )(ranks.reshape(1, home_rows), lse.T, keys, values, output_gradient, outputs)


def pack_rows_kernel(me_ref, q_ref, do_ref, *outs):
    me = me_ref[0]
    for out, partners in zip(outs, [(chip, chip ^ CORE) for chip in CHIPS] + [(CORE,)]):
        for n, partner in enumerate(partners):
            start = pl.multiple_of((me ^ partner) * WIDTH, HEAD_SIZE)
            out[n, :, :WIDTH] = q_ref[:, pl.ds(start, WIDTH)]
            out[n, :, WIDTH:] = do_ref[:, pl.ds(start, WIDTH)]


def pack_rows(me, queries, output_gradient):
    home_rows = queries.shape[0]
    pair = jax.ShapeDtypeStruct((2, home_rows, 2 * WIDTH), queries.dtype)
    beside = jax.ShapeDtypeStruct((1, home_rows, 2 * WIDTH), queries.dtype)
    return pl.pallas_call(
        pack_rows_kernel,
        out_shape=(pair, pair, pair, beside),
        in_specs=[SMEM] + [VMEM] * 2,
        out_specs=[VMEM] * 4,
        compiler_params=pltpu.CompilerParams(vmem_limit_bytes=32 * 1024 * 1024),
        name="pack_rows",
    )(me, queries, output_gradient)


def compact_kernel(arrived, out, small, counts_ref):
    home_rows = arrived.shape[1] - INFO_ROWS
    capacity = out.shape[0] - INFO_ROWS
    row = lax.broadcasted_iota(jnp.int32, (capacity, home_rows), 0)
    within = lax.broadcasted_iota(jnp.int32, (capacity, home_rows), 1)
    total = jnp.int32(0)
    picked = []
    for block in range(KEY_VALUE_HEADS):
        info = arrived[block, home_rows:, :]
        small[block] = info
        count = jnp.max(info.astype(jnp.float32)[GROUP : GROUP + 1, :home_rows]).astype(jnp.int32)
        counts_ref[block] = count
        hit = (row == within + total) & (within < count)
        picked.append(jnp.where(hit, 1.0, 0.0).astype(jnp.bfloat16))
        total = total + count
    acc = jnp.zeros((capacity, out.shape[1]), jnp.float32)
    for block in range(KEY_VALUE_HEADS):
        acc += jnp.dot(
            picked[block], arrived[block, :home_rows, :], preferred_element_type=jnp.float32
        )
    out[:capacity, :] = acc.astype(out.dtype)
    line = lax.broadcasted_iota(jnp.int32, (INFO_ROWS, out.shape[1]), 0)
    out[capacity:, :] = (
        jnp.where(line == 0, total // 64, jnp.where(line == 1, total % 64, 0))
        .astype(jnp.float32)
        .astype(out.dtype)
    )


def compact(arrived):
    blocks, rows, columns = arrived.shape
    capacity = blocks * (rows - INFO_ROWS) // 2
    return pl.pallas_call(
        compact_kernel,
        out_shape=(
            jax.ShapeDtypeStruct((capacity + INFO_ROWS, columns), arrived.dtype),
            jax.ShapeDtypeStruct((blocks, INFO_ROWS, columns), arrived.dtype),
            jax.ShapeDtypeStruct((blocks,), jnp.int32),
        ),
        in_specs=[VMEM],
        out_specs=(VMEM, VMEM, SMEM),
        compiler_params=pltpu.CompilerParams(vmem_limit_bytes=32 * 1024 * 1024),
        name="compact",
    )(arrived)


def load_rows(me, counts_ref, arrays, q_s, do_s, sems):
    home_rows = q_s.shape[0] // KEY_VALUE_HEADS
    q_hbm, do_hbm, beside, pairs, crossed = arrays
    column = pl.ds(pl.multiple_of(me * WIDTH, HEAD_SIZE), WIDTH)
    left, right = pl.ds(0, WIDTH), pl.ds(WIDTH, WIDTH)
    sources = [
        (0, q_hbm.at[:, column], do_hbm.at[:, column]),
        (CORE, beside.at[0, :, left], beside.at[0, :, right]),
    ]
    for chip, pair, cross in zip(CHIPS, pairs, crossed):
        sources.append((chip, pair.at[0, :, left], pair.at[0, :, right]))
        sources.append((chip ^ CORE, cross.at[0, :, left], cross.at[0, :, right]))
    plans = []
    for n, (partner, q, do) in enumerate(sources):
        source = me ^ partner
        rows = pl.ds(pl.multiple_of(source * home_rows, 64), home_rows)
        shard = counts_ref[source & ~1] + counts_ref[source | 1]
        needed = ((source & 1) == 0) | (shard > ROW_TILE)
        plans.append(
            (
                needed,
                [
                    pltpu.make_async_copy(q, q_s.at[rows, :], sems.at[2 * n]),
                    pltpu.make_async_copy(do, do_s.at[rows, :], sems.at[2 * n + 1]),
                ],
            )
        )

    def each(act):
        for needed, copies in plans:

            @pl.when(needed)
            def _():
                for copy in copies:
                    act(copy)

    return each


def list_tiles(counts_ref, tiles, starts):
    length = jnp.int32(0)
    total = jnp.int32(0)
    for shard in range(KEY_VALUE_HEADS // 2):
        count = counts_ref[2 * shard] + counts_ref[2 * shard + 1]
        starts[shard] = total
        total = total + count
        for t in range(SHARD_TILES):
            live = count > t * ROW_TILE

            @pl.when(live)
            def _():
                tiles[length] = SHARD_TILES * shard + t

            length = length + live.astype(jnp.int32)
    return length, total


def spread_lanes(aux_s, lse_s, delta_s):
    lane = lax.broadcasted_iota(jnp.int32, (INFO_ROWS, ROW_TILE), 1)
    for shard in range(KEY_VALUE_HEADS // 2):
        low = aux_s[2 * shard].astype(jnp.float32)
        high = aux_s[2 * shard + 1].astype(jnp.float32)
        half = ROW_TILE // 2
        middle = jnp.where(
            lane < half, low[:, ROW_TILE:], pltpu.roll(high[:, :ROW_TILE], half, axis=1)
        )
        last = pltpu.roll(high, AUX_LANES - half, axis=1)[:, :ROW_TILE]
        for t, rows in enumerate((low[:, :ROW_TILE], middle, last)):
            row = SHARD_TILES * shard + t
            for h in range(GROUP):
                columns = slice(h * ROW_TILE, (h + 1) * ROW_TILE)
                lse_s[row : row + 1, columns] = rows[h : h + 1] * LOG2E
                delta_s[row : row + 1, columns] = rows[DELTA_ROW + h : DELTA_ROW + 1 + h]


def row_tile(tile, q_s, do_s, lse_s, delta_s):
    def stack(ref):
        rows = ref[pl.ds(pl.multiple_of(tile * ROW_TILE, ROW_TILE), ROW_TILE), :]
        return jnp.concatenate(
            [rows[:, h * HEAD_SIZE : (h + 1) * HEAD_SIZE] for h in range(GROUP)], axis=0
        )

    return stack(q_s), stack(do_s), lse_s[pl.ds(tile, 1), :], delta_s[pl.ds(tile, 1), :]


def tile_step(key, value, key_t, rows, position, bound, acc_k, acc_v, add_dq):
    q, do, lse, delta = rows
    scale = HEAD_SIZE ** (-0.5)
    dims = (((1,), (1,)), ((), ()))
    scores = lax.dot_general(key, q, dims, preferred_element_type=jnp.float32)
    prob = jnp.where(position <= bound, jnp.exp2(scores * (scale * LOG2E) - lse), 0.0)
    dprob = lax.dot_general(value, do, dims, preferred_element_type=jnp.float32)
    dscore = (prob * (dprob - delta)).astype(jnp.bfloat16)
    acc_v[...] += jnp.dot(prob.astype(jnp.bfloat16), do, preferred_element_type=jnp.float32)
    acc_k[...] += jnp.dot(dscore, q, preferred_element_type=jnp.float32)
    add_dq(jnp.dot(key_t, dscore, preferred_element_type=jnp.float32))


def attention_kernel(first, me_ref, counts_ref, *rest):
    aux_s, arrays, kvs, rest = rest[0], rest[1:10], rest[10:12], rest[12:]
    arrays = (*arrays[:3], arrays[3:6], arrays[6:9])
    if first:
        far, downs, dqt_out, full_ref, rest = 2, rest[:2], rest[2], rest[3], rest[4:]
    else:
        dqt_in, far, downs, rest = rest[0], 1, rest[1:2], rest[2:]
        dq_out, own_out, full_ref, rest = rest[0], rest[1], rest[2], rest[3:]
    (
        q_s, do_s, lse_s, delta_s, dqt, kv_s, acc_k, acc_v, tiles, starts, limits, sems,
        kv_sem, down_sem, dqt_sem, down_s,
    ) = rest[:16]
    if not first:
        out_sem, dq_s, own, before = rest[16:]
    capacity = downs[0].shape[0] - INFO_ROWS
    scale = HEAD_SIZE ** (-0.5)
    each = load_rows(me_ref[0], counts_ref, arrays, q_s, do_s, sems)
    each(lambda copy: copy.start())
    kv_copies = [
        pltpu.make_async_copy(source, kv_s.at[n], kv_sem.at[n])
        for n, source in enumerate(kvs)
    ]
    for copy in kv_copies:
        copy.start()
    length, total = list_tiles(counts_ref, tiles, starts)

    def each_tile(act):
        def step(n, carry):
            act(n, tiles[n])
            return carry

        lax.fori_loop(0, length, step, 0)

    def zero_tile(n, tile):
        dqt[tile] = jnp.zeros(dqt.shape[1:], jnp.float32)

    each_tile(zero_tile)
    spread_lanes(aux_s, lse_s, delta_s)
    if not first:

        def load(n, tile):
            return pltpu.make_async_copy(dqt_in.at[tile], before.at[tile], dqt_sem.at[n])

        each_tile(lambda n, tile: load(n, tile).start())
        own[...] = jnp.zeros_like(own)
    for copy in kv_copies:
        copy.wait()
    most = total
    for n in range(far):
        info = kv_s[n, capacity:, :].astype(jnp.float32)
        limit = (jnp.max(info[0:1]) * 64.0 + jnp.max(info[1:2])).astype(jnp.int32)
        limits[n] = jnp.minimum(limit, capacity)
        most = jnp.maximum(most, limit)
    full_ref[0] = (most > capacity).astype(jnp.int32)
    for n in range(far):
        down_s[n, capacity:, :] = jnp.full(
            (INFO_ROWS, 2 * HEAD_SIZE), jnp.where(most > capacity, 1.0, 0.0)
        ).astype(jnp.bfloat16)
    each(lambda copy: copy.wait())
    lane = lax.broadcasted_iota(jnp.int32, (1, WIDTH), 1) % ROW_TILE

    def block_step(step, carry):
        index = far - 1 - step
        limit = limits[index]

        def run(rows):
            key = kv_s[index, :rows, :HEAD_SIZE]
            value = kv_s[index, :rows, HEAD_SIZE:]
            key_t = key.T
            acc_k[:rows] = jnp.zeros((rows, HEAD_SIZE), jnp.float32)
            acc_v[:rows] = jnp.zeros((rows, HEAD_SIZE), jnp.float32)
            position = lax.broadcasted_iota(jnp.int32, (rows, 1), 0)

            def row_step(n, inner):
                tile = tiles[n]
                shard = tile // SHARD_TILES
                count = counts_ref[2 * shard] + counts_ref[2 * shard + 1]
                alive = lane < count - (tile % SHARD_TILES) * ROW_TILE
                bound = jnp.where(alive, limit - 1, -1)

                def add_dq(part):
                    dqt[tile] += part

                tile_step(
                    key, value, key_t, row_tile(tile, q_s, do_s, lse_s, delta_s), position, bound,
                    acc_k.at[pl.ds(0, rows), :], acc_v.at[pl.ds(0, rows), :], add_dq,
                )
                return inner

            lax.fori_loop(0, length, row_step, 0)
            down_s[index, :rows, :HEAD_SIZE] = (acc_k[:rows] * scale).astype(jnp.bfloat16)
            down_s[index, :rows, HEAD_SIZE:] = acc_v[:rows].astype(jnp.bfloat16)
            if rows < capacity:
                down_s[index, rows:capacity, :] = jnp.zeros(
                    (capacity - rows, 2 * HEAD_SIZE), jnp.bfloat16
                )

        below = 0
        for rows in PASS_ROWS:

            @pl.when((limit > below) & (limit <= rows))
            def _():
                run(rows)

            below = rows

        @pl.when(limit == 0)
        def _():
            down_s[index, :capacity, :] = jnp.zeros((capacity, 2 * HEAD_SIZE), jnp.bfloat16)

        return carry

    lax.fori_loop(0, far, block_step, 0)
    down_copies = [
        pltpu.make_async_copy(down_s.at[n], downs[n], down_sem.at[n]) for n in range(far)
    ]
    for copy in down_copies:
        copy.start()

    if first:

        def save(n, tile):
            return pltpu.make_async_copy(dqt.at[tile], dqt_out.at[tile], dqt_sem.at[n])

        each_tile(lambda n, tile: save(n, tile).start())
        for copy in down_copies:
            copy.wait()
        each_tile(lambda n, tile: save(n, tile).wait())
        return

    limit = jnp.minimum(total, capacity)

    def key_step(kt, carry):
        start = pl.multiple_of(kt * KEY_TILE, KEY_TILE)
        key = kv_s[1, pl.ds(start, KEY_TILE), :HEAD_SIZE]
        value = kv_s[1, pl.ds(start, KEY_TILE), HEAD_SIZE:]
        key_t = key.T
        own_k = acc_k.at[pl.ds(0, KEY_TILE), :]
        own_v = acc_v.at[pl.ds(0, KEY_TILE), :]
        own_k[...] = jnp.zeros_like(own_k)
        own_v[...] = jnp.zeros_like(own_v)
        position = start + lax.broadcasted_iota(jnp.int32, (KEY_TILE, 1), 0)

        def row_step(n, inner):
            tile = tiles[n]
            shard = tile // SHARD_TILES
            offset = (tile % SHARD_TILES) * ROW_TILE
            count = counts_ref[2 * shard] + counts_ref[2 * shard + 1]
            first = starts[shard] + offset

            @pl.when(first + ROW_TILE > start)
            def _():
                bound = jnp.where(lane < count - offset, first + lane, -1)

                def add_dq(part):
                    dqt[tile] += part

                tile_step(
                    key, value, key_t, row_tile(tile, q_s, do_s, lse_s, delta_s), position, bound,
                    own_k, own_v, add_dq,
                )

            return inner

        lax.fori_loop(0, length, row_step, 0)
        own[pl.ds(start, KEY_TILE), :HEAD_SIZE] = own_k[...] * scale
        own[pl.ds(start, KEY_TILE), HEAD_SIZE:] = own_v[...]
        return carry

    lax.fori_loop(0, (limit + KEY_TILE - 1) // KEY_TILE, key_step, 0)
    own_copy = pltpu.make_async_copy(own, own_out, down_sem.at[1])
    own_copy.start()
    each_tile(lambda n, tile: load(n, tile).wait())

    half = ROW_TILE // 2
    copies = []
    for block in range(KEY_VALUE_HEADS):
        shard = block // 2
        count = counts_ref[2 * shard] + counts_ref[2 * shard + 1]
        if block % 2 == 0:
            pieces = ((0, ROW_TILE, 0, 0), (ROW_TILE, half, 1, 0))
        else:
            pieces = ((0, half, 1, half), (half, ROW_TILE, 2, 0))
        for offset, size, t, first in pieces:
            live = count > t * ROW_TILE
            rows = slice(offset, offset + size)

            @pl.when(live)
            def _():
                for h in range(GROUP):
                    columns = slice(h * HEAD_SIZE, (h + 1) * HEAD_SIZE)
                    tile = SHARD_TILES * shard + t
                    part = ((dqt[tile, :, columns] + before[tile, :, columns]) * scale).T
                    dq_s[block, rows, columns] = part[first : first + size].astype(jnp.bfloat16)

            @pl.when(jnp.logical_not(live))
            def _():
                dq_s[block, rows, :] = jnp.zeros((size, WIDTH), jnp.bfloat16)

        copy = pltpu.make_async_copy(dq_s.at[block], dq_out.at[block], out_sem.at[block])
        copy.start()
        copies.append(copy)
    for copy in (*copies, *down_copies, own_copy):
        copy.wait()


def row_scratch(plane_rows):
    bf16, f32 = jnp.bfloat16, jnp.float32
    tile_count = plane_rows // ROW_TILE
    return [
        pltpu.VMEM((plane_rows, WIDTH), bf16),
        pltpu.VMEM((plane_rows, WIDTH), bf16),
        pltpu.VMEM((tile_count, WIDTH), f32),
        pltpu.VMEM((tile_count, WIDTH), f32),
        pltpu.VMEM((tile_count, HEAD_SIZE, WIDTH), f32),
    ]


def attention(first, me, counts, small, arrays, kvs, *before):
    bf16, f32 = jnp.bfloat16, jnp.float32
    blocks = KEY_VALUE_HEADS
    rows = kvs[0].shape[0]
    capacity = rows - INFO_ROWS
    columns = 2 * HEAD_SIZE
    plane_rows = 2 * capacity
    tile_count = plane_rows // ROW_TILE
    dq = (blocks, plane_rows // blocks, WIDTH)
    dqt = (tile_count, HEAD_SIZE, WIDTH)
    down = jax.ShapeDtypeStruct((rows, columns), bf16)
    flag = jax.ShapeDtypeStruct((1,), jnp.int32)
    if first:
        outs = (down, down, jax.ShapeDtypeStruct(dqt, f32), flag)
        more = []
    else:
        own = jax.ShapeDtypeStruct((capacity, columns), f32)
        outs = (down, jax.ShapeDtypeStruct(dq, bf16), own, flag)
        more = [
            pltpu.SemaphoreType.DMA((blocks,)),
            pltpu.VMEM(dq, bf16),
            pltpu.VMEM((capacity, columns), f32),
            pltpu.VMEM(dqt, f32),
        ]
    return pl.pallas_call(
        functools.partial(attention_kernel, first),
        out_shape=outs,
        in_specs=[SMEM] * 2 + [VMEM] + [HBM] * (11 + len(before)),
        out_specs=[HBM] * 3 + [SMEM],
        scratch_shapes=[
            pltpu.VMEM((plane_rows, WIDTH), bf16),
            pltpu.VMEM((plane_rows, WIDTH), bf16),
            pltpu.VMEM((tile_count, WIDTH), f32),
            pltpu.VMEM((tile_count, WIDTH), f32),
            pltpu.VMEM(dqt, f32),
            pltpu.VMEM((2, rows, columns), bf16),
            pltpu.VMEM((capacity, HEAD_SIZE), f32),
            pltpu.VMEM((capacity, HEAD_SIZE), f32),
            pltpu.SMEM((tile_count + 1,), jnp.int32),
            pltpu.SMEM((blocks,), jnp.int32),
            pltpu.SMEM((2,), jnp.int32),
            pltpu.SemaphoreType.DMA((2 * blocks,)),
            pltpu.SemaphoreType.DMA((2,)),
            pltpu.SemaphoreType.DMA((2,)),
            pltpu.SemaphoreType.DMA((tile_count,)),
            pltpu.VMEM((2, rows, columns), bf16),
            *more,
        ],
        compiler_params=pltpu.CompilerParams(vmem_limit_bytes=48 * 1024 * 1024),
        cost_estimate=pl.CostEstimate(
            flops=5_000_000_000, bytes_accessed=12_000_000, transcendentals=4_000_000
        ),
        name="attention",
    )(me, counts, small, *arrays, *kvs, *before)


def unpack_rows_kernel(parts, out):
    for g in range(KEY_VALUE_HEADS):
        out[:, g * WIDTH : (g + 1) * WIDTH] = parts[g]


def unpack_rows(parts):
    return pl.pallas_call(
        unpack_rows_kernel,
        out_shape=jax.ShapeDtypeStruct((parts.shape[1], KEY_VALUE_HEADS * WIDTH), parts.dtype),
        in_specs=[VMEM],
        out_specs=VMEM,
        name="unpack_rows",
    )(parts)


def combine_kernel(counts_ref, own, *rest):
    backs, out = rest[:3], rest[3]
    home_rows = out.shape[1]
    capacity = own.shape[0]
    total = own[...]
    for back in backs:
        total += back[:capacity, :].astype(jnp.float32)
    total = total.astype(jnp.bfloat16)
    within = lax.broadcasted_iota(jnp.int32, (home_rows, capacity), 0)
    place = lax.broadcasted_iota(jnp.int32, (home_rows, capacity), 1)
    start = jnp.int32(0)
    for block in range(KEY_VALUE_HEADS):
        count = counts_ref[block]
        hit = (place == within + start) & (within < count)
        out[block] = jnp.dot(
            jnp.where(hit, 1.0, 0.0).astype(jnp.bfloat16),
            total,
            preferred_element_type=jnp.float32,
        ).astype(jnp.bfloat16)
        start = start + count


def combine(counts, own, backs, home_rows):
    blocks = KEY_VALUE_HEADS
    return pl.pallas_call(
        combine_kernel,
        out_shape=jax.ShapeDtypeStruct((blocks, home_rows, own.shape[1]), jnp.bfloat16),
        in_specs=[SMEM] + [VMEM] * 4,
        out_specs=VMEM,
        compiler_params=pltpu.CompilerParams(vmem_limit_bytes=32 * 1024 * 1024),
        name="combine",
    )(counts, own, *backs)


def plane_device(queries, keys, values, outputs, output_gradient, lse, ranks):
    planes = lax.axis_size("outer")
    plane = ("inner", "head")
    blocks = KEY_VALUE_HEADS
    home_rows = queries.shape[0]
    plane_rows = blocks * home_rows
    capacity = plane_rows // 2
    surviving_tokens = BALANCED_TOKENS * planes * lax.axis_size("inner")
    bf16, f32 = jnp.bfloat16, jnp.float32
    me = lax.axis_index(plane).reshape(1).astype(jnp.int32)

    def swap(array, k):
        return lax.ppermute(array, plane, [(i, i ^ k) for i in range(blocks)])

    sent = pack_pairs(
        surviving_tokens, ranks, lse, keys, values, output_gradient, outputs
    )
    me, sent = lax.optimization_barrier((me, sent))
    arrived = lax.all_to_all(sent, plane, split_axis=0, concat_axis=0, tiled=True)
    *packed, beside = pack_rows(me, queries, output_gradient)
    pairs = [swap(rows, chip) for rows, chip in zip(packed, CHIPS)]
    beside = swap(beside, CORE)
    arrived, beside = lax.optimization_barrier((arrived, beside))
    mine, small, counts = compact(arrived)
    up = [lax.ppermute(mine, "outer", [(i, i + 1) for i in range(planes - 1)])]
    last = lax.ppermute(mine, "outer", [(0, planes - 1)])
    up.append(lax.ppermute(up[0], "outer", [(i, i + 1) for i in range(1, planes - 1)]))
    up.append(last)
    up[1], up[2], *pairs = lax.optimization_barrier((up[1], up[2], *pairs))
    crossed = [swap(pair[1:], CORE) for pair in pairs]
    arrays = [queries, output_gradient, beside, *pairs, *crossed]

    def lower(rows, k):
        return lax.ppermute(rows, "outer", [(i + k, i) for i in range(planes - k)])

    down2, down3, dqt, full1 = attention(True, me, counts, small, arrays, [up[1], up[2]])
    back2 = lower(down2, 2)
    down1, dq, own, full2 = attention(False, me, counts, small, arrays, [up[0], mine], dqt)
    dq, back2 = lax.optimization_barrier((dq, back2))
    backs = [lower(down3, 3), back2, lower(down1, 1)]
    dq = lax.all_to_all(dq, plane, split_axis=0, concat_axis=0, tiled=True)
    spread = combine(counts, own, backs, home_rows)
    dq, spread = lax.optimization_barrier((dq, spread))
    dq_home = unpack_rows(dq)
    kv_home = lax.all_to_all(spread, plane, split_axis=0, concat_axis=0, tiled=True)
    full = (full1[0] + full2[0]) > 0
    for back in backs:
        full = full | (back[capacity, 0] > 0)
    dk = kv_home[:, :, :HEAD_SIZE].transpose(1, 0, 2).reshape(home_rows, blocks * HEAD_SIZE)
    dv = kv_home[:, :, HEAD_SIZE:].transpose(1, 0, 2).reshape(home_rows, blocks * HEAD_SIZE)
    return (dq_home, dk, dv), full


def solution(mesh):
    spec = P(("seq", "head"), None)
    heads = mesh.shape["head"]
    inner = max(KEY_VALUE_HEADS // heads, 1)
    planes = mesh.shape["seq"] // inner
    if planes != 4 or inner * heads != KEY_VALUE_HEADS:
        return jax.shard_map(
            per_device,
            mesh=mesh,
            in_specs=(spec,) * 6 + (P(("seq", "head")),),
            out_specs=(spec,) * 3,
            check_vma=False,
        )
    axes = ("outer", "inner", "head")

    def device(*blocks):
        fast, full = plane_device(*blocks)
        return lax.cond(full, lambda: per_device(*blocks, seq=("outer", "inner")), lambda: fast)

    return jax.shard_map(
        device,
        mesh=Mesh(mesh.devices.reshape(planes, inner, heads), axes),
        in_specs=(P(axes, None),) * 6 + (P(axes),),
        out_specs=(P(axes, None),) * 3,
        check_vma=False,
    )
```

```python
import functools

import jax
import jax.numpy as jnp
from jax import lax
from jax.experimental import pallas as pl
from jax.experimental.pallas import tpu as pltpu
from jax.sharding import Mesh
from jax.sharding import PartitionSpec as P

QUERY_HEADS = 40
KEY_VALUE_HEADS = 8
HEAD_SIZE = 128
BALANCED_TOKENS = 128


block_keys = 512


def gather(array, axis):
    count = lax.axis_size(axis)
    copies = jnp.broadcast_to(array[None], (count, *array.shape))
    got = lax.all_to_all(copies, axis, split_axis=0, concat_axis=0, tiled=True)
    return got.reshape(count * array.shape[0], *array.shape[1:])


def per_device(queries, keys, values, outputs, output_gradient, lse, ranks, seq="seq"):
    sequence_count = lax.axis_size(seq)
    head_total = lax.axis_size("head")
    home_rows = queries.shape[0]
    capacity = home_rows * head_total
    slots = capacity // sequence_count
    surviving_tokens = BALANCED_TOKENS * sequence_count
    group_size = QUERY_HEADS // KEY_VALUE_HEADS
    local_key_value = KEY_VALUE_HEADS // head_total
    scale = HEAD_SIZE ** (-0.5)

    def split_heads(array):
        return array.reshape(home_rows, head_total, array.shape[1] // head_total)

    moved = (
        lax.all_to_all(split_heads(queries), "head", split_axis=1, concat_axis=0, tiled=True),
        lax.all_to_all(split_heads(keys), "head", split_axis=1, concat_axis=0, tiled=True),
        lax.all_to_all(split_heads(values), "head", split_axis=1, concat_axis=0, tiled=True),
        lax.all_to_all(
            split_heads(output_gradient), "head", split_axis=1, concat_axis=0, tiled=True
        ),
        lax.all_to_all(split_heads(lse), "head", split_axis=1, concat_axis=0, tiled=True),
        lax.all_to_all(split_heads(outputs), "head", split_axis=1, concat_axis=0, tiled=True),
    )
    shard_rank_list = gather(ranks, "head")
    first_rank = shard_rank_list[0]
    living_count = jnp.sum((shard_rank_list < surviving_tokens).astype(jnp.int32))
    table = gather(jnp.stack([first_rank, living_count])[None, :], seq)

    def to_pairs(array):
        flat = array.reshape(slots, sequence_count, array.shape[-1])
        return jnp.roll(flat, first_rank, axis=1)

    arrived = (
        lax.all_to_all(to_pairs(moved[0]), seq, split_axis=1, concat_axis=1, tiled=True),
        lax.all_to_all(to_pairs(moved[1]), seq, split_axis=1, concat_axis=1, tiled=True),
        lax.all_to_all(to_pairs(moved[2]), seq, split_axis=1, concat_axis=1, tiled=True),
        lax.all_to_all(to_pairs(moved[3]), seq, split_axis=1, concat_axis=1, tiled=True),
        lax.all_to_all(to_pairs(moved[4]), seq, split_axis=1, concat_axis=1, tiled=True),
        lax.all_to_all(to_pairs(moved[5]), seq, split_axis=1, concat_axis=1, tiled=True),
    )
    my_index = lax.axis_index(seq)
    starts = table[:, 0]
    count_table = table[:, 1]
    offset = (my_index - starts) % sequence_count
    within = jnp.arange(slots, dtype=jnp.int32)[:, None] * sequence_count + offset[None, :]
    alive = within < count_table[None, :]
    target_rank = jnp.where(
        alive, (starts[None, :] + within) // sequence_count, BALANCED_TOKENS
    ).reshape(-1)

    def place(array):
        width = array.shape[-1]
        return (
            jnp.zeros((BALANCED_TOKENS, width), array.dtype)
            .at[target_rank]
            .set(array.reshape(slots * sequence_count, width), mode="drop")
        )

    query_row_block = place(arrived[0]).reshape(
        BALANCED_TOKENS, local_key_value, group_size, HEAD_SIZE
    )
    key_row_block = place(arrived[1]).reshape(BALANCED_TOKENS, local_key_value, HEAD_SIZE)
    value_row_block = place(arrived[2]).reshape(BALANCED_TOKENS, local_key_value, HEAD_SIZE)
    grad_rows = place(arrived[3]).reshape(BALANCED_TOKENS, local_key_value, group_size, HEAD_SIZE)
    lse_rows = (
        place(arrived[4]).astype(jnp.float32).reshape(BALANCED_TOKENS, local_key_value, group_size)
    )
    out_rows = (
        place(arrived[5])
        .astype(jnp.float32)
        .reshape(BALANCED_TOKENS, local_key_value, group_size, HEAD_SIZE)
    )
    delta_rows = (
        jnp.sum(grad_rows.astype(jnp.float32) * out_rows, axis=-1)
        .astype(jnp.bfloat16)
        .astype(jnp.float32)
    )
    gathered = (
        gather(key_row_block, seq),
        gather(value_row_block, seq),
    )
    all_keys = gathered[0].reshape(sequence_count, BALANCED_TOKENS, local_key_value, HEAD_SIZE)
    all_values = gathered[1].reshape(sequence_count, BALANCED_TOKENS, local_key_value, HEAD_SIZE)
    rows_per = block_keys // sequence_count
    inner = 1
    outer = BALANCED_TOKENS // rows_per // inner
    query_rank = jnp.arange(BALANCED_TOKENS, dtype=jnp.int32) * sequence_count + my_index
    lse_t = lse_rows.transpose(1, 2, 0)
    delta_t = delta_rows.transpose(1, 2, 0)
    position = jnp.arange(sequence_count * rows_per, dtype=jnp.int32)

    def key_step(query_acc, row_start):
        key_blk = lax.dynamic_slice_in_dim(all_keys, row_start, rows_per, 1).reshape(
            sequence_count * rows_per, local_key_value, HEAD_SIZE
        )
        value_blk = lax.dynamic_slice_in_dim(all_values, row_start, rows_per, 1).reshape(
            sequence_count * rows_per, local_key_value, HEAD_SIZE
        )
        key_owner_rank = (row_start + position % rows_per) * sequence_count + position // rows_per
        mask = key_owner_rank[None, None, None, :] <= query_rank[None, None, :, None]
        scores = (
            jnp.einsum(
                "rgmc,kgc->gmrk", query_row_block, key_blk, preferred_element_type=jnp.float32
            )
            * scale
        )
        probs = jnp.where(mask, jnp.exp(scores - lse_t[..., None]), 0.0)
        dprob = jnp.einsum(
            "rgmc,kgc->gmrk", grad_rows, value_blk, preferred_element_type=jnp.float32
        )
        dscore = probs * (dprob - delta_t[..., None])
        probs_low = probs.astype(jnp.bfloat16)
        dscore_low = dscore.astype(jnp.bfloat16)
        query_acc = query_acc + scale * jnp.einsum(
            "gmrk,kgc->rgmc", dscore_low, key_blk, preferred_element_type=jnp.float32
        )
        key_part = scale * jnp.einsum(
            "gmrk,rgmc->kgc", dscore_low, query_row_block, preferred_element_type=jnp.float32
        )
        value_part = jnp.einsum(
            "gmrk,rgmc->kgc", probs_low, grad_rows, preferred_element_type=jnp.float32
        )
        return (
            query_acc,
            key_part.reshape(sequence_count, rows_per, local_key_value * HEAD_SIZE),
            value_part.reshape(sequence_count, rows_per, local_key_value * HEAD_SIZE),
        )

    def outer_step(query_acc, outer_index):

        def inner_step(query_inner, inner_index):
            row_start = (outer_index * inner + inner_index) * rows_per
            query_new, key_part, value_part = key_step(query_inner, row_start)
            return (query_new, (key_part, value_part))

        query_acc, (key_parts, value_parts) = lax.scan(
            inner_step, query_acc, jnp.arange(inner, dtype=jnp.int32)
        )
        key_parts = key_parts.transpose(1, 0, 2, 3).reshape(
            sequence_count, inner * rows_per, local_key_value * HEAD_SIZE
        )
        value_parts = value_parts.transpose(1, 0, 2, 3).reshape(
            sequence_count, inner * rows_per, local_key_value * HEAD_SIZE
        )
        received = (
            lax.all_to_all(key_parts, seq, split_axis=0, concat_axis=0, tiled=True),
            lax.all_to_all(value_parts, seq, split_axis=0, concat_axis=0, tiled=True),
        )
        return (query_acc, (jnp.sum(received[0], axis=0), jnp.sum(received[1], axis=0)))

    start_acc = jnp.zeros((BALANCED_TOKENS, local_key_value, group_size, HEAD_SIZE), jnp.float32)
    query_acc, (key_sums, value_sums) = lax.scan(
        outer_step, start_acc, jnp.arange(outer, dtype=jnp.int32)
    )
    query_done = query_acc.reshape(
        BALANCED_TOKENS, local_key_value * group_size * HEAD_SIZE
    ).astype(jnp.bfloat16)
    key_done = key_sums.reshape(BALANCED_TOKENS, local_key_value * HEAD_SIZE).astype(jnp.bfloat16)
    value_done = value_sums.reshape(BALANCED_TOKENS, local_key_value * HEAD_SIZE).astype(
        jnp.bfloat16
    )
    safe_rows = jnp.minimum(target_rank, BALANCED_TOKENS - 1)
    alive_flat = alive.reshape(-1)

    def collect(array):
        picked = jnp.where(alive_flat[:, None], array[safe_rows], jnp.zeros((), array.dtype))
        return picked.reshape(slots, sequence_count, array.shape[-1])

    returned = (
        lax.all_to_all(collect(query_done), seq, split_axis=1, concat_axis=1, tiled=True),
        lax.all_to_all(collect(key_done), seq, split_axis=1, concat_axis=1, tiled=True),
        lax.all_to_all(collect(value_done), seq, split_axis=1, concat_axis=1, tiled=True),
    )

    def to_home(array):
        unrolled = jnp.roll(array, -first_rank, axis=1)
        return unrolled.reshape(capacity, 1, array.shape[-1])

    homed = (
        lax.all_to_all(to_home(returned[0]), "head", split_axis=0, concat_axis=1, tiled=True),
        lax.all_to_all(to_home(returned[1]), "head", split_axis=0, concat_axis=1, tiled=True),
        lax.all_to_all(to_home(returned[2]), "head", split_axis=0, concat_axis=1, tiled=True),
    )
    query_grads = homed[0].reshape(home_rows, head_total * homed[0].shape[-1])
    key_gradient_output = homed[1].reshape(home_rows, head_total * homed[1].shape[-1])
    value_gradient = homed[2].reshape(home_rows, head_total * homed[2].shape[-1])
    return (query_grads, key_gradient_output, value_gradient)

LOG2E = 1.4426950408889634
KEY_TILE = 256
ROW_TILE = 128
INFO_ROWS = 16
AUX_LANES = 256
DELTA_ROW = 8
SMEM = pl.BlockSpec(memory_space=pltpu.SMEM)
VMEM = pl.BlockSpec(memory_space=pltpu.VMEM)
HBM = pl.BlockSpec(memory_space=pltpu.HBM)
GROUP = QUERY_HEADS // KEY_VALUE_HEADS
WIDTH = GROUP * HEAD_SIZE
CHIPS = (5, 4, 1)
CORE = 2
SHARD_TILES = 3
PASS_ROWS = (256, 512, 768)


def pack_pairs_kernel(limit, ranks_ref, lse_ref, k_ref, v_ref, do_ref, o_ref, out_ref, columns):
    home_rows = k_ref.shape[0]
    columns[...] = jnp.zeros_like(columns)
    for h in range(QUERY_HEADS):
        head = slice(h * HEAD_SIZE, (h + 1) * HEAD_SIZE)
        product = do_ref[:, head].astype(jnp.float32) * o_ref[:, head].astype(jnp.float32)
        column = 8 * (h // GROUP) + h % GROUP
        columns[:, column : column + 1] = jnp.sum(product, axis=1, keepdims=True)
    delta = columns[...].T
    lse = lse_ref[...].astype(jnp.float32)
    live = jnp.where(ranks_ref[...] < limit, 1.0, 0.0)
    count = jnp.broadcast_to(jnp.sum(live, axis=1, keepdims=True), (8 - GROUP, home_rows))
    for g in range(KEY_VALUE_HEADS):
        head = slice(g * HEAD_SIZE, (g + 1) * HEAD_SIZE)
        out_ref[g, :home_rows, :HEAD_SIZE] = k_ref[:, head]
        out_ref[g, :home_rows, HEAD_SIZE:] = v_ref[:, head]
        info = jnp.concatenate(
            [lse[g * GROUP : (g + 1) * GROUP], count, delta[8 * g : 8 * g + 8]], axis=0
        )
        out_ref[g, home_rows:, :home_rows] = info.astype(out_ref.dtype)


def pack_pairs(limit, ranks, lse, keys, values, output_gradient, outputs):
    home_rows = keys.shape[0]
    return pl.pallas_call(
        functools.partial(pack_pairs_kernel, limit),
        out_shape=jax.ShapeDtypeStruct(
            (KEY_VALUE_HEADS, home_rows + INFO_ROWS, 2 * HEAD_SIZE), keys.dtype
        ),
        in_specs=[VMEM] * 6,
        out_specs=VMEM,
        scratch_shapes=[pltpu.VMEM((home_rows, HEAD_SIZE), jnp.float32)],
        compiler_params=pltpu.CompilerParams(vmem_limit_bytes=32 * 1024 * 1024),
        name="pack_pairs",
    )(ranks.reshape(1, home_rows), lse.T, keys, values, output_gradient, outputs)


def pack_rows_kernel(me_ref, q_ref, do_ref, *outs):
    me = me_ref[0]
    for out, partners in zip(outs, [(chip, chip ^ CORE) for chip in CHIPS] + [(CORE,)]):
        for n, partner in enumerate(partners):
            start = pl.multiple_of((me ^ partner) * WIDTH, HEAD_SIZE)
            out[n, :, :WIDTH] = q_ref[:, pl.ds(start, WIDTH)]
            out[n, :, WIDTH:] = do_ref[:, pl.ds(start, WIDTH)]


def pack_rows(me, queries, output_gradient):
    home_rows = queries.shape[0]
    pair = jax.ShapeDtypeStruct((2, home_rows, 2 * WIDTH), queries.dtype)
    beside = jax.ShapeDtypeStruct((1, home_rows, 2 * WIDTH), queries.dtype)
    return pl.pallas_call(
        pack_rows_kernel,
        out_shape=(pair, pair, pair, beside),
        in_specs=[SMEM] + [VMEM] * 2,
        out_specs=[VMEM] * 4,
        compiler_params=pltpu.CompilerParams(vmem_limit_bytes=32 * 1024 * 1024),
        name="pack_rows",
    )(me, queries, output_gradient)


def compact_kernel(arrived, out, small, counts_ref):
    home_rows = arrived.shape[1] - INFO_ROWS
    capacity = out.shape[0] - INFO_ROWS
    row = lax.broadcasted_iota(jnp.int32, (capacity, home_rows), 0)
    within = lax.broadcasted_iota(jnp.int32, (capacity, home_rows), 1)
    total = jnp.int32(0)
    picked = []
    for block in range(KEY_VALUE_HEADS):
        info = arrived[block, home_rows:, :]
        small[block] = info
        count = jnp.max(info.astype(jnp.float32)[GROUP : GROUP + 1, :home_rows]).astype(jnp.int32)
        counts_ref[block] = count
        hit = (row == within + total) & (within < count)
        picked.append(jnp.where(hit, 1.0, 0.0).astype(jnp.bfloat16))
        total = total + count
    acc = jnp.zeros((capacity, out.shape[1]), jnp.float32)
    for block in range(KEY_VALUE_HEADS):
        acc += jnp.dot(
            picked[block], arrived[block, :home_rows, :], preferred_element_type=jnp.float32
        )
    out[:capacity, :] = acc.astype(out.dtype)
    line = lax.broadcasted_iota(jnp.int32, (INFO_ROWS, out.shape[1]), 0)
    out[capacity:, :] = (
        jnp.where(line == 0, total // 64, jnp.where(line == 1, total % 64, 0))
        .astype(jnp.float32)
        .astype(out.dtype)
    )


def compact(arrived):
    blocks, rows, columns = arrived.shape
    capacity = blocks * (rows - INFO_ROWS) // 2
    return pl.pallas_call(
        compact_kernel,
        out_shape=(
            jax.ShapeDtypeStruct((capacity + INFO_ROWS, columns), arrived.dtype),
            jax.ShapeDtypeStruct((blocks, INFO_ROWS, columns), arrived.dtype),
            jax.ShapeDtypeStruct((blocks,), jnp.int32),
        ),
        in_specs=[VMEM],
        out_specs=(VMEM, VMEM, SMEM),
        compiler_params=pltpu.CompilerParams(vmem_limit_bytes=32 * 1024 * 1024),
        name="compact",
    )(arrived)


def load_rows(me, counts_ref, arrays, q_s, do_s, sems):
    home_rows = q_s.shape[0] // KEY_VALUE_HEADS
    q_hbm, do_hbm, beside, pairs, crossed = arrays
    column = pl.ds(pl.multiple_of(me * WIDTH, HEAD_SIZE), WIDTH)
    left, right = pl.ds(0, WIDTH), pl.ds(WIDTH, WIDTH)
    sources = [
        (0, q_hbm.at[:, column], do_hbm.at[:, column]),
        (CORE, beside.at[0, :, left], beside.at[0, :, right]),
    ]
    for chip, pair, cross in zip(CHIPS, pairs, crossed):
        sources.append((chip, pair.at[0, :, left], pair.at[0, :, right]))
        sources.append((chip ^ CORE, cross.at[0, :, left], cross.at[0, :, right]))
    plans = []
    for n, (partner, q, do) in enumerate(sources):
        source = me ^ partner
        rows = pl.ds(pl.multiple_of(source * home_rows, 64), home_rows)
        shard = counts_ref[source & ~1] + counts_ref[source | 1]
        needed = ((source & 1) == 0) | (shard > ROW_TILE)
        plans.append(
            (
                needed,
                [
                    pltpu.make_async_copy(q, q_s.at[rows, :], sems.at[2 * n]),
                    pltpu.make_async_copy(do, do_s.at[rows, :], sems.at[2 * n + 1]),
                ],
            )
        )

    def each(act):
        for needed, copies in plans:

            @pl.when(needed)
            def _():
                for copy in copies:
                    act(copy)

    return each


def list_tiles(counts_ref, tiles, starts):
    length = jnp.int32(0)
    total = jnp.int32(0)
    for shard in range(KEY_VALUE_HEADS // 2):
        count = counts_ref[2 * shard] + counts_ref[2 * shard + 1]
        starts[shard] = total
        total = total + count
        for t in range(SHARD_TILES):
            live = count > t * ROW_TILE

            @pl.when(live)
            def _():
                tiles[length] = SHARD_TILES * shard + t

            length = length + live.astype(jnp.int32)
    return length, total


def spread_lanes(aux_s, lse_s, delta_s):
    lane = lax.broadcasted_iota(jnp.int32, (INFO_ROWS, ROW_TILE), 1)
    for shard in range(KEY_VALUE_HEADS // 2):
        low = aux_s[2 * shard].astype(jnp.float32)
        high = aux_s[2 * shard + 1].astype(jnp.float32)
        half = ROW_TILE // 2
        middle = jnp.where(
            lane < half, low[:, ROW_TILE:], pltpu.roll(high[:, :ROW_TILE], half, axis=1)
        )
        last = pltpu.roll(high, AUX_LANES - half, axis=1)[:, :ROW_TILE]
        for t, rows in enumerate((low[:, :ROW_TILE], middle, last)):
            row = SHARD_TILES * shard + t
            for h in range(GROUP):
                columns = slice(h * ROW_TILE, (h + 1) * ROW_TILE)
                lse_s[row : row + 1, columns] = rows[h : h + 1] * LOG2E
                delta_s[row : row + 1, columns] = rows[DELTA_ROW + h : DELTA_ROW + 1 + h]


def row_tile(tile, q_s, do_s, lse_s, delta_s):
    def stack(ref):
        rows = ref[pl.ds(pl.multiple_of(tile * ROW_TILE, ROW_TILE), ROW_TILE), :]
        return jnp.concatenate(
            [rows[:, h * HEAD_SIZE : (h + 1) * HEAD_SIZE] for h in range(GROUP)], axis=0
        )

    return stack(q_s), stack(do_s), lse_s[pl.ds(tile, 1), :], delta_s[pl.ds(tile, 1), :]


def tile_step(key, value, key_t, rows, position, bound, acc_k, acc_v, add_dq):
    q, do, lse, delta = rows
    scale = HEAD_SIZE ** (-0.5)
    dims = (((1,), (1,)), ((), ()))
    scores = lax.dot_general(key, q, dims, preferred_element_type=jnp.float32)
    prob = jnp.where(position <= bound, jnp.exp2(scores * (scale * LOG2E) - lse), 0.0)
    dprob = lax.dot_general(value, do, dims, preferred_element_type=jnp.float32)
    dscore = (prob * (dprob - delta)).astype(jnp.bfloat16)
    acc_v[...] += jnp.dot(prob.astype(jnp.bfloat16), do, preferred_element_type=jnp.float32)
    acc_k[...] += jnp.dot(dscore, q, preferred_element_type=jnp.float32)
    add_dq(jnp.dot(key_t, dscore, preferred_element_type=jnp.float32))


def attention_kernel(first, me_ref, counts_ref, *rest):
    aux_s, arrays, kvs, rest = rest[0], rest[1:10], rest[10:12], rest[12:]
    arrays = (*arrays[:3], arrays[3:6], arrays[6:9])
    if first:
        far, downs, dqt_out, full_ref, rest = 2, rest[:2], rest[2], rest[3], rest[4:]
    else:
        dqt_in, far, downs, rest = rest[0], 1, rest[1:2], rest[2:]
        dq_out, own_out, full_ref, rest = rest[0], rest[1], rest[2], rest[3:]
    (
        q_s, do_s, lse_s, delta_s, dqt, kv_s, acc_k, acc_v, tiles, starts, limits, sems,
        kv_sem, down_sem, dqt_sem, down_s,
    ) = rest[:16]
    if not first:
        out_sem, dq_s, own, before = rest[16:]
    capacity = downs[0].shape[0] - INFO_ROWS
    scale = HEAD_SIZE ** (-0.5)
    each = load_rows(me_ref[0], counts_ref, arrays, q_s, do_s, sems)
    each(lambda copy: copy.start())
    kv_copies = [
        pltpu.make_async_copy(source, kv_s.at[n], kv_sem.at[n])
        for n, source in enumerate(kvs)
    ]
    for copy in kv_copies:
        copy.start()
    length, total = list_tiles(counts_ref, tiles, starts)

    def each_tile(act):
        def step(n, carry):
            act(n, tiles[n])
            return carry

        lax.fori_loop(0, length, step, 0)

    def zero_tile(n, tile):
        dqt[tile] = jnp.zeros(dqt.shape[1:], jnp.float32)

    each_tile(zero_tile)
    spread_lanes(aux_s, lse_s, delta_s)
    if not first:

        def load(n, tile):
            return pltpu.make_async_copy(dqt_in.at[tile], before.at[tile], dqt_sem.at[n])

        each_tile(lambda n, tile: load(n, tile).start())
        own[...] = jnp.zeros_like(own)
    for copy in kv_copies:
        copy.wait()
    most = total
    for n in range(far):
        info = kv_s[n, capacity:, :].astype(jnp.float32)
        limit = (jnp.max(info[0:1]) * 64.0 + jnp.max(info[1:2])).astype(jnp.int32)
        limits[n] = jnp.minimum(limit, capacity)
        most = jnp.maximum(most, limit)
    full_ref[0] = (most > capacity).astype(jnp.int32)
    for n in range(far):
        down_s[n, capacity:, :] = jnp.full(
            (INFO_ROWS, 2 * HEAD_SIZE), jnp.where(most > capacity, 1.0, 0.0)
        ).astype(jnp.bfloat16)
    each(lambda copy: copy.wait())
    lane = lax.broadcasted_iota(jnp.int32, (1, WIDTH), 1) % ROW_TILE

    def block_step(step, carry):
        index = far - 1 - step
        limit = limits[index]

        def run(rows):
            key = kv_s[index, :rows, :HEAD_SIZE]
            value = kv_s[index, :rows, HEAD_SIZE:]
            key_t = key.T
            acc_k[:rows] = jnp.zeros((rows, HEAD_SIZE), jnp.float32)
            acc_v[:rows] = jnp.zeros((rows, HEAD_SIZE), jnp.float32)
            position = lax.broadcasted_iota(jnp.int32, (rows, 1), 0)

            def go(chosen):
                parts, bounds = [], []
                for tile in chosen:
                    shard = tile // SHARD_TILES
                    count = counts_ref[2 * shard] + counts_ref[2 * shard + 1]
                    alive = lane < count - (tile % SHARD_TILES) * ROW_TILE
                    parts.append(row_tile(tile, q_s, do_s, lse_s, delta_s))
                    bounds.append(jnp.where(alive, limit - 1, -1))

                def add_dq(part):
                    for m, tile in enumerate(chosen):
                        dqt[tile] += part[:, m * WIDTH : (m + 1) * WIDTH]

                joined = [
                    jnp.concatenate(pieces, axis=axis)
                    for pieces, axis in zip(zip(*parts), (0, 0, 1, 1))
                ]
                tile_step(
                    key, value, key_t, joined, position, jnp.concatenate(bounds, axis=1),
                    acc_k.at[pl.ds(0, rows), :], acc_v.at[pl.ds(0, rows), :], add_dq,
                )

            def pair_step(n, inner):
                go((tiles[2 * n], tiles[2 * n + 1]))
                return inner

            lax.fori_loop(0, length // 2, pair_step, 0)

            @pl.when(length % 2 == 1)
            def _():
                go((tiles[length - 1],))

            down_s[index, :rows, :HEAD_SIZE] = (acc_k[:rows] * scale).astype(jnp.bfloat16)
            down_s[index, :rows, HEAD_SIZE:] = acc_v[:rows].astype(jnp.bfloat16)
            if rows < capacity:
                down_s[index, rows:capacity, :] = jnp.zeros(
                    (capacity - rows, 2 * HEAD_SIZE), jnp.bfloat16
                )

        below = 0
        for rows in PASS_ROWS:

            @pl.when((limit > below) & (limit <= rows))
            def _():
                run(rows)

            below = rows

        @pl.when(limit == 0)
        def _():
            down_s[index, :capacity, :] = jnp.zeros((capacity, 2 * HEAD_SIZE), jnp.bfloat16)

        return carry

    lax.fori_loop(0, far, block_step, 0)
    down_copies = [
        pltpu.make_async_copy(down_s.at[n], downs[n], down_sem.at[n]) for n in range(far)
    ]
    for copy in down_copies:
        copy.start()

    if first:

        def save(n, tile):
            return pltpu.make_async_copy(dqt.at[tile], dqt_out.at[tile], dqt_sem.at[n])

        each_tile(lambda n, tile: save(n, tile).start())
        for copy in down_copies:
            copy.wait()
        each_tile(lambda n, tile: save(n, tile).wait())
        return

    limit = jnp.minimum(total, capacity)

    def key_step(kt, carry):
        start = pl.multiple_of(kt * KEY_TILE, KEY_TILE)
        key = kv_s[1, pl.ds(start, KEY_TILE), :HEAD_SIZE]
        value = kv_s[1, pl.ds(start, KEY_TILE), HEAD_SIZE:]
        key_t = key.T
        own_k = acc_k.at[pl.ds(0, KEY_TILE), :]
        own_v = acc_v.at[pl.ds(0, KEY_TILE), :]
        own_k[...] = jnp.zeros_like(own_k)
        own_v[...] = jnp.zeros_like(own_v)
        position = start + lax.broadcasted_iota(jnp.int32, (KEY_TILE, 1), 0)

        def row_step(n, inner):
            tile = tiles[n]
            shard = tile // SHARD_TILES
            offset = (tile % SHARD_TILES) * ROW_TILE
            count = counts_ref[2 * shard] + counts_ref[2 * shard + 1]
            first = starts[shard] + offset

            @pl.when(first + ROW_TILE > start)
            def _():
                bound = jnp.where(lane < count - offset, first + lane, -1)

                def add_dq(part):
                    dqt[tile] += part

                tile_step(
                    key, value, key_t, row_tile(tile, q_s, do_s, lse_s, delta_s), position, bound,
                    own_k, own_v, add_dq,
                )

            return inner

        lax.fori_loop(0, length, row_step, 0)
        own[pl.ds(start, KEY_TILE), :HEAD_SIZE] = own_k[...] * scale
        own[pl.ds(start, KEY_TILE), HEAD_SIZE:] = own_v[...]
        return carry

    lax.fori_loop(0, (limit + KEY_TILE - 1) // KEY_TILE, key_step, 0)
    own_copy = pltpu.make_async_copy(own, own_out, down_sem.at[1])
    own_copy.start()
    each_tile(lambda n, tile: load(n, tile).wait())

    half = ROW_TILE // 2
    copies = []
    for block in range(KEY_VALUE_HEADS):
        shard = block // 2
        count = counts_ref[2 * shard] + counts_ref[2 * shard + 1]
        if block % 2 == 0:
            pieces = ((0, ROW_TILE, 0, 0), (ROW_TILE, half, 1, 0))
        else:
            pieces = ((0, half, 1, half), (half, ROW_TILE, 2, 0))
        for offset, size, t, first in pieces:
            live = count > t * ROW_TILE
            rows = slice(offset, offset + size)

            @pl.when(live)
            def _():
                for h in range(GROUP):
                    columns = slice(h * HEAD_SIZE, (h + 1) * HEAD_SIZE)
                    tile = SHARD_TILES * shard + t
                    part = ((dqt[tile, :, columns] + before[tile, :, columns]) * scale).T
                    dq_s[block, rows, columns] = part[first : first + size].astype(jnp.bfloat16)

            @pl.when(jnp.logical_not(live))
            def _():
                dq_s[block, rows, :] = jnp.zeros((size, WIDTH), jnp.bfloat16)

        copy = pltpu.make_async_copy(dq_s.at[block], dq_out.at[block], out_sem.at[block])
        copy.start()
        copies.append(copy)
    for copy in (*copies, *down_copies, own_copy):
        copy.wait()


def row_scratch(plane_rows):
    bf16, f32 = jnp.bfloat16, jnp.float32
    tile_count = plane_rows // ROW_TILE
    return [
        pltpu.VMEM((plane_rows, WIDTH), bf16),
        pltpu.VMEM((plane_rows, WIDTH), bf16),
        pltpu.VMEM((tile_count, WIDTH), f32),
        pltpu.VMEM((tile_count, WIDTH), f32),
        pltpu.VMEM((tile_count, HEAD_SIZE, WIDTH), f32),
    ]


def attention(first, me, counts, small, arrays, kvs, *before):
    bf16, f32 = jnp.bfloat16, jnp.float32
    blocks = KEY_VALUE_HEADS
    rows = kvs[0].shape[0]
    capacity = rows - INFO_ROWS
    columns = 2 * HEAD_SIZE
    plane_rows = 2 * capacity
    tile_count = plane_rows // ROW_TILE
    dq = (blocks, plane_rows // blocks, WIDTH)
    dqt = (tile_count, HEAD_SIZE, WIDTH)
    down = jax.ShapeDtypeStruct((rows, columns), bf16)
    flag = jax.ShapeDtypeStruct((1,), jnp.int32)
    if first:
        outs = (down, down, jax.ShapeDtypeStruct(dqt, f32), flag)
        more = []
    else:
        own = jax.ShapeDtypeStruct((capacity, columns), f32)
        outs = (down, jax.ShapeDtypeStruct(dq, bf16), own, flag)
        more = [
            pltpu.SemaphoreType.DMA((blocks,)),
            pltpu.VMEM(dq, bf16),
            pltpu.VMEM((capacity, columns), f32),
            pltpu.VMEM(dqt, f32),
        ]
    return pl.pallas_call(
        functools.partial(attention_kernel, first),
        out_shape=outs,
        in_specs=[SMEM] * 2 + [VMEM] + [HBM] * (11 + len(before)),
        out_specs=[HBM] * 3 + [SMEM],
        scratch_shapes=[
            pltpu.VMEM((plane_rows, WIDTH), bf16),
            pltpu.VMEM((plane_rows, WIDTH), bf16),
            pltpu.VMEM((tile_count, WIDTH), f32),
            pltpu.VMEM((tile_count, WIDTH), f32),
            pltpu.VMEM(dqt, f32),
            pltpu.VMEM((2, rows, columns), bf16),
            pltpu.VMEM((capacity, HEAD_SIZE), f32),
            pltpu.VMEM((capacity, HEAD_SIZE), f32),
            pltpu.SMEM((tile_count + 1,), jnp.int32),
            pltpu.SMEM((blocks,), jnp.int32),
            pltpu.SMEM((2,), jnp.int32),
            pltpu.SemaphoreType.DMA((2 * blocks,)),
            pltpu.SemaphoreType.DMA((2,)),
            pltpu.SemaphoreType.DMA((2,)),
            pltpu.SemaphoreType.DMA((tile_count,)),
            pltpu.VMEM((2, rows, columns), bf16),
            *more,
        ],
        compiler_params=pltpu.CompilerParams(vmem_limit_bytes=48 * 1024 * 1024),
        cost_estimate=pl.CostEstimate(
            flops=5_000_000_000, bytes_accessed=12_000_000, transcendentals=4_000_000
        ),
        name="attention",
    )(me, counts, small, *arrays, *kvs, *before)


def unpack_rows_kernel(parts, out):
    for g in range(KEY_VALUE_HEADS):
        out[:, g * WIDTH : (g + 1) * WIDTH] = parts[g]


def unpack_rows(parts):
    return pl.pallas_call(
        unpack_rows_kernel,
        out_shape=jax.ShapeDtypeStruct((parts.shape[1], KEY_VALUE_HEADS * WIDTH), parts.dtype),
        in_specs=[VMEM],
        out_specs=VMEM,
        name="unpack_rows",
    )(parts)


def combine_kernel(counts_ref, own, *rest):
    backs, out = rest[:3], rest[3]
    home_rows = out.shape[1]
    capacity = own.shape[0]
    total = own[...]
    for back in backs:
        total += back[:capacity, :].astype(jnp.float32)
    total = total.astype(jnp.bfloat16)
    within = lax.broadcasted_iota(jnp.int32, (home_rows, capacity), 0)
    place = lax.broadcasted_iota(jnp.int32, (home_rows, capacity), 1)
    start = jnp.int32(0)
    for block in range(KEY_VALUE_HEADS):
        count = counts_ref[block]
        hit = (place == within + start) & (within < count)
        out[block] = jnp.dot(
            jnp.where(hit, 1.0, 0.0).astype(jnp.bfloat16),
            total,
            preferred_element_type=jnp.float32,
        ).astype(jnp.bfloat16)
        start = start + count


def combine(counts, own, backs, home_rows):
    blocks = KEY_VALUE_HEADS
    return pl.pallas_call(
        combine_kernel,
        out_shape=jax.ShapeDtypeStruct((blocks, home_rows, own.shape[1]), jnp.bfloat16),
        in_specs=[SMEM] + [VMEM] * 4,
        out_specs=VMEM,
        compiler_params=pltpu.CompilerParams(vmem_limit_bytes=32 * 1024 * 1024),
        name="combine",
    )(counts, own, *backs)


def plane_device(queries, keys, values, outputs, output_gradient, lse, ranks):
    planes = lax.axis_size("outer")
    plane = ("inner", "head")
    blocks = KEY_VALUE_HEADS
    home_rows = queries.shape[0]
    plane_rows = blocks * home_rows
    capacity = plane_rows // 2
    surviving_tokens = BALANCED_TOKENS * planes * lax.axis_size("inner")
    bf16, f32 = jnp.bfloat16, jnp.float32
    me = lax.axis_index(plane).reshape(1).astype(jnp.int32)

    def swap(array, k):
        return lax.ppermute(array, plane, [(i, i ^ k) for i in range(blocks)])

    sent = pack_pairs(
        surviving_tokens, ranks, lse, keys, values, output_gradient, outputs
    )
    me, sent = lax.optimization_barrier((me, sent))
    arrived = lax.all_to_all(sent, plane, split_axis=0, concat_axis=0, tiled=True)
    *packed, beside = pack_rows(me, queries, output_gradient)
    pairs = [swap(rows, chip) for rows, chip in zip(packed, CHIPS)]
    beside = swap(beside, CORE)
    arrived, beside = lax.optimization_barrier((arrived, beside))
    mine, small, counts = compact(arrived)
    up = [lax.ppermute(mine, "outer", [(i, i + 1) for i in range(planes - 1)])]
    last = lax.ppermute(mine, "outer", [(0, planes - 1)])
    up.append(lax.ppermute(up[0], "outer", [(i, i + 1) for i in range(1, planes - 1)]))
    up.append(last)
    up[1], up[2], *pairs = lax.optimization_barrier((up[1], up[2], *pairs))
    crossed = [swap(pair[1:], CORE) for pair in pairs]
    arrays = [queries, output_gradient, beside, *pairs, *crossed]

    def lower(rows, k):
        return lax.ppermute(rows, "outer", [(i + k, i) for i in range(planes - k)])

    down2, down3, dqt, full1 = attention(True, me, counts, small, arrays, [up[1], up[2]])
    back2 = lower(down2, 2)
    down1, dq, own, full2 = attention(False, me, counts, small, arrays, [up[0], mine], dqt)
    dq, back2 = lax.optimization_barrier((dq, back2))
    backs = [lower(down3, 3), back2, lower(down1, 1)]
    dq = lax.all_to_all(dq, plane, split_axis=0, concat_axis=0, tiled=True)
    spread = combine(counts, own, backs, home_rows)
    dq, spread = lax.optimization_barrier((dq, spread))
    dq_home = unpack_rows(dq)
    kv_home = lax.all_to_all(spread, plane, split_axis=0, concat_axis=0, tiled=True)
    full = (full1[0] + full2[0]) > 0
    for back in backs:
        full = full | (back[capacity, 0] > 0)
    dk = kv_home[:, :, :HEAD_SIZE].transpose(1, 0, 2).reshape(home_rows, blocks * HEAD_SIZE)
    dv = kv_home[:, :, HEAD_SIZE:].transpose(1, 0, 2).reshape(home_rows, blocks * HEAD_SIZE)
    return (dq_home, dk, dv), full


def solution(mesh):
    spec = P(("seq", "head"), None)
    heads = mesh.shape["head"]
    inner = max(KEY_VALUE_HEADS // heads, 1)
    planes = mesh.shape["seq"] // inner
    if planes != 4 or inner * heads != KEY_VALUE_HEADS:
        return jax.shard_map(
            per_device,
            mesh=mesh,
            in_specs=(spec,) * 6 + (P(("seq", "head")),),
            out_specs=(spec,) * 3,
            check_vma=False,
        )
    axes = ("outer", "inner", "head")

    def device(*blocks):
        fast, full = plane_device(*blocks)
        return lax.cond(full, lambda: per_device(*blocks, seq=("outer", "inner")), lambda: fast)

    return jax.shard_map(
        device,
        mesh=Mesh(mesh.devices.reshape(planes, inner, heads), axes),
        in_specs=(P(axes, None),) * 6 + (P(axes),),
        out_specs=(P(axes, None),) * 3,
        check_vma=False,
    )
```

```python
import functools

import jax
import jax.numpy as jnp
from jax import lax
from jax.experimental import pallas as pl
from jax.experimental.pallas import tpu as pltpu
from jax.sharding import Mesh
from jax.sharding import PartitionSpec as P

QUERY_HEADS = 40
KEY_VALUE_HEADS = 8
HEAD_SIZE = 128
BALANCED_TOKENS = 128


block_keys = 512


def gather(array, axis):
    count = lax.axis_size(axis)
    copies = jnp.broadcast_to(array[None], (count, *array.shape))
    got = lax.all_to_all(copies, axis, split_axis=0, concat_axis=0, tiled=True)
    return got.reshape(count * array.shape[0], *array.shape[1:])


def per_device(queries, keys, values, outputs, output_gradient, lse, ranks, seq="seq"):
    sequence_count = lax.axis_size(seq)
    head_total = lax.axis_size("head")
    home_rows = queries.shape[0]
    capacity = home_rows * head_total
    slots = capacity // sequence_count
    surviving_tokens = BALANCED_TOKENS * sequence_count
    group_size = QUERY_HEADS // KEY_VALUE_HEADS
    local_key_value = KEY_VALUE_HEADS // head_total
    scale = HEAD_SIZE ** (-0.5)

    def split_heads(array):
        return array.reshape(home_rows, head_total, array.shape[1] // head_total)

    moved = (
        lax.all_to_all(split_heads(queries), "head", split_axis=1, concat_axis=0, tiled=True),
        lax.all_to_all(split_heads(keys), "head", split_axis=1, concat_axis=0, tiled=True),
        lax.all_to_all(split_heads(values), "head", split_axis=1, concat_axis=0, tiled=True),
        lax.all_to_all(
            split_heads(output_gradient), "head", split_axis=1, concat_axis=0, tiled=True
        ),
        lax.all_to_all(split_heads(lse), "head", split_axis=1, concat_axis=0, tiled=True),
        lax.all_to_all(split_heads(outputs), "head", split_axis=1, concat_axis=0, tiled=True),
    )
    shard_rank_list = gather(ranks, "head")
    first_rank = shard_rank_list[0]
    living_count = jnp.sum((shard_rank_list < surviving_tokens).astype(jnp.int32))
    table = gather(jnp.stack([first_rank, living_count])[None, :], seq)

    def to_pairs(array):
        flat = array.reshape(slots, sequence_count, array.shape[-1])
        return jnp.roll(flat, first_rank, axis=1)

    arrived = (
        lax.all_to_all(to_pairs(moved[0]), seq, split_axis=1, concat_axis=1, tiled=True),
        lax.all_to_all(to_pairs(moved[1]), seq, split_axis=1, concat_axis=1, tiled=True),
        lax.all_to_all(to_pairs(moved[2]), seq, split_axis=1, concat_axis=1, tiled=True),
        lax.all_to_all(to_pairs(moved[3]), seq, split_axis=1, concat_axis=1, tiled=True),
        lax.all_to_all(to_pairs(moved[4]), seq, split_axis=1, concat_axis=1, tiled=True),
        lax.all_to_all(to_pairs(moved[5]), seq, split_axis=1, concat_axis=1, tiled=True),
    )
    my_index = lax.axis_index(seq)
    starts = table[:, 0]
    count_table = table[:, 1]
    offset = (my_index - starts) % sequence_count
    within = jnp.arange(slots, dtype=jnp.int32)[:, None] * sequence_count + offset[None, :]
    alive = within < count_table[None, :]
    target_rank = jnp.where(
        alive, (starts[None, :] + within) // sequence_count, BALANCED_TOKENS
    ).reshape(-1)

    def place(array):
        width = array.shape[-1]
        return (
            jnp.zeros((BALANCED_TOKENS, width), array.dtype)
            .at[target_rank]
            .set(array.reshape(slots * sequence_count, width), mode="drop")
        )

    query_row_block = place(arrived[0]).reshape(
        BALANCED_TOKENS, local_key_value, group_size, HEAD_SIZE
    )
    key_row_block = place(arrived[1]).reshape(BALANCED_TOKENS, local_key_value, HEAD_SIZE)
    value_row_block = place(arrived[2]).reshape(BALANCED_TOKENS, local_key_value, HEAD_SIZE)
    grad_rows = place(arrived[3]).reshape(BALANCED_TOKENS, local_key_value, group_size, HEAD_SIZE)
    lse_rows = (
        place(arrived[4]).astype(jnp.float32).reshape(BALANCED_TOKENS, local_key_value, group_size)
    )
    out_rows = (
        place(arrived[5])
        .astype(jnp.float32)
        .reshape(BALANCED_TOKENS, local_key_value, group_size, HEAD_SIZE)
    )
    delta_rows = (
        jnp.sum(grad_rows.astype(jnp.float32) * out_rows, axis=-1)
        .astype(jnp.bfloat16)
        .astype(jnp.float32)
    )
    gathered = (
        gather(key_row_block, seq),
        gather(value_row_block, seq),
    )
    all_keys = gathered[0].reshape(sequence_count, BALANCED_TOKENS, local_key_value, HEAD_SIZE)
    all_values = gathered[1].reshape(sequence_count, BALANCED_TOKENS, local_key_value, HEAD_SIZE)
    rows_per = block_keys // sequence_count
    inner = 1
    outer = BALANCED_TOKENS // rows_per // inner
    query_rank = jnp.arange(BALANCED_TOKENS, dtype=jnp.int32) * sequence_count + my_index
    lse_t = lse_rows.transpose(1, 2, 0)
    delta_t = delta_rows.transpose(1, 2, 0)
    position = jnp.arange(sequence_count * rows_per, dtype=jnp.int32)

    def key_step(query_acc, row_start):
        key_blk = lax.dynamic_slice_in_dim(all_keys, row_start, rows_per, 1).reshape(
            sequence_count * rows_per, local_key_value, HEAD_SIZE
        )
        value_blk = lax.dynamic_slice_in_dim(all_values, row_start, rows_per, 1).reshape(
            sequence_count * rows_per, local_key_value, HEAD_SIZE
        )
        key_owner_rank = (row_start + position % rows_per) * sequence_count + position // rows_per
        mask = key_owner_rank[None, None, None, :] <= query_rank[None, None, :, None]
        scores = (
            jnp.einsum(
                "rgmc,kgc->gmrk", query_row_block, key_blk, preferred_element_type=jnp.float32
            )
            * scale
        )
        probs = jnp.where(mask, jnp.exp(scores - lse_t[..., None]), 0.0)
        dprob = jnp.einsum(
            "rgmc,kgc->gmrk", grad_rows, value_blk, preferred_element_type=jnp.float32
        )
        dscore = probs * (dprob - delta_t[..., None])
        probs_low = probs.astype(jnp.bfloat16)
        dscore_low = dscore.astype(jnp.bfloat16)
        query_acc = query_acc + scale * jnp.einsum(
            "gmrk,kgc->rgmc", dscore_low, key_blk, preferred_element_type=jnp.float32
        )
        key_part = scale * jnp.einsum(
            "gmrk,rgmc->kgc", dscore_low, query_row_block, preferred_element_type=jnp.float32
        )
        value_part = jnp.einsum(
            "gmrk,rgmc->kgc", probs_low, grad_rows, preferred_element_type=jnp.float32
        )
        return (
            query_acc,
            key_part.reshape(sequence_count, rows_per, local_key_value * HEAD_SIZE),
            value_part.reshape(sequence_count, rows_per, local_key_value * HEAD_SIZE),
        )

    def outer_step(query_acc, outer_index):

        def inner_step(query_inner, inner_index):
            row_start = (outer_index * inner + inner_index) * rows_per
            query_new, key_part, value_part = key_step(query_inner, row_start)
            return (query_new, (key_part, value_part))

        query_acc, (key_parts, value_parts) = lax.scan(
            inner_step, query_acc, jnp.arange(inner, dtype=jnp.int32)
        )
        key_parts = key_parts.transpose(1, 0, 2, 3).reshape(
            sequence_count, inner * rows_per, local_key_value * HEAD_SIZE
        )
        value_parts = value_parts.transpose(1, 0, 2, 3).reshape(
            sequence_count, inner * rows_per, local_key_value * HEAD_SIZE
        )
        received = (
            lax.all_to_all(key_parts, seq, split_axis=0, concat_axis=0, tiled=True),
            lax.all_to_all(value_parts, seq, split_axis=0, concat_axis=0, tiled=True),
        )
        return (query_acc, (jnp.sum(received[0], axis=0), jnp.sum(received[1], axis=0)))

    start_acc = jnp.zeros((BALANCED_TOKENS, local_key_value, group_size, HEAD_SIZE), jnp.float32)
    query_acc, (key_sums, value_sums) = lax.scan(
        outer_step, start_acc, jnp.arange(outer, dtype=jnp.int32)
    )
    query_done = query_acc.reshape(
        BALANCED_TOKENS, local_key_value * group_size * HEAD_SIZE
    ).astype(jnp.bfloat16)
    key_done = key_sums.reshape(BALANCED_TOKENS, local_key_value * HEAD_SIZE).astype(jnp.bfloat16)
    value_done = value_sums.reshape(BALANCED_TOKENS, local_key_value * HEAD_SIZE).astype(
        jnp.bfloat16
    )
    safe_rows = jnp.minimum(target_rank, BALANCED_TOKENS - 1)
    alive_flat = alive.reshape(-1)

    def collect(array):
        picked = jnp.where(alive_flat[:, None], array[safe_rows], jnp.zeros((), array.dtype))
        return picked.reshape(slots, sequence_count, array.shape[-1])

    returned = (
        lax.all_to_all(collect(query_done), seq, split_axis=1, concat_axis=1, tiled=True),
        lax.all_to_all(collect(key_done), seq, split_axis=1, concat_axis=1, tiled=True),
        lax.all_to_all(collect(value_done), seq, split_axis=1, concat_axis=1, tiled=True),
    )

    def to_home(array):
        unrolled = jnp.roll(array, -first_rank, axis=1)
        return unrolled.reshape(capacity, 1, array.shape[-1])

    homed = (
        lax.all_to_all(to_home(returned[0]), "head", split_axis=0, concat_axis=1, tiled=True),
        lax.all_to_all(to_home(returned[1]), "head", split_axis=0, concat_axis=1, tiled=True),
        lax.all_to_all(to_home(returned[2]), "head", split_axis=0, concat_axis=1, tiled=True),
    )
    query_grads = homed[0].reshape(home_rows, head_total * homed[0].shape[-1])
    key_gradient_output = homed[1].reshape(home_rows, head_total * homed[1].shape[-1])
    value_gradient = homed[2].reshape(home_rows, head_total * homed[2].shape[-1])
    return (query_grads, key_gradient_output, value_gradient)

LOG2E = 1.4426950408889634
KEY_TILE = 256
ROW_TILE = 128
INFO_ROWS = 16
AUX_LANES = 256
DELTA_ROW = 8
SMEM = pl.BlockSpec(memory_space=pltpu.SMEM)
VMEM = pl.BlockSpec(memory_space=pltpu.VMEM)
HBM = pl.BlockSpec(memory_space=pltpu.HBM)
GROUP = QUERY_HEADS // KEY_VALUE_HEADS
WIDTH = GROUP * HEAD_SIZE
CHIPS = (5, 4, 1)
CORE = 2
SHARD_TILES = 3
PASS_ROWS = (256, 512, 768)


def pack_pairs_kernel(limit, ranks_ref, lse_ref, k_ref, v_ref, do_ref, o_ref, out_ref, columns):
    home_rows = k_ref.shape[0]
    columns[...] = jnp.zeros_like(columns)
    for h in range(QUERY_HEADS):
        head = slice(h * HEAD_SIZE, (h + 1) * HEAD_SIZE)
        product = do_ref[:, head].astype(jnp.float32) * o_ref[:, head].astype(jnp.float32)
        column = 8 * (h // GROUP) + h % GROUP
        columns[:, column : column + 1] = jnp.sum(product, axis=1, keepdims=True)
    delta = columns[...].T
    lse = lse_ref[...].astype(jnp.float32)
    live = jnp.where(ranks_ref[...] < limit, 1.0, 0.0)
    count = jnp.broadcast_to(jnp.sum(live, axis=1, keepdims=True), (8 - GROUP, home_rows))
    for g in range(KEY_VALUE_HEADS):
        head = slice(g * HEAD_SIZE, (g + 1) * HEAD_SIZE)
        out_ref[g, :home_rows, :HEAD_SIZE] = k_ref[:, head]
        out_ref[g, :home_rows, HEAD_SIZE:] = v_ref[:, head]
        info = jnp.concatenate(
            [lse[g * GROUP : (g + 1) * GROUP], count, delta[8 * g : 8 * g + 8]], axis=0
        )
        out_ref[g, home_rows:, :home_rows] = info.astype(out_ref.dtype)


def pack_pairs(limit, ranks, lse, keys, values, output_gradient, outputs):
    home_rows = keys.shape[0]
    return pl.pallas_call(
        functools.partial(pack_pairs_kernel, limit),
        out_shape=jax.ShapeDtypeStruct(
            (KEY_VALUE_HEADS, home_rows + INFO_ROWS, 2 * HEAD_SIZE), keys.dtype
        ),
        in_specs=[VMEM] * 6,
        out_specs=VMEM,
        scratch_shapes=[pltpu.VMEM((home_rows, HEAD_SIZE), jnp.float32)],
        compiler_params=pltpu.CompilerParams(vmem_limit_bytes=32 * 1024 * 1024),
        name="pack_pairs",
    )(ranks.reshape(1, home_rows), lse.T, keys, values, output_gradient, outputs)


def pack_rows_kernel(me_ref, q_ref, do_ref, *outs):
    me = me_ref[0]
    for out, partners in zip(outs, [(chip, chip ^ CORE) for chip in CHIPS] + [(CORE,)]):
        for n, partner in enumerate(partners):
            start = pl.multiple_of((me ^ partner) * WIDTH, HEAD_SIZE)
            out[n, :, :WIDTH] = q_ref[:, pl.ds(start, WIDTH)]
            out[n, :, WIDTH:] = do_ref[:, pl.ds(start, WIDTH)]


def pack_rows(me, queries, output_gradient):
    home_rows = queries.shape[0]
    pair = jax.ShapeDtypeStruct((2, home_rows, 2 * WIDTH), queries.dtype)
    beside = jax.ShapeDtypeStruct((1, home_rows, 2 * WIDTH), queries.dtype)
    return pl.pallas_call(
        pack_rows_kernel,
        out_shape=(pair, pair, pair, beside),
        in_specs=[SMEM] + [VMEM] * 2,
        out_specs=[VMEM] * 4,
        compiler_params=pltpu.CompilerParams(vmem_limit_bytes=32 * 1024 * 1024),
        name="pack_rows",
    )(me, queries, output_gradient)


def compact_kernel(arrived, out, small, counts_ref):
    home_rows = arrived.shape[1] - INFO_ROWS
    capacity = out.shape[0] - INFO_ROWS
    row = lax.broadcasted_iota(jnp.int32, (capacity, home_rows), 0)
    within = lax.broadcasted_iota(jnp.int32, (capacity, home_rows), 1)
    total = jnp.int32(0)
    picked = []
    for block in range(KEY_VALUE_HEADS):
        info = arrived[block, home_rows:, :]
        small[block] = info
        count = jnp.max(info.astype(jnp.float32)[GROUP : GROUP + 1, :home_rows]).astype(jnp.int32)
        counts_ref[block] = count
        hit = (row == within + total) & (within < count)
        picked.append(jnp.where(hit, 1.0, 0.0).astype(jnp.bfloat16))
        total = total + count
    acc = jnp.zeros((capacity, out.shape[1]), jnp.float32)
    for block in range(KEY_VALUE_HEADS):
        acc += jnp.dot(
            picked[block], arrived[block, :home_rows, :], preferred_element_type=jnp.float32
        )
    out[:capacity, :] = acc.astype(out.dtype)
    line = lax.broadcasted_iota(jnp.int32, (INFO_ROWS, out.shape[1]), 0)
    out[capacity:, :] = (
        jnp.where(line == 0, total // 64, jnp.where(line == 1, total % 64, 0))
        .astype(jnp.float32)
        .astype(out.dtype)
    )


def compact(arrived):
    blocks, rows, columns = arrived.shape
    capacity = blocks * (rows - INFO_ROWS) // 2
    return pl.pallas_call(
        compact_kernel,
        out_shape=(
            jax.ShapeDtypeStruct((capacity + INFO_ROWS, columns), arrived.dtype),
            jax.ShapeDtypeStruct((blocks, INFO_ROWS, columns), arrived.dtype),
            jax.ShapeDtypeStruct((blocks,), jnp.int32),
        ),
        in_specs=[VMEM],
        out_specs=(VMEM, VMEM, SMEM),
        compiler_params=pltpu.CompilerParams(vmem_limit_bytes=32 * 1024 * 1024),
        name="compact",
    )(arrived)


def load_rows(me, counts_ref, arrays, q_s, do_s, sems):
    home_rows = q_s.shape[0] // KEY_VALUE_HEADS
    q_hbm, do_hbm, beside, pairs, crossed = arrays
    column = pl.ds(pl.multiple_of(me * WIDTH, HEAD_SIZE), WIDTH)
    left, right = pl.ds(0, WIDTH), pl.ds(WIDTH, WIDTH)
    sources = [
        (0, q_hbm.at[:, column], do_hbm.at[:, column]),
        (CORE, beside.at[0, :, left], beside.at[0, :, right]),
    ]
    for chip, pair, cross in zip(CHIPS, pairs, crossed):
        sources.append((chip, pair.at[0, :, left], pair.at[0, :, right]))
        sources.append((chip ^ CORE, cross.at[0, :, left], cross.at[0, :, right]))
    plans = []
    for n, (partner, q, do) in enumerate(sources):
        source = me ^ partner
        rows = pl.ds(pl.multiple_of(source * home_rows, 64), home_rows)
        shard = counts_ref[source & ~1] + counts_ref[source | 1]
        needed = ((source & 1) == 0) | (shard > ROW_TILE)
        plans.append(
            (
                needed,
                [
                    pltpu.make_async_copy(q, q_s.at[rows, :], sems.at[2 * n]),
                    pltpu.make_async_copy(do, do_s.at[rows, :], sems.at[2 * n + 1]),
                ],
            )
        )

    def each(act):
        for needed, copies in plans:

            @pl.when(needed)
            def _():
                for copy in copies:
                    act(copy)

    return each


def list_tiles(counts_ref, tiles, starts):
    length = jnp.int32(0)
    total = jnp.int32(0)
    for shard in range(KEY_VALUE_HEADS // 2):
        count = counts_ref[2 * shard] + counts_ref[2 * shard + 1]
        starts[shard] = total
        total = total + count
        for t in range(SHARD_TILES):
            live = count > t * ROW_TILE

            @pl.when(live)
            def _():
                tiles[length] = SHARD_TILES * shard + t

            length = length + live.astype(jnp.int32)
    return length, total


def spread_lanes(aux_s, lse_s, delta_s):
    lane = lax.broadcasted_iota(jnp.int32, (INFO_ROWS, ROW_TILE), 1)
    for shard in range(KEY_VALUE_HEADS // 2):
        low = aux_s[2 * shard].astype(jnp.float32)
        high = aux_s[2 * shard + 1].astype(jnp.float32)
        half = ROW_TILE // 2
        middle = jnp.where(
            lane < half, low[:, ROW_TILE:], pltpu.roll(high[:, :ROW_TILE], half, axis=1)
        )
        last = pltpu.roll(high, AUX_LANES - half, axis=1)[:, :ROW_TILE]
        for t, rows in enumerate((low[:, :ROW_TILE], middle, last)):
            row = SHARD_TILES * shard + t
            for h in range(GROUP):
                columns = slice(h * ROW_TILE, (h + 1) * ROW_TILE)
                lse_s[row : row + 1, columns] = rows[h : h + 1] * LOG2E
                delta_s[row : row + 1, columns] = rows[DELTA_ROW + h : DELTA_ROW + 1 + h]


def row_tile(tile, q_s, do_s, lse_s, delta_s):
    def stack(ref):
        rows = ref[pl.ds(pl.multiple_of(tile * ROW_TILE, ROW_TILE), ROW_TILE), :]
        return jnp.concatenate(
            [rows[:, h * HEAD_SIZE : (h + 1) * HEAD_SIZE] for h in range(GROUP)], axis=0
        )

    return stack(q_s), stack(do_s), lse_s[pl.ds(tile, 1), :], delta_s[pl.ds(tile, 1), :]


def tile_step(key, value, key_t, rows, position, bound, acc_k, acc_v, add_dq):
    q, do, lse, delta = rows
    scale = HEAD_SIZE ** (-0.5)
    dims = (((1,), (1,)), ((), ()))
    scores = lax.dot_general(key, q, dims, preferred_element_type=jnp.float32)
    prob = jnp.where(position <= bound, jnp.exp2(scores * (scale * LOG2E) - lse), 0.0)
    dprob = lax.dot_general(value, do, dims, preferred_element_type=jnp.float32)
    dscore = (prob * (dprob - delta)).astype(jnp.bfloat16)
    acc_v[...] += jnp.dot(prob.astype(jnp.bfloat16), do, preferred_element_type=jnp.float32)
    acc_k[...] += jnp.dot(dscore, q, preferred_element_type=jnp.float32)
    add_dq(jnp.dot(key_t, dscore, preferred_element_type=jnp.float32))


def attention_kernel(first, me_ref, counts_ref, *rest):
    aux_s, arrays, kvs, rest = rest[0], rest[1:10], rest[10:12], rest[12:]
    arrays = (*arrays[:3], arrays[3:6], arrays[6:9])
    if first:
        far, downs, dqt_out, full_ref, rest = 2, rest[:2], rest[2], rest[3], rest[4:]
    else:
        dqt_in, far, downs, rest = rest[0], 1, rest[1:2], rest[2:]
        dq_out, own_out, full_ref, rest = rest[0], rest[1], rest[2], rest[3:]
    (
        q_s, do_s, lse_s, delta_s, dqt, kv_s, acc_k, acc_v, tiles, starts, limits, sems,
        kv_sem, down_sem, dqt_sem, down_s,
    ) = rest[:16]
    if not first:
        out_sem, dq_s, own, before = rest[16:]
    capacity = downs[0].shape[0] - INFO_ROWS
    scale = HEAD_SIZE ** (-0.5)
    each = load_rows(me_ref[0], counts_ref, arrays, q_s, do_s, sems)
    each(lambda copy: copy.start())
    kv_copies = [
        pltpu.make_async_copy(source, kv_s.at[n], kv_sem.at[n])
        for n, source in enumerate(kvs)
    ]
    for copy in kv_copies:
        copy.start()
    length, total = list_tiles(counts_ref, tiles, starts)

    def each_tile(act):
        def step(n, carry):
            act(n, tiles[n])
            return carry

        lax.fori_loop(0, length, step, 0)

    def zero_tile(n, tile):
        dqt[tile] = jnp.zeros(dqt.shape[1:], jnp.float32)

    each_tile(zero_tile)
    spread_lanes(aux_s, lse_s, delta_s)
    if not first:

        def load(n, tile):
            return pltpu.make_async_copy(dqt_in.at[tile], before.at[tile], dqt_sem.at[n])

        each_tile(lambda n, tile: load(n, tile).start())
        own[...] = jnp.zeros_like(own)
    for copy in kv_copies:
        copy.wait()
    most = total
    for n in range(far):
        info = kv_s[n, capacity:, :].astype(jnp.float32)
        limit = (jnp.max(info[0:1]) * 64.0 + jnp.max(info[1:2])).astype(jnp.int32)
        limits[n] = jnp.minimum(limit, capacity)
        most = jnp.maximum(most, limit)
    full_ref[0] = (most > capacity).astype(jnp.int32)
    for n in range(far):
        down_s[n, capacity:, :] = jnp.full(
            (INFO_ROWS, 2 * HEAD_SIZE), jnp.where(most > capacity, 1.0, 0.0)
        ).astype(jnp.bfloat16)
    each(lambda copy: copy.wait())
    lane = lax.broadcasted_iota(jnp.int32, (1, WIDTH), 1) % ROW_TILE

    def block_step(step, carry):
        index = far - 1 - step
        limit = limits[index]

        def run(rows):
            key = kv_s[index, :rows, :HEAD_SIZE]
            value = kv_s[index, :rows, HEAD_SIZE:]
            key_t = key.T
            acc_k[:rows] = jnp.zeros((rows, HEAD_SIZE), jnp.float32)
            acc_v[:rows] = jnp.zeros((rows, HEAD_SIZE), jnp.float32)
            position = lax.broadcasted_iota(jnp.int32, (rows, 1), 0)

            def row_step(n, inner):
                tile = tiles[n]
                shard = tile // SHARD_TILES
                count = counts_ref[2 * shard] + counts_ref[2 * shard + 1]
                alive = lane < count - (tile % SHARD_TILES) * ROW_TILE
                bound = jnp.where(alive, limit - 1, -1)

                def add_dq(part):
                    dqt[tile] += part

                tile_step(
                    key, value, key_t, row_tile(tile, q_s, do_s, lse_s, delta_s), position, bound,
                    acc_k.at[pl.ds(0, rows), :], acc_v.at[pl.ds(0, rows), :], add_dq,
                )
                return inner

            lax.fori_loop(0, length, row_step, 0)
            down_s[index, :rows, :HEAD_SIZE] = (acc_k[:rows] * scale).astype(jnp.bfloat16)
            down_s[index, :rows, HEAD_SIZE:] = acc_v[:rows].astype(jnp.bfloat16)
            if rows < capacity:
                down_s[index, rows:capacity, :] = jnp.zeros(
                    (capacity - rows, 2 * HEAD_SIZE), jnp.bfloat16
                )

        below = 0
        for rows in PASS_ROWS:

            @pl.when((limit > below) & (limit <= rows))
            def _():
                run(rows)

            below = rows

        @pl.when(limit == 0)
        def _():
            down_s[index, :capacity, :] = jnp.zeros((capacity, 2 * HEAD_SIZE), jnp.bfloat16)

        return carry

    lax.fori_loop(0, far, block_step, 0)
    down_copies = [
        pltpu.make_async_copy(down_s.at[n], downs[n], down_sem.at[n]) for n in range(far)
    ]
    for copy in down_copies:
        copy.start()

    if first:

        def save(n, tile):
            return pltpu.make_async_copy(dqt.at[tile], dqt_out.at[tile], dqt_sem.at[n])

        each_tile(lambda n, tile: save(n, tile).start())
        for copy in down_copies:
            copy.wait()
        each_tile(lambda n, tile: save(n, tile).wait())
        return

    limit = jnp.minimum(total, capacity)

    def key_step(kt, carry):
        start = pl.multiple_of(kt * KEY_TILE, KEY_TILE)
        key = kv_s[1, pl.ds(start, KEY_TILE), :HEAD_SIZE]
        value = kv_s[1, pl.ds(start, KEY_TILE), HEAD_SIZE:]
        key_t = key.T
        own_k = acc_k.at[pl.ds(0, KEY_TILE), :]
        own_v = acc_v.at[pl.ds(0, KEY_TILE), :]
        own_k[...] = jnp.zeros_like(own_k)
        own_v[...] = jnp.zeros_like(own_v)
        position = start + lax.broadcasted_iota(jnp.int32, (KEY_TILE, 1), 0)

        def row_step(n, inner):
            tile = tiles[n]
            shard = tile // SHARD_TILES
            offset = (tile % SHARD_TILES) * ROW_TILE
            count = counts_ref[2 * shard] + counts_ref[2 * shard + 1]
            first = starts[shard] + offset

            @pl.when(first + ROW_TILE > start)
            def _():
                bound = jnp.where(lane < count - offset, first + lane, -1)

                def add_dq(part):
                    dqt[tile] += part

                tile_step(
                    key, value, key_t, row_tile(tile, q_s, do_s, lse_s, delta_s), position, bound,
                    own_k, own_v, add_dq,
                )

            return inner

        lax.fori_loop(0, length, row_step, 0)
        own[pl.ds(start, KEY_TILE), :HEAD_SIZE] = own_k[...] * scale
        own[pl.ds(start, KEY_TILE), HEAD_SIZE:] = own_v[...]
        return carry

    lax.fori_loop(0, (limit + KEY_TILE - 1) // KEY_TILE, key_step, 0)
    own_copy = pltpu.make_async_copy(own, own_out, down_sem.at[1])
    own_copy.start()
    each_tile(lambda n, tile: load(n, tile).wait())

    half = ROW_TILE // 2
    copies = []
    for block in range(KEY_VALUE_HEADS):
        shard = block // 2
        count = counts_ref[2 * shard] + counts_ref[2 * shard + 1]
        if block % 2 == 0:
            pieces = ((0, ROW_TILE, 0, 0), (ROW_TILE, half, 1, 0))
        else:
            pieces = ((0, half, 1, half), (half, ROW_TILE, 2, 0))
        for offset, size, t, first in pieces:
            live = count > t * ROW_TILE
            rows = slice(offset, offset + size)

            @pl.when(live)
            def _():
                for h in range(GROUP):
                    columns = slice(h * HEAD_SIZE, (h + 1) * HEAD_SIZE)
                    tile = SHARD_TILES * shard + t
                    part = ((dqt[tile, :, columns] + before[tile, :, columns]) * scale).T
                    dq_s[block, rows, columns] = part[first : first + size].astype(jnp.bfloat16)

            @pl.when(jnp.logical_not(live))
            def _():
                dq_s[block, rows, :] = jnp.zeros((size, WIDTH), jnp.bfloat16)

        copy = pltpu.make_async_copy(dq_s.at[block], dq_out.at[block], out_sem.at[block])
        copy.start()
        copies.append(copy)
    for copy in (*copies, *down_copies, own_copy):
        copy.wait()


def row_scratch(plane_rows):
    bf16, f32 = jnp.bfloat16, jnp.float32
    tile_count = plane_rows // ROW_TILE
    return [
        pltpu.VMEM((plane_rows, WIDTH), bf16),
        pltpu.VMEM((plane_rows, WIDTH), bf16),
        pltpu.VMEM((tile_count, WIDTH), f32),
        pltpu.VMEM((tile_count, WIDTH), f32),
        pltpu.VMEM((tile_count, HEAD_SIZE, WIDTH), f32),
    ]


def attention(first, me, counts, small, arrays, kvs, *before):
    bf16, f32 = jnp.bfloat16, jnp.float32
    blocks = KEY_VALUE_HEADS
    rows = kvs[0].shape[0]
    capacity = rows - INFO_ROWS
    columns = 2 * HEAD_SIZE
    plane_rows = 2 * capacity
    tile_count = plane_rows // ROW_TILE
    dq = (blocks, plane_rows // blocks, WIDTH)
    dqt = (tile_count, HEAD_SIZE, WIDTH)
    down = jax.ShapeDtypeStruct((rows, columns), bf16)
    flag = jax.ShapeDtypeStruct((1,), jnp.int32)
    if first:
        outs = (down, down, jax.ShapeDtypeStruct(dqt, f32), flag)
        more = []
    else:
        own = jax.ShapeDtypeStruct((capacity, columns), f32)
        outs = (down, jax.ShapeDtypeStruct(dq, bf16), own, flag)
        more = [
            pltpu.SemaphoreType.DMA((blocks,)),
            pltpu.VMEM(dq, bf16),
            pltpu.VMEM((capacity, columns), f32),
            pltpu.VMEM(dqt, f32),
        ]
    return pl.pallas_call(
        functools.partial(attention_kernel, first),
        out_shape=outs,
        in_specs=[SMEM] * 2 + [VMEM] + [HBM] * (11 + len(before)),
        out_specs=[HBM] * 3 + [SMEM],
        scratch_shapes=[
            pltpu.VMEM((plane_rows, WIDTH), bf16),
            pltpu.VMEM((plane_rows, WIDTH), bf16),
            pltpu.VMEM((tile_count, WIDTH), f32),
            pltpu.VMEM((tile_count, WIDTH), f32),
            pltpu.VMEM(dqt, f32),
            pltpu.VMEM((2, rows, columns), bf16),
            pltpu.VMEM((capacity, HEAD_SIZE), f32),
            pltpu.VMEM((capacity, HEAD_SIZE), f32),
            pltpu.SMEM((tile_count + 1,), jnp.int32),
            pltpu.SMEM((blocks,), jnp.int32),
            pltpu.SMEM((2,), jnp.int32),
            pltpu.SemaphoreType.DMA((2 * blocks,)),
            pltpu.SemaphoreType.DMA((2,)),
            pltpu.SemaphoreType.DMA((2,)),
            pltpu.SemaphoreType.DMA((tile_count,)),
            pltpu.VMEM((2, rows, columns), bf16),
            *more,
        ],
        compiler_params=pltpu.CompilerParams(vmem_limit_bytes=60 * 1024 * 1024),
        cost_estimate=pl.CostEstimate(
            flops=5_000_000_000, bytes_accessed=12_000_000, transcendentals=4_000_000
        ),
        name="attention",
    )(me, counts, small, *arrays, *kvs, *before)


def unpack_rows_kernel(parts, out):
    for g in range(KEY_VALUE_HEADS):
        out[:, g * WIDTH : (g + 1) * WIDTH] = parts[g]


def unpack_rows(parts):
    return pl.pallas_call(
        unpack_rows_kernel,
        out_shape=jax.ShapeDtypeStruct((parts.shape[1], KEY_VALUE_HEADS * WIDTH), parts.dtype),
        in_specs=[VMEM],
        out_specs=VMEM,
        name="unpack_rows",
    )(parts)


def combine_kernel(counts_ref, own, *rest):
    backs, out = rest[:3], rest[3]
    home_rows = out.shape[1]
    capacity = own.shape[0]
    total = own[...]
    for back in backs:
        total += back[:capacity, :].astype(jnp.float32)
    total = total.astype(jnp.bfloat16)
    within = lax.broadcasted_iota(jnp.int32, (home_rows, capacity), 0)
    place = lax.broadcasted_iota(jnp.int32, (home_rows, capacity), 1)
    start = jnp.int32(0)
    for block in range(KEY_VALUE_HEADS):
        count = counts_ref[block]
        hit = (place == within + start) & (within < count)
        out[block] = jnp.dot(
            jnp.where(hit, 1.0, 0.0).astype(jnp.bfloat16),
            total,
            preferred_element_type=jnp.float32,
        ).astype(jnp.bfloat16)
        start = start + count


def combine(counts, own, backs, home_rows):
    blocks = KEY_VALUE_HEADS
    return pl.pallas_call(
        combine_kernel,
        out_shape=jax.ShapeDtypeStruct((blocks, home_rows, own.shape[1]), jnp.bfloat16),
        in_specs=[SMEM] + [VMEM] * 4,
        out_specs=VMEM,
        compiler_params=pltpu.CompilerParams(vmem_limit_bytes=32 * 1024 * 1024),
        name="combine",
    )(counts, own, *backs)


def plane_device(queries, keys, values, outputs, output_gradient, lse, ranks):
    planes = lax.axis_size("outer")
    plane = ("inner", "head")
    blocks = KEY_VALUE_HEADS
    home_rows = queries.shape[0]
    plane_rows = blocks * home_rows
    capacity = plane_rows // 2
    surviving_tokens = BALANCED_TOKENS * planes * lax.axis_size("inner")
    bf16, f32 = jnp.bfloat16, jnp.float32
    me = lax.axis_index(plane).reshape(1).astype(jnp.int32)

    def swap(array, k):
        return lax.ppermute(array, plane, [(i, i ^ k) for i in range(blocks)])

    sent = pack_pairs(
        surviving_tokens, ranks, lse, keys, values, output_gradient, outputs
    )
    me, sent = lax.optimization_barrier((me, sent))
    arrived = lax.all_to_all(sent, plane, split_axis=0, concat_axis=0, tiled=True)
    *packed, beside = pack_rows(me, queries, output_gradient)
    pairs = [swap(rows, chip) for rows, chip in zip(packed, CHIPS)]
    beside = swap(beside, CORE)
    arrived, beside = lax.optimization_barrier((arrived, beside))
    mine, small, counts = compact(arrived)
    up = [lax.ppermute(mine, "outer", [(i, i + 1) for i in range(planes - 1)])]
    last = lax.ppermute(mine, "outer", [(0, planes - 1)])
    up.append(lax.ppermute(up[0], "outer", [(i, i + 1) for i in range(1, planes - 1)]))
    up.append(last)
    up[1], up[2], *pairs = lax.optimization_barrier((up[1], up[2], *pairs))
    crossed = [swap(pair[1:], CORE) for pair in pairs]
    arrays = [queries, output_gradient, beside, *pairs, *crossed]

    def lower(rows, k):
        return lax.ppermute(rows, "outer", [(i + k, i) for i in range(planes - k)])

    down2, down3, dqt, full1 = attention(True, me, counts, small, arrays, [up[1], up[2]])
    back2 = lower(down2, 2)
    down1, dq, own, full2 = attention(False, me, counts, small, arrays, [up[0], mine], dqt)
    dq, back2 = lax.optimization_barrier((dq, back2))
    backs = [lower(down3, 3), back2, lower(down1, 1)]
    dq = lax.all_to_all(dq, plane, split_axis=0, concat_axis=0, tiled=True)
    spread = combine(counts, own, backs, home_rows)
    dq, spread = lax.optimization_barrier((dq, spread))
    dq_home = unpack_rows(dq)
    kv_home = lax.all_to_all(spread, plane, split_axis=0, concat_axis=0, tiled=True)
    full = (full1[0] + full2[0]) > 0
    for back in backs:
        full = full | (back[capacity, 0] > 0)
    dk = kv_home[:, :, :HEAD_SIZE].transpose(1, 0, 2).reshape(home_rows, blocks * HEAD_SIZE)
    dv = kv_home[:, :, HEAD_SIZE:].transpose(1, 0, 2).reshape(home_rows, blocks * HEAD_SIZE)
    return (dq_home, dk, dv), full


def solution(mesh):
    spec = P(("seq", "head"), None)
    heads = mesh.shape["head"]
    inner = max(KEY_VALUE_HEADS // heads, 1)
    planes = mesh.shape["seq"] // inner
    if planes != 4 or inner * heads != KEY_VALUE_HEADS:
        return jax.shard_map(
            per_device,
            mesh=mesh,
            in_specs=(spec,) * 6 + (P(("seq", "head")),),
            out_specs=(spec,) * 3,
            check_vma=False,
        )
    axes = ("outer", "inner", "head")

    def device(*blocks):
        fast, full = plane_device(*blocks)
        return lax.cond(full, lambda: per_device(*blocks, seq=("outer", "inner")), lambda: fast)

    return jax.shard_map(
        device,
        mesh=Mesh(mesh.devices.reshape(planes, inner, heads), axes),
        in_specs=(P(axes, None),) * 6 + (P(axes),),
        out_specs=(P(axes, None),) * 3,
        check_vma=False,
    )
```
